32 devices in a mesh: seq: 8 (over z, y), ch: 4 (over x, core).
Axes of the slice: x: 2, y: 2, z: 4, core: 2. Of those that a mesh axis runs over, the one named last changes fastest.
Arguments:
- tokens_in: bfloat16 [4, 1024, 2048], P(None, 'seq', 'ch'), may hold values from -6 to 6
- modality: int32 [4, 1024], P(None, 'seq'), may hold values from 0 to 2, as said below
- starts: int32 [4, 2], replicated, may hold values from 0 to 640, as said below
- cotangent: bfloat16 [4, 1024, 2048], P(None, 'seq', 'ch'), may hold values from -6 to 6
- in_weight: float32 [3, 2048, 2, 4096], P(None, 'seq', None, 'ch'), may hold values from -0.125 to 0.125
- in_first: float32 [3, 2048, 2, 4096], P(None, 'seq', None, 'ch'), may hold values from -0.00018310547 to 0.00018310547
- in_second: float32 [3, 2048, 2, 4096], P(None, 'seq', None, 'ch'), may hold values from 3.2856215e-10 to 5.3075424e-09
- dt_weight: float32 [3, 128, 4096], P(None, 'seq', 'ch'), may hold values from -0.5 to 0.5
- dt_first: float32 [3, 128, 4096], P(None, 'seq', 'ch'), may hold values from -0.00018310547 to 0.00018310547
- dt_second: float32 [3, 128, 4096], P(None, 'seq', 'ch'), may hold values from 3.2856215e-10 to 5.3075424e-09
- out_weight: float32 [3, 2048, 4096], P(None, 'seq', 'ch'), may hold values from -0.09375 to 0.09375
- out_first: float32 [3, 2048, 4096], P(None, 'seq', 'ch'), may hold values from -0.00018310547 to 0.00018310547
- out_second: float32 [3, 2048, 4096], P(None, 'seq', 'ch'), may hold values from 3.2856215e-10 to 5.3075424e-09
- x_weight: float32 [3, 160, 4096], P(None, None, 'ch'), may hold values from -0.09375 to 0.09375
- x_first: float32 [3, 160, 4096], P(None, None, 'ch'), may hold values from -0.00018310547 to 0.00018310547
- x_second: float32 [3, 160, 4096], P(None, None, 'ch'), may hold values from 3.2856215e-10 to 5.3075424e-09
- channel_params: float32 [23, 4096], P(None, 'ch'), as said below
- channel_first: float32 [23, 4096], P(None, 'ch'), may hold values from -0.00018310547 to 0.00018310547
- channel_second: float32 [23, 4096], P(None, 'ch'), may hold values from 3.2856215e-10 to 5.3075424e-09
- gain: float32 [2048], replicated, may hold values from 0.28 to 3.2, as said below
- gain_first: float32 [2048], replicated, may hold values from -0.00018310547 to 0.00018310547
- gain_second: float32 [2048], replicated, may hold values from 3.2856215e-10 to 5.3075424e-09
Outputs:
- mixed: bfloat16 [4, 1024, 2048], P(None, 'seq', 'ch')
- input_grad: float32 [4, 1024, 2048], P(None, 'seq', 'ch')
- grad_norm: float32 [], replicated
- in_grad: float32 [3, 2048, 2, 4096], P(None, 'seq', None, 'ch')
- in_new: float32 [3, 2048, 2, 4096], P(None, 'seq', None, 'ch')
- in_first_new: float32 [3, 2048, 2, 4096], P(None, 'seq', None, 'ch')
- in_second_new: float32 [3, 2048, 2, 4096], P(None, 'seq', None, 'ch')
- dt_grad: float32 [3, 128, 4096], P(None, 'seq', 'ch')
- dt_new: float32 [3, 128, 4096], P(None, 'seq', 'ch')
- dt_first_new: float32 [3, 128, 4096], P(None, 'seq', 'ch')
- dt_second_new: float32 [3, 128, 4096], P(None, 'seq', 'ch')
- out_grad: float32 [3, 2048, 4096], P(None, 'seq', 'ch')
- out_new: float32 [3, 2048, 4096], P(None, 'seq', 'ch')
- out_first_new: float32 [3, 2048, 4096], P(None, 'seq', 'ch')
- out_second_new: float32 [3, 2048, 4096], P(None, 'seq', 'ch')
- x_grad: float32 [3, 160, 4096], P(None, None, 'ch')
- x_new: float32 [3, 160, 4096], P(None, None, 'ch')
- x_first_new: float32 [3, 160, 4096], P(None, None, 'ch')
- x_second_new: float32 [3, 160, 4096], P(None, None, 'ch')
- channel_grad: float32 [23, 4096], P(None, 'ch')
- channel_new: float32 [23, 4096], P(None, 'ch')
- channel_first_new: float32 [23, 4096], P(None, 'ch')
- channel_second_new: float32 [23, 4096], P(None, 'ch')
- gain_grad: float32 [2048], replicated
- gain_new: float32 [2048], replicated
- gain_first_new: float32 [2048], replicated
- gain_second_new: float32 [2048], replicated
- in_copy: bfloat16 [3, 2048, 2, 4096], P(None, 'seq', None, 'ch')
- dt_copy: bfloat16 [3, 128, 4096], P(None, 'seq', 'ch')
- out_copy: bfloat16 [3, 2048, 4096], P(None, 'seq', 'ch')
- x_copy: bfloat16 [3, 160, 4096], P(None, None, 'ch')
The draws below stay inside these ranges and needn't reach their ends.
Inputs may be any that keep to these rules, and one draw needn't show every extreme that they name: `modality`: 0 text, 1 image, 2 speech; the mix is drawn per block of 128 tokens to the next. Per micro-batch, start positions in ascending order, the first one 0; a repeated value starts nothing new. `gain`: positive norm gains. `channel_params`: rows in the order given by the argument's meaning.
All inputs are finite; a program needn't handle non-finite values.
Results may differ from the reference program's by a relative error of at most 0.012.
Values may be sent and summed in bfloat16 or wider, within the bound.
No kernel may reach another device: no remote copies, remote signals or barrier semaphores. Data moves between devices by JAX's collectives and lax.ppermute only.
A program may use at most 392 MiB of HBM per device.

```python
import math
import jax
import jax.numpy as jnp
from jax import lax

D = 2048
DI = 4096
N = 16
K = 4
R = 128
TOK_DEV = 128
MICRO = 4
SEQS = 2
STEP = 10
XW = 160
SEQ_TOKENS = 1024
PARAMS = 79132672


def draw_modality(key, part):
    key = jax.random.fold_in(key, 11)
    key_kind, key_dice = jax.random.split(key)
    blocks = SEQ_TOKENS // TOK_DEV
    heavy_text = jax.random.randint(key_kind, (MICRO, blocks, 1), 0, 2)
    dice_roll = jax.random.randint(key_dice, (MICRO, blocks, TOK_DEV), 0, 100)
    text_cut = 15 + 60 * heavy_text
    modal_ids = (dice_roll >= text_cut).astype(jnp.int32) + (dice_roll >= 90).astype(jnp.int32)
    return modal_ids.reshape(MICRO, SEQ_TOKENS).astype(jnp.int32)


def draw_starts(key, part):
    key = jax.random.fold_in(key, 12)
    key_whole, key_move = jax.random.split(key)
    whole_batch = jax.random.randint(key_whole, (), 0, MICRO)
    jitter_span = SEQ_TOKENS // (4 * SEQS)
    offsets_moved = jax.random.randint(key_move, (MICRO, SEQS), -jitter_span, jitter_span + 1)
    column = jnp.arange(SEQS, dtype=jnp.int32)[None, :]
    row_index = jnp.arange(MICRO, dtype=jnp.int32)[:, None]
    far_batch = (whole_batch + 1) % MICRO
    offsets_moved = jnp.where((row_index == far_batch) & (column == SEQS - 1), jitter_span, offsets_moved)
    start_base = column * (SEQ_TOKENS // SEQS) + offsets_moved
    start_base = jnp.where(column == 0, 0, start_base)
    return jnp.where(row_index == whole_batch, 0, start_base).astype(jnp.int32)


def draw_channel_params(key, part):
    key = jax.random.fold_in(key, 13)
    keys = jax.random.split(key, 6)
    conv_taps = 0.5 * jax.random.normal(keys[0], (K, DI))
    conv_bias = 0.5 * jax.random.normal(keys[1], (1, DI))
    slow_share = 5
    slow_mask = jax.random.randint(keys[2], (1, DI), 0, 10) < slow_share
    time_factor = jnp.exp(jax.random.uniform(keys[3], (1, DI), minval=-0.69, maxval=0.69))
    rate_factor = jnp.exp(jax.random.uniform(keys[4], (N, DI), minval=-0.69, maxval=0.69))
    root_len = float(SEQ_TOKENS) ** (-0.5)
    step_base = jnp.where(slow_mask, root_len, 0.1) * time_factor
    step_bias = jnp.log(jnp.expm1(step_base))
    rate_base = jnp.where(slow_mask, 0.5 * root_len, 0.25) * rate_factor
    skip_gain = jax.random.uniform(keys[5], (1, DI), minval=0.5, maxval=1.5)
    return jnp.concatenate([conv_taps, conv_bias, step_bias, skip_gain, jnp.log(rate_base)], 0).astype(jnp.float32)


def draw_gain(key, part):
    key = jax.random.fold_in(key, 14)
    ramp_line = jnp.arange(D, dtype=jnp.float32) / D
    return ((0.5 + 1.5 * ramp_line) * jax.random.uniform(key, (D,), minval=0.8, maxval=1.2)).astype(jnp.float32)


def level_of(own_key, shape, cuts, low, largest):
    def one(dim, shards_of):
        steps = jax.random.uniform(jax.random.fold_in(jax.random.fold_in(own_key, 6), dim), (shards_of,), jnp.float32, low / len(cuts), largest / len(cuts))
        return jnp.repeat(jnp.exp(steps), shape[dim] // shards_of).reshape((-1,) + (1,) * (len(shape) - dim - 1))

    factor_of = one(*cuts[0])
    for cut in cuts[1:]:
        factor_of = factor_of * one(*cut)
    return factor_of


def gaussian(rng, shape, spread, limit, cuts=(), kind=jnp.bfloat16):
    entries = jax.random.normal(rng, shape, jnp.float32) * spread
    if len(cuts) > 0:
        entries = level_of(rng, shape, cuts, -0.22, 0.18) * entries
    return jnp.clip(entries, min=-limit, max=limit).astype(kind)


def setup_inputs(seed: int = 0) -> dict:
    streams_of = jax.random.split(jax.random.key(seed), 23)
    return {
        "tokens_in": gaussian(streams_of[0], (MICRO, SEQ_TOKENS, D), 1.0, 6.0, ((1, 8), (2, 4))),
        "modality": draw_modality(jax.random.fold_in(streams_of[22], 71), 0),
        "starts": draw_starts(jax.random.fold_in(streams_of[22], 71), 0),
        "cotangent": gaussian(streams_of[3], (MICRO, SEQ_TOKENS, D), 1.0, 6.0, ((1, 8), (2, 4))),
        "in_weight": gaussian(streams_of[4], (3, D, 2, DI), D ** -0.5, 0.125, ((1, 8), (3, 4)), jnp.float32),
        "in_first": gaussian(streams_of[5], (3, D, 2, DI), (0.11 * PARAMS ** -0.5), 0.00018310547, ((1, 8), (3, 4)), jnp.float32),
        "in_second": jnp.clip(jnp.exp(math.log(5.30754240557485e-09) - 2.7821582 * jax.random.uniform(streams_of[6], (3, D, 2, DI), jnp.float32) ** level_of(streams_of[6], (3, D, 2, DI), ((1, 8), (3, 4)), -0.2, 0.2)), 3.2856214970955477e-10, 5.30754240557485e-09),
        "dt_weight": gaussian(streams_of[7], (3, R, DI), R ** -0.5, 0.5, ((1, 8), (2, 4)), jnp.float32),
        "dt_first": gaussian(streams_of[8], (3, R, DI), (0.11 * PARAMS ** -0.5), 0.00018310547, ((1, 8), (2, 4)), jnp.float32),
        "dt_second": jnp.clip(jnp.exp(math.log(5.30754240557485e-09) - 2.7821582 * jax.random.uniform(streams_of[9], (3, R, DI), jnp.float32) ** level_of(streams_of[9], (3, R, DI), ((1, 8), (2, 4)), -0.2, 0.2)), 3.2856214970955477e-10, 5.30754240557485e-09),
        "out_weight": gaussian(streams_of[10], (3, D, DI), DI ** -0.5, 0.09375, ((1, 8), (2, 4)), jnp.float32),
        "out_first": gaussian(streams_of[11], (3, D, DI), (0.11 * PARAMS ** -0.5), 0.00018310547, ((1, 8), (2, 4)), jnp.float32),
        "out_second": jnp.clip(jnp.exp(math.log(5.30754240557485e-09) - 2.7821582 * jax.random.uniform(streams_of[12], (3, D, DI), jnp.float32) ** level_of(streams_of[12], (3, D, DI), ((1, 8), (2, 4)), -0.2, 0.2)), 3.2856214970955477e-10, 5.30754240557485e-09),
        "x_weight": gaussian(streams_of[13], (3, XW, DI), DI ** -0.5, 0.09375, ((2, 4),), jnp.float32),
        "x_first": gaussian(streams_of[14], (3, XW, DI), (0.11 * PARAMS ** -0.5), 0.00018310547, ((2, 4),), jnp.float32),
        "x_second": jnp.clip(jnp.exp(math.log(5.30754240557485e-09) - 2.7821582 * jax.random.uniform(streams_of[15], (3, XW, DI), jnp.float32) ** level_of(streams_of[15], (3, XW, DI), ((2, 4),), -0.2, 0.2)), 3.2856214970955477e-10, 5.30754240557485e-09),
        "channel_params": draw_channel_params(jax.random.fold_in(streams_of[22], 71), 0),
        "channel_first": gaussian(streams_of[17], (K + 3 + N, DI), (0.11 * PARAMS ** -0.5), 0.00018310547, ((1, 4),), jnp.float32),
        "channel_second": jnp.clip(jnp.exp(math.log(5.30754240557485e-09) - 2.7821582 * jax.random.uniform(streams_of[18], (K + 3 + N, DI), jnp.float32) ** level_of(streams_of[18], (K + 3 + N, DI), ((1, 4),), -0.2, 0.2)), 3.2856214970955477e-10, 5.30754240557485e-09),
        "gain": draw_gain(jax.random.fold_in(streams_of[22], 71), 0),
        "gain_first": gaussian(streams_of[20], (D,), (0.11 * PARAMS ** -0.5), 0.00018310547, (), jnp.float32),
        "gain_second": jnp.clip(jnp.exp(jax.random.uniform(streams_of[21], (D,), jnp.float32, math.log(3.2856214970955477e-10), math.log(5.30754240557485e-09))), 3.2856214970955477e-10, 5.30754240557485e-09),
    }


HIGHEST_PREC = lax.Precision.HIGHEST
NORM_EPS = 1e-05
BETA_ONE = 0.9
BETA_TWO = 0.95
ADAM_EPS = 1e-08
DECAY = 0.1
CLIP_LIMIT = 1.0

@jax.custom_vjp
def low(v):
    return lax.optimization_barrier(v.astype(jnp.bfloat16)).astype(jnp.float32)

@jax.custom_vjp
def low_back(v):
    return v

def low_keep(v):
    return (low(v), None)

def low_pass(kept, grad):
    return (grad,)

def back_keep(v):
    return (v, None)

def back_low(kept, grad):
    return (low(grad),)
low.defvjp(low_keep, low_pass)
low_back.defvjp(back_keep, back_low)

def scan_tokens(carry, pieces):
    state, neg_rate = carry

    def one_token(hstate, item):
        step_size, value, b_row, c_row, keep_one = item
        hstate = jnp.exp(step_size[None, :] * neg_rate) * keep_one * hstate + (step_size * value)[None, :] * b_row[:, None]
        return (hstate, lax.optimization_barrier(jnp.sum(c_row[:, None] * hstate, axis=0)))
    state, outputs = lax.scan(one_token, state, pieces)
    return ((state, neg_rate), outputs)

def selective_scan(step_size, activated, b_mat, c_mat, keep_mask, neg_rate):
    length, chan_width = step_size.shape
    blocks = length // 64
    pieces = (step_size.reshape(blocks, 64, chan_width), activated.reshape(blocks, 64, chan_width), b_mat.reshape(blocks, 64, N), c_mat.reshape(blocks, 64, N), keep_mask.reshape(blocks, 64))
    start_state = (jnp.zeros((N, chan_width), jnp.float32), neg_rate)
    final_state, outputs = lax.scan(jax.checkpoint(scan_tokens), start_state, pieces)
    return outputs.reshape(length, chan_width)

def mamba_block(row_block, modal_ids, start_row, in16, dt16, out16, x16, channel, gains):
    length = row_block.shape[0]
    inv_rms = lax.rsqrt(lax.optimization_barrier(jnp.mean(row_block * row_block, axis=-1, keepdims=True)) + NORM_EPS)
    normed = low(row_block * inv_rms * gains)
    masks = [modal_ids == k for k in range(3)]
    projected = sum((jnp.where(masks[k][:, None, None], jnp.einsum('td,dgc->tgc', normed, in16[k], precision=HIGHEST_PREC), 0.0) for k in range(3)))
    projected = low_back(projected)
    inner_part = projected[:, 0]
    gate_part = projected[:, 1]
    positions = jnp.arange(length, dtype=jnp.int32)
    segment = lax.optimization_barrier(jnp.sum((start_row[None, :] <= positions[:, None]).astype(jnp.int32), axis=1))
    keep_mask = 1.0 - jnp.any(start_row[None, :] == positions[:, None], axis=1).astype(jnp.float32)
    padded = jnp.concatenate([jnp.zeros((K - 1, inner_part.shape[1]), jnp.float32), inner_part], 0)
    seg_pad = jnp.concatenate([jnp.full((K - 1,), -1, jnp.int32), segment], 0)
    conv_out = channel[K][None, :] + sum((channel[j][None, :] * padded[K - 1 - j:K - 1 - j + length] * (seg_pad[K - 1 - j:K - 1 - j + length] == segment).astype(jnp.float32)[:, None] for j in range(K)))
    activated = low(jax.nn.silu(conv_out))
    projected_x = low_back(sum((jnp.where(masks[k][:, None], jnp.dot(activated, x16[k].T, precision=HIGHEST_PREC), 0.0) for k in range(3))))
    dt_low = low(projected_x[:, :R])
    b_mat = projected_x[:, R:R + N]
    c_mat = projected_x[:, R + N:]
    dt_pre = low_back(sum((jnp.where(masks[k][:, None], jnp.dot(dt_low, dt16[k], precision=HIGHEST_PREC), 0.0) for k in range(3))) + channel[K + 1][None, :])
    step_size = jax.nn.softplus(dt_pre)
    neg_rate = -jnp.exp(channel[K + 3:K + 3 + N])
    y_scan = selective_scan(step_size, activated, b_mat, c_mat, keep_mask, neg_rate) + channel[K + 2][None, :] * activated
    mixed_in = low(y_scan * jax.nn.silu(gate_part))
    branch = sum((jnp.where(masks[k][:, None], jnp.dot(mixed_in, out16[k].T, precision=HIGHEST_PREC), 0.0) for k in range(3)))
    return row_block + branch

def adam_update(weight, gradient, first_moment, second, clip_scale, step_rate):
    clipped = gradient * clip_scale
    first_new = BETA_ONE * first_moment + (1.0 - BETA_ONE) * clipped
    second_new = BETA_TWO * second + (1.0 - BETA_TWO) * clipped * clipped
    first_hat = first_new / (1.0 - BETA_ONE ** STEP)
    second_hat = second_new / (1.0 - BETA_TWO ** STEP)
    weight_new = weight - step_rate * (first_hat / (jnp.sqrt(second_hat) + ADAM_EPS) + DECAY * weight)
    return (weight_new, first_new, second_new)

def reference(tokens_in, modality, starts, cotangent, in_weight, in_first, in_second, dt_weight, dt_first, dt_second, out_weight, out_first, out_second, x_weight, x_first, x_second, channel_params, channel_first, channel_second, gain, gain_first, gain_second):

    def forward(row_all, w_in, w_dt, w_out, w_x, channel, gains):
        in16 = low(w_in)
        dt16 = low(w_dt)
        out16 = low(w_out)
        x16 = low(w_x)
        results = [mamba_block(row_all[m], modality[m], starts[m], in16, dt16, out16, x16, channel, gains) for m in range(MICRO)]
        return jnp.stack(results)
    primal, pull = jax.vjp(forward, tokens_in.astype(jnp.float32), in_weight, dt_weight, out_weight, x_weight, channel_params, gain)
    grads = pull(cotangent.astype(jnp.float32))
    mixed = primal.astype(jnp.bfloat16)
    input_grad = grads[0]
    g_in, g_dt, g_out, g_x, g_chan, g_gain = grads[1:]
    grad_norm = jnp.sqrt(sum((jnp.sum(g * g) for g in grads[1:])))
    clip_scale = CLIP_LIMIT / jnp.maximum(grad_norm, CLIP_LIMIT)
    in_new, in_first_new, in_second_new = adam_update(in_weight, g_in, in_first, in_second, clip_scale, D ** (-0.5))
    dt_new, dt_first_new, dt_second_new = adam_update(dt_weight, g_dt, dt_first, dt_second, clip_scale, R ** (-0.5))
    out_new, out_first_new, out_second_new = adam_update(out_weight, g_out, out_first, out_second, clip_scale, DI ** (-0.5))
    x_new, x_first_new, x_second_new = adam_update(x_weight, g_x, x_first, x_second, clip_scale, DI ** (-0.5))
    chan_new, chan_first_new, chan_second_new = adam_update(channel_params, g_chan, channel_first, channel_second, clip_scale, 0.5)
    gain_new, gain_first_new, gain_second_new = adam_update(gain, g_gain, gain_first, gain_second, clip_scale, 0.5)
    return (mixed, input_grad, grad_norm, g_in, in_new, in_first_new, in_second_new, g_dt, dt_new, dt_first_new, dt_second_new, g_out, out_new, out_first_new, out_second_new, g_x, x_new, x_first_new, x_second_new, g_chan, chan_new, chan_first_new, chan_second_new, g_gain, gain_new, gain_first_new, gain_second_new, in_new.astype(jnp.bfloat16), dt_new.astype(jnp.bfloat16), out_new.astype(jnp.bfloat16), x_new.astype(jnp.bfloat16))
```

```python
import functools

import jax
import jax.numpy as jnp
from jax import lax
from jax.experimental import pallas as pl
from jax.experimental.pallas import tpu as pltpu
from jax.sharding import Mesh
from jax.sharding import PartitionSpec as P

N = 16
K = 4
STEP = 10

NORM_EPS = 1e-05
BETA_ONE = 0.9
BETA_TWO = 0.95
ADAM_EPS = 1e-08
DECAY = 0.1
CLIP_LIMIT = 1.0
LANES = 128
SCAN_ROWS = 128
GROUP = 2
f32 = jnp.float32
bf16 = jnp.bfloat16


def silu_grad(value):
    sigma = jax.nn.sigmoid(value)
    return sigma * (1.0 + value * (1.0 - sigma))


def adam_update(weight, gradient, first_moment, second, clip_scale, step_rate):
    clipped = gradient * clip_scale
    first_new = BETA_ONE * first_moment + (1.0 - BETA_ONE) * clipped
    second_new = BETA_TWO * second + (1.0 - BETA_TWO) * clipped * clipped
    first_hat = first_new / (1.0 - BETA_ONE**STEP)
    second_hat = second_new / (1.0 - BETA_TWO**STEP)
    weight_new = weight - step_rate * (
        first_hat / (jnp.sqrt(second_hat) + ADAM_EPS) + DECAY * weight
    )
    return (weight_new, first_new, second_new)


def scan_forward_kernel(
    step_ref, act_ref, pull_ref, keep_ref, b_ref, c_ref, rate_ref, start_ref,
    y_ref, before_ref, grad_c_ref, final_ref, state_ref,
):
    micros, rows, _ = step_ref.shape
    block = pl.program_id(0)
    rate = rate_ref[...]
    lane = lax.broadcasted_iota(jnp.int32, (N, LANES), 1)

    @pl.when(block == 0)
    def _():
        state_ref[...] = start_ref[...]

    def eight(turn, carried):
        states, b_now, c_now, grads = carried
        states, b_now, c_now, grads = list(states), list(b_now), list(c_now), list(grads)
        base = pl.multiple_of(turn * 8, 8)
        for m in range(micros):
            grads[m] = pltpu.roll(grads[m], LANES - 8, 1)
        for j in range(8):
            for m in range(micros):
                row = pl.ds(base + j, 1)
                step_row = step_ref[m, row, :]
                drive_row = step_row * act_ref[m, row, :]
                pull_row = pull_ref[m, row, :]
                keep = keep_ref[m, block * rows + base + j]
                before = states[m]
                before_ref[m, base + j] = before
                state = jnp.exp(step_row * rate) * (before * keep) + drive_row * b_now[m][:, j : j + 1]
                states[m] = state
                y_ref[m, row, :] = jnp.sum(state * c_now[m][:, j : j + 1], axis=0, keepdims=True)
                lane_sum = jnp.sum(state * pull_row, axis=1, keepdims=True)
                grads[m] = jnp.where(lane == LANES - 8 + j, lane_sum, grads[m])
        for m in range(micros):
            b_now[m] = pltpu.roll(b_now[m], LANES - 8, 1)
            c_now[m] = pltpu.roll(c_now[m], LANES - 8, 1)
        return (tuple(states), tuple(b_now), tuple(c_now), tuple(grads))

    begin = (
        tuple(state_ref[m] for m in range(micros)),
        tuple(b_ref[m] for m in range(micros)),
        tuple(c_ref[m] for m in range(micros)),
        tuple(jnp.zeros((N, LANES), f32) for m in range(micros)),
    )
    states, _, _, grads = lax.fori_loop(0, rows // 8, eight, begin)
    for m in range(micros):
        state_ref[m] = states[m]
        grad_c_ref[m] = grads[m]
        final_ref[m] = states[m]


def scan_forward(step, act, pull, keep, b_t, c_t, rate, start):
    micros, length, _ = step.shape
    tall = pl.BlockSpec((micros, SCAN_ROWS, LANES), lambda i: (0, i, 0))
    wide = pl.BlockSpec((micros, N, SCAN_ROWS), lambda i: (0, 0, i))
    fixed = pl.BlockSpec((micros, N, LANES), lambda i: (0, 0, 0))
    return pl.pallas_call(
        scan_forward_kernel,
        grid=(length // SCAN_ROWS,),
        in_specs=[
            tall, tall, tall,
            pl.BlockSpec(memory_space=pltpu.SMEM),
            wide, wide,
            pl.BlockSpec((N, LANES), lambda i: (0, 0)),
            fixed,
        ],
        out_specs=[
            tall,
            pl.BlockSpec((micros, SCAN_ROWS, N, LANES), lambda i: (0, i, 0, 0)),
            wide,
            fixed,
        ],
        out_shape=[
            jax.ShapeDtypeStruct((micros, length, LANES), f32),
            jax.ShapeDtypeStruct((micros, length, N, LANES), f32),
            jax.ShapeDtypeStruct((micros, N, length), f32),
            jax.ShapeDtypeStruct((micros, N, LANES), f32),
        ],
        scratch_shapes=[pltpu.VMEM((micros, N, LANES), f32)],
        cost_estimate=pl.CostEstimate(
            flops=micros * length * N * LANES * 40,
            bytes_accessed=micros * length * N * LANES * 4,
            transcendentals=micros * length * N * LANES,
        ),
        compiler_params=pltpu.CompilerParams(
            dimension_semantics=("arbitrary",), vmem_limit_bytes=24 * 1024 * 1024
        ),
        name="scan_forward",
    )(step, act, pull, keep, b_t, c_t, rate, start)


def scan_backward_kernel(
    step_ref, act_ref, pull_ref, keep_ref, b_ref, c_ref, rate_ref, start_ref, before_ref,
    b_pull_ref, rate_pull_ref, grad_b_ref, grad_rate_ref, final_ref, state_ref,
):
    micros, rows, _ = step_ref.shape
    block = pl.num_programs(0) - 1 - pl.program_id(0)
    rate = rate_ref[...]
    lane = lax.broadcasted_iota(jnp.int32, (N, LANES), 1)

    @pl.when(pl.program_id(0) == 0)
    def _():
        state_ref[...] = start_ref[...]
        grad_rate_ref[...] = jnp.zeros_like(grad_rate_ref)

    def eight(turn, carried):
        states, b_now, c_now, grads, rates = (list(part) for part in carried)
        base = pl.multiple_of(rows - 8 - turn * 8, 8)
        for m in range(micros):
            grads[m] = pltpu.roll(grads[m], 8, 1)
            b_now[m] = pltpu.roll(b_now[m], 8, 1)
            c_now[m] = pltpu.roll(c_now[m], 8, 1)
        for j in range(7, -1, -1):
            for m in range(micros):
                row = pl.ds(base + j, 1)
                step_row = step_ref[m, row, :]
                drive_row = step_row * act_ref[m, row, :]
                pull_row = pull_ref[m, row, :]
                keep = keep_ref[m, block * rows + base + j]
                adjoint = c_now[m][:, j : j + 1] * pull_row + states[m]
                passed = jnp.exp(step_row * rate) * (adjoint * keep)
                states[m] = passed
                decay_pull = passed * before_ref[m, base + j]
                b_pull_ref[m, row, :] = jnp.sum(
                    adjoint * b_now[m][:, j : j + 1], axis=0, keepdims=True
                )
                rate_pull_ref[m, row, :] = jnp.sum(decay_pull * rate, axis=0, keepdims=True)
                rates[m] = rates[m] + decay_pull * step_row
                lane_sum = jnp.sum(adjoint * drive_row, axis=1, keepdims=True)
                grads[m] = jnp.where(lane == j, lane_sum, grads[m])
        return (tuple(states), tuple(b_now), tuple(c_now), tuple(grads), tuple(rates))

    zeros = tuple(jnp.zeros((N, LANES), f32) for m in range(micros))
    begin = (
        tuple(state_ref[m] for m in range(micros)),
        tuple(b_ref[m] for m in range(micros)),
        tuple(c_ref[m] for m in range(micros)),
        zeros,
        zeros,
    )
    states, _, _, grads, rates = lax.fori_loop(0, rows // 8, eight, begin)
    for m in range(micros):
        state_ref[m] = states[m]
        grad_b_ref[m] = grads[m]
        grad_rate_ref[m] += rates[m]
        final_ref[m] = states[m]


def scan_backward(step, act, pull, keep, b_t, c_t, rate, start, before):
    micros, length, _ = step.shape
    last = length // SCAN_ROWS - 1
    tall = pl.BlockSpec((micros, SCAN_ROWS, LANES), lambda i: (0, last - i, 0))
    wide = pl.BlockSpec((micros, N, SCAN_ROWS), lambda i: (0, 0, last - i))
    fixed = pl.BlockSpec((micros, N, LANES), lambda i: (0, 0, 0))
    return pl.pallas_call(
        scan_backward_kernel,
        grid=(length // SCAN_ROWS,),
        in_specs=[
            tall, tall, tall,
            pl.BlockSpec(memory_space=pltpu.SMEM),
            wide, wide,
            pl.BlockSpec((N, LANES), lambda i: (0, 0)),
            fixed,
            pl.BlockSpec((micros, SCAN_ROWS, N, LANES), lambda i: (0, last - i, 0, 0)),
        ],
        out_specs=[tall, tall, wide, fixed, fixed],
        out_shape=[
            jax.ShapeDtypeStruct((micros, length, LANES), f32),
            jax.ShapeDtypeStruct((micros, length, LANES), f32),
            jax.ShapeDtypeStruct((micros, N, length), f32),
            jax.ShapeDtypeStruct((micros, N, LANES), f32),
            jax.ShapeDtypeStruct((micros, N, LANES), f32),
        ],
        scratch_shapes=[pltpu.VMEM((micros, N, LANES), f32)],
        cost_estimate=pl.CostEstimate(
            flops=micros * length * N * LANES * 60,
            bytes_accessed=micros * length * N * LANES * 4,
            transcendentals=micros * length * N * LANES,
        ),
        compiler_params=pltpu.CompilerParams(
            dimension_semantics=("arbitrary",), vmem_limit_bytes=24 * 1024 * 1024
        ),
        name="scan_backward",
    )(step, act, pull, keep, b_t, c_t, rate, start, before)


def body(
    groups, parts, chans,
    tokens_in, modality, starts, cotangent,
    in_weight, in_first, in_second,
    dt_weight, dt_first, dt_second,
    out_weight, out_first, out_second,
    x_weight, x_first, x_second,
    channel_params, channel_first, channel_second,
    gain, gain_first, gain_second,
):
    micros, tok_rows, part_width = tokens_in.shape
    model = gain.shape[0]
    own_rows = in_weight.shape[1]
    chan_width = in_weight.shape[3]
    half = chan_width // 2
    own = half // chans
    inner_all = chan_width * chans
    x_width = x_weight.shape[1]
    rank = x_width - 2 * N
    dt_rows = dt_weight.shape[1]
    span = parts * tok_rows
    edge = K - 1
    t_at = lax.axis_index("t")
    p_at = lax.axis_index("p")
    c_at = lax.axis_index("c")
    odd = p_at % 2
    s_at = t_at * parts + p_at
    everywhere = ("t", "p", "c")

    order = [0]
    bit = chans // 2
    while bit >= 1:
        order = order + [k ^ bit for k in order]
        bit //= 2

    def flat(t, p, c):
        return (t * parts + p) * chans + c

    def round_pairs(turn):
        pairs = []
        for t in range(groups):
            for p in range(parts):
                for c in range(chans):
                    s = t * parts + p
                    to_t = (s % (2 * groups)) // 2
                    to_p = 2 * c + (turn + p) % 2
                    pairs.append((flat(t, p, c), flat(to_t, to_p, s // (2 * groups))))
        return pairs

    small_pairs = [
        (flat(t, p, c), flat(t, 2 * c + p % 2, p // 2))
        for t in range(groups)
        for p in range(parts)
        for c in range(chans)
    ]

    def send(value, pairs, back=False):
        if back:
            pairs = [(b, a) for a, b in pairs]
        return lax.ppermute(value, everywhere, pairs)

    def swap(value, distance):
        return lax.ppermute(value, "c", [(i, i ^ distance) for i in range(chans)])

    def along_groups(value, by):
        pairs = [(i, i + by) for i in range(groups) if 0 <= i + by < groups]
        return lax.ppermute(value, "t", pairs)

    def gather_chans(value):
        distance = chans // 2
        while distance >= 1:
            value = jnp.concatenate([value, swap(value, distance)], -1)
            distance //= 2
        return value

    def scatter_chans(keep, sent):
        distance = 1
        out = sent().astype(bf16)
        got = swap(out, distance)
        total = keep() + got.astype(f32)
        distance *= 2
        while distance < chans:
            width = total.shape[-1] // 2
            got = swap(total[..., width:].astype(bf16), distance)
            total = total[..., :width] + got.astype(f32)
            distance *= 2
        return total

    to_c = s_at // (2 * groups)

    def rel_blocks(value, turn, width):
        piece = (turn + p_at) % 2
        return jnp.concatenate(
            [
                lax.dynamic_slice_in_dim(
                    value, piece * half + (to_c ^ k) * own, own, value.ndim - 1
                )
                for k in order
            ],
            -1,
        )

    def rows_in_order(first, second):
        low = jnp.where(odd == 0, first, second)
        high = jnp.where(odd == 0, second, first)
        full = jnp.concatenate([low, high], 1)
        if groups > 1:
            full = lax.all_gather(full, "t", axis=1, tiled=True)
        return full

    in16 = in_weight.astype(bf16)
    sent_in = [
        jnp.concatenate(
            [rel_blocks(in16[:, :, 0], turn, own), rel_blocks(in16[:, :, 1], turn, own)], -1
        )
        for turn in range(2)
    ]
    got_in = [send(sent_in[turn], round_pairs(turn)) for turn in range(2)]
    out16 = jnp.concatenate([out_weight.astype(bf16), dt_weight.astype(bf16)], 1)
    got_out = [send(rel_blocks(out16, turn, own), round_pairs(turn)) for turn in range(2)]
    small = jnp.concatenate([x_weight.reshape(3 * x_width, chan_width), channel_params], 0)
    small = lax.dynamic_slice_in_dim(small, odd * half + (p_at // 2) * own, own, 1)
    small = send(small, small_pairs)

    tokens_all = lax.all_gather(tokens_in, "p")
    back_all = lax.all_gather(cotangent, "p")
    tok_float = tokens_in.astype(f32)
    stat = jnp.stack(
        [
            jnp.sum(tok_float * tok_float, axis=-1),
            jnp.where(c_at == 0, modality.astype(f32), 0.0),
        ]
    )
    slots = (jnp.arange(parts) == p_at).astype(f32)
    stat = lax.psum(stat[:, :, None, :] * slots[None, None, :, None], ("p", "c"))
    stat = stat.reshape(2, micros, span)
    inv_all = lax.rsqrt(stat[0] / model + NORM_EPS)
    kinds = (stat[1] + 0.5).astype(jnp.int32)
    inv_own = lax.dynamic_slice_in_dim(inv_all, p_at * tok_rows, tok_rows, 1)[..., None]
    tokens_all = tokens_all.transpose(1, 0, 2, 3).reshape(micros, span, part_width)
    back_all = back_all.transpose(1, 0, 2, 3).reshape(micros, span, part_width)
    gain_part = lax.dynamic_slice_in_dim(gain, c_at * part_width, part_width, 0)

    w_in = rows_in_order(*got_in)
    w_inner = w_in[..., :half]
    w_gate = w_in[..., half:]
    low_half = half // 2
    w_keep = jnp.concatenate([w_inner[..., :low_half], w_gate[..., :low_half]], -1)
    w_sent = jnp.concatenate([w_inner[..., low_half:], w_gate[..., low_half:]], -1)
    w_out = rows_in_order(*(g[:, :own_rows] for g in got_out))
    dt_part = rows_in_order(*(g[:, own_rows:] for g in got_out))
    dt_all = lax.all_gather(dt_part, "c")
    place = jnp.array([order.index(k) for k in range(chans)], jnp.int32)
    w_dt = jnp.concatenate(
        [
            lax.dynamic_slice_in_dim(dt_all[k], place[c_at ^ k] * own, own, 2)
            for k in range(chans)
        ],
        1,
    )
    w_x = small[: 3 * x_width].astype(bf16).reshape(3, x_width, own)
    channel = small[3 * x_width :]
    conv_taps = channel[:K]
    conv_bias = channel[K]
    dt_bias = channel[K + 1]
    skip_gain = channel[K + 2]
    neg_rate = -jnp.exp(channel[K + 3 :])

    def by_kind(value, kind):
        pick = (kind[:, None] == jnp.arange(3)[None, :])[:, :, None]
        return jnp.where(pick, value[:, None, :], jnp.zeros((), value.dtype))

    def dot(spec, left, right):
        return jnp.einsum(spec, left, right, preferred_element_type=f32)

    acc = dict(gate=0.0, inner=0.0, out=0.0, dt=0.0, x=0.0, chan=0.0, gain=0.0)
    outs, rows_back = [], []

    chunk = min(GROUP, micros)
    def summed(value, at):
        return lax.psum(value, ("p", "c") if at == 0 else ("c", "p"))

    for at in range(0, micros, chunk):
        ms = slice(at, at + chunk)
        kind = kinds[ms].reshape(-1)
        x_hat = tokens_all[ms].astype(f32) * inv_all[ms][..., None]
        normed = (x_hat * gain_part).astype(bf16).reshape(-1, part_width)
        normed3 = by_kind(normed, kind)
        back3 = by_kind(back_all[ms].reshape(-1, part_width), kind)
        projected = scatter_chans(
            lambda: dot("tkd,kde->te", normed3, w_keep).reshape(-1, 2, low_half),
            lambda: dot("tkd,kde->te", normed3, w_sent).reshape(-1, 2, low_half),
        ).reshape(chunk, span, 2, own)
        d_mixed = scatter_chans(
            lambda: dot("tkd,kdc->tc", back3, w_out[..., :low_half]),
            lambda: dot("tkd,kdc->tc", back3, w_out[..., low_half:]),
        ).reshape(chunk, span, own)
        inner_part = projected[:, :, 0]
        gate_part = projected[:, :, 1]
        positions = t_at * span - edge + jnp.arange(span + 2 * edge, dtype=jnp.int32)
        begin = starts[ms]
        segment = jnp.sum(
            (begin[:, None, :] <= positions[None, :, None]).astype(jnp.int32), axis=2
        )
        keep_mask = 1.0 - jnp.any(
            begin[:, None, :] == positions[None, edge : edge + span, None], axis=2
        ).astype(f32)
        same_doc = [
            (
                segment[:, edge - j : edge - j + span + edge]
                == segment[:, edge : edge + span + edge]
            ).astype(f32)[..., None]
            for j in range(K)
        ]
        none = jnp.zeros((chunk, edge, own), f32)
        before = along_groups(inner_part[:, span - edge :], 1) if groups > 1 else none
        padded = jnp.concatenate([before, inner_part], 1)
        conv_out = conv_bias + sum(
            conv_taps[j] * padded[:, edge - j : edge - j + span] * same_doc[j][:, :span]
            for j in range(K)
        )
        activated = jax.nn.silu(conv_out).astype(bf16)
        act_float = activated.astype(f32)
        act3 = by_kind(activated.reshape(-1, own), kind)
        projected_x = summed(dot("tkc,kxc->tx", act3, w_x), at)
        dt_low = projected_x[:, :rank].astype(bf16)
        mats = projected_x[:, rank:].reshape(chunk, span, 2, N).transpose(2, 0, 3, 1)
        low3 = by_kind(dt_low, kind)
        dt_pre = dot("tkr,krc->tc", low3, w_dt).reshape(chunk, span, own) + dt_bias
        step_size = jax.nn.softplus(dt_pre)
        gate_act = jax.nn.silu(gate_part)
        d_scan = d_mixed * gate_act
        zero_state = jnp.zeros((chunk, N, own), f32)
        args = (step_size, act_float, d_scan, keep_mask, mats[0], mats[1], neg_rate)
        state_in = zero_state
        if groups > 1:
            ends = scan_forward(*args, zero_state)[3]
            whole = jnp.exp(jnp.sum(step_size, axis=1)[:, None, :] * neg_rate)
            whole = whole * jnp.prod(keep_mask, axis=1)[:, None, None]
            for _ in range(groups - 1):
                state_in = along_groups(whole * state_in + ends, 1)
        y_part, states_before, grad_c, _ = scan_forward(*args, state_in)
        y_scan = y_part + skip_gain * act_float
        mixed_in = (y_scan * gate_act).astype(bf16)
        d_gate = (d_mixed * y_scan * silu_grad(gate_part)).astype(bf16)
        pair = gather_chans(jnp.stack([mixed_in, d_gate]).reshape(2, chunk * span, own))
        mixed_row, gate_row = pair[0], pair[1]
        mixed3 = by_kind(mixed_row, kind)
        partial_out = dot("tkc,kdc->td", mixed3, w_out)
        partial_out = partial_out.reshape(chunk, parts, tok_rows, part_width).transpose(1, 0, 2, 3)
        outs.append(lax.psum_scatter(partial_out.astype(bf16), "p", scatter_dimension=0))
        acc["out"] += dot("tkd,tc->kdc", back3, mixed_row)
        acc["gate"] += dot("tkd,te->kde", normed3, gate_row)

        adj_in = zero_state
        if groups > 1:
            ends = scan_backward(*args, zero_state, states_before)[4]
            for _ in range(groups - 1):
                adj_in = along_groups(whole * adj_in + ends, -1)
        b_pull, rate_pull, grad_b, grad_rate, _ = scan_backward(*args, adj_in, states_before)
        d_step = rate_pull + act_float * b_pull
        d_rate = jnp.sum(grad_rate, axis=0) * neg_rate
        d_act = d_scan * skip_gain + step_size * b_pull
        d_skip = jnp.sum(d_scan * act_float, axis=(0, 1))
        d_pre = (d_step * jax.nn.sigmoid(dt_pre)).astype(bf16)
        d_bias = jnp.sum(d_pre.astype(f32), axis=(0, 1))
        d_pre = d_pre.reshape(-1, own)
        d_low = dot("tkc,krc->tr", by_kind(d_pre, kind), w_dt)
        acc["dt"] += dot("tkr,tc->krc", low3, d_pre)
        grad_bc = jnp.stack([grad_b, grad_c]).transpose(1, 3, 0, 2).reshape(-1, 2 * N)
        d_projx = summed(jnp.concatenate([d_low, grad_bc], 1), at).astype(bf16)
        projx3 = by_kind(d_projx, kind)
        d_act = d_act + dot("tkx,kxc->tc", projx3, w_x).reshape(chunk, span, own)
        acc["x"] += dot("tkx,tc->kxc", projx3, activated.reshape(-1, own))
        d_conv = d_act * silu_grad(conv_out)
        after = along_groups(d_conv[:, :edge], -1) if groups > 1 else none
        d_conv_ext = jnp.concatenate([d_conv, after], 1)
        d_inner = sum(
            conv_taps[j] * d_conv_ext[:, j : j + span] * same_doc[j][:, j : j + span]
            for j in range(K)
        )
        d_taps = jnp.stack(
            [
                jnp.sum(
                    d_conv * padded[:, edge - j : edge - j + span] * same_doc[j][:, :span],
                    axis=(0, 1),
                )
                for j in range(K)
            ]
        )
        d_conv_bias = jnp.sum(d_conv, axis=(0, 1))
        acc["chan"] += jnp.concatenate(
            [d_taps, d_conv_bias[None], d_bias[None], d_skip[None], d_rate], 0
        )
        inner_row = gather_chans(d_inner.astype(bf16).reshape(-1, own))
        acc["inner"] += dot("tkd,te->kde", normed3, inner_row)
        d_normed = dot("tke,kde->td", by_kind(gate_row, kind), w_gate) + dot(
            "tke,kde->td", by_kind(inner_row, kind), w_inner
        )
        acc["gain"] += jnp.sum(d_normed * x_hat.reshape(-1, part_width), axis=0)
        d_normed = d_normed.reshape(chunk, parts, tok_rows, part_width).transpose(1, 0, 2, 3)
        rows_back.append(lax.psum_scatter(d_normed.astype(bf16), "p", scatter_dimension=0))

    def over_groups(value):
        return lax.psum(value, "t") if groups > 1 else value

    def rows_of_group(value):
        if groups > 1:
            return lax.psum_scatter(value, "t", scatter_dimension=1, tiled=True)
        return value

    g_gate = rows_of_group(acc["gate"])
    g_inner = rows_of_group(acc["inner"])
    g_out = rows_of_group(acc["out"])
    g_small = over_groups(
        jnp.concatenate([acc["x"].reshape(3 * x_width, own), acc["chan"]], 0)
    )
    g_dt = over_groups(acc["dt"])
    local_sq = (
        jnp.sum(g_gate * g_gate)
        + jnp.sum(g_inner * g_inner)
        + jnp.sum(g_out * g_out)
        + (jnp.sum(g_small * g_small) + jnp.sum(g_dt * g_dt)) / groups
    )
    here = (jnp.arange(chans) == c_at).astype(f32)
    tail = jnp.concatenate([(here[:, None] * acc["gain"]).reshape(-1), local_sq[None]])
    tail = lax.psum(tail, everywhere)
    grad_gain = tail[:model]
    grad_norm = jnp.sqrt(tail[model] + jnp.sum(grad_gain * grad_gain))
    clip_scale = CLIP_LIMIT / jnp.maximum(grad_norm, CLIP_LIMIT)

    def piece_rows(value, rows, turn):
        return lax.dynamic_slice_in_dim(value, ((turn + p_at) % 2) * rows, rows, 1)

    def send_back(value, rows):
        return [send(piece_rows(value, rows, turn), round_pairs(turn), True) for turn in range(2)]

    def chan_order(first, second, relative):
        low = jnp.where(odd == 0, first, second).astype(f32)
        high = jnp.where(odd == 0, second, first).astype(f32)
        both = jnp.concatenate([low, high], -1)
        if not relative:
            return both
        return jnp.concatenate(
            [
                lax.dynamic_slice_in_dim(
                    both, base * half + place[to_c ^ k] * own, own, both.ndim - 1
                )
                for base in range(2)
                for k in range(chans)
            ],
            -1,
        )

    grad_out = chan_order(*send_back(g_out.astype(bf16), own_rows), True)
    grad_gate = chan_order(*send_back(g_gate.astype(bf16), own_rows), True)
    grad_inner = chan_order(*send_back(g_inner.astype(bf16), own_rows), True)
    grad_in = jnp.stack([grad_inner, grad_gate], 2)
    dt_by_c = lax.all_gather(g_dt, "c")
    dt_slice = lax.dynamic_slice_in_dim(
        dt_by_c, (c_at * groups + t_at) * 2 * dt_rows, 2 * dt_rows, 2
    )
    dt_slice = dt_slice.transpose(1, 2, 0, 3).reshape(3, 2 * dt_rows, half)
    grad_dt = chan_order(*send_back(dt_slice, dt_rows), False)
    small_back = lax.all_gather(send(g_small, small_pairs, True), "p")
    small_back = small_back.reshape(chans, 2, -1, own).transpose(2, 1, 0, 3).reshape(-1, chan_width)
    grad_x = small_back[: 3 * x_width].reshape(3, x_width, chan_width)
    grad_chan = small_back[3 * x_width :]

    mixed = (
        tok_float + jnp.concatenate(outs, 0).astype(f32)
    ).astype(bf16)
    d_own = jnp.concatenate(rows_back, 0).astype(f32)
    x_hat_own = tok_float * inv_own
    d_hat = d_own * gain_part
    mean = lax.psum(jnp.sum(d_hat * x_hat_own, axis=-1), "c")[..., None] / model
    input_grad = cotangent.astype(f32) + inv_own * (d_hat - x_hat_own * mean)

    in_new, in_first_new, in_second_new = adam_update(
        in_weight, grad_in, in_first, in_second, clip_scale, model ** (-0.5)
    )
    dt_new, dt_first_new, dt_second_new = adam_update(
        dt_weight, grad_dt, dt_first, dt_second, clip_scale, rank ** (-0.5)
    )
    out_new, out_first_new, out_second_new = adam_update(
        out_weight, grad_out, out_first, out_second, clip_scale, inner_all ** (-0.5)
    )
    x_new, x_first_new, x_second_new = adam_update(
        x_weight, grad_x, x_first, x_second, clip_scale, inner_all ** (-0.5)
    )
    chan_new, chan_first_new, chan_second_new = adam_update(
        channel_params, grad_chan, channel_first, channel_second, clip_scale, 0.5
    )
    gain_new, gain_first_new, gain_second_new = adam_update(
        gain, grad_gain, gain_first, gain_second, clip_scale, 0.5
    )
    return (
        mixed, input_grad, grad_norm,
        grad_in, in_new, in_first_new, in_second_new,
        grad_dt, dt_new, dt_first_new, dt_second_new,
        grad_out, out_new, out_first_new, out_second_new,
        grad_x, x_new, x_first_new, x_second_new,
        grad_chan, chan_new, chan_first_new, chan_second_new,
        grad_gain, gain_new, gain_first_new, gain_second_new,
        in_new.astype(bf16), dt_new.astype(bf16), out_new.astype(bf16), x_new.astype(bf16),
    )


def solution(mesh):
    chans = mesh.shape["ch"]
    parts = 2 * chans
    groups = mesh.shape["seq"] // parts
    inside = Mesh(mesh.devices.reshape(groups, parts, chans), ("t", "p", "c"))
    seq = ("t", "p")
    tok = P(None, seq, "c")
    wide = P(None, seq, None, "c")
    rows = P(None, seq, "c")
    flat = P(None, None, "c")
    chan = P(None, "c")
    return jax.shard_map(
        functools.partial(body, groups, parts, chans),
        mesh=inside,
        in_specs=(tok, P(None, seq), P(), tok)
        + (wide,) * 3 + (rows,) * 3 + (rows,) * 3 + (flat,) * 3 + (chan,) * 3 + (P(),) * 3,
        out_specs=(tok, tok, P())
        + (wide,) * 4 + (rows,) * 4 + (rows,) * 4 + (flat,) * 4 + (chan,) * 4 + (P(),) * 4
        + (wide, rows, rows, flat),
        check_vma=False,
    )
```

```python
import functools

import jax
import jax.numpy as jnp
from jax import lax
from jax.experimental import pallas as pl
from jax.experimental.pallas import tpu as pltpu
from jax.sharding import Mesh
from jax.sharding import PartitionSpec as P

N = 16
K = 4
STEP = 10

NORM_EPS = 1e-05
BETA_ONE = 0.9
BETA_TWO = 0.95
ADAM_EPS = 1e-08
DECAY = 0.1
CLIP_LIMIT = 1.0
LANES = 128
SCAN_ROWS = 128
MEGA = 1024 * 1024
GROUP = 2
f32 = jnp.float32
bf16 = jnp.bfloat16


def silu_grad(value):
    sigma = jax.nn.sigmoid(value)
    return sigma * (1.0 + value * (1.0 - sigma))


def adam_update(weight, gradient, first_moment, second, clip_scale, step_rate):
    clipped = gradient * clip_scale
    first_new = BETA_ONE * first_moment + (1.0 - BETA_ONE) * clipped
    second_new = BETA_TWO * second + (1.0 - BETA_TWO) * clipped * clipped
    first_hat = first_new / (1.0 - BETA_ONE**STEP)
    second_hat = second_new / (1.0 - BETA_TWO**STEP)
    weight_new = weight - step_rate * (
        first_hat / (jnp.sqrt(second_hat) + ADAM_EPS) + DECAY * weight
    )
    return (weight_new, first_new, second_new)


def sum_rows(parts):
    at = lax.broadcasted_iota(jnp.int32, parts[0].shape, 0)
    for distance in (1, 2, 4):
        low = at % (2 * distance) < distance
        parts = [
            jnp.where(low, a, b) + pltpu.roll(jnp.where(low, b, a), distance, 0)
            for a, b in zip(parts[0::2], parts[1::2])
        ]
    return parts[0]


def scan_forward_kernel(
    step_ref, act_ref, pull_ref, keep_ref, b_ref, c_ref, rate_ref, start_ref,
    y_ref, before_ref, grad_c_ref, final_ref, state_ref,
):
    micros, rows, _ = step_ref.shape
    block = pl.program_id(0)
    rate = rate_ref[...]
    lane = lax.broadcasted_iota(jnp.int32, (N, LANES), 1)

    @pl.when(block == 0)
    def _():
        state_ref[...] = start_ref[...]

    def eight(turn, carried):
        states, b_now, c_now, grads = (list(part) for part in carried)
        base = pl.multiple_of(turn * 8, 8)
        tile = pl.ds(base, 8)
        steps = [step_ref[m, tile, :] for m in range(micros)]
        drives = [steps[m] * act_ref[m, tile, :] for m in range(micros)]
        pulls = [pull_ref[m, tile, :] for m in range(micros)]
        keeps = [
            [keep_ref[m, block * rows + base + j] for j in range(8)] for m in range(micros)
        ]
        y_parts = [[] for _ in range(micros)]
        for m in range(micros):
            grads[m] = pltpu.roll(grads[m], LANES - 8, 1)
        for j in range(8):
            for m in range(micros):
                before = states[m]
                before_ref[m, base + j] = before
                decay = jnp.exp(steps[m][j : j + 1] * rate)
                state = decay * (before * keeps[m][j]) + drives[m][j : j + 1] * b_now[m][:, j : j + 1]
                states[m] = state
                shown = state * c_now[m][:, j : j + 1]
                y_parts[m].append(shown[:8] + shown[8:])
                lane_sum = jnp.sum(state * pulls[m][j : j + 1], axis=1, keepdims=True)
                grads[m] = jnp.where(lane == LANES - 8 + j, lane_sum, grads[m])
        for m in range(micros):
            y_ref[m, tile, :] = sum_rows(y_parts[m])
            b_now[m] = pltpu.roll(b_now[m], LANES - 8, 1)
            c_now[m] = pltpu.roll(c_now[m], LANES - 8, 1)
        return (tuple(states), tuple(b_now), tuple(c_now), tuple(grads))

    begin = (
        tuple(state_ref[m] for m in range(micros)),
        tuple(b_ref[m] for m in range(micros)),
        tuple(c_ref[m] for m in range(micros)),
        tuple(jnp.zeros((N, LANES), f32) for m in range(micros)),
    )
    states, _, _, grads = lax.fori_loop(0, rows // 8, eight, begin)
    for m in range(micros):
        state_ref[m] = states[m]
        grad_c_ref[m] = grads[m]
        final_ref[m] = states[m]


def scan_forward(step, act, pull, keep, b_t, c_t, rate, start):
    micros, length, _ = step.shape
    tall = pl.BlockSpec((micros, SCAN_ROWS, LANES), lambda i: (0, i, 0))
    wide = pl.BlockSpec((micros, N, SCAN_ROWS), lambda i: (0, 0, i))
    fixed = pl.BlockSpec((micros, N, LANES), lambda i: (0, 0, 0))
    return pl.pallas_call(
        scan_forward_kernel,
        grid=(length // SCAN_ROWS,),
        in_specs=[
            tall, tall, tall,
            pl.BlockSpec(memory_space=pltpu.SMEM),
            wide, wide,
            pl.BlockSpec((N, LANES), lambda i: (0, 0)),
            fixed,
        ],
        out_specs=[
            tall,
            pl.BlockSpec((micros, SCAN_ROWS, N, LANES), lambda i: (0, i, 0, 0)),
            wide,
            fixed,
        ],
        out_shape=[
            jax.ShapeDtypeStruct((micros, length, LANES), f32),
            jax.ShapeDtypeStruct((micros, length, N, LANES), f32),
            jax.ShapeDtypeStruct((micros, N, length), f32),
            jax.ShapeDtypeStruct((micros, N, LANES), f32),
        ],
        scratch_shapes=[pltpu.VMEM((micros, N, LANES), f32)],
        cost_estimate=pl.CostEstimate(
            flops=micros * length * N * LANES * 40,
            bytes_accessed=micros * length * N * LANES * 4,
            transcendentals=micros * length * N * LANES,
        ),
        compiler_params=pltpu.CompilerParams(
            dimension_semantics=("arbitrary",), vmem_limit_bytes=24 * 1024 * 1024
        ),
        name="scan_forward",
    )(step, act, pull, keep, b_t, c_t, rate, start)


def scan_backward_kernel(
    step_ref, act_ref, pull_ref, keep_ref, b_ref, c_ref, rate_ref, start_ref, before_ref,
    b_pull_ref, rate_pull_ref, grad_b_ref, grad_rate_ref, final_ref, state_ref,
):
    micros, rows, _ = step_ref.shape
    block = pl.num_programs(0) - 1 - pl.program_id(0)
    rate = rate_ref[...]
    lane = lax.broadcasted_iota(jnp.int32, (N, LANES), 1)

    @pl.when(pl.program_id(0) == 0)
    def _():
        state_ref[...] = start_ref[...]
        grad_rate_ref[...] = jnp.zeros_like(grad_rate_ref)

    def eight(turn, carried):
        states, b_now, c_now, grads, rates = (list(part) for part in carried)
        base = pl.multiple_of(rows - 8 - turn * 8, 8)
        tile = pl.ds(base, 8)
        steps = [step_ref[m, tile, :] for m in range(micros)]
        drives = [steps[m] * act_ref[m, tile, :] for m in range(micros)]
        pulls = [pull_ref[m, tile, :] for m in range(micros)]
        keeps = [
            [keep_ref[m, block * rows + base + j] for j in range(8)] for m in range(micros)
        ]
        b_parts = [[None] * 8 for _ in range(micros)]
        rate_parts = [[None] * 8 for _ in range(micros)]
        for m in range(micros):
            grads[m] = pltpu.roll(grads[m], 8, 1)
            b_now[m] = pltpu.roll(b_now[m], 8, 1)
            c_now[m] = pltpu.roll(c_now[m], 8, 1)
        for j in range(7, -1, -1):
            for m in range(micros):
                adjoint = c_now[m][:, j : j + 1] * pulls[m][j : j + 1] + states[m]
                passed = jnp.exp(steps[m][j : j + 1] * rate) * (adjoint * keeps[m][j])
                states[m] = passed
                decay_pull = passed * before_ref[m, base + j]
                shown = adjoint * b_now[m][:, j : j + 1]
                b_parts[m][j] = shown[:8] + shown[8:]
                shown = decay_pull * rate
                rate_parts[m][j] = shown[:8] + shown[8:]
                rates[m] = rates[m] + decay_pull * steps[m][j : j + 1]
                lane_sum = jnp.sum(adjoint * drives[m][j : j + 1], axis=1, keepdims=True)
                grads[m] = jnp.where(lane == j, lane_sum, grads[m])
        for m in range(micros):
            b_pull_ref[m, tile, :] = sum_rows(b_parts[m])
            rate_pull_ref[m, tile, :] = sum_rows(rate_parts[m])
        return (tuple(states), tuple(b_now), tuple(c_now), tuple(grads), tuple(rates))

    zeros = tuple(jnp.zeros((N, LANES), f32) for m in range(micros))
    begin = (
        tuple(state_ref[m] for m in range(micros)),
        tuple(b_ref[m] for m in range(micros)),
        tuple(c_ref[m] for m in range(micros)),
        zeros,
        zeros,
    )
    states, _, _, grads, rates = lax.fori_loop(0, rows // 8, eight, begin)
    for m in range(micros):
        state_ref[m] = states[m]
        grad_b_ref[m] = grads[m]
        grad_rate_ref[m] += rates[m]
        final_ref[m] = states[m]


def scan_backward(step, act, pull, keep, b_t, c_t, rate, start, before):
    micros, length, _ = step.shape
    last = length // SCAN_ROWS - 1
    tall = pl.BlockSpec((micros, SCAN_ROWS, LANES), lambda i: (0, last - i, 0))
    wide = pl.BlockSpec((micros, N, SCAN_ROWS), lambda i: (0, 0, last - i))
    fixed = pl.BlockSpec((micros, N, LANES), lambda i: (0, 0, 0))
    return pl.pallas_call(
        scan_backward_kernel,
        grid=(length // SCAN_ROWS,),
        in_specs=[
            tall, tall, tall,
            pl.BlockSpec(memory_space=pltpu.SMEM),
            wide, wide,
            pl.BlockSpec((N, LANES), lambda i: (0, 0)),
            fixed,
            pl.BlockSpec((micros, SCAN_ROWS, N, LANES), lambda i: (0, last - i, 0, 0)),
        ],
        out_specs=[tall, tall, wide, fixed, fixed],
        out_shape=[
            jax.ShapeDtypeStruct((micros, length, LANES), f32),
            jax.ShapeDtypeStruct((micros, length, LANES), f32),
            jax.ShapeDtypeStruct((micros, N, length), f32),
            jax.ShapeDtypeStruct((micros, N, LANES), f32),
            jax.ShapeDtypeStruct((micros, N, LANES), f32),
        ],
        scratch_shapes=[pltpu.VMEM((micros, N, LANES), f32)],
        cost_estimate=pl.CostEstimate(
            flops=micros * length * N * LANES * 60,
            bytes_accessed=micros * length * N * LANES * 4,
            transcendentals=micros * length * N * LANES,
        ),
        compiler_params=pltpu.CompilerParams(
            dimension_semantics=("arbitrary",), vmem_limit_bytes=24 * 1024 * 1024
        ),
        name="scan_backward",
    )(step, act, pull, keep, b_t, c_t, rate, start, before)


def turned(ref, turn, x_at):
    width = ref.shape[-1] // 2
    return pl.ds(pl.multiple_of((turn ^ x_at) * width, width), width)


def three(tile, info):
    return jnp.concatenate([(tile * info[:, k + 1 : k + 2]).astype(bf16) for k in range(3)], -1)


def across(left, right, dims):
    return lax.dot_general(left, right, ((dims[0:1], dims[1:2]), ((), ())), preferred_element_type=f32)


def stacked(ref):
    kinds, rows, cols = ref.shape
    return ref[...].reshape(kinds * rows, cols)


def split_blocks(total, place_ref, sent_ref, keep_ref, scratch_ref, offset):
    scratch_ref[...] = total
    core = place_ref[1]
    for x in range(2):
        away = pl.ds(pl.multiple_of((2 * x + 1 - core) * LANES, LANES), LANES)
        here = pl.ds(pl.multiple_of((2 * x + core) * LANES, LANES), LANES)
        sent_ref[x, :, offset : offset + LANES] = scratch_ref[:, away].astype(bf16)
        keep_ref[x, :, offset : offset + LANES] = scratch_ref[:, here]


def tile_rows(ref):
    return ref[...].reshape(-1, ref.shape[-1])


def wide_product(tile_ref, info, w_refs, scratch_ref, x_at):
    total = None
    for turn, w_ref in enumerate(w_refs):
        left = three(tile_ref[:, turned(tile_ref, turn, x_at)], info)
        part = across(left, stacked(w_ref), (1, 0))
        total = part if total is None else total + part
    return total


def inner_kernel(place_ref, x_ref, info_ref, gain_ref, w0_ref, w1_ref,
                 normed_ref, sent_ref, keep_ref, tile_ref, scratch_ref):
    info = info_ref[...]
    normed = tile_rows(x_ref).astype(f32) * info[:, :1] * gain_ref[...]
    normed = normed.astype(bf16)
    normed_ref[...] = normed
    tile_ref[...] = normed.astype(f32)
    total = wide_product(tile_ref, info, (w0_ref, w1_ref), scratch_ref, place_ref[0])
    split_blocks(total, place_ref, sent_ref, keep_ref, scratch_ref, 0)


def gate_kernel(place_ref, normed_ref, back_ref, info_ref, g0_ref, g1_ref, o0_ref, o1_ref,
                sent_ref, keep_ref, tile_ref, scratch_ref):
    info = info_ref[...]
    tile_ref[...] = normed_ref[...].astype(f32)
    total = wide_product(tile_ref, info, (g0_ref, g1_ref), scratch_ref, place_ref[0])
    split_blocks(total, place_ref, sent_ref, keep_ref, scratch_ref, 0)
    tile_ref[...] = tile_rows(back_ref).astype(f32)
    total = wide_product(tile_ref, info, (o0_ref, o1_ref), scratch_ref, place_ref[0])
    split_blocks(total, place_ref, sent_ref, keep_ref, scratch_ref, LANES)


def gathered(scratch_ref, place_ref, refs):
    at = 2 * place_ref[0] + place_ref[1]
    for distance, ref in zip((0, 2, 1, 3), refs):
        lanes = pl.ds(pl.multiple_of((at ^ distance) * LANES, LANES), LANES)
        scratch_ref[:, lanes] = tile_of(ref).astype(f32)


def tile_of(ref):
    return ref[...].reshape(-1, ref.shape[-1])


def split_parts(total, place_ref, sent_ref, keep_ref):
    y = place_ref[2]
    half = total.shape[0] // 2
    low, high = total[:half], total[half:]
    mine = jnp.full(low.shape, y, jnp.int32) == 0
    sent_ref[...] = jnp.where(mine, high, low).astype(bf16).reshape(sent_ref.shape)
    keep_ref[...] = jnp.where(mine, low, high).reshape(keep_ref.shape)


def out_kernel(place_ref, a_ref, b_ref, c_ref, d_ref, info_ref, w0_ref, w1_ref,
               sent_ref, keep_ref, tile_ref, total_ref):
    gathered(tile_ref, place_ref, (a_ref, b_ref, c_ref, d_ref))
    left = three(tile_ref[...], info_ref[...])
    width = tile_ref.shape[1]
    for turn, w_ref in enumerate((w0_ref, w1_ref)):
        total = None
        for k in range(3):
            part = across(left[:, k * width : (k + 1) * width], w_ref[k], (1, 1))
            total = part if total is None else total + part
        total_ref[:, turned(total_ref, turn, place_ref[0])] = total
    split_parts(total_ref[...], place_ref, sent_ref, keep_ref)


def normed_kernel(place_ref, ga_ref, gb_ref, gc_ref, gd_ref, ia_ref, ib_ref, ic_ref, id_ref,
                  info_ref, x_ref, g0_ref, g1_ref, i0_ref, i1_ref,
                  sent_ref, keep_ref, gain_ref, tile_ref, total_ref):
    info = info_ref[...]
    width = tile_ref.shape[1]
    gathered(tile_ref, place_ref, (ga_ref, gb_ref, gc_ref, gd_ref))
    gates = three(tile_ref[...], info)
    gathered(tile_ref, place_ref, (ia_ref, ib_ref, ic_ref, id_ref))
    inners = three(tile_ref[...], info)
    for turn, (g_ref, i_ref) in enumerate(((g0_ref, i0_ref), (g1_ref, i1_ref))):
        total = None
        for k in range(3):
            lanes = slice(k * width, (k + 1) * width)
            part = across(gates[:, lanes], g_ref[k], (1, 1)) + across(inners[:, lanes], i_ref[k], (1, 1))
            total = part if total is None else total + part
        total_ref[:, turned(total_ref, turn, place_ref[0])] = total
    total = total_ref[...]
    split_parts(total, place_ref, sent_ref, keep_ref)

    @pl.when((pl.program_id(0) == 0) & (pl.program_id(1) == 0))
    def _():
        gain_ref[...] = jnp.zeros_like(gain_ref)

    x_hat = tile_rows(x_ref).astype(f32) * info[:, :1]
    gain_ref[...] += jnp.sum((total * x_hat).reshape(-1, 8, total.shape[1]), axis=0)


def weight_grad_kernel(chunks, steps, place_ref, info_ref, *refs):
    ins, (out0_ref, out1_ref, square_ref, tile_ref, sum_ref) = refs[: 5 * chunks], refs[5 * chunks :]
    at = pl.program_id(0)

    @pl.when(at == 0)
    def _():
        sum_ref[...] = jnp.zeros_like(sum_ref)

    for chunk in range(chunks):
        left_ref, *blocks = ins[5 * chunk : 5 * chunk + 5]

        @pl.when((at >= chunk * steps) & (at < (chunk + 1) * steps))
        def _(left_ref=left_ref, blocks=blocks):
            gathered(tile_ref, place_ref, blocks)
            right = three(tile_ref[...], info_ref[...])
            left = left_ref[...].reshape(-1, left_ref.shape[-1])
            sum_ref[...] += across(left, right, (0, 0))

    @pl.when(at == chunks * steps - 1)
    def _():
        half = sum_ref.shape[0] // 2
        width = tile_ref.shape[1]
        for turn, out_ref in enumerate((out0_ref, out1_ref)):
            rows = pl.ds(pl.multiple_of((turn ^ place_ref[0]) * half, half), half)
            for k in range(3):
                out_ref[k] = sum_ref[rows, k * width : (k + 1) * width].astype(out_ref.dtype)
        total = sum_ref[...]
        square_ref[...] = jnp.sum((total * total).reshape(-1, 8, total.shape[1]), axis=0)


SCALARS = pl.BlockSpec(memory_space=pltpu.SMEM)


def whole(array):
    return pl.BlockSpec(array.shape, lambda *at: (0,) * array.ndim)


def shape_of(shape, dtype):
    return jax.ShapeDtypeStruct(shape, dtype)


def call(kernel, name, grid, in_specs, out_specs, out_shape, scratch, flops, moved, args):
    return pl.pallas_call(
        kernel,
        grid=grid,
        in_specs=in_specs,
        out_specs=out_specs,
        out_shape=out_shape,
        scratch_shapes=scratch,
        cost_estimate=pl.CostEstimate(flops=flops, bytes_accessed=moved, transcendentals=0),
        compiler_params=pltpu.CompilerParams(
            dimension_semantics=("arbitrary",) * len(grid), vmem_limit_bytes=48 * MEGA
        ),
        name=name,
    )(*args)


class Tiles:
    def __init__(self, first, micros, parts, rows):
        self.first, self.micros, self.pairs, self.rows = first, micros, parts // 2, rows
        self.grid = (micros, self.pairs)
        self.tile = 2 * rows

    def raw(self, width):
        return pl.BlockSpec((2, 1, self.rows, width), lambda m, z: (z, self.first + m, 0, 0))

    def flat(self, width):
        return pl.BlockSpec((self.tile, width), lambda m, z: (m * self.pairs + z, 0))

    def info(self, width):
        first, pairs = self.first, self.pairs
        return pl.BlockSpec((self.tile, width), lambda m, z: ((first + m) * pairs + z, 0))

    def kindred(self, which, width):
        return pl.BlockSpec((1, self.tile, width), lambda m, z: (which, m * self.pairs + z, 0))

    def blocks(self, width):
        return pl.BlockSpec((2, self.tile, width), lambda m, z: (0, m * self.pairs + z, 0))

    def parted(self, width):
        return pl.BlockSpec((1, 1, self.rows, width), lambda m, z: (m, z, 0, 0))


def inner_product(tiles, place, tokens, info, gain, w):
    width = tokens.shape[-1]
    chans = w[0].shape[-1]
    rows = tiles.micros * tiles.pairs * tiles.tile
    return call(
        inner_kernel, "inner_product", tiles.grid,
        [SCALARS, tiles.raw(width), tiles.info(info.shape[1]), whole(gain), whole(w[0]), whole(w[1])],
        [tiles.flat(width), tiles.blocks(LANES), tiles.blocks(LANES)],
        [shape_of((rows, width), bf16), shape_of((2, rows, LANES), bf16), shape_of((2, rows, LANES), f32)],
        [pltpu.VMEM((tiles.tile, width), f32), pltpu.VMEM((tiles.tile, chans), f32)],
        6 * rows * width * chans, 8 * MEGA,
        (place, tokens, info, gain, *w),
    )


def gate_product(tiles, place, normed, back, info, w_gate, w_out):
    width = normed.shape[-1]
    chans = w_out[0].shape[-1]
    rows = normed.shape[0]
    return call(
        gate_kernel, "gate_product", tiles.grid,
        [SCALARS, tiles.flat(width), tiles.raw(width), tiles.info(info.shape[1])]
        + [whole(w) for w in (*w_gate, *w_out)],
        [tiles.blocks(2 * LANES), tiles.blocks(2 * LANES)],
        [shape_of((2, rows, 2 * LANES), bf16), shape_of((2, rows, 2 * LANES), f32)],
        [pltpu.VMEM((tiles.tile, width), f32), pltpu.VMEM((tiles.tile, chans), f32)],
        12 * rows * width * chans, 16 * MEGA,
        (place, normed, back, info, *w_gate, *w_out),
    )


def out_product(tiles, place, pairs, info, w_out):
    width = 2 * w_out[0].shape[1]
    chans = w_out[0].shape[-1]
    rows = pairs[0].shape[1]
    parted = (tiles.micros, tiles.pairs, tiles.rows, width)
    return call(
        out_kernel, "out_product", tiles.grid,
        [SCALARS] + [tiles.kindred(0, LANES)] * 4 + [tiles.info(info.shape[1]), whole(w_out[0]), whole(w_out[1])],
        [tiles.parted(width), tiles.parted(width)],
        [shape_of(parted, bf16), shape_of(parted, f32)],
        [pltpu.VMEM((tiles.tile, chans), f32), pltpu.VMEM((tiles.tile, width), f32)],
        6 * rows * width * chans, 8 * MEGA,
        (place, *pairs, info, *w_out),
    )


def normed_grad(tiles, place, pairs, inners, info, tokens, w_gate, w_inner):
    width = 2 * w_gate[0].shape[1]
    chans = w_gate[0].shape[-1]
    rows = inners[0].shape[0]
    parted = (tiles.micros, tiles.pairs, tiles.rows, width)
    return call(
        normed_kernel, "normed_grad", tiles.grid,
        [SCALARS] + [tiles.kindred(1, LANES)] * 4 + [tiles.flat(LANES)] * 4
        + [tiles.info(info.shape[1]), tiles.raw(width)] + [whole(w) for w in (*w_gate, *w_inner)],
        [tiles.parted(width), tiles.parted(width), pl.BlockSpec((8, width), lambda m, z: (0, 0))],
        [shape_of(parted, bf16), shape_of(parted, f32), shape_of((8, width), f32)],
        [pltpu.VMEM((tiles.tile, chans), f32), pltpu.VMEM((tiles.tile, width), f32)],
        12 * rows * width * chans, 16 * MEGA,
        (place, *pairs, *inners, info, tokens, *w_gate, *w_inner),
    )


def weight_grad(place, info, lefts, left_at, rights, right_at, span, dtype):
    chunks = len(lefts)
    width = lefts[0].shape[-1]
    chans = 4 * LANES
    steps = info.shape[0] // span // chunks
    piece = (3, width // 2, chans)
    specs, args = [], []
    for chunk in range(chunks):
        def held(spec, chunk=chunk):
            shape, at = spec
            low = chunk * steps
            return pl.BlockSpec(shape, lambda i: at(jnp.clip(i - low, 0, steps - 1), chunk))

        specs += [held(left_at)] + [held(right_at)] * 4
        args += [lefts[chunk], *rights[chunk]]
    return call(
        functools.partial(weight_grad_kernel, chunks, steps), "weight_grad", (chunks * steps,),
        [SCALARS, pl.BlockSpec((span, info.shape[1]), lambda i: (i, 0))] + specs,
        [pl.BlockSpec(piece, lambda i: (0, 0, 0))] * 2 + [pl.BlockSpec((8, 3 * chans), lambda i: (0, 0))],
        [shape_of(piece, dtype), shape_of(piece, dtype), shape_of((8, 3 * chans), f32)],
        [pltpu.VMEM((span, chans), f32), pltpu.VMEM((width, 3 * chans), f32)],
        6 * info.shape[0] * width * chans, 24 * MEGA,
        (place, info, *args),
    )


def pack_kernel(plane, flag_ref, after_ref, w_ref, *out_refs):
    half = w_ref.shape[-1] // 2
    for turn, out_ref in enumerate(out_refs):
        lanes = pl.ds(pl.multiple_of((turn ^ flag_ref[0]) * half, half), half)
        at = (0, slice(None), lanes) if plane is None else (0, slice(None), plane, lanes)
        out_ref[0] = w_ref[at].astype(bf16)


def pack(flag, after, weight, plane=None):
    kinds, rows = weight.shape[:2]
    chans = weight.shape[-1]
    half = chans // 2
    return call(
        functools.partial(pack_kernel, plane), "pack", (kinds,),
        [SCALARS, SCALARS, pl.BlockSpec((1,) + weight.shape[1:], lambda k: (k,) + (0,) * (weight.ndim - 1))],
        [pl.BlockSpec((1, rows, half), lambda k: (k, 0, 0))] * 2,
        [shape_of((kinds, rows, half), bf16)] * 2,
        [], 0, weight.size * 6, (flag, after, weight),
    )


def adam_kernel(rate, flag_ref, clip_ref, w_ref, m_ref, v_ref, *refs):
    pieces, (grad_ref, new_ref, first_ref, second_ref) = refs[:4], refs[4:]
    half = w_ref.shape[-1] // 2
    clip = clip_ref[0]
    for plane in range(2):
        for turn in range(2):
            lanes = pl.ds(pl.multiple_of((turn ^ flag_ref[0]) * half, half), half)
            at = (0, slice(None), plane, lanes)
            grad = pieces[2 * plane + turn][0].astype(f32)
            new, first, second = adam_update(w_ref[at], grad, m_ref[at], v_ref[at], clip, rate)
            grad_ref[at] = grad
            new_ref[at] = new
            first_ref[at] = first
            second_ref[at] = second


def adam(flag, clip, weight, first, second, pieces, rate):
    kinds, rows, _, chans = weight.shape
    block = min(rows, 64)
    full = pl.BlockSpec((1, block, 2, chans), lambda k, r: (k, r, 0, 0))
    piece = pl.BlockSpec((1, block, chans // 2), lambda k, r: (k, r, 0))
    return call(
        functools.partial(adam_kernel, rate), "adam", (kinds, rows // block),
        [SCALARS, SCALARS, full, full, full] + [piece] * 4,
        [full] * 4,
        [shape_of(weight.shape, f32)] * 4,
        [], weight.size * 20, weight.size * 32,
        (flag, clip, weight, first, second, *pieces),
    )


def body(
    groups, parts, chans,
    tokens_in, modality, starts, cotangent,
    in_weight, in_first, in_second,
    dt_weight, dt_first, dt_second,
    out_weight, out_first, out_second,
    x_weight, x_first, x_second,
    channel_params, channel_first, channel_second,
    gain, gain_first, gain_second,
):
    micros, tok_rows, part_width = tokens_in.shape
    model = gain.shape[0]
    chan_width = in_weight.shape[3]
    half = chan_width // 2
    own = half // chans
    cores = chans // 2
    inner_all = chan_width * chans
    x_width = x_weight.shape[1]
    rank = x_width - 2 * N
    dt_rows = dt_weight.shape[1]
    span = parts * tok_rows
    edge = K - 1
    t_at = lax.axis_index("t")
    p_at = lax.axis_index("p")
    c_at = lax.axis_index("c")
    z_at, y_at = p_at // 2, p_at % 2
    x_at, core_at = c_at // cores, c_at % cores
    s_at = t_at * parts + p_at
    slice_at = s_at // (2 * groups)
    everywhere = ("t", "p", "c")
    place = jnp.stack([x_at, core_at, y_at, z_at]).astype(jnp.int32)

    def flat(t, p, c):
        return (t * parts + p) * chans + c

    def part_of(c, j):
        return 2 * (2 * (c % cores) + j) + c // cores

    devices = [(t, p, c) for t in range(groups) for p in range(parts) for c in range(chans)]

    def first_hop(turn):
        pairs = []
        for t, p, c in devices:
            s = t * parts + p
            to_slice, i = s // (2 * groups), (s % (2 * groups)) // groups
            j = turn ^ (to_slice // cores)
            to = flat(s % groups, 2 * (2 * (c % cores) + j) + i, c // cores * cores + to_slice % cores)
            pairs.append((flat(t, p, c), to))
        return pairs

    def second_hop(turn):
        return [
            (flat(t, p, c), flat(t, p - p % 2 + c // cores, (turn ^ (p % 2)) * cores + c % cores))
            for t, p, c in devices
        ]

    small_pairs = [(flat(t, p, c), flat(t, part_of(c, p % 2), p // 2)) for t, p, c in devices]

    def send(value, pairs, back=False):
        if back:
            pairs = [(b, a) for a, b in pairs]
        return lax.ppermute(value, everywhere, pairs)

    def swap(value, axis, distance):
        return lax.ppermute(value, axis, [(i, i ^ distance) for i in range(lax.axis_size(axis))])

    def crossed(pair, flag):
        first, second = pair
        return jnp.where(flag == 0, first, second), jnp.where(flag == 0, second, first)

    between = y_at ^ (z_at % 2)

    def token(*values):
        return sum(value[(0,) * value.ndim].astype(f32) for value in values)[None]

    def weights_there(pair):
        pair = [send(value, first_hop(turn)) for turn, value in enumerate(pair)]
        arrived = token(*pair)
        pair = crossed(pair, between)
        pair = [send(value, second_hop(turn)) for turn, value in enumerate(pair)]
        if groups > 1:
            pair = [lax.all_gather(value, "t", axis=1, tiled=True) for value in pair]
        return tuple(pair), arrived

    def grads_back(pair):
        pair = [send(value, second_hop(turn), True) for turn, value in enumerate(pair)]
        pair = crossed(pair, between)
        return [send(value, first_hop(turn), True) for turn, value in enumerate(pair)]

    def along_groups(value, by):
        pairs = [(i, i + by) for i in range(groups) if 0 <= i + by < groups]
        return lax.ppermute(value, "t", pairs)

    def pick(value, at, axis):
        return lax.dynamic_index_in_dim(value, at, axis, keepdims=False)

    def scattered_chans(sent, keep):
        total = keep + swap(sent, "c", 1).astype(f32)
        got = swap(pick(total, 1 - x_at, 0).astype(bf16), "c", cores)
        return pick(total, x_at, 0) + got.astype(f32)

    def gathered_chans(value):
        across_x = swap(value, "c", cores)
        across_core = swap(value, "c", 1)
        return (value, across_x, across_core, swap(across_x, "c", 1))

    def scattered_parts(sent, keep):
        total = keep + swap(sent, "p", 1).astype(f32)
        total = total.reshape(total.shape[0], -1, 2, *total.shape[2:])
        got = swap(pick(total, 1 - z_at % 2, 2).astype(bf16), "p", 2)
        total = pick(total, z_at % 2, 2) + got.astype(f32)
        got = swap(pick(total, 1 - z_at // 2, 1).astype(bf16), "p", 4)
        return pick(total, z_at // 2, 1) + got.astype(f32)

    def in_pair(mine, other, flag, axis):
        low, high = jnp.where(flag == 0, mine, other), jnp.where(flag == 0, other, mine)
        return jnp.stack([low, high], axis)

    earlier = []

    def summed(value, kind):
        rows, length = value.shape
        total = value.reshape(rows, 2, 2, length // 4)
        got = swap(pick(total, 1 - core_at, 2).astype(kind), "c", 1)
        total = pick(total, core_at, 2) + got.astype(f32)
        got = swap(pick(total, 1 - x_at, 1).astype(kind), "c", cores)
        total = pick(total, x_at, 1) + got.astype(f32)
        if earlier:
            total = total + 0.0 * earlier[-1]
        total = lax.psum(total, "p")
        earlier.append(token(total))
        total = total.astype(kind)
        total = in_pair(total, swap(total, "c", cores), x_at, 1)
        total = in_pair(total, swap(total, "c", 1), core_at, 2)
        return total.reshape(rows, length)

    kinds = lax.all_gather(modality, "p").transpose(1, 0, 2).reshape(micros, span)
    tokens_all = lax.all_gather(tokens_in, "p")
    flag = (slice_at // cores).astype(jnp.int32)[None]
    w_inner, arrived = weights_there(pack(flag, jnp.zeros((1,), f32), in_weight, 0))
    small = jnp.concatenate([x_weight.reshape(3 * x_width, chan_width), channel_params], 0)
    own_lanes = y_at * half + z_at * own
    small = send(lax.dynamic_slice_in_dim(small, own_lanes, own, 1), small_pairs)
    w_gate, arrived = weights_there(pack(flag, arrived, in_weight, 1))
    w_out, _ = weights_there(pack(flag, arrived, out_weight))
    back_all = lax.all_gather(cotangent, "p")
    dt_all = lax.all_gather(dt_weight.astype(bf16), ("t", "p"), axis=1, tiled=True)
    w_dt = send(lax.dynamic_slice_in_dim(dt_all, own_lanes, own, 2), small_pairs)

    squares = jnp.sum(jnp.square(tokens_all.astype(f32)), axis=-1)
    squares = lax.psum(squares, "c").transpose(1, 0, 2).reshape(micros, span)
    inv_all = lax.rsqrt(squares / model + NORM_EPS)
    inv_own = lax.dynamic_slice_in_dim(inv_all, p_at * tok_rows, tok_rows, 1)[..., None]
    masks = [(kinds == k).astype(f32) for k in range(3)]
    info = jnp.stack([inv_all, *masks], -1).reshape(micros * span, 4)
    gain_part = lax.dynamic_slice_in_dim(gain, c_at * part_width, part_width, 0)[None]

    w_x = small[: 3 * x_width].astype(bf16).reshape(3, x_width, own)
    channel = small[3 * x_width :]
    conv_taps = channel[:K]
    conv_bias = channel[K]
    dt_bias = channel[K + 1]
    skip_gain = channel[K + 2]
    neg_rate = -jnp.exp(channel[K + 3 :])

    def by_kind(value, kind):
        hit = (kind[:, None] == jnp.arange(3)[None, :])[:, :, None]
        return jnp.where(hit, value[:, None, :], jnp.zeros((), value.dtype))

    def dot(spec, left, right):
        return jnp.einsum(spec, left, right, preferred_element_type=f32)

    grad_dt_sum = grad_x_sum = grad_chan_sum = grad_gain_sum = 0.0
    outs, rows_back, held, products = [], [], [], []
    all_normed, all_pairs, all_inners = [], [], []
    chunk = min(GROUP, micros)
    for at in range(0, micros, chunk):
        ms = slice(at, at + chunk)
        tiles = Tiles(at, chunk, parts, tok_rows)
        kind = kinds[ms].reshape(-1)
        normed, sent, keep = inner_product(tiles, place, tokens_all, info, gain_part, w_inner)
        inner_part = scattered_chans(sent, keep).reshape(chunk, span, own)
        sent, keep = gate_product(tiles, place, normed, back_all, info, w_gate, w_out)
        pair = scattered_chans(sent, keep).reshape(chunk, span, 2, own)
        gate_part, d_mixed = pair[:, :, 0], pair[:, :, 1]
        positions = t_at * span - edge + jnp.arange(span + 2 * edge, dtype=jnp.int32)
        begin = starts[ms]
        segment = jnp.sum(
            (begin[:, None, :] <= positions[None, :, None]).astype(jnp.int32), axis=2
        )
        keep_mask = 1.0 - jnp.any(
            begin[:, None, :] == positions[None, edge : edge + span, None], axis=2
        ).astype(f32)
        same_doc = [
            (
                segment[:, edge - j : edge - j + span + edge]
                == segment[:, edge : edge + span + edge]
            ).astype(f32)[..., None]
            for j in range(K)
        ]
        none = jnp.zeros((chunk, edge, own), f32)
        before = along_groups(inner_part[:, span - edge :], 1) if groups > 1 else none
        padded = jnp.concatenate([before, inner_part], 1)
        conv_out = conv_bias + sum(
            conv_taps[j] * padded[:, edge - j : edge - j + span] * same_doc[j][:, :span]
            for j in range(K)
        )
        activated = jax.nn.silu(conv_out).astype(bf16)
        act_float = activated.astype(f32)
        act3 = by_kind(activated.reshape(-1, own), kind)
        projected_x = summed(dot("kxc,tkc->xt", w_x, act3), f32)
        low_t = projected_x[:rank].astype(bf16)
        mats = projected_x[rank:].reshape(2, N, chunk, span).transpose(0, 2, 1, 3)
        low3 = by_kind(low_t.T, kind)
        dt_pre = dot("tkr,krc->tc", low3, w_dt).reshape(chunk, span, own) + dt_bias
        step_size = jax.nn.softplus(dt_pre)
        gate_act = jax.nn.silu(gate_part)
        d_scan = d_mixed * gate_act
        zero_state = jnp.zeros((chunk, N, own), f32)
        args = (step_size, act_float, d_scan, keep_mask, mats[0], mats[1], neg_rate)
        state_in = zero_state
        if groups > 1:
            ends = scan_forward(*args, zero_state)[3]
            passed_all = jnp.exp(jnp.sum(step_size, axis=1)[:, None, :] * neg_rate)
            passed_all = passed_all * jnp.prod(keep_mask, axis=1)[:, None, None]
            for _ in range(groups - 1):
                state_in = along_groups(passed_all * state_in + ends, 1)
        y_part, states_before, grad_c, _ = scan_forward(*args, state_in)
        y_scan = y_part + skip_gain * act_float
        mixed_in = (y_scan * gate_act).astype(bf16)
        d_gate = (d_mixed * y_scan * silu_grad(gate_part)).astype(bf16)
        pairs = gathered_chans(jnp.stack([mixed_in, d_gate]).reshape(2, chunk * span, own))
        products.append(out_product(tiles, place, pairs, info, w_out))
        outs.append(scattered_parts(*products[-1]))

        adj_in = zero_state
        if groups > 1:
            ends = scan_backward(*args, zero_state, states_before)[4]
            for _ in range(groups - 1):
                adj_in = along_groups(passed_all * adj_in + ends, -1)
        b_pull, rate_pull, grad_b, grad_rate, _ = scan_backward(*args, adj_in, states_before)
        d_step = rate_pull + act_float * b_pull
        d_rate = jnp.sum(grad_rate, axis=0) * neg_rate
        d_act = d_scan * skip_gain + step_size * b_pull
        d_skip = jnp.sum(d_scan * act_float, axis=(0, 1))
        d_pre = (d_step * jax.nn.sigmoid(dt_pre)).astype(bf16)
        d_bias = jnp.sum(d_pre.astype(f32), axis=(0, 1))
        d_pre = d_pre.reshape(-1, own)
        d_low = dot("krc,tkc->rt", w_dt, by_kind(d_pre, kind))
        grad_dt_sum += dot("tkr,tc->krc", low3, d_pre)
        grad_bc = jnp.stack([grad_b, grad_c]).transpose(0, 2, 1, 3).reshape(2 * N, -1)
        d_projx = summed(jnp.concatenate([d_low, grad_bc], 0), bf16)
        all_normed.append(normed)
        all_pairs.append(pairs)
        held.append(
            (tiles, kind, d_projx, d_act, activated, conv_out, padded, same_doc, none)
            + (d_bias, d_skip, d_rate)
        )

    kept = f32 if groups > 1 else bf16

    def kindred(which):
        return ((1, span, own), lambda m, chunk_at: (which, m, 0))

    rows_at = ((span, part_width), lambda m, chunk_at: (m, 0))
    raw_at = ((parts, 1, tok_rows, part_width), lambda m, chunk_at: (0, chunk_at * chunk + m, 0, 0))
    backs = [back_all] * len(all_pairs)
    *g_out, out_sq = weight_grad(place, info, backs, raw_at, all_pairs, kindred(0), span, kept)
    *g_gate, gate_sq = weight_grad(place, info, all_normed, rows_at, all_pairs, kindred(1), span, kept)
    done = [token(*(sent for sent, _ in products)), token(out_sq, gate_sq)]

    for at, stage in enumerate(held):
        tiles, kind, d_projx, d_act, activated, conv_out, padded, same_doc, none = stage[:9]
        d_bias, d_skip, d_rate = stage[9:]
        projx3 = by_kind(d_projx.T, kind)
        w_x_now = w_x + (0.0 * done[min(at, 1)]).astype(bf16)
        d_act = d_act + dot("tkx,kxc->tc", projx3, w_x_now).reshape(chunk, span, own)
        grad_x_sum += dot("tkx,tc->kxc", projx3, activated.reshape(-1, own))
        d_conv = d_act * silu_grad(conv_out)
        after = along_groups(d_conv[:, :edge], -1) if groups > 1 else none
        d_conv_ext = jnp.concatenate([d_conv, after], 1)
        d_inner = sum(
            conv_taps[j] * d_conv_ext[:, j : j + span] * same_doc[j][:, j : j + span]
            for j in range(K)
        )
        d_taps = jnp.stack(
            [
                jnp.sum(
                    d_conv * padded[:, edge - j : edge - j + span] * same_doc[j][:, :span],
                    axis=(0, 1),
                )
                for j in range(K)
            ]
        )
        d_conv_bias = jnp.sum(d_conv, axis=(0, 1))
        grad_chan_sum += jnp.concatenate(
            [d_taps, d_conv_bias[None], d_bias[None], d_skip[None], d_rate], 0
        )
        inners = gathered_chans(d_inner.astype(bf16).reshape(chunk * span, own))
        sent, keep, gain_rows = normed_grad(
            tiles, place, all_pairs[at], inners, info, tokens_all, w_gate, w_inner
        )
        grad_gain_sum += jnp.sum(gain_rows, axis=0)
        rows_back.append(scattered_parts(sent, keep))
        all_inners.append(inners)

    flat_at = ((span, own), lambda m, chunk_at: (m, 0))
    *g_inner, inner_sq = weight_grad(place, info, all_normed, rows_at, all_inners, flat_at, span, kept)
    g_small = jnp.concatenate(
        [grad_x_sum.reshape(-1, own), grad_dt_sum.reshape(-1, own), grad_chan_sum], 0
    )
    if groups > 1:
        g_small = lax.psum(g_small, "t")
        over = lambda pair: [
            lax.psum_scatter(value, "t", scatter_dimension=1, tiled=True) for value in pair
        ]
        g_out, g_gate, g_inner = over(g_out), over(g_gate), over(g_inner)
        large_sq = sum(jnp.sum(value * value) for value in (*g_out, *g_gate, *g_inner))
        g_out, g_gate, g_inner = (
            [value.astype(bf16) for value in pair] for pair in (g_out, g_gate, g_inner)
        )
    else:
        large_sq = jnp.sum(out_sq) + jnp.sum(gate_sq) + jnp.sum(inner_sq)
    local_sq = large_sq + jnp.sum(g_small * g_small) / groups
    here = (jnp.arange(chans) == c_at).astype(f32)
    tail = jnp.concatenate([(here[:, None] * grad_gain_sum).reshape(-1), local_sq[None]])
    tail = lax.psum(tail, everywhere)
    grad_gain = tail[:model]
    grad_norm = jnp.sqrt(tail[model] + jnp.sum(grad_gain * grad_gain))
    clip_scale = CLIP_LIMIT / jnp.maximum(grad_norm, CLIP_LIMIT)

    def back_whole(pair):
        return jnp.concatenate(crossed(grads_back(pair), flag[0]), -1).astype(f32)

    grad_out = back_whole(g_out)
    in_pieces = (*grads_back(g_inner), *grads_back(g_gate))
    small_back = lax.all_gather(send(g_small.astype(bf16), small_pairs, True), "p")
    small_back = small_back.reshape(chans, 2, -1, own).transpose(2, 1, 0, 3)
    small_back = small_back.reshape(-1, chan_width).astype(f32)
    grad_x = small_back[: 3 * x_width].reshape(3, x_width, chan_width)
    grad_dt = small_back[3 * x_width : 3 * x_width + 3 * rank].reshape(3, rank, chan_width)
    grad_dt = lax.dynamic_slice_in_dim(grad_dt, s_at * dt_rows, dt_rows, 1)
    grad_chan = small_back[3 * x_width + 3 * rank :]

    tok_float = tokens_in.astype(f32)
    mixed = (tok_float + jnp.concatenate(outs, 0)).astype(bf16)
    d_own = jnp.concatenate(rows_back, 0)
    x_hat_own = tok_float * inv_own
    d_hat = d_own * gain_part
    mean = lax.psum(jnp.sum(d_hat * x_hat_own, axis=-1), "c")[..., None] / model
    input_grad = cotangent.astype(f32) + inv_own * (d_hat - x_hat_own * mean)

    grad_in, in_new, in_first_new, in_second_new = adam(
        flag, clip_scale[None], in_weight, in_first, in_second, in_pieces, model ** (-0.5)
    )
    dt_new, dt_first_new, dt_second_new = adam_update(
        dt_weight, grad_dt, dt_first, dt_second, clip_scale, rank ** (-0.5)
    )
    out_new, out_first_new, out_second_new = adam_update(
        out_weight, grad_out, out_first, out_second, clip_scale, inner_all ** (-0.5)
    )
    x_new, x_first_new, x_second_new = adam_update(
        x_weight, grad_x, x_first, x_second, clip_scale, inner_all ** (-0.5)
    )
    chan_new, chan_first_new, chan_second_new = adam_update(
        channel_params, grad_chan, channel_first, channel_second, clip_scale, 0.5
    )
    gain_new, gain_first_new, gain_second_new = adam_update(
        gain, grad_gain, gain_first, gain_second, clip_scale, 0.5
    )
    return (
        mixed, input_grad, grad_norm,
        grad_in, in_new, in_first_new, in_second_new,
        grad_dt, dt_new, dt_first_new, dt_second_new,
        grad_out, out_new, out_first_new, out_second_new,
        grad_x, x_new, x_first_new, x_second_new,
        grad_chan, chan_new, chan_first_new, chan_second_new,
        grad_gain, gain_new, gain_first_new, gain_second_new,
        in_new.astype(bf16), dt_new.astype(bf16), out_new.astype(bf16), x_new.astype(bf16),
    )


def solution(mesh):
    chans = mesh.shape["ch"]
    parts = 2 * chans
    groups = mesh.shape["seq"] // parts
    inside = Mesh(mesh.devices.reshape(groups, parts, chans), ("t", "p", "c"))
    seq = ("t", "p")
    tok = P(None, seq, "c")
    wide = P(None, seq, None, "c")
    rows = P(None, seq, "c")
    flat = P(None, None, "c")
    chan = P(None, "c")
    return jax.shard_map(
        functools.partial(body, groups, parts, chans),
        mesh=inside,
        in_specs=(tok, P(None, seq), P(), tok)
        + (wide,) * 3 + (rows,) * 3 + (rows,) * 3 + (flat,) * 3 + (chan,) * 3 + (P(),) * 3,
        out_specs=(tok, tok, P())
        + (wide,) * 4 + (rows,) * 4 + (rows,) * 4 + (flat,) * 4 + (chan,) * 4 + (P(),) * 4
        + (wide, rows, rows, flat),
        check_vma=False,
    )
```

```python
import functools

import jax
import jax.numpy as jnp
from jax import lax
from jax.experimental import pallas as pl
from jax.experimental.pallas import tpu as pltpu
from jax.sharding import Mesh
from jax.sharding import PartitionSpec as P

N = 16
K = 4
STEP = 10

NORM_EPS = 1e-05
BETA_ONE = 0.9
BETA_TWO = 0.95
ADAM_EPS = 1e-08
DECAY = 0.1
CLIP_LIMIT = 1.0
LANES = 128
SCAN_ROWS = 128
MEGA = 1024 * 1024
GROUP = 2
f32 = jnp.float32
bf16 = jnp.bfloat16


def silu_grad(value):
    sigma = jax.nn.sigmoid(value)
    return sigma * (1.0 + value * (1.0 - sigma))


def adam_update(weight, gradient, first_moment, second, clip_scale, step_rate):
    clipped = gradient * clip_scale
    first_new = BETA_ONE * first_moment + (1.0 - BETA_ONE) * clipped
    second_new = BETA_TWO * second + (1.0 - BETA_TWO) * clipped * clipped
    first_hat = first_new / (1.0 - BETA_ONE**STEP)
    second_hat = second_new / (1.0 - BETA_TWO**STEP)
    weight_new = weight - step_rate * (
        first_hat / (jnp.sqrt(second_hat) + ADAM_EPS) + DECAY * weight
    )
    return (weight_new, first_new, second_new)


def sum_rows(parts):
    at = lax.broadcasted_iota(jnp.int32, parts[0].shape, 0)
    for distance in (1, 2, 4):
        low = at % (2 * distance) < distance
        parts = [
            jnp.where(low, a, b) + pltpu.roll(jnp.where(low, b, a), distance, 0)
            for a, b in zip(parts[0::2], parts[1::2])
        ]
    return parts[0]


def split_lanes(b_mat, c_mat):
    def parts(value):
        out = []
        for _ in range(3):
            part = lax.reduce_precision(value, 8, 7)
            out.append(part)
            value = value - part
        return out

    blank = jnp.zeros(b_mat.shape[:-1] + (LANES // 2 - 3 * N,), f32)
    return jnp.concatenate([*parts(b_mat), blank, *parts(c_mat), blank], -1)


def lane_rules():
    lanes = jnp.arange(LANES)
    used = lanes % (LANES // 2) < 3 * N
    mask = ((lanes[None, :] % N == jnp.arange(N)[:, None]) & used[None, :]).astype(f32)
    side = (lanes[:, None] // (LANES // 2) == jnp.arange(2 * LANES)[None, :] // LANES).astype(bf16)
    return mask, side


def matmul(left, right):
    return jnp.dot(left, right, preferred_element_type=f32)


def spread(rows_ref, m, base, mask, side):
    left = [rows_ref[m, pl.ds(base + j, 1), :] * mask for j in range(8)]
    return matmul(jnp.concatenate(left, 0).astype(bf16), side)


def lane_sums(product_ref, m, grads, lane, base, ones):
    sums = matmul(product_ref[m], ones)
    for j in range(8):
        grads = jnp.where(lane == base + j, sums[N * j : N * j + N], grads)
    return grads


def scan_forward_kernel(
    step_ref, act_ref, pull_ref, keep_ref, rows_ref, mask_ref, side_ref, rate_ref, start_ref,
    y_ref, before_ref, grad_c_ref, final_ref,
    state_ref, wide_a, wide_b, product_a, product_b,
):
    micros, rows, _ = step_ref.shape
    block = pl.program_id(0)
    rate = rate_ref[...]
    mask = mask_ref[...]
    side = side_ref[...]
    ones = jnp.ones((LANES, LANES), bf16)
    lane = lax.broadcasted_iota(jnp.int32, (N, LANES), 1)

    @pl.when(block == 0)
    def _():
        state_ref[...] = start_ref[...]

    for m in range(micros):
        wide_a[m] = spread(rows_ref, m, 0, mask, side)

    def sixteen(turn, carried):
        states, grads = (list(part) for part in carried)
        for half in range(2):
            base = pl.multiple_of(turn * 16 + 8 * half, 8)
            wide, wide_next = (wide_a, wide_b) if half == 0 else (wide_b, wide_a)
            product, product_last = (product_a, product_b) if half == 0 else (product_b, product_a)
            following = jnp.minimum(base + 8, rows - 8)
            for m in range(micros):
                wide_next[m] = spread(rows_ref, m, following, mask, side)
                grads[m] = lane_sums(product_last, m, grads[m], lane, base - 8, ones)
            y_parts = [[] for _ in range(micros)]
            for j in range(8):
                for m in range(micros):
                    row = pl.ds(base + j, 1)
                    own = slice(N * j, N * j + N)
                    step = step_ref[m, row, :]
                    before = states[m]
                    before_ref[m, base + j] = before
                    before = before * keep_ref[m, block * rows + base + j]
                    drive = step * act_ref[m, row, :]
                    state = jnp.exp(step * rate) * before + drive * wide[m, own, :LANES]
                    states[m] = state
                    shown = state * wide[m, own, LANES:]
                    y_parts[m].append(shown[:8] + shown[8:])
                    product[m, own, :] = (state * pull_ref[m, row, :]).astype(bf16)
            for m in range(micros):
                y_ref[m, pl.ds(base, 8), :] = sum_rows(y_parts[m])
        return (tuple(states), tuple(grads))

    begin = (
        tuple(state_ref[m] for m in range(micros)),
        tuple(jnp.zeros((N, LANES), f32) for m in range(micros)),
    )
    states, grads = lax.fori_loop(0, rows // 16, sixteen, begin)
    for m in range(micros):
        state_ref[m] = states[m]
        grad_c_ref[m] = lane_sums(product_b, m, grads[m], lane, rows - 8, ones)
        final_ref[m] = states[m]


def scan_scratch(micros):
    wide = pltpu.VMEM((micros, 8 * N, 2 * LANES), f32)
    product = pltpu.VMEM((micros, 8 * N, LANES), bf16)
    return [pltpu.VMEM((micros, N, LANES), f32), wide, wide, product, product]


def scan_forward(step, act, pull, keep, rows, mask, side, rate, start):
    micros, length, _ = step.shape
    tall = pl.BlockSpec((micros, SCAN_ROWS, LANES), lambda i: (0, i, 0))
    wide = pl.BlockSpec((micros, N, SCAN_ROWS), lambda i: (0, 0, i))
    fixed = pl.BlockSpec((micros, N, LANES), lambda i: (0, 0, 0))
    small = pl.BlockSpec((N, LANES), lambda i: (0, 0))
    return pl.pallas_call(
        scan_forward_kernel,
        grid=(length // SCAN_ROWS,),
        in_specs=[
            tall, tall, tall,
            pl.BlockSpec(memory_space=pltpu.SMEM),
            tall, small,
            pl.BlockSpec((LANES, 2 * LANES), lambda i: (0, 0)),
            small, fixed,
        ],
        out_specs=[
            tall,
            pl.BlockSpec((micros, SCAN_ROWS, N, LANES), lambda i: (0, i, 0, 0)),
            wide,
            fixed,
        ],
        out_shape=[
            jax.ShapeDtypeStruct((micros, length, LANES), f32),
            jax.ShapeDtypeStruct((micros, length, N, LANES), f32),
            jax.ShapeDtypeStruct((micros, N, length), f32),
            jax.ShapeDtypeStruct((micros, N, LANES), f32),
        ],
        scratch_shapes=scan_scratch(micros),
        cost_estimate=pl.CostEstimate(
            flops=micros * length * N * LANES * 40,
            bytes_accessed=micros * length * N * LANES * 4,
            transcendentals=micros * length * N * LANES,
        ),
        compiler_params=pltpu.CompilerParams(
            dimension_semantics=("arbitrary",), vmem_limit_bytes=24 * MEGA
        ),
        name="scan_forward",
    )(step, act, pull, keep, rows, mask, side, rate, start)


def scan_backward_kernel(
    step_ref, act_ref, pull_ref, keep_ref, rows_ref, mask_ref, side_ref, rate_ref, start_ref,
    before_ref,
    b_pull_ref, rate_pull_ref, grad_b_ref, grad_rate_ref, final_ref,
    state_ref, wide_a, wide_b, product_a, product_b,
):
    micros, rows, _ = step_ref.shape
    block = pl.num_programs(0) - 1 - pl.program_id(0)
    rate = rate_ref[...]
    mask = mask_ref[...]
    side = side_ref[...]
    ones = jnp.ones((LANES, LANES), bf16)
    lane = lax.broadcasted_iota(jnp.int32, (N, LANES), 1)

    @pl.when(pl.program_id(0) == 0)
    def _():
        state_ref[...] = start_ref[...]
        grad_rate_ref[...] = jnp.zeros_like(grad_rate_ref)

    for m in range(micros):
        wide_a[m] = spread(rows_ref, m, rows - 8, mask, side)

    def sixteen(turn, carried):
        states, grads, rates = (list(part) for part in carried)
        for half in range(2):
            base = pl.multiple_of(rows - 8 - turn * 16 - 8 * half, 8)
            wide, wide_next = (wide_a, wide_b) if half == 0 else (wide_b, wide_a)
            product, product_last = (product_a, product_b) if half == 0 else (product_b, product_a)
            following = jnp.maximum(base - 8, 0)
            for m in range(micros):
                wide_next[m] = spread(rows_ref, m, following, mask, side)
                grads[m] = lane_sums(product_last, m, grads[m], lane, base + 8, ones)
            b_parts = [[None] * 8 for _ in range(micros)]
            rate_parts = [[None] * 8 for _ in range(micros)]
            for j in range(7, -1, -1):
                for m in range(micros):
                    row = pl.ds(base + j, 1)
                    own = slice(N * j, N * j + N)
                    step = step_ref[m, row, :]
                    adjoint = wide[m, own, LANES:] * pull_ref[m, row, :] + states[m]
                    passed = jnp.exp(step * rate) * (
                        adjoint * keep_ref[m, block * rows + base + j]
                    )
                    states[m] = passed
                    decay_pull = passed * before_ref[m, base + j]
                    shown = adjoint * wide[m, own, :LANES]
                    b_parts[m][j] = shown[:8] + shown[8:]
                    shown = decay_pull * rate
                    rate_parts[m][j] = shown[:8] + shown[8:]
                    rates[m] = rates[m] + decay_pull * step
                    drive = step * act_ref[m, row, :]
                    product[m, own, :] = (adjoint * drive).astype(bf16)
            for m in range(micros):
                b_pull_ref[m, pl.ds(base, 8), :] = sum_rows(b_parts[m])
                rate_pull_ref[m, pl.ds(base, 8), :] = sum_rows(rate_parts[m])
        return (tuple(states), tuple(grads), tuple(rates))

    zeros = tuple(jnp.zeros((N, LANES), f32) for m in range(micros))
    begin = (tuple(state_ref[m] for m in range(micros)), zeros, zeros)
    states, grads, rates = lax.fori_loop(0, rows // 16, sixteen, begin)
    for m in range(micros):
        state_ref[m] = states[m]
        grad_b_ref[m] = lane_sums(product_b, m, grads[m], lane, 0, ones)
        grad_rate_ref[m] += rates[m]
        final_ref[m] = states[m]


def scan_backward(step, act, pull, keep, rows, mask, side, rate, start, before):
    micros, length, _ = step.shape
    last = length // SCAN_ROWS - 1
    tall = pl.BlockSpec((micros, SCAN_ROWS, LANES), lambda i: (0, last - i, 0))
    wide = pl.BlockSpec((micros, N, SCAN_ROWS), lambda i: (0, 0, last - i))
    fixed = pl.BlockSpec((micros, N, LANES), lambda i: (0, 0, 0))
    small = pl.BlockSpec((N, LANES), lambda i: (0, 0))
    return pl.pallas_call(
        scan_backward_kernel,
        grid=(length // SCAN_ROWS,),
        in_specs=[
            tall, tall, tall,
            pl.BlockSpec(memory_space=pltpu.SMEM),
            tall, small,
            pl.BlockSpec((LANES, 2 * LANES), lambda i: (0, 0)),
            small, fixed,
            pl.BlockSpec((micros, SCAN_ROWS, N, LANES), lambda i: (0, last - i, 0, 0)),
        ],
        out_specs=[tall, tall, wide, fixed, fixed],
        out_shape=[
            jax.ShapeDtypeStruct((micros, length, LANES), f32),
            jax.ShapeDtypeStruct((micros, length, LANES), f32),
            jax.ShapeDtypeStruct((micros, N, length), f32),
            jax.ShapeDtypeStruct((micros, N, LANES), f32),
            jax.ShapeDtypeStruct((micros, N, LANES), f32),
        ],
        scratch_shapes=scan_scratch(micros),
        cost_estimate=pl.CostEstimate(
            flops=micros * length * N * LANES * 60,
            bytes_accessed=micros * length * N * LANES * 4,
            transcendentals=micros * length * N * LANES,
        ),
        compiler_params=pltpu.CompilerParams(
            dimension_semantics=("arbitrary",), vmem_limit_bytes=24 * MEGA
        ),
        name="scan_backward",
    )(step, act, pull, keep, rows, mask, side, rate, start, before)


def turned(ref, turn, x_at):
    width = ref.shape[-1] // 2
    return pl.ds(pl.multiple_of((turn ^ x_at) * width, width), width)


def three(tile, info):
    return jnp.concatenate([(tile * info[:, k + 1 : k + 2]).astype(bf16) for k in range(3)], -1)


def across(left, right, dims):
    return lax.dot_general(left, right, ((dims[0:1], dims[1:2]), ((), ())), preferred_element_type=f32)


def stacked(ref):
    kinds, rows, cols = ref.shape
    return ref[...].reshape(kinds * rows, cols)


def split_blocks(total, place_ref, sent_ref, keep_ref, scratch_ref, offset):
    scratch_ref[...] = total
    core = place_ref[1]
    for x in range(2):
        away = pl.ds(pl.multiple_of((2 * x + 1 - core) * LANES, LANES), LANES)
        here = pl.ds(pl.multiple_of((2 * x + core) * LANES, LANES), LANES)
        sent_ref[x, :, offset : offset + LANES] = scratch_ref[:, away].astype(bf16)
        keep_ref[x, :, offset : offset + LANES] = scratch_ref[:, here]


def tile_rows(ref):
    return ref[...].reshape(-1, ref.shape[-1])


def wide_product(tile_ref, info, w_refs, scratch_ref, x_at):
    total = None
    for turn, w_ref in enumerate(w_refs):
        left = three(tile_ref[:, turned(tile_ref, turn, x_at)], info)
        part = across(left, stacked(w_ref), (1, 0))
        total = part if total is None else total + part
    return total


def inner_kernel(place_ref, x_ref, info_ref, gain_ref, w0_ref, w1_ref,
                 normed_ref, sent_ref, keep_ref, tile_ref, scratch_ref):
    info = info_ref[...]
    normed = tile_rows(x_ref).astype(f32) * info[:, :1] * gain_ref[...]
    normed = normed.astype(bf16)
    normed_ref[...] = normed
    tile_ref[...] = normed.astype(f32)
    total = wide_product(tile_ref, info, (w0_ref, w1_ref), scratch_ref, place_ref[0])
    split_blocks(total, place_ref, sent_ref, keep_ref, scratch_ref, 0)


def gate_kernel(place_ref, normed_ref, back_ref, info_ref, g0_ref, g1_ref, o0_ref, o1_ref,
                sent_ref, keep_ref, tile_ref, scratch_ref):
    info = info_ref[...]
    tile_ref[...] = normed_ref[...].astype(f32)
    total = wide_product(tile_ref, info, (g0_ref, g1_ref), scratch_ref, place_ref[0])
    split_blocks(total, place_ref, sent_ref, keep_ref, scratch_ref, 0)
    tile_ref[...] = tile_rows(back_ref).astype(f32)
    total = wide_product(tile_ref, info, (o0_ref, o1_ref), scratch_ref, place_ref[0])
    split_blocks(total, place_ref, sent_ref, keep_ref, scratch_ref, LANES)


def gathered(scratch_ref, place_ref, refs):
    at = 2 * place_ref[0] + place_ref[1]
    for distance, ref in zip((0, 2, 1, 3), refs):
        lanes = pl.ds(pl.multiple_of((at ^ distance) * LANES, LANES), LANES)
        scratch_ref[:, lanes] = tile_of(ref).astype(f32)


def tile_of(ref):
    return ref[...].reshape(-1, ref.shape[-1])


def split_parts(total, place_ref, sent_ref, keep_ref):
    y = place_ref[2]
    half = total.shape[0] // 2
    low, high = total[:half], total[half:]
    mine = jnp.full(low.shape, y, jnp.int32) == 0
    sent_ref[...] = jnp.where(mine, high, low).astype(bf16).reshape(sent_ref.shape)
    keep_ref[...] = jnp.where(mine, low, high).reshape(keep_ref.shape)


def out_kernel(place_ref, a_ref, b_ref, c_ref, d_ref, info_ref, w0_ref, w1_ref,
               sent_ref, keep_ref, tile_ref, total_ref):
    gathered(tile_ref, place_ref, (a_ref, b_ref, c_ref, d_ref))
    left = three(tile_ref[...], info_ref[...])
    width = tile_ref.shape[1]
    for turn, w_ref in enumerate((w0_ref, w1_ref)):
        total = None
        for k in range(3):
            part = across(left[:, k * width : (k + 1) * width], w_ref[k], (1, 1))
            total = part if total is None else total + part
        total_ref[:, turned(total_ref, turn, place_ref[0])] = total
    split_parts(total_ref[...], place_ref, sent_ref, keep_ref)


def normed_kernel(place_ref, ga_ref, gb_ref, gc_ref, gd_ref, ia_ref, ib_ref, ic_ref, id_ref,
                  info_ref, x_ref, g0_ref, g1_ref, i0_ref, i1_ref,
                  sent_ref, keep_ref, gain_ref, tile_ref, total_ref):
    info = info_ref[...]
    width = tile_ref.shape[1]
    gathered(tile_ref, place_ref, (ga_ref, gb_ref, gc_ref, gd_ref))
    gates = three(tile_ref[...], info)
    gathered(tile_ref, place_ref, (ia_ref, ib_ref, ic_ref, id_ref))
    inners = three(tile_ref[...], info)
    for turn, (g_ref, i_ref) in enumerate(((g0_ref, i0_ref), (g1_ref, i1_ref))):
        total = None
        for k in range(3):
            lanes = slice(k * width, (k + 1) * width)
            part = across(gates[:, lanes], g_ref[k], (1, 1)) + across(inners[:, lanes], i_ref[k], (1, 1))
            total = part if total is None else total + part
        total_ref[:, turned(total_ref, turn, place_ref[0])] = total
    total = total_ref[...]
    split_parts(total, place_ref, sent_ref, keep_ref)

    @pl.when((pl.program_id(0) == 0) & (pl.program_id(1) == 0))
    def _():
        gain_ref[...] = jnp.zeros_like(gain_ref)

    x_hat = tile_rows(x_ref).astype(f32) * info[:, :1]
    gain_ref[...] += jnp.sum((total * x_hat).reshape(-1, 8, total.shape[1]), axis=0)


def weight_grad_kernel(chunks, steps, place_ref, info_ref, *refs):
    ins, (out0_ref, out1_ref, square_ref, tile_ref, sum_ref) = refs[: 5 * chunks], refs[5 * chunks :]
    at = pl.program_id(0)

    @pl.when(at == 0)
    def _():
        sum_ref[...] = jnp.zeros_like(sum_ref)

    for chunk in range(chunks):
        left_ref, *blocks = ins[5 * chunk : 5 * chunk + 5]

        @pl.when((at >= chunk * steps) & (at < (chunk + 1) * steps))
        def _(left_ref=left_ref, blocks=blocks):
            gathered(tile_ref, place_ref, blocks)
            right = three(tile_ref[...], info_ref[...])
            left = left_ref[...].reshape(-1, left_ref.shape[-1])
            sum_ref[...] += across(left, right, (0, 0))

    @pl.when(at == chunks * steps - 1)
    def _():
        half = sum_ref.shape[0] // 2
        width = tile_ref.shape[1]
        for turn, out_ref in enumerate((out0_ref, out1_ref)):
            rows = pl.ds(pl.multiple_of((turn ^ place_ref[0]) * half, half), half)
            for k in range(3):
                out_ref[k] = sum_ref[rows, k * width : (k + 1) * width].astype(out_ref.dtype)
        total = sum_ref[...]
        square_ref[...] = jnp.sum((total * total).reshape(-1, 8, total.shape[1]), axis=0)


SCALARS = pl.BlockSpec(memory_space=pltpu.SMEM)


def whole(array):
    return pl.BlockSpec(array.shape, lambda *at: (0,) * array.ndim)


def shape_of(shape, dtype):
    return jax.ShapeDtypeStruct(shape, dtype)


def call(kernel, name, grid, in_specs, out_specs, out_shape, scratch, flops, moved, args):
    return pl.pallas_call(
        kernel,
        grid=grid,
        in_specs=in_specs,
        out_specs=out_specs,
        out_shape=out_shape,
        scratch_shapes=scratch,
        cost_estimate=pl.CostEstimate(flops=flops, bytes_accessed=moved, transcendentals=0),
        compiler_params=pltpu.CompilerParams(
            dimension_semantics=("arbitrary",) * len(grid), vmem_limit_bytes=48 * MEGA
        ),
        name=name,
    )(*args)


class Tiles:
    def __init__(self, first, micros, parts, rows):
        self.first, self.micros, self.pairs, self.rows = first, micros, parts // 2, rows
        self.grid = (micros, self.pairs)
        self.tile = 2 * rows

    def raw(self, width):
        return pl.BlockSpec((2, 1, self.rows, width), lambda m, z: (z, self.first + m, 0, 0))

    def flat(self, width):
        return pl.BlockSpec((self.tile, width), lambda m, z: (m * self.pairs + z, 0))

    def info(self, width):
        first, pairs = self.first, self.pairs
        return pl.BlockSpec((self.tile, width), lambda m, z: ((first + m) * pairs + z, 0))

    def kindred(self, which, width):
        return pl.BlockSpec((1, self.tile, width), lambda m, z: (which, m * self.pairs + z, 0))

    def blocks(self, width):
        return pl.BlockSpec((2, self.tile, width), lambda m, z: (0, m * self.pairs + z, 0))

    def parted(self, width):
        return pl.BlockSpec((1, 1, self.rows, width), lambda m, z: (m, z, 0, 0))


def inner_product(tiles, place, tokens, info, gain, w):
    width = tokens.shape[-1]
    chans = w[0].shape[-1]
    rows = tiles.micros * tiles.pairs * tiles.tile
    return call(
        inner_kernel, "inner_product", tiles.grid,
        [SCALARS, tiles.raw(width), tiles.info(info.shape[1]), whole(gain), whole(w[0]), whole(w[1])],
        [tiles.flat(width), tiles.blocks(LANES), tiles.blocks(LANES)],
        [shape_of((rows, width), bf16), shape_of((2, rows, LANES), bf16), shape_of((2, rows, LANES), f32)],
        [pltpu.VMEM((tiles.tile, width), f32), pltpu.VMEM((tiles.tile, chans), f32)],
        6 * rows * width * chans, 8 * MEGA,
        (place, tokens, info, gain, *w),
    )


def gate_product(tiles, place, normed, back, info, w_gate, w_out):
    width = normed.shape[-1]
    chans = w_out[0].shape[-1]
    rows = normed.shape[0]
    return call(
        gate_kernel, "gate_product", tiles.grid,
        [SCALARS, tiles.flat(width), tiles.raw(width), tiles.info(info.shape[1])]
        + [whole(w) for w in (*w_gate, *w_out)],
        [tiles.blocks(2 * LANES), tiles.blocks(2 * LANES)],
        [shape_of((2, rows, 2 * LANES), bf16), shape_of((2, rows, 2 * LANES), f32)],
        [pltpu.VMEM((tiles.tile, width), f32), pltpu.VMEM((tiles.tile, chans), f32)],
        12 * rows * width * chans, 16 * MEGA,
        (place, normed, back, info, *w_gate, *w_out),
    )


def out_product(tiles, place, pairs, info, w_out):
    width = 2 * w_out[0].shape[1]
    chans = w_out[0].shape[-1]
    rows = pairs[0].shape[1]
    parted = (tiles.micros, tiles.pairs, tiles.rows, width)
    return call(
        out_kernel, "out_product", tiles.grid,
        [SCALARS] + [tiles.kindred(0, LANES)] * 4 + [tiles.info(info.shape[1]), whole(w_out[0]), whole(w_out[1])],
        [tiles.parted(width), tiles.parted(width)],
        [shape_of(parted, bf16), shape_of(parted, f32)],
        [pltpu.VMEM((tiles.tile, chans), f32), pltpu.VMEM((tiles.tile, width), f32)],
        6 * rows * width * chans, 8 * MEGA,
        (place, *pairs, info, *w_out),
    )


def normed_grad(tiles, place, pairs, inners, info, tokens, w_gate, w_inner):
    width = 2 * w_gate[0].shape[1]
    chans = w_gate[0].shape[-1]
    rows = inners[0].shape[0]
    parted = (tiles.micros, tiles.pairs, tiles.rows, width)
    return call(
        normed_kernel, "normed_grad", tiles.grid,
        [SCALARS] + [tiles.kindred(1, LANES)] * 4 + [tiles.flat(LANES)] * 4
        + [tiles.info(info.shape[1]), tiles.raw(width)] + [whole(w) for w in (*w_gate, *w_inner)],
        [tiles.parted(width), tiles.parted(width), pl.BlockSpec((8, width), lambda m, z: (0, 0))],
        [shape_of(parted, bf16), shape_of(parted, f32), shape_of((8, width), f32)],
        [pltpu.VMEM((tiles.tile, chans), f32), pltpu.VMEM((tiles.tile, width), f32)],
        12 * rows * width * chans, 16 * MEGA,
        (place, *pairs, *inners, info, tokens, *w_gate, *w_inner),
    )


def weight_grad(place, info, lefts, left_at, rights, right_at, span, dtype):
    chunks = len(lefts)
    width = lefts[0].shape[-1]
    chans = 4 * LANES
    steps = info.shape[0] // span // chunks
    piece = (3, width // 2, chans)
    specs, args = [], []
    for chunk in range(chunks):
        def held(spec, chunk=chunk):
            shape, at = spec
            low = chunk * steps
            return pl.BlockSpec(shape, lambda i: at(jnp.clip(i - low, 0, steps - 1), chunk))

        specs += [held(left_at)] + [held(right_at)] * 4
        args += [lefts[chunk], *rights[chunk]]
    return call(
        functools.partial(weight_grad_kernel, chunks, steps), "weight_grad", (chunks * steps,),
        [SCALARS, pl.BlockSpec((span, info.shape[1]), lambda i: (i, 0))] + specs,
        [pl.BlockSpec(piece, lambda i: (0, 0, 0))] * 2 + [pl.BlockSpec((8, 3 * chans), lambda i: (0, 0))],
        [shape_of(piece, dtype), shape_of(piece, dtype), shape_of((8, 3 * chans), f32)],
        [pltpu.VMEM((span, chans), f32), pltpu.VMEM((width, 3 * chans), f32)],
        6 * info.shape[0] * width * chans, 24 * MEGA,
        (place, info, *args),
    )


def pack_kernel(plane, flag_ref, after_ref, w_ref, *out_refs):
    half = w_ref.shape[-1] // 2
    for turn, out_ref in enumerate(out_refs):
        lanes = pl.ds(pl.multiple_of((turn ^ flag_ref[0]) * half, half), half)
        at = (0, slice(None), lanes) if plane is None else (0, slice(None), plane, lanes)
        out_ref[0] = w_ref[at].astype(bf16)


def pack(flag, after, weight, plane=None):
    kinds, rows = weight.shape[:2]
    chans = weight.shape[-1]
    half = chans // 2
    return call(
        functools.partial(pack_kernel, plane), "pack", (kinds,),
        [SCALARS, SCALARS, pl.BlockSpec((1,) + weight.shape[1:], lambda k: (k,) + (0,) * (weight.ndim - 1))],
        [pl.BlockSpec((1, rows, half), lambda k: (k, 0, 0))] * 2,
        [shape_of((kinds, rows, half), bf16)] * 2,
        [], 0, weight.size * 6, (flag, after, weight),
    )


def adam_kernel(rate, flag_ref, clip_ref, w_ref, m_ref, v_ref, *refs):
    pieces, (grad_ref, new_ref, first_ref, second_ref) = refs[:4], refs[4:]
    half = w_ref.shape[-1] // 2
    clip = clip_ref[0]
    for plane in range(2):
        for turn in range(2):
            lanes = pl.ds(pl.multiple_of((turn ^ flag_ref[0]) * half, half), half)
            at = (0, slice(None), plane, lanes)
            grad = pieces[2 * plane + turn][0].astype(f32)
            new, first, second = adam_update(w_ref[at], grad, m_ref[at], v_ref[at], clip, rate)
            grad_ref[at] = grad
            new_ref[at] = new
            first_ref[at] = first
            second_ref[at] = second


def adam(flag, clip, weight, first, second, pieces, rate):
    kinds, rows, _, chans = weight.shape
    block = min(rows, 64)
    full = pl.BlockSpec((1, block, 2, chans), lambda k, r: (k, r, 0, 0))
    piece = pl.BlockSpec((1, block, chans // 2), lambda k, r: (k, r, 0))
    return call(
        functools.partial(adam_kernel, rate), "adam", (kinds, rows // block),
        [SCALARS, SCALARS, full, full, full] + [piece] * 4,
        [full] * 4,
        [shape_of(weight.shape, f32)] * 4,
        [], weight.size * 20, weight.size * 32,
        (flag, clip, weight, first, second, *pieces),
    )


def body(
    groups, parts, chans,
    tokens_in, modality, starts, cotangent,
    in_weight, in_first, in_second,
    dt_weight, dt_first, dt_second,
    out_weight, out_first, out_second,
    x_weight, x_first, x_second,
    channel_params, channel_first, channel_second,
    gain, gain_first, gain_second,
):
    micros, tok_rows, part_width = tokens_in.shape
    model = gain.shape[0]
    chan_width = in_weight.shape[3]
    half = chan_width // 2
    own = half // chans
    cores = chans // 2
    inner_all = chan_width * chans
    x_width = x_weight.shape[1]
    rank = x_width - 2 * N
    dt_rows = dt_weight.shape[1]
    span = parts * tok_rows
    edge = K - 1
    t_at = lax.axis_index("t")
    p_at = lax.axis_index("p")
    c_at = lax.axis_index("c")
    z_at, y_at = p_at // 2, p_at % 2
    x_at, core_at = c_at // cores, c_at % cores
    s_at = t_at * parts + p_at
    slice_at = s_at // (2 * groups)
    everywhere = ("t", "p", "c")
    place = jnp.stack([x_at, core_at, y_at, z_at]).astype(jnp.int32)

    def flat(t, p, c):
        return (t * parts + p) * chans + c

    def part_of(c, j):
        return 2 * (2 * (c % cores) + j) + c // cores

    devices = [(t, p, c) for t in range(groups) for p in range(parts) for c in range(chans)]

    def first_hop(turn):
        pairs = []
        for t, p, c in devices:
            s = t * parts + p
            to_slice, i = s // (2 * groups), (s % (2 * groups)) // groups
            j = turn ^ (to_slice // cores)
            to = flat(s % groups, 2 * (2 * (c % cores) + j) + i, c // cores * cores + to_slice % cores)
            pairs.append((flat(t, p, c), to))
        return pairs

    def second_hop(turn):
        return [
            (flat(t, p, c), flat(t, p - p % 2 + c // cores, (turn ^ (p % 2)) * cores + c % cores))
            for t, p, c in devices
        ]

    small_pairs = [(flat(t, p, c), flat(t, part_of(c, p % 2), p // 2)) for t, p, c in devices]

    def send(value, pairs, back=False):
        if back:
            pairs = [(b, a) for a, b in pairs]
        return lax.ppermute(value, everywhere, pairs)

    def swap(value, axis, distance):
        return lax.ppermute(value, axis, [(i, i ^ distance) for i in range(lax.axis_size(axis))])

    def crossed(pair, flag):
        first, second = pair
        return jnp.where(flag == 0, first, second), jnp.where(flag == 0, second, first)

    between = y_at ^ (z_at % 2)

    def token(*values):
        return sum(value[(0,) * value.ndim].astype(f32) for value in values)[None]

    def weights_there(pair):
        pair = [send(value, first_hop(turn)) for turn, value in enumerate(pair)]
        arrived = token(*pair)
        pair = crossed(pair, between)
        pair = [send(value, second_hop(turn)) for turn, value in enumerate(pair)]
        if groups > 1:
            pair = [lax.all_gather(value, "t", axis=1, tiled=True) for value in pair]
        return tuple(pair), arrived

    def grads_back(pair):
        pair = [send(value, second_hop(turn), True) for turn, value in enumerate(pair)]
        pair = crossed(pair, between)
        return [send(value, first_hop(turn), True) for turn, value in enumerate(pair)]

    def along_groups(value, by):
        pairs = [(i, i + by) for i in range(groups) if 0 <= i + by < groups]
        return lax.ppermute(value, "t", pairs)

    def over_chans(value):
        distance = 1
        while distance < chans:
            value = value + swap(value, "c", distance)
            distance *= 2
        return value

    def pick(value, at, axis):
        return lax.dynamic_index_in_dim(value, at, axis, keepdims=False)

    def scattered_chans(sent, keep):
        total = keep + swap(sent, "c", 1).astype(f32)
        got = swap(pick(total, 1 - x_at, 0).astype(bf16), "c", cores)
        return pick(total, x_at, 0) + got.astype(f32)

    def gathered_chans(value):
        across_x = swap(value, "c", cores)
        across_core = swap(value, "c", 1)
        return (value, across_x, across_core, swap(across_x, "c", 1))

    def scattered_parts(sent, keep):
        total = keep + swap(sent, "p", 1).astype(f32)
        total = total.reshape(total.shape[0], -1, 2, *total.shape[2:])
        got = swap(pick(total, 1 - z_at % 2, 2).astype(bf16), "p", 2)
        total = pick(total, z_at % 2, 2) + got.astype(f32)
        got = swap(pick(total, 1 - z_at // 2, 1).astype(bf16), "p", 4)
        return pick(total, z_at // 2, 1) + got.astype(f32)

    def in_pair(mine, other, flag, axis):
        low, high = jnp.where(flag == 0, mine, other), jnp.where(flag == 0, other, mine)
        return jnp.stack([low, high], axis)

    def summed(value, kind):
        rows, length = value.shape
        total = value.reshape(rows, 2, 2, length // 4)
        got = swap(pick(total, 1 - core_at, 2).astype(kind), "c", 1)
        total = pick(total, core_at, 2) + got.astype(f32)
        got = swap(pick(total, 1 - x_at, 1).astype(kind), "c", cores)
        total = pick(total, x_at, 1) + got.astype(f32)
        distance = 1
        while distance < parts:
            total = total.astype(kind)
            total = total.astype(f32) + swap(total, "p", distance).astype(f32)
            distance *= 2
        total = total.astype(kind)
        total = in_pair(total, swap(total, "c", cores), x_at, 1)
        total = in_pair(total, swap(total, "c", 1), core_at, 2)
        return total.reshape(rows, length)

    extra = jnp.pad(modality.astype(bf16)[:, None, :], ((0, 0), (0, 15), (0, part_width - tok_rows)))
    tokens_all = lax.all_gather(jnp.concatenate([tokens_in, extra], 1), "p")
    kinds = tokens_all[:, :, tok_rows, :tok_rows].astype(jnp.int32)
    kinds = kinds.transpose(1, 0, 2).reshape(micros, span)
    flag = (slice_at // cores).astype(jnp.int32)[None]
    w_inner, arrived = weights_there(pack(flag, jnp.zeros((1,), f32), in_weight, 0))
    small = jnp.concatenate([x_weight.reshape(3 * x_width, chan_width), channel_params], 0)
    own_lanes = y_at * half + z_at * own
    small = send(lax.dynamic_slice_in_dim(small, own_lanes, own, 1), small_pairs)
    w_gate, arrived = weights_there(pack(flag, arrived, in_weight, 1))
    w_out, _ = weights_there(pack(flag, arrived, out_weight))
    back_all = lax.all_gather(cotangent, "p")
    dt_all = lax.all_gather(dt_weight.astype(bf16), ("t", "p"), axis=1, tiled=True)
    w_dt = send(lax.dynamic_slice_in_dim(dt_all, own_lanes, own, 2), small_pairs)

    squares = jnp.sum(jnp.square(tokens_all[:, :, :tok_rows].astype(f32)), axis=-1)
    squares = over_chans(squares).transpose(1, 0, 2).reshape(micros, span)
    inv_all = lax.rsqrt(squares / model + NORM_EPS)
    inv_own = lax.dynamic_slice_in_dim(inv_all, p_at * tok_rows, tok_rows, 1)[..., None]
    masks = [(kinds == k).astype(f32) for k in range(3)]
    info = jnp.stack([inv_all, *masks], -1).reshape(micros * span, 4)
    gain_part = lax.dynamic_slice_in_dim(gain, c_at * part_width, part_width, 0)[None]

    w_x = small[: 3 * x_width].astype(bf16).reshape(3, x_width, own)
    channel = small[3 * x_width :]
    conv_taps = channel[:K]
    conv_bias = channel[K]
    dt_bias = channel[K + 1]
    skip_gain = channel[K + 2]
    neg_rate = -jnp.exp(channel[K + 3 :])
    rules = lane_rules()

    def by_kind(value, kind):
        hit = (kind[:, None] == jnp.arange(3)[None, :])[:, :, None]
        return jnp.where(hit, value[:, None, :], jnp.zeros((), value.dtype))

    def dot(spec, left, right):
        return jnp.einsum(spec, left, right, preferred_element_type=f32)

    grad_dt_sum = grad_x_sum = grad_chan_sum = grad_gain_sum = 0.0
    outs, rows_back, held, products = [], [], [], []
    all_normed, all_pairs, all_inners = [], [], []
    chunk = min(GROUP, micros)
    for at in range(0, micros, chunk):
        ms = slice(at, at + chunk)
        tiles = Tiles(at, chunk, parts, tok_rows)
        kind = kinds[ms].reshape(-1)
        normed, sent, keep = inner_product(tiles, place, tokens_all, info, gain_part, w_inner)
        inner_part = scattered_chans(sent, keep).reshape(chunk, span, own)
        sent, keep = gate_product(tiles, place, normed, back_all, info, w_gate, w_out)
        pair = scattered_chans(sent, keep).reshape(chunk, span, 2, own)
        gate_part, d_mixed = pair[:, :, 0], pair[:, :, 1]
        positions = t_at * span - edge + jnp.arange(span + 2 * edge, dtype=jnp.int32)
        begin = starts[ms]
        segment = jnp.sum(
            (begin[:, None, :] <= positions[None, :, None]).astype(jnp.int32), axis=2
        )
        keep_mask = 1.0 - jnp.any(
            begin[:, None, :] == positions[None, edge : edge + span, None], axis=2
        ).astype(f32)
        same_doc = [
            (
                segment[:, edge - j : edge - j + span + edge]
                == segment[:, edge : edge + span + edge]
            ).astype(f32)[..., None]
            for j in range(K)
        ]
        none = jnp.zeros((chunk, edge, own), f32)
        before = along_groups(inner_part[:, span - edge :], 1) if groups > 1 else none
        padded = jnp.concatenate([before, inner_part], 1)
        conv_out = conv_bias + sum(
            conv_taps[j] * padded[:, edge - j : edge - j + span] * same_doc[j][:, :span]
            for j in range(K)
        )
        activated = jax.nn.silu(conv_out).astype(bf16)
        act_float = activated.astype(f32)
        act3 = by_kind(activated.reshape(-1, own), kind)
        projected_x = summed(dot("kxc,tkc->xt", w_x, act3), f32)
        low_t = projected_x[:rank].astype(bf16)
        mats = projected_x[rank:].reshape(2, N, chunk, span).transpose(0, 2, 1, 3)
        low3 = by_kind(low_t.T, kind)
        dt_pre = dot("tkr,krc->tc", low3, w_dt).reshape(chunk, span, own) + dt_bias
        step_size = jax.nn.softplus(dt_pre)
        gate_act = jax.nn.silu(gate_part)
        d_scan = d_mixed * gate_act
        zero_state = jnp.zeros((chunk, N, own), f32)
        lanes = split_lanes(mats[0].swapaxes(1, 2), mats[1].swapaxes(1, 2))
        args = (step_size, act_float, d_scan, keep_mask, lanes, *rules, neg_rate)
        state_in = zero_state
        if groups > 1:
            ends = scan_forward(*args, zero_state)[3]
            passed_all = jnp.exp(jnp.sum(step_size, axis=1)[:, None, :] * neg_rate)
            passed_all = passed_all * jnp.prod(keep_mask, axis=1)[:, None, None]
            for _ in range(groups - 1):
                state_in = along_groups(passed_all * state_in + ends, 1)
        y_part, states_before, grad_c, _ = scan_forward(*args, state_in)
        y_scan = y_part + skip_gain * act_float
        mixed_in = (y_scan * gate_act).astype(bf16)
        d_gate = (d_mixed * y_scan * silu_grad(gate_part)).astype(bf16)
        pairs = gathered_chans(jnp.stack([mixed_in, d_gate]).reshape(2, chunk * span, own))
        all_normed.append(normed)
        all_pairs.append(pairs)
        held.append(
            (tiles, kind, args, states_before, step_size, act_float, d_scan, dt_pre, low3, grad_c)
            + (activated, conv_out, padded, same_doc, none)
        )

    for at, stage in enumerate(held):
        tiles, kind, args, states_before, step_size, act_float, d_scan, dt_pre, low3 = stage[:9]
        grad_c = stage[9]
        order = token(states_before if at else held[-1][3], *(sent for sent, _ in products))
        args = (*args[:-1], neg_rate + 0.0 * order)
        adj_in = zero_state
        if groups > 1:
            ends = scan_backward(*args, zero_state, states_before)[4]
            passed_all = jnp.exp(jnp.sum(step_size, axis=1)[:, None, :] * neg_rate)
            passed_all = passed_all * jnp.prod(args[3], axis=1)[:, None, None]
            for _ in range(groups - 1):
                adj_in = along_groups(passed_all * adj_in + ends, -1)
        b_pull, rate_pull, grad_b, grad_rate, _ = scan_backward(*args, adj_in, states_before)
        d_step = rate_pull + act_float * b_pull
        d_rate = jnp.sum(grad_rate, axis=0) * neg_rate
        d_act = d_scan * skip_gain + step_size * b_pull
        d_skip = jnp.sum(d_scan * act_float, axis=(0, 1))
        d_pre = (d_step * jax.nn.sigmoid(dt_pre)).astype(bf16)
        d_bias = jnp.sum(d_pre.astype(f32), axis=(0, 1))
        d_pre = d_pre.reshape(-1, own)
        d_low = dot("krc,tkc->rt", w_dt, by_kind(d_pre, kind))
        grad_dt_sum += dot("tkr,tc->krc", low3, d_pre)
        grad_bc = jnp.stack([grad_b, grad_c]).transpose(0, 2, 1, 3).reshape(2 * N, -1)
        d_projx = summed(jnp.concatenate([d_low, grad_bc], 0), bf16)
        held[at] = (tiles, kind, d_projx, d_act, *stage[10:], d_bias, d_skip, d_rate)
        products.append(out_product(tiles, place, all_pairs[at], info, w_out))
        outs.append(scattered_parts(*products[-1]))

    kept = f32 if groups > 1 else bf16

    def kindred(which):
        return ((1, span, own), lambda m, chunk_at: (which, m, 0))

    rows_at = ((span, part_width), lambda m, chunk_at: (m, 0))
    raw_at = ((parts, 1, tok_rows, part_width), lambda m, chunk_at: (0, chunk_at * chunk + m, 0, 0))
    backs = [back_all] * len(all_pairs)
    *g_out, out_sq = weight_grad(place, info, backs, raw_at, all_pairs, kindred(0), span, kept)
    *g_gate, gate_sq = weight_grad(place, info, all_normed, rows_at, all_pairs, kindred(1), span, kept)
    done = [token(*(sent for sent, _ in products)), token(out_sq, gate_sq)]

    for at, stage in enumerate(held):
        tiles, kind, d_projx, d_act, activated, conv_out, padded, same_doc, none = stage[:9]
        d_bias, d_skip, d_rate = stage[9:]
        projx3 = by_kind(d_projx.T, kind)
        w_x_now = w_x + (0.0 * done[min(at, 1)]).astype(bf16)
        d_act = d_act + dot("tkx,kxc->tc", projx3, w_x_now).reshape(chunk, span, own)
        grad_x_sum += dot("tkx,tc->kxc", projx3, activated.reshape(-1, own))
        d_conv = d_act * silu_grad(conv_out)
        after = along_groups(d_conv[:, :edge], -1) if groups > 1 else none
        d_conv_ext = jnp.concatenate([d_conv, after], 1)
        d_inner = sum(
            conv_taps[j] * d_conv_ext[:, j : j + span] * same_doc[j][:, j : j + span]
            for j in range(K)
        )
        d_taps = jnp.stack(
            [
                jnp.sum(
                    d_conv * padded[:, edge - j : edge - j + span] * same_doc[j][:, :span],
                    axis=(0, 1),
                )
                for j in range(K)
            ]
        )
        d_conv_bias = jnp.sum(d_conv, axis=(0, 1))
        grad_chan_sum += jnp.concatenate(
            [d_taps, d_conv_bias[None], d_bias[None], d_skip[None], d_rate], 0
        )
        inners = gathered_chans(d_inner.astype(bf16).reshape(chunk * span, own))
        sent, keep, gain_rows = normed_grad(
            tiles, place, all_pairs[at], inners, info, tokens_all, w_gate, w_inner
        )
        grad_gain_sum += jnp.sum(gain_rows, axis=0)
        rows_back.append(scattered_parts(sent, keep))
        all_inners.append(inners)

    flat_at = ((span, own), lambda m, chunk_at: (m, 0))
    *g_inner, inner_sq = weight_grad(place, info, all_normed, rows_at, all_inners, flat_at, span, kept)
    g_small = jnp.concatenate(
        [grad_x_sum.reshape(-1, own), grad_dt_sum.reshape(-1, own), grad_chan_sum], 0
    )
    if groups > 1:
        g_small = lax.psum(g_small, "t")
        over = lambda pair: [
            lax.psum_scatter(value, "t", scatter_dimension=1, tiled=True) for value in pair
        ]
        g_out, g_gate, g_inner = over(g_out), over(g_gate), over(g_inner)
        large_sq = sum(jnp.sum(value * value) for value in (*g_out, *g_gate, *g_inner))
        g_out, g_gate, g_inner = (
            [value.astype(bf16) for value in pair] for pair in (g_out, g_gate, g_inner)
        )
    else:
        large_sq = jnp.sum(out_sq) + jnp.sum(gate_sq) + jnp.sum(inner_sq)
    local_sq = large_sq + jnp.sum(g_small * g_small) / groups
    here = (jnp.arange(chans) == c_at).astype(f32)
    tail = jnp.concatenate([(here[:, None] * grad_gain_sum).reshape(-1), local_sq[None]])
    tail = lax.psum(tail, everywhere)
    grad_gain = tail[:model]
    grad_norm = jnp.sqrt(tail[model] + jnp.sum(grad_gain * grad_gain))
    clip_scale = CLIP_LIMIT / jnp.maximum(grad_norm, CLIP_LIMIT)

    def back_whole(pair):
        return jnp.concatenate(crossed(grads_back(pair), flag[0]), -1).astype(f32)

    grad_out = back_whole(g_out)
    in_pieces = (*grads_back(g_inner), *grads_back(g_gate))
    small_back = lax.all_gather(send(g_small.astype(bf16), small_pairs, True), "p")
    small_back = small_back.reshape(chans, 2, -1, own).transpose(2, 1, 0, 3)
    small_back = small_back.reshape(-1, chan_width).astype(f32)
    grad_x = small_back[: 3 * x_width].reshape(3, x_width, chan_width)
    grad_dt = small_back[3 * x_width : 3 * x_width + 3 * rank].reshape(3, rank, chan_width)
    grad_dt = lax.dynamic_slice_in_dim(grad_dt, s_at * dt_rows, dt_rows, 1)
    grad_chan = small_back[3 * x_width + 3 * rank :]

    tok_float = tokens_in.astype(f32)
    mixed = (tok_float + jnp.concatenate(outs, 0)).astype(bf16)
    d_own = jnp.concatenate(rows_back, 0)
    x_hat_own = tok_float * inv_own
    d_hat = d_own * gain_part
    mean = over_chans(jnp.sum(d_hat * x_hat_own, axis=-1))[..., None] / model
    input_grad = cotangent.astype(f32) + inv_own * (d_hat - x_hat_own * mean)

    grad_in, in_new, in_first_new, in_second_new = adam(
        flag, clip_scale[None], in_weight, in_first, in_second, in_pieces, model ** (-0.5)
    )
    dt_new, dt_first_new, dt_second_new = adam_update(
        dt_weight, grad_dt, dt_first, dt_second, clip_scale, rank ** (-0.5)
    )
    out_new, out_first_new, out_second_new = adam_update(
        out_weight, grad_out, out_first, out_second, clip_scale, inner_all ** (-0.5)
    )
    x_new, x_first_new, x_second_new = adam_update(
        x_weight, grad_x, x_first, x_second, clip_scale, inner_all ** (-0.5)
    )
    chan_new, chan_first_new, chan_second_new = adam_update(
        channel_params, grad_chan, channel_first, channel_second, clip_scale, 0.5
    )
    gain_new, gain_first_new, gain_second_new = adam_update(
        gain, grad_gain, gain_first, gain_second, clip_scale, 0.5
    )
    return (
        mixed, input_grad, grad_norm,
        grad_in, in_new, in_first_new, in_second_new,
        grad_dt, dt_new, dt_first_new, dt_second_new,
        grad_out, out_new, out_first_new, out_second_new,
        grad_x, x_new, x_first_new, x_second_new,
        grad_chan, chan_new, chan_first_new, chan_second_new,
        grad_gain, gain_new, gain_first_new, gain_second_new,
        in_new.astype(bf16), dt_new.astype(bf16), out_new.astype(bf16), x_new.astype(bf16),
    )


def solution(mesh):
    chans = mesh.shape["ch"]
    parts = 2 * chans
    groups = mesh.shape["seq"] // parts
    inside = Mesh(mesh.devices.reshape(groups, parts, chans), ("t", "p", "c"))
    seq = ("t", "p")
    tok = P(None, seq, "c")
    wide = P(None, seq, None, "c")
    rows = P(None, seq, "c")
    flat = P(None, None, "c")
    chan = P(None, "c")
    return jax.shard_map(
        functools.partial(body, groups, parts, chans),
        mesh=inside,
        in_specs=(tok, P(None, seq), P(), tok)
        + (wide,) * 3 + (rows,) * 3 + (rows,) * 3 + (flat,) * 3 + (chan,) * 3 + (P(),) * 3,
        out_specs=(tok, tok, P())
        + (wide,) * 4 + (rows,) * 4 + (rows,) * 4 + (flat,) * 4 + (chan,) * 4 + (P(),) * 4
        + (wide, rows, rows, flat),
        check_vma=False,
    )
```

```python
import functools

import jax
import jax.numpy as jnp
from jax import lax
from jax.experimental import pallas as pl
from jax.experimental.pallas import tpu as pltpu
from jax.sharding import Mesh
from jax.sharding import PartitionSpec as P

N = 16
K = 4
STEP = 10

NORM_EPS = 1e-05
BETA_ONE = 0.9
BETA_TWO = 0.95
ADAM_EPS = 1e-08
DECAY = 0.1
CLIP_LIMIT = 1.0
LANES = 128
SCAN_ROWS = 128
MEGA = 1024 * 1024
GROUP = 2
f32 = jnp.float32
bf16 = jnp.bfloat16


def silu_grad(value):
    sigma = jax.nn.sigmoid(value)
    return sigma * (1.0 + value * (1.0 - sigma))


def adam_update(weight, gradient, first_moment, second, clip_scale, step_rate):
    clipped = gradient * clip_scale
    first_new = BETA_ONE * first_moment + (1.0 - BETA_ONE) * clipped
    second_new = BETA_TWO * second + (1.0 - BETA_TWO) * clipped * clipped
    first_hat = first_new / (1.0 - BETA_ONE**STEP)
    second_hat = second_new / (1.0 - BETA_TWO**STEP)
    weight_new = weight - step_rate * (
        first_hat / (jnp.sqrt(second_hat) + ADAM_EPS) + DECAY * weight
    )
    return (weight_new, first_new, second_new)


def sum_rows(parts):
    at = lax.broadcasted_iota(jnp.int32, parts[0].shape, 0)
    for distance in (1, 2, 4):
        low = at % (2 * distance) < distance
        parts = [
            jnp.where(low, a, b) + pltpu.roll(jnp.where(low, b, a), distance, 0)
            for a, b in zip(parts[0::2], parts[1::2])
        ]
    return parts[0]


def lane_rules():
    lanes = jnp.arange(LANES)
    used = lanes % (LANES // 2) < 3 * N
    mask = ((lanes[None, :] % N == jnp.arange(N)[:, None]) & used[None, :]).astype(f32)
    side = (lanes[:, None] // (LANES // 2) == jnp.arange(2 * LANES)[None, :] // LANES).astype(bf16)
    return mask, side


def matmul(left, right):
    return jnp.dot(left, right, preferred_element_type=f32)


def spread(rows_ref, m, base, mask, side):
    left = [rows_ref[m, pl.ds(base + j, 1), :] * mask for j in range(8)]
    return matmul(jnp.concatenate(left, 0).astype(bf16), side)


def lane_sums(product_ref, m, grads, lane, base, ones):
    sums = matmul(product_ref[m], ones)
    for j in range(8):
        grads = jnp.where(lane == base + j, sums[N * j : N * j + N], grads)
    return grads


def turned(ref, turn, x_at):
    width = ref.shape[-1] // 2
    return pl.ds(pl.multiple_of((turn ^ x_at) * width, width), width)


def three(tile, info):
    return jnp.concatenate([(tile * info[:, k + 1 : k + 2]).astype(bf16) for k in range(3)], -1)


def across(left, right, dims):
    return lax.dot_general(left, right, ((dims[0:1], dims[1:2]), ((), ())), preferred_element_type=f32)


def stacked(ref):
    kinds, rows, cols = ref.shape
    return ref[...].reshape(kinds * rows, cols)


def split_blocks(total, place_ref, sent_ref, keep_ref, scratch_ref, offset):
    scratch_ref[...] = total
    core = place_ref[1]
    for x in range(2):
        away = pl.ds(pl.multiple_of((2 * x + 1 - core) * LANES, LANES), LANES)
        here = pl.ds(pl.multiple_of((2 * x + core) * LANES, LANES), LANES)
        sent_ref[x, :, offset : offset + LANES] = scratch_ref[:, away].astype(bf16)
        keep_ref[x, :, offset : offset + LANES] = scratch_ref[:, here]


def tile_rows(ref):
    return ref[...].reshape(-1, ref.shape[-1])


def wide_product(tile_ref, info, w_refs, scratch_ref, x_at):
    total = None
    for turn, w_ref in enumerate(w_refs):
        left = three(tile_ref[:, turned(tile_ref, turn, x_at)], info)
        part = across(left, stacked(w_ref), (1, 0))
        total = part if total is None else total + part
    return total


def inner_kernel(place_ref, x_ref, info_ref, gain_ref, w0_ref, w1_ref,
                 normed_ref, sent_ref, keep_ref, tile_ref, scratch_ref):
    info = info_ref[...]
    normed = tile_rows(x_ref).astype(f32) * info[:, :1] * gain_ref[...]
    normed = normed.astype(bf16)
    normed_ref[...] = normed
    tile_ref[...] = normed.astype(f32)
    total = wide_product(tile_ref, info, (w0_ref, w1_ref), scratch_ref, place_ref[0])
    split_blocks(total, place_ref, sent_ref, keep_ref, scratch_ref, 0)


def gate_kernel(place_ref, normed_ref, back_ref, info_ref, g0_ref, g1_ref, o0_ref, o1_ref,
                sent_ref, keep_ref, tile_ref, scratch_ref):
    info = info_ref[...]
    tile_ref[...] = normed_ref[...].astype(f32)
    total = wide_product(tile_ref, info, (g0_ref, g1_ref), scratch_ref, place_ref[0])
    split_blocks(total, place_ref, sent_ref, keep_ref, scratch_ref, 0)
    tile_ref[...] = tile_rows(back_ref).astype(f32)
    total = wide_product(tile_ref, info, (o0_ref, o1_ref), scratch_ref, place_ref[0])
    split_blocks(total, place_ref, sent_ref, keep_ref, scratch_ref, LANES)


def gathered(scratch_ref, place_ref, refs):
    at = 2 * place_ref[0] + place_ref[1]
    for distance, ref in zip((0, 2, 1, 3), refs):
        lanes = pl.ds(pl.multiple_of((at ^ distance) * LANES, LANES), LANES)
        scratch_ref[:, lanes] = tile_of(ref).astype(f32)


def tile_of(ref):
    return ref[...].reshape(-1, ref.shape[-1])


def split_parts(total, place_ref, sent_ref, keep_ref):
    y = place_ref[2]
    half = total.shape[0] // 2
    low, high = total[:half], total[half:]
    mine = jnp.full(low.shape, y, jnp.int32) == 0
    sent_ref[...] = jnp.where(mine, high, low).astype(bf16).reshape(sent_ref.shape)
    keep_ref[...] = jnp.where(mine, low, high).reshape(keep_ref.shape)


def out_kernel(place_ref, a_ref, b_ref, c_ref, d_ref, info_ref, w0_ref, w1_ref,
               sent_ref, keep_ref, tile_ref, total_ref):
    gathered(tile_ref, place_ref, (a_ref, b_ref, c_ref, d_ref))
    left = three(tile_ref[...], info_ref[...])
    width = tile_ref.shape[1]
    for turn, w_ref in enumerate((w0_ref, w1_ref)):
        total = None
        for k in range(3):
            part = across(left[:, k * width : (k + 1) * width], w_ref[k], (1, 1))
            total = part if total is None else total + part
        total_ref[:, turned(total_ref, turn, place_ref[0])] = total
    split_parts(total_ref[...], place_ref, sent_ref, keep_ref)


def normed_kernel(place_ref, ga_ref, gb_ref, gc_ref, gd_ref, ia_ref, ib_ref, ic_ref, id_ref,
                  info_ref, x_ref, g0_ref, g1_ref, i0_ref, i1_ref,
                  sent_ref, keep_ref, gain_ref, tile_ref, total_ref):
    info = info_ref[...]
    width = tile_ref.shape[1]
    gathered(tile_ref, place_ref, (ga_ref, gb_ref, gc_ref, gd_ref))
    gates = three(tile_ref[...], info)
    gathered(tile_ref, place_ref, (ia_ref, ib_ref, ic_ref, id_ref))
    inners = three(tile_ref[...], info)
    for turn, (g_ref, i_ref) in enumerate(((g0_ref, i0_ref), (g1_ref, i1_ref))):
        total = None
        for k in range(3):
            lanes = slice(k * width, (k + 1) * width)
            part = across(gates[:, lanes], g_ref[k], (1, 1)) + across(inners[:, lanes], i_ref[k], (1, 1))
            total = part if total is None else total + part
        total_ref[:, turned(total_ref, turn, place_ref[0])] = total
    total = total_ref[...]
    split_parts(total, place_ref, sent_ref, keep_ref)

    @pl.when((pl.program_id(0) == 0) & (pl.program_id(1) == 0))
    def _():
        gain_ref[...] = jnp.zeros_like(gain_ref)

    x_hat = tile_rows(x_ref).astype(f32) * info[:, :1]
    gain_ref[...] += jnp.sum((total * x_hat).reshape(-1, 8, total.shape[1]), axis=0)


def weight_grad_kernel(chunks, steps, place_ref, info_ref, *refs):
    ins, (out0_ref, out1_ref, square_ref, tile_ref, sum_ref) = refs[: 5 * chunks], refs[5 * chunks :]
    at = pl.program_id(0)

    @pl.when(at == 0)
    def _():
        sum_ref[...] = jnp.zeros_like(sum_ref)

    for chunk in range(chunks):
        left_ref, *blocks = ins[5 * chunk : 5 * chunk + 5]

        @pl.when((at >= chunk * steps) & (at < (chunk + 1) * steps))
        def _(left_ref=left_ref, blocks=blocks):
            gathered(tile_ref, place_ref, blocks)
            right = three(tile_ref[...], info_ref[...])
            left = left_ref[...].reshape(-1, left_ref.shape[-1])
            sum_ref[...] += across(left, right, (0, 0))

    @pl.when(at == chunks * steps - 1)
    def _():
        half = sum_ref.shape[0] // 2
        width = tile_ref.shape[1]
        for turn, out_ref in enumerate((out0_ref, out1_ref)):
            rows = pl.ds(pl.multiple_of((turn ^ place_ref[0]) * half, half), half)
            for k in range(3):
                out_ref[k] = sum_ref[rows, k * width : (k + 1) * width].astype(out_ref.dtype)
        total = sum_ref[...]
        square_ref[...] = jnp.sum((total * total).reshape(-1, 8, total.shape[1]), axis=0)


SCALARS = pl.BlockSpec(memory_space=pltpu.SMEM)


def whole(array):
    return pl.BlockSpec(array.shape, lambda *at: (0,) * array.ndim)


def shape_of(shape, dtype):
    return jax.ShapeDtypeStruct(shape, dtype)


def call(kernel, name, grid, in_specs, out_specs, out_shape, scratch, flops, moved, args):
    return pl.pallas_call(
        kernel,
        grid=grid,
        in_specs=in_specs,
        out_specs=out_specs,
        out_shape=out_shape,
        scratch_shapes=scratch,
        cost_estimate=pl.CostEstimate(flops=flops, bytes_accessed=moved, transcendentals=0),
        compiler_params=pltpu.CompilerParams(
            dimension_semantics=("arbitrary",) * len(grid), vmem_limit_bytes=48 * MEGA
        ),
        name=name,
    )(*args)


class Tiles:
    def __init__(self, first, micros, parts, rows):
        self.first, self.micros, self.pairs, self.rows = first, micros, parts // 2, rows
        self.grid = (micros, self.pairs)
        self.tile = 2 * rows

    def raw(self, width):
        return pl.BlockSpec((2, 1, self.rows, width), lambda m, z: (z, self.first + m, 0, 0))

    def flat(self, width):
        return pl.BlockSpec((self.tile, width), lambda m, z: (m * self.pairs + z, 0))

    def info(self, width):
        first, pairs = self.first, self.pairs
        return pl.BlockSpec((self.tile, width), lambda m, z: ((first + m) * pairs + z, 0))

    def kindred(self, which, width):
        return pl.BlockSpec((1, self.tile, width), lambda m, z: (which, m * self.pairs + z, 0))

    def blocks(self, width):
        return pl.BlockSpec((2, self.tile, width), lambda m, z: (0, m * self.pairs + z, 0))

    def parted(self, width):
        return pl.BlockSpec((1, 1, self.rows, width), lambda m, z: (m, z, 0, 0))


def inner_product(tiles, place, tokens, info, gain, w):
    width = tokens.shape[-1]
    chans = w[0].shape[-1]
    rows = tiles.micros * tiles.pairs * tiles.tile
    return call(
        inner_kernel, "inner_product", tiles.grid,
        [SCALARS, tiles.raw(width), tiles.info(info.shape[1]), whole(gain), whole(w[0]), whole(w[1])],
        [tiles.flat(width), tiles.blocks(LANES), tiles.blocks(LANES)],
        [shape_of((rows, width), bf16), shape_of((2, rows, LANES), bf16), shape_of((2, rows, LANES), f32)],
        [pltpu.VMEM((tiles.tile, width), f32), pltpu.VMEM((tiles.tile, chans), f32)],
        6 * rows * width * chans, 8 * MEGA,
        (place, tokens, info, gain, *w),
    )


def gate_product(tiles, place, normed, back, info, w_gate, w_out):
    width = normed.shape[-1]
    chans = w_out[0].shape[-1]
    rows = normed.shape[0]
    return call(
        gate_kernel, "gate_product", tiles.grid,
        [SCALARS, tiles.flat(width), tiles.raw(width), tiles.info(info.shape[1])]
        + [whole(w) for w in (*w_gate, *w_out)],
        [tiles.blocks(2 * LANES), tiles.blocks(2 * LANES)],
        [shape_of((2, rows, 2 * LANES), bf16), shape_of((2, rows, 2 * LANES), f32)],
        [pltpu.VMEM((tiles.tile, width), f32), pltpu.VMEM((tiles.tile, chans), f32)],
        12 * rows * width * chans, 16 * MEGA,
        (place, normed, back, info, *w_gate, *w_out),
    )


def out_product(tiles, place, pairs, info, w_out):
    width = 2 * w_out[0].shape[1]
    chans = w_out[0].shape[-1]
    rows = pairs[0].shape[1]
    parted = (tiles.micros, tiles.pairs, tiles.rows, width)
    return call(
        out_kernel, "out_product", tiles.grid,
        [SCALARS] + [tiles.kindred(0, LANES)] * 4 + [tiles.info(info.shape[1]), whole(w_out[0]), whole(w_out[1])],
        [tiles.parted(width), tiles.parted(width)],
        [shape_of(parted, bf16), shape_of(parted, f32)],
        [pltpu.VMEM((tiles.tile, chans), f32), pltpu.VMEM((tiles.tile, width), f32)],
        6 * rows * width * chans, 8 * MEGA,
        (place, *pairs, info, *w_out),
    )


def normed_grad(tiles, place, pairs, inners, info, tokens, w_gate, w_inner):
    width = 2 * w_gate[0].shape[1]
    chans = w_gate[0].shape[-1]
    rows = inners[0].shape[0]
    parted = (tiles.micros, tiles.pairs, tiles.rows, width)
    return call(
        normed_kernel, "normed_grad", tiles.grid,
        [SCALARS] + [tiles.kindred(1, LANES)] * 4 + [tiles.flat(LANES)] * 4
        + [tiles.info(info.shape[1]), tiles.raw(width)] + [whole(w) for w in (*w_gate, *w_inner)],
        [tiles.parted(width), tiles.parted(width), pl.BlockSpec((8, width), lambda m, z: (0, 0))],
        [shape_of(parted, bf16), shape_of(parted, f32), shape_of((8, width), f32)],
        [pltpu.VMEM((tiles.tile, chans), f32), pltpu.VMEM((tiles.tile, width), f32)],
        12 * rows * width * chans, 16 * MEGA,
        (place, *pairs, *inners, info, tokens, *w_gate, *w_inner),
    )


def weight_grad(place, info, lefts, left_at, rights, right_at, span, dtype):
    chunks = len(lefts)
    width = lefts[0].shape[-1]
    chans = 4 * LANES
    steps = info.shape[0] // span // chunks
    piece = (3, width // 2, chans)
    specs, args = [], []
    for chunk in range(chunks):
        def held(spec, chunk=chunk):
            shape, at = spec
            low = chunk * steps
            return pl.BlockSpec(shape, lambda i: at(jnp.clip(i - low, 0, steps - 1), chunk))

        specs += [held(left_at)] + [held(right_at)] * 4
        args += [lefts[chunk], *rights[chunk]]
    return call(
        functools.partial(weight_grad_kernel, chunks, steps), "weight_grad", (chunks * steps,),
        [SCALARS, pl.BlockSpec((span, info.shape[1]), lambda i: (i, 0))] + specs,
        [pl.BlockSpec(piece, lambda i: (0, 0, 0))] * 2 + [pl.BlockSpec((8, 3 * chans), lambda i: (0, 0))],
        [shape_of(piece, dtype), shape_of(piece, dtype), shape_of((8, 3 * chans), f32)],
        [pltpu.VMEM((span, chans), f32), pltpu.VMEM((width, 3 * chans), f32)],
        6 * info.shape[0] * width * chans, 24 * MEGA,
        (place, info, *args),
    )


def masked_sum(wide, info):
    width = wide.shape[1] // 3
    return sum(wide[:, k * width : (k + 1) * width] * info[:, k + 1 : k + 2] for k in range(3))


def halves(place_ref, micro, second, own_ref, x_ref, core_ref, both_ref):
    shape = own_ref.shape
    same_x = jnp.full(shape, place_ref[0] ^ micro, jnp.int32) == 0
    same_core = jnp.full(shape, place_ref[1] ^ second, jnp.int32) == 0
    own, across_x, across_core, both = (
        ref[...].astype(f32) for ref in (own_ref, x_ref, core_ref, both_ref)
    )
    return jnp.where(same_core, jnp.where(same_x, own, across_x), jnp.where(same_x, across_core, both))


def scan_scratch(micros):
    wide = pltpu.VMEM((micros, 8 * N, 2 * LANES), f32)
    product = pltpu.VMEM((micros, 8 * N, LANES), bf16)
    tile = pltpu.VMEM((micros, SCAN_ROWS, LANES), f32)
    return [pltpu.VMEM((micros, N, LANES), f32), wide, wide, product, product, tile, tile, tile]


def mix_forward_kernel(
    place_ref, keep_ref, own_ref, x_ref, core_ref, both_ref, act_ref, pair_ref, info_ref,
    dt_ref, mask_ref, side_ref, rate_ref, bias_ref, start_ref,
    kinds_ref, before_ref, step_ref, slope_ref, pull_ref, rows_ref, low_ref, grad_c_ref, final_ref,
    state_ref, wide_a, wide_b, product_a, product_b, drive_ref, y_ref, scaled_ref,
):
    micros, rows, _ = step_ref.shape
    block = pl.program_id(0)
    second = (2 * block) // pl.num_programs(0)
    rank = low_ref.shape[1]
    rate = rate_ref[...]
    mask = mask_ref[...]
    side = side_ref[...]
    ones = jnp.ones((LANES, LANES), bf16)
    lane = lax.broadcasted_iota(jnp.int32, (N, LANES), 1)
    dt_bias, skip = bias_ref[0:1], bias_ref[1:2]

    @pl.when(block == 0)
    def _():
        state_ref[...] = start_ref[...]

    for m in range(micros):
        shared = halves(place_ref, m, second, own_ref, x_ref, core_ref, both_ref)
        low = shared[:rank].astype(bf16)
        low_ref[m] = low
        dt_pre = masked_sum(across(low, dt_ref[...], (0, 0)), info_ref[m]) + dt_bias
        small = jnp.exp(-jnp.abs(dt_pre))
        step = jnp.maximum(dt_pre, 0.0) + jnp.log1p(small)
        step_ref[m] = step
        slope_ref[m] = jnp.where(dt_pre >= 0, 1.0, small) / (1.0 + small)
        drive_ref[m] = step * act_ref[m].astype(f32)
        gate = pair_ref[m, :, :LANES]
        pull_ref[m] = pair_ref[m, :, LANES:] * (gate * jax.nn.sigmoid(gate))
        parts = []
        for left in (shared[rank : rank + N], shared[rank + N :]):
            for _ in range(3):
                part = left.astype(bf16).astype(f32)
                parts.append(part)
                left = left - part
            parts.append(jnp.zeros_like(left))
        rows_ref[m] = jnp.concatenate(parts, 0).T
        wide_a[m] = spread(rows_ref, m, 0, mask, side)

    def sixteen(turn, carried):
        states, grads = (list(part) for part in carried)
        for half in range(2):
            base = pl.multiple_of(turn * 16 + 8 * half, 8)
            wide, wide_next = (wide_a, wide_b) if half == 0 else (wide_b, wide_a)
            product, product_last = (product_a, product_b) if half == 0 else (product_b, product_a)
            following = jnp.minimum(base + 8, rows - 8)
            for m in range(micros):
                wide_next[m] = spread(rows_ref, m, following, mask, side)
                grads[m] = lane_sums(product_last, m, grads[m], lane, base - 8, ones)
            y_parts = [[] for _ in range(micros)]
            for j in range(8):
                for m in range(micros):
                    row = pl.ds(base + j, 1)
                    own = slice(N * j, N * j + N)
                    before = states[m]
                    before_ref[m, base + j] = before
                    before = before * keep_ref[m, block * rows + base + j]
                    state = (
                        jnp.exp(step_ref[m, row, :] * rate) * before
                        + drive_ref[m, row, :] * wide[m, own, :LANES]
                    )
                    states[m] = state
                    shown = state * wide[m, own, LANES:]
                    y_parts[m].append(shown[:8] + shown[8:])
                    product[m, own, :] = (state * pull_ref[m, row, :]).astype(bf16)
            for m in range(micros):
                y_ref[m, pl.ds(base, 8), :] = sum_rows(y_parts[m])
        return (tuple(states), tuple(grads))

    begin = (
        tuple(state_ref[m] for m in range(micros)),
        tuple(jnp.zeros((N, LANES), f32) for m in range(micros)),
    )
    states, grads = lax.fori_loop(0, rows // 16, sixteen, begin)
    for m in range(micros):
        state_ref[m] = states[m]
        grad_c_ref[m] = lane_sums(product_b, m, grads[m], lane, rows - 8, ones)
        final_ref[m] = states[m]
        gate, d_mixed = pair_ref[m, :, :LANES], pair_ref[m, :, LANES:]
        sigma = jax.nn.sigmoid(gate)
        y_scan = y_ref[m] + skip * act_ref[m].astype(f32)
        kinds_ref[0, m] = (y_scan * (gate * sigma)).astype(bf16)
        slope = sigma * (1.0 + gate * (1.0 - sigma))
        kinds_ref[1, m] = (d_mixed * y_scan * slope).astype(bf16)


def time_specs(micros, blocks, at, first):
    tall = pl.BlockSpec((micros, SCAN_ROWS, LANES), lambda i: (0, at(i), 0))
    return dict(
        tall=tall,
        pair=pl.BlockSpec((micros, SCAN_ROWS, 2 * LANES), lambda i: (0, at(i), 0)),
        turned=pl.BlockSpec((micros, LANES, SCAN_ROWS), lambda i: (0, 0, at(i))),
        wide=pl.BlockSpec((micros, N, SCAN_ROWS), lambda i: (0, 0, at(i))),
        states=pl.BlockSpec((micros, SCAN_ROWS, N, LANES), lambda i: (0, at(i), 0, 0)),
        info=pl.BlockSpec((micros, SCAN_ROWS, 8), lambda i: (first // micros, at(i), 0)),
        fixed=pl.BlockSpec((micros, N, LANES), lambda i: (0, 0, 0)),
    )


def const(shape):
    return pl.BlockSpec(shape, lambda *at: (0,) * len(shape))


def mix_forward(place, first, keep, quarters, act, pair, info, dt, rules, rate, bias, start):
    micros, length, _ = act.shape
    blocks = length // SCAN_ROWS
    spec = time_specs(micros, blocks, lambda i: i, first)
    width = quarters[0].shape[0]
    quarter = pl.BlockSpec((width, SCAN_ROWS), lambda i: (0, i % (blocks // 2)))
    tall = jax.ShapeDtypeStruct((micros, length, LANES), f32)
    return pl.pallas_call(
        mix_forward_kernel,
        grid=(blocks,),
        in_specs=[
            SCALARS, SCALARS, *[quarter] * 4, spec["tall"], spec["pair"], spec["info"],
            const(dt.shape), const(rules[0].shape), const(rules[1].shape),
            const(rate.shape), const(bias.shape), spec["fixed"],
        ],
        out_specs=[
            pl.BlockSpec((2, micros, SCAN_ROWS, LANES), lambda i: (0, 0, i, 0)),
            spec["states"], *[spec["tall"]] * 4, spec["turned"], spec["wide"], spec["fixed"],
        ],
        out_shape=[
            jax.ShapeDtypeStruct((2, micros, length, LANES), bf16),
            jax.ShapeDtypeStruct((micros, length, N, LANES), f32),
            tall, tall, tall, tall,
            jax.ShapeDtypeStruct((micros, width - 2 * N, length), bf16),
            jax.ShapeDtypeStruct((micros, N, length), f32),
            jax.ShapeDtypeStruct((micros, N, LANES), f32),
        ],
        scratch_shapes=scan_scratch(micros),
        cost_estimate=pl.CostEstimate(
            flops=micros * length * N * LANES * 40,
            bytes_accessed=micros * length * N * LANES * 12,
            transcendentals=micros * length * N * LANES,
        ),
        compiler_params=pltpu.CompilerParams(
            dimension_semantics=("arbitrary",), vmem_limit_bytes=40 * MEGA
        ),
        name="mix_forward",
    )(place, keep, *quarters, act, pair, info, dt, *rules, rate, bias, start)


def mix_backward_kernel(
    place_ref, keep_ref, act_ref, info_ref, dt_ref, mask_ref, side_ref, rate_ref, bias_ref, start_ref,
    before_ref, step_ref, slope_ref, pull_ref, rows_ref, low_ref, grad_c_ref,
    shared_ref, d_act_ref, grad_dt_ref, sums_ref, grad_rate_ref, final_ref,
    state_ref, wide_a, wide_b, product_a, product_b, drive_ref, b_pull_ref, rate_pull_ref,
):
    micros, rows, _ = step_ref.shape
    block = pl.num_programs(0) - 1 - pl.program_id(0)
    rank = low_ref.shape[1]
    rate = rate_ref[...]
    mask = mask_ref[...]
    side = side_ref[...]
    skip = bias_ref[1:2]
    ones = jnp.ones((LANES, LANES), bf16)
    lane = lax.broadcasted_iota(jnp.int32, (N, LANES), 1)

    @pl.when(pl.program_id(0) == 0)
    def _():
        state_ref[...] = start_ref[...]
        grad_rate_ref[...] = jnp.zeros_like(grad_rate_ref)
        grad_dt_ref[...] = jnp.zeros_like(grad_dt_ref)
        sums_ref[...] = jnp.zeros_like(sums_ref)

    for m in range(micros):
        drive_ref[m] = step_ref[m] * act_ref[m].astype(f32)
        wide_a[m] = spread(rows_ref, m, rows - 8, mask, side)

    def sixteen(turn, carried):
        states, grads, rates = (list(part) for part in carried)
        for half in range(2):
            base = pl.multiple_of(rows - 8 - turn * 16 - 8 * half, 8)
            wide, wide_next = (wide_a, wide_b) if half == 0 else (wide_b, wide_a)
            product, product_last = (product_a, product_b) if half == 0 else (product_b, product_a)
            following = jnp.maximum(base - 8, 0)
            for m in range(micros):
                wide_next[m] = spread(rows_ref, m, following, mask, side)
                grads[m] = lane_sums(product_last, m, grads[m], lane, base + 8, ones)
            b_parts = [[None] * 8 for _ in range(micros)]
            rate_parts = [[None] * 8 for _ in range(micros)]
            for j in range(7, -1, -1):
                for m in range(micros):
                    row = pl.ds(base + j, 1)
                    own = slice(N * j, N * j + N)
                    step = step_ref[m, row, :]
                    adjoint = wide[m, own, LANES:] * pull_ref[m, row, :] + states[m]
                    passed = jnp.exp(step * rate) * (
                        adjoint * keep_ref[m, block * rows + base + j]
                    )
                    states[m] = passed
                    decay_pull = passed * before_ref[m, base + j]
                    shown = adjoint * wide[m, own, :LANES]
                    b_parts[m][j] = shown[:8] + shown[8:]
                    shown = decay_pull * rate
                    rate_parts[m][j] = shown[:8] + shown[8:]
                    rates[m] = rates[m] + decay_pull * step
                    product[m, own, :] = (adjoint * drive_ref[m, row, :]).astype(bf16)
            for m in range(micros):
                b_pull_ref[m, pl.ds(base, 8), :] = sum_rows(b_parts[m])
                rate_pull_ref[m, pl.ds(base, 8), :] = sum_rows(rate_parts[m])
        return (tuple(states), tuple(grads), tuple(rates))

    zeros = tuple(jnp.zeros((N, LANES), f32) for m in range(micros))
    begin = (tuple(state_ref[m] for m in range(micros)), zeros, zeros)
    states, grads, rates = lax.fori_loop(0, rows // 16, sixteen, begin)
    for m in range(micros):
        state_ref[m] = states[m]
        grad_rate_ref[...] += rates[m]
        final_ref[m] = states[m]
        act = act_ref[m].astype(f32)
        pull = pull_ref[m]
        b_pull = b_pull_ref[m]
        d_act_ref[m] = pull * skip + step_ref[m] * b_pull
        d_pre = ((rate_pull_ref[m] + act * b_pull) * slope_ref[m]).astype(bf16).astype(f32)
        sums_ref[0:8] += jnp.sum(d_pre.reshape(-1, 8, LANES), axis=0)
        sums_ref[8:16] += jnp.sum((pull * act).reshape(-1, 8, LANES), axis=0)
        d_pre3 = three(d_pre, info_ref[m])
        shared_ref[m, :rank] = across(dt_ref[...], d_pre3, (1, 1))
        shared_ref[m, rank : rank + N] = lane_sums(product_b, m, grads[m], lane, 0, ones)
        shared_ref[m, rank + N :] = grad_c_ref[m]
        grad_dt_ref[...] += across(low_ref[m], d_pre3, (1, 0))


def mix_backward(place, first, keep, act, info, dt, rules, rate, bias, start, saved):
    before, step, slope, pull, rows, low, grad_c = saved
    micros, length, _ = act.shape
    blocks = length // SCAN_ROWS
    spec = time_specs(micros, blocks, lambda i: blocks - 1 - i, first)
    rank = low.shape[1]
    width = rank + 2 * N
    return pl.pallas_call(
        mix_backward_kernel,
        grid=(blocks,),
        in_specs=[
            SCALARS, SCALARS, spec["tall"], spec["info"],
            const(dt.shape), const(rules[0].shape), const(rules[1].shape),
            const(rate.shape), const(bias.shape), spec["fixed"],
            spec["states"], *[spec["tall"]] * 4, spec["turned"], spec["wide"],
        ],
        out_specs=[
            pl.BlockSpec((micros, width, SCAN_ROWS), lambda i: (0, 0, blocks - 1 - i)),
            spec["tall"], const(dt.shape), const((16, LANES)), const((N, LANES)), spec["fixed"],
        ],
        out_shape=[
            jax.ShapeDtypeStruct((micros, width, length), f32),
            jax.ShapeDtypeStruct((micros, length, LANES), f32),
            jax.ShapeDtypeStruct(dt.shape, f32),
            jax.ShapeDtypeStruct((16, LANES), f32),
            jax.ShapeDtypeStruct((N, LANES), f32),
            jax.ShapeDtypeStruct((micros, N, LANES), f32),
        ],
        scratch_shapes=scan_scratch(micros),
        cost_estimate=pl.CostEstimate(
            flops=micros * length * N * LANES * 60,
            bytes_accessed=micros * length * N * LANES * 12,
            transcendentals=micros * length * N * LANES,
        ),
        compiler_params=pltpu.CompilerParams(
            dimension_semantics=("arbitrary",), vmem_limit_bytes=40 * MEGA
        ),
        name="mix_backward",
    )(place, keep, act, info, dt, *rules, rate, bias, start, *saved)


def shifted(scratch_ref, j, rows):
    return scratch_ref[8 - j : 8 - j + rows, :]


def conv_forward_kernel(inner_ref, edge_ref, info_ref, taps_ref, wx_ref,
                        act_ref, conv_ref, shared_ref, scratch_ref):
    rows = inner_ref.shape[1]
    scratch_ref[:8] = edge_ref[0]
    scratch_ref[8:] = inner_ref[0]
    info = info_ref[0]
    total = taps_ref[K : K + 1] + taps_ref[0:1] * inner_ref[0]
    for j in range(1, K):
        total = total + taps_ref[j : j + 1] * (shifted(scratch_ref, j, rows) * info[:, 3 + j : 4 + j])
    conv_ref[0] = total
    act = (total * jax.nn.sigmoid(total)).astype(bf16)
    act_ref[0] = act
    shared_ref[0] = across(wx_ref[...], three(act.astype(f32), info), (1, 1))


def conv_forward(first, inner, edge, info, taps, wx):
    micros, rows, _ = inner.shape
    one = pl.BlockSpec((1, rows, LANES), lambda m: (m, 0, 0))
    width = wx.shape[0]
    return call(
        conv_forward_kernel, "conv_forward", (micros,),
        [
            one, pl.BlockSpec((1, 8, LANES), lambda m: (m, 0, 0)),
            pl.BlockSpec((1, rows, 8), lambda m: (first + m, 0, 0)), const(taps.shape), const(wx.shape),
        ],
        [one, one, pl.BlockSpec((1, width, rows), lambda m: (m, 0, 0))],
        [
            shape_of(inner.shape, bf16), shape_of(inner.shape, f32),
            shape_of((micros, width, rows), f32),
        ],
        [pltpu.VMEM((rows + 8, LANES), f32)],
        2 * micros * rows * wx.size, 4 * MEGA,
        (inner, edge, info, taps, wx),
    )


def conv_backward_kernel(place_ref, own_ref, x_ref, core_ref, both_ref, d_act_ref, conv_ref, inner_ref,
                         edge_ref, act_ref, info_ref, taps_ref, wx_ref,
                         d_inner_ref, grad_x_ref, sums_ref, head_ref, last_ref, scratch_ref, ahead_ref):
    rows = inner_ref.shape[1]
    micro = pl.program_id(0)
    info = info_ref[0]

    @pl.when(micro == 0)
    def _():
        grad_x_ref[...] = jnp.zeros_like(grad_x_ref)
        sums_ref[...] = jnp.zeros_like(sums_ref)

    shared = jnp.concatenate(
        [
            halves(place_ref, micro, half, own_ref, x_ref, core_ref, both_ref)
            for half in range(2)
        ],
        1,
    ).astype(bf16)
    d_act = d_act_ref[0] + masked_sum(across(shared, wx_ref[...], (0, 0)), info)
    grad_x_ref[...] += across(shared, three(act_ref[0].astype(f32), info), (1, 0))
    conv = conv_ref[0]
    sigma = jax.nn.sigmoid(conv)
    d_conv = d_act * (sigma * (1.0 + conv * (1.0 - sigma)))
    head_ref[0] = d_conv[:8]
    scratch_ref[:8] = edge_ref[0]
    scratch_ref[8:] = inner_ref[0]
    ahead_ref[rows:] = jnp.zeros((8, LANES), f32)
    total = taps_ref[0:1] * d_conv
    sums_ref[0:8] += jnp.sum((d_conv * inner_ref[0]).reshape(-1, 8, LANES), axis=0)
    for j in range(1, K):
        masked = d_conv * info[:, 3 + j : 4 + j]
        pulled = (masked * shifted(scratch_ref, j, rows)).reshape(-1, 8, LANES)
        sums_ref[8 * j : 8 * j + 8] += jnp.sum(pulled, axis=0)
        ahead_ref[:rows] = masked
        total = total + taps_ref[j : j + 1] * ahead_ref[j : j + rows, :]
    sums_ref[8 * K : 8 * K + 8] += jnp.sum(d_conv.reshape(-1, 8, LANES), axis=0)
    d_inner_ref[0] = total.astype(bf16)
    last_ref[0] = total[rows - 8 :]


def conv_backward(place, first, quarters, d_act, conv, inner, edge, act, info, taps, wx):
    micros, rows, _ = inner.shape
    one = pl.BlockSpec((1, rows, LANES), lambda m: (m, 0, 0))
    eight = pl.BlockSpec((1, 8, LANES), lambda m: (m, 0, 0))
    sums = (8 * (K + 1), LANES)
    return call(
        conv_backward_kernel, "conv_backward", (micros,),
        [
            SCALARS, *[const(quarters[0].shape)] * 4, one, one, one, eight, one,
            pl.BlockSpec((1, rows, 8), lambda m: (first + m, 0, 0)), const(taps.shape), const(wx.shape),
        ],
        [one, const(wx.shape), const(sums), eight, eight],
        [
            shape_of(inner.shape, bf16), shape_of(wx.shape, f32), shape_of(sums, f32),
            shape_of((micros, 8, LANES), f32), shape_of((micros, 8, LANES), f32),
        ],
        [pltpu.VMEM((rows + 8, LANES), f32), pltpu.VMEM((rows + 8, LANES), f32)],
        4 * micros * rows * wx.size, 6 * MEGA,
        (place, *quarters, d_act, conv, inner, edge, act, info, taps, wx),
    )


def pack_kernel(plane, flag_ref, after_ref, w_ref, *out_refs):
    half = w_ref.shape[-1] // 2
    for turn, out_ref in enumerate(out_refs):
        lanes = pl.ds(pl.multiple_of((turn ^ flag_ref[0]) * half, half), half)
        at = (0, slice(None), lanes) if plane is None else (0, slice(None), plane, lanes)
        out_ref[0] = w_ref[at].astype(bf16)


def pack(flag, after, weight, plane=None):
    kinds, rows = weight.shape[:2]
    chans = weight.shape[-1]
    half = chans // 2
    return call(
        functools.partial(pack_kernel, plane), "pack", (kinds,),
        [SCALARS, SCALARS, pl.BlockSpec((1,) + weight.shape[1:], lambda k: (k,) + (0,) * (weight.ndim - 1))],
        [pl.BlockSpec((1, rows, half), lambda k: (k, 0, 0))] * 2,
        [shape_of((kinds, rows, half), bf16)] * 2,
        [], 0, weight.size * 6, (flag, after, weight),
    )


def adam_kernel(rate, flag_ref, clip_ref, w_ref, m_ref, v_ref, *refs):
    pieces, (grad_ref, new_ref, first_ref, second_ref) = refs[:4], refs[4:]
    half = w_ref.shape[-1] // 2
    clip = clip_ref[0]
    for plane in range(2):
        for turn in range(2):
            lanes = pl.ds(pl.multiple_of((turn ^ flag_ref[0]) * half, half), half)
            at = (0, slice(None), plane, lanes)
            grad = pieces[2 * plane + turn][0].astype(f32)
            new, first, second = adam_update(w_ref[at], grad, m_ref[at], v_ref[at], clip, rate)
            grad_ref[at] = grad
            new_ref[at] = new
            first_ref[at] = first
            second_ref[at] = second


def adam(flag, clip, weight, first, second, pieces, rate):
    kinds, rows, _, chans = weight.shape
    block = min(rows, 64)
    full = pl.BlockSpec((1, block, 2, chans), lambda k, r: (k, r, 0, 0))
    piece = pl.BlockSpec((1, block, chans // 2), lambda k, r: (k, r, 0))
    return call(
        functools.partial(adam_kernel, rate), "adam", (kinds, rows // block),
        [SCALARS, SCALARS, full, full, full] + [piece] * 4,
        [full] * 4,
        [shape_of(weight.shape, f32)] * 4,
        [], weight.size * 20, weight.size * 32,
        (flag, clip, weight, first, second, *pieces),
    )


def body(
    groups, parts, chans,
    tokens_in, modality, starts, cotangent,
    in_weight, in_first, in_second,
    dt_weight, dt_first, dt_second,
    out_weight, out_first, out_second,
    x_weight, x_first, x_second,
    channel_params, channel_first, channel_second,
    gain, gain_first, gain_second,
):
    micros, tok_rows, part_width = tokens_in.shape
    model = gain.shape[0]
    chan_width = in_weight.shape[3]
    half = chan_width // 2
    own = half // chans
    cores = chans // 2
    inner_all = chan_width * chans
    x_width = x_weight.shape[1]
    rank = x_width - 2 * N
    dt_rows = dt_weight.shape[1]
    span = parts * tok_rows
    edge = K - 1
    t_at = lax.axis_index("t")
    p_at = lax.axis_index("p")
    c_at = lax.axis_index("c")
    z_at, y_at = p_at // 2, p_at % 2
    x_at, core_at = c_at // cores, c_at % cores
    s_at = t_at * parts + p_at
    slice_at = s_at // (2 * groups)
    everywhere = ("t", "p", "c")
    place = jnp.stack([x_at, core_at, y_at, z_at]).astype(jnp.int32)

    def flat(t, p, c):
        return (t * parts + p) * chans + c

    def part_of(c, j):
        return 2 * (2 * (c % cores) + j) + c // cores

    devices = [(t, p, c) for t in range(groups) for p in range(parts) for c in range(chans)]

    def first_hop(turn):
        pairs = []
        for t, p, c in devices:
            s = t * parts + p
            to_slice, i = s // (2 * groups), (s % (2 * groups)) // groups
            j = turn ^ (to_slice // cores)
            to = flat(s % groups, 2 * (2 * (c % cores) + j) + i, c // cores * cores + to_slice % cores)
            pairs.append((flat(t, p, c), to))
        return pairs

    def second_hop(turn):
        return [
            (flat(t, p, c), flat(t, p - p % 2 + c // cores, (turn ^ (p % 2)) * cores + c % cores))
            for t, p, c in devices
        ]

    small_pairs = [(flat(t, p, c), flat(t, part_of(c, p % 2), p // 2)) for t, p, c in devices]

    def send(value, pairs, back=False):
        if back:
            pairs = [(b, a) for a, b in pairs]
        return lax.ppermute(value, everywhere, pairs)

    def swap(value, axis, distance):
        return lax.ppermute(value, axis, [(i, i ^ distance) for i in range(lax.axis_size(axis))])

    def crossed(pair, flag):
        first, second = pair
        return jnp.where(flag == 0, first, second), jnp.where(flag == 0, second, first)

    between = y_at ^ (z_at % 2)

    def token(*values):
        return sum(value[(0,) * value.ndim].astype(f32) for value in values)[None]

    def weights_there(pair):
        pair = [send(value, first_hop(turn)) for turn, value in enumerate(pair)]
        arrived = token(*pair)
        pair = crossed(pair, between)
        pair = [send(value, second_hop(turn)) for turn, value in enumerate(pair)]
        return pair, arrived

    def there_whole(pair):
        if groups > 1:
            pair = [lax.all_gather(value, "t", axis=1, tiled=True) for value in pair]
        return tuple(pair)

    def grads_back(pair):
        pair = [send(value, second_hop(turn), True) for turn, value in enumerate(pair)]
        pair = crossed(pair, between)
        return [send(value, first_hop(turn), True) for turn, value in enumerate(pair)]

    def along_groups(value, by):
        pairs = [(i, i + by) for i in range(groups) if 0 <= i + by < groups]
        return lax.ppermute(value, "t", pairs)

    def over_chans(value):
        distance = 1
        while distance < chans:
            value = value + swap(value, "c", distance)
            distance *= 2
        return value

    def pick(value, at, axis):
        return lax.dynamic_index_in_dim(value, at, axis, keepdims=False)

    def scattered_chans(sent, keep):
        total = keep + swap(sent, "c", 1).astype(f32)
        got = swap(pick(total, 1 - x_at, 0).astype(bf16), "c", cores)
        return pick(total, x_at, 0) + got.astype(f32)

    def gathered_chans(value):
        across_x = swap(value, "c", cores)
        across_core = swap(value, "c", 1)
        return (value, across_x, across_core, swap(across_x, "c", 1))

    def scattered_parts(sent, keep):
        total = keep + swap(sent, "p", 1).astype(f32)
        total = total.reshape(total.shape[0], -1, 2, *total.shape[2:])
        got = swap(pick(total, 1 - z_at % 2, 2).astype(bf16), "p", 2)
        total = pick(total, z_at % 2, 2) + got.astype(f32)
        got = swap(pick(total, 1 - z_at // 2, 1).astype(bf16), "p", 4)
        return pick(total, z_at // 2, 1) + got.astype(f32)

    def quarters_of(value, kind):
        length = value.shape[2] // 2

        def half_of(at):
            return lax.dynamic_slice_in_dim(value, at * length, length, 2)

        total = half_of(core_at) + swap(half_of(1 - core_at).astype(kind), "c", 1).astype(f32)
        got = swap(pick(total, 1 - x_at, 0).astype(kind), "c", cores)
        total = pick(total, x_at, 0) + got.astype(f32)
        distance = 1
        while distance < parts:
            total = total.astype(kind)
            total = total.astype(f32) + swap(total, "p", distance).astype(f32)
            distance *= 2
        return gathered_chans(total.astype(kind))

    def over_all(value):
        value = over_chans(value)
        distance = 1
        while distance < parts:
            value = value + swap(value, "p", distance)
            distance *= 2
        return lax.psum(value, "t") if groups > 1 else value

    def after(value, *others):
        return value + (0.0 * token(*others)).astype(jnp.int32)

    extra = jnp.pad(modality.astype(bf16)[:, None, :], ((0, 0), (0, 15), (0, part_width - tok_rows)))
    tokens_all = lax.all_gather(jnp.concatenate([tokens_in, extra], 1), "p")
    kinds = tokens_all[:, :, tok_rows, :tok_rows].astype(jnp.int32)
    kinds = kinds.transpose(1, 0, 2).reshape(micros, span)
    flag = (slice_at // cores).astype(jnp.int32)[None]
    w_inner, arrived = weights_there(pack(flag, jnp.zeros((1,), f32), in_weight, 0))
    w_inner = there_whole(w_inner)
    small = jnp.concatenate([x_weight.reshape(3 * x_width, chan_width), channel_params], 0)
    own_lanes = y_at * half + z_at * own
    small = send(lax.dynamic_slice_in_dim(small, own_lanes, own, 1), small_pairs)
    w_gate, arrived = weights_there(pack(flag, arrived, in_weight, 1))
    w_gate = there_whole(w_gate)
    dt16 = dt_weight.astype(bf16)
    dt_pair = crossed((dt16[..., :half], dt16[..., half:]), flag[0])
    out_pair = pack(flag, arrived, out_weight)
    out_rows = out_weight.shape[1]
    both = [jnp.concatenate(pair, 1) for pair in zip(out_pair, dt_pair)]
    both, _ = weights_there(both)
    w_out = there_whole([value[:, :out_rows] for value in both])
    dt_part = jnp.concatenate(
        crossed(there_whole([value[:, out_rows:] for value in both]), x_at), 1
    )
    dt_blocks = []
    for distance in range(chans):
        block = lax.dynamic_slice_in_dim(dt_part, (c_at ^ distance) * own, own, 2)
        dt_blocks.append(swap(block, "c", distance) if distance else block)
    dt_blocks = jnp.stack(dt_blocks)
    w_dt = jnp.concatenate([pick(dt_blocks, c_at ^ k, 0) for k in range(chans)], 1)
    w_dt = w_dt.transpose(1, 0, 2).reshape(rank, 3 * own)
    back_all = lax.all_gather(cotangent, "p")
    squares = jnp.sum(jnp.square(tokens_all[:, :, :tok_rows].astype(f32)), axis=-1)
    squares = over_chans(squares).transpose(1, 0, 2).reshape(micros, span)
    inv_all = lax.rsqrt(squares / model + NORM_EPS)
    inv_own = lax.dynamic_slice_in_dim(inv_all, p_at * tok_rows, tok_rows, 1)[..., None]
    positions = t_at * span - edge + jnp.arange(span + 2 * edge, dtype=jnp.int32)
    segment = jnp.sum((starts[:, None, :] <= positions[None, :, None]).astype(jnp.int32), axis=2)
    keep_mask = 1.0 - jnp.any(
        starts[:, None, :] == positions[None, edge : edge + span, None], axis=2
    ).astype(f32)
    same_doc = [
        (segment[:, edge - j : 2 * edge - j + span] == segment[:, edge:]).astype(f32)
        for j in range(1, K)
    ]
    masks = [(kinds == k).astype(f32) for k in range(3)]
    valid = [same[:, :span] for same in same_doc]
    info3 = jnp.stack([inv_all, *masks, *valid, inv_all], -1)
    info = info3.reshape(micros * span, 8)
    gain_part = lax.dynamic_slice_in_dim(gain, c_at * part_width, part_width, 0)[None]

    w_x = small[: 3 * x_width].astype(bf16).reshape(3, x_width, own)
    w_x = w_x.transpose(1, 0, 2).reshape(x_width, 3 * own)
    channel = small[3 * x_width :]
    taps = channel[:8]
    biases = jnp.pad(channel[K + 1 : K + 3], ((0, 6), (0, 0)))
    neg_rate = -jnp.exp(channel[K + 3 :])
    rules = lane_rules()

    grad_dt_sum = grad_x_sum = grad_chan_sum = grad_gain_sum = 0.0
    outs, rows_back, held, products = [], [], [], []
    all_normed, all_pairs, all_inners = [], [], []
    chunk = min(GROUP, micros)
    zero_state = jnp.zeros((chunk, N, own), f32)
    for at in range(0, micros, chunk):
        ms = slice(at, at + chunk)
        tiles = Tiles(at, chunk, parts, tok_rows)
        normed, sent, keep = inner_product(tiles, place, tokens_all, info, gain_part, w_inner)
        inner = scattered_chans(sent, keep).reshape(chunk, span, own)
        sent, keep = gate_product(tiles, place, normed, back_all, info, w_gate, w_out)
        pair = scattered_chans(sent, keep).reshape(chunk, span, 2 * own)
        edge_rows = jnp.zeros((chunk, 8, own), f32)
        if groups > 1:
            edge_rows = along_groups(inner[:, span - 8 :], 1)
        act, conv, shared = conv_forward(at, inner, edge_rows, info3, taps, w_x)
        quarters = quarters_of(shared, f32)
        keeps = keep_mask[ms]
        args = (at, keeps, quarters, act, pair, info3, w_dt, rules, neg_rate, biases)
        state_in = zero_state
        if groups > 1:
            first_pass = mix_forward(place, *args, zero_state)
            ends, step = first_pass[8], first_pass[2]
            passed_all = jnp.exp(jnp.sum(step, axis=1)[:, None, :] * neg_rate)
            passed_all = passed_all * jnp.prod(keeps, axis=1)[:, None, None]
            for _ in range(groups - 1):
                state_in = along_groups(passed_all * state_in + ends, 1)
        kinds_out, *saved, _ = mix_forward(place, *args, state_in)
        pairs = gathered_chans(kinds_out.reshape(2, chunk * span, own))
        all_normed.append(normed)
        all_pairs.append(pairs)
        held.append((tiles, at, keeps, act, saved, inner, edge_rows, conv))

    for at, (tiles, first, keeps, act, saved, inner, edge_rows, conv) in enumerate(held):
        order = after(place, saved[1] if at else held[-1][4][1], *(sent for sent, _ in products))
        args = (first, keeps, act, info3, w_dt, rules, neg_rate, biases)
        adj_in = zero_state
        if groups > 1:
            ends = mix_backward(order, *args, zero_state, saved)[5]
            passed_all = jnp.exp(jnp.sum(saved[1], axis=1)[:, None, :] * neg_rate)
            passed_all = passed_all * jnp.prod(keeps, axis=1)[:, None, None]
            for _ in range(groups - 1):
                adj_in = along_groups(passed_all * adj_in + ends, -1)
        shared, d_act, grad_dt, sums, grad_rate, _ = mix_backward(order, *args, adj_in, saved)
        grad_dt_sum += grad_dt
        sums = jnp.sum(sums.reshape(2, 8, own), axis=1)
        quarters = quarters_of(shared, bf16)
        held[at] = (tiles, first, act, inner, edge_rows, conv, d_act, quarters, sums, grad_rate * neg_rate)
        products.append(out_product(tiles, after(place, d_act), all_pairs[at], info, w_out))
        outs.append(scattered_parts(*products[-1]))

    kept = f32 if groups > 1 else bf16

    def kindred(which):
        return ((1, span, own), lambda m, chunk_at: (which, m, 0))

    rows_at = ((span, part_width), lambda m, chunk_at: (m, 0))
    raw_at = ((parts, 1, tok_rows, part_width), lambda m, chunk_at: (0, chunk_at * chunk + m, 0, 0))
    backs = [back_all] * len(all_pairs)
    order = after(place, held[-1][6])
    *g_out, out_sq = weight_grad(order, info, backs, raw_at, all_pairs, kindred(0), span, kept)
    *g_gate, gate_sq = weight_grad(order, info, all_normed, rows_at, all_pairs, kindred(1), span, kept)
    done = [(sent for sent, _ in products), (out_sq, gate_sq)]

    for at, stage in enumerate(held):
        tiles, first, act, inner, edge_rows, conv, d_act, quarters, mix_sums, d_rate = stage
        order = after(place, *done[min(at, 1)])
        d_inner, grad_x, sums, head, last = conv_backward(
            order, first, quarters, d_act, conv, inner, edge_rows, act, info3, taps, w_x
        )
        if groups > 1:
            ahead = along_groups(head, -1)[:, :edge]
            for j in range(1, K):
                gone = taps[j] * ahead * same_doc[j - 1][first : first + chunk, span:, None]
                last = last.at[:, 8 - j :].add(gone[:, :j])
            d_inner = jnp.concatenate([d_inner[:, : span - 8], last.astype(bf16)], 1)
        grad_x_sum += grad_x
        sums = jnp.sum(sums.reshape(K + 1, 8, own), axis=1)
        grad_chan_sum += jnp.concatenate([sums, mix_sums, d_rate], 0)
        all_inners.append(gathered_chans(d_inner.reshape(chunk * span, own)))

    flat_at = ((span, own), lambda m, chunk_at: (m, 0))
    *g_inner, inner_sq = weight_grad(place, info, all_normed, rows_at, all_inners, flat_at, span, kept)
    for at, stage in enumerate(held):
        order = after(place, inner_sq) if at else place
        sent, keep, gain_rows = normed_grad(
            stage[0], order, all_pairs[at], all_inners[at], info, tokens_all, w_gate, w_inner
        )
        grad_gain_sum += jnp.sum(gain_rows, axis=0)
        rows_back.append(scattered_parts(sent, keep))

    grad_x_sum = grad_x_sum.reshape(x_width, 3, own).transpose(1, 0, 2)
    grad_dt_sum = grad_dt_sum.reshape(rank, 3, own).transpose(1, 0, 2)
    g_small = jnp.concatenate(
        [grad_x_sum.reshape(-1, own), grad_dt_sum.reshape(-1, own), grad_chan_sum], 0
    )
    if groups > 1:
        g_small = lax.psum(g_small, "t")
        over = lambda pair: [
            lax.psum_scatter(value, "t", scatter_dimension=1, tiled=True) for value in pair
        ]
        g_out, g_gate, g_inner = over(g_out), over(g_gate), over(g_inner)
        large_sq = sum(jnp.sum(value * value) for value in (*g_out, *g_gate, *g_inner))
        g_out, g_gate, g_inner = (
            [value.astype(bf16) for value in pair] for pair in (g_out, g_gate, g_inner)
        )
    else:
        large_sq = jnp.sum(out_sq) + jnp.sum(gate_sq) + jnp.sum(inner_sq)
    local_sq = large_sq + jnp.sum(g_small * g_small) / groups
    here = (jnp.arange(chans) == c_at).astype(f32)
    tail = jnp.concatenate([(here[:, None] * grad_gain_sum).reshape(-1), local_sq[None]])
    tail = over_all(tail)
    grad_gain = tail[:model]
    grad_norm = jnp.sqrt(tail[model] + jnp.sum(grad_gain * grad_gain))
    clip_scale = CLIP_LIMIT / jnp.maximum(grad_norm, CLIP_LIMIT)

    def back_whole(pair):
        return jnp.concatenate(crossed(grads_back(pair), flag[0]), -1).astype(f32)

    grad_out = back_whole(g_out)
    in_pieces = (*grads_back(g_inner), *grads_back(g_gate))
    small_back = lax.all_gather(send(g_small.astype(bf16), small_pairs, True), "p")
    small_back = small_back.reshape(chans, 2, -1, own).transpose(2, 1, 0, 3)
    small_back = small_back.reshape(-1, chan_width).astype(f32)
    grad_x = small_back[: 3 * x_width].reshape(3, x_width, chan_width)
    grad_dt = small_back[3 * x_width : 3 * x_width + 3 * rank].reshape(3, rank, chan_width)
    grad_dt = lax.dynamic_slice_in_dim(grad_dt, s_at * dt_rows, dt_rows, 1)
    grad_chan = small_back[3 * x_width + 3 * rank :]

    tok_float = tokens_in.astype(f32)
    mixed = (tok_float + jnp.concatenate(outs, 0)).astype(bf16)
    d_own = jnp.concatenate(rows_back, 0)
    x_hat_own = tok_float * inv_own
    d_hat = d_own * gain_part
    mean = over_chans(jnp.sum(d_hat * x_hat_own, axis=-1))[..., None] / model
    input_grad = cotangent.astype(f32) + inv_own * (d_hat - x_hat_own * mean)

    grad_in, in_new, in_first_new, in_second_new = adam(
        flag, clip_scale[None], in_weight, in_first, in_second, in_pieces, model ** (-0.5)
    )
    dt_new, dt_first_new, dt_second_new = adam_update(
        dt_weight, grad_dt, dt_first, dt_second, clip_scale, rank ** (-0.5)
    )
    out_new, out_first_new, out_second_new = adam_update(
        out_weight, grad_out, out_first, out_second, clip_scale, inner_all ** (-0.5)
    )
    x_new, x_first_new, x_second_new = adam_update(
        x_weight, grad_x, x_first, x_second, clip_scale, inner_all ** (-0.5)
    )
    chan_new, chan_first_new, chan_second_new = adam_update(
        channel_params, grad_chan, channel_first, channel_second, clip_scale, 0.5
    )
    gain_new, gain_first_new, gain_second_new = adam_update(
        gain, grad_gain, gain_first, gain_second, clip_scale, 0.5
    )
    return (
        mixed, input_grad, grad_norm,
        grad_in, in_new, in_first_new, in_second_new,
        grad_dt, dt_new, dt_first_new, dt_second_new,
        grad_out, out_new, out_first_new, out_second_new,
        grad_x, x_new, x_first_new, x_second_new,
        grad_chan, chan_new, chan_first_new, chan_second_new,
        grad_gain, gain_new, gain_first_new, gain_second_new,
        in_new.astype(bf16), dt_new.astype(bf16), out_new.astype(bf16), x_new.astype(bf16),
    )


def solution(mesh):
    chans = mesh.shape["ch"]
    parts = 2 * chans
    groups = mesh.shape["seq"] // parts
    inside = Mesh(mesh.devices.reshape(groups, parts, chans), ("t", "p", "c"))
    seq = ("t", "p")
    tok = P(None, seq, "c")
    wide = P(None, seq, None, "c")
    rows = P(None, seq, "c")
    flat = P(None, None, "c")
    chan = P(None, "c")
    return jax.shard_map(
        functools.partial(body, groups, parts, chans),
        mesh=inside,
        in_specs=(tok, P(None, seq), P(), tok)
        + (wide,) * 3 + (rows,) * 3 + (rows,) * 3 + (flat,) * 3 + (chan,) * 3 + (P(),) * 3,
        out_specs=(tok, tok, P())
        + (wide,) * 4 + (rows,) * 4 + (rows,) * 4 + (flat,) * 4 + (chan,) * 4 + (P(),) * 4
        + (wide, rows, rows, flat),
        check_vma=False,
    )
```

```python
import functools

import jax
import jax.numpy as jnp
from jax import lax
from jax.experimental import pallas as pl
from jax.experimental.pallas import tpu as pltpu
from jax.sharding import Mesh
from jax.sharding import PartitionSpec as P

N = 16
K = 4
STEP = 10

NORM_EPS = 1e-05
BETA_ONE = 0.9
BETA_TWO = 0.95
ADAM_EPS = 1e-08
DECAY = 0.1
CLIP_LIMIT = 1.0
LANES = 128
SCAN_ROWS = 128
MEGA = 1024 * 1024
GROUP = 2
f32 = jnp.float32
bf16 = jnp.bfloat16


def silu_grad(value):
    sigma = jax.nn.sigmoid(value)
    return sigma * (1.0 + value * (1.0 - sigma))


def adam_update(weight, gradient, first_moment, second, clip_scale, step_rate):
    clipped = gradient * clip_scale
    first_new = BETA_ONE * first_moment + (1.0 - BETA_ONE) * clipped
    second_new = BETA_TWO * second + (1.0 - BETA_TWO) * clipped * clipped
    first_hat = first_new * (1.0 / (1.0 - BETA_ONE**STEP))
    second_hat = second_new * (1.0 / (1.0 - BETA_TWO**STEP))
    weight_new = weight - step_rate * (
        first_hat / (jnp.sqrt(second_hat) + ADAM_EPS) + DECAY * weight
    )
    return (weight_new, first_new, second_new)


def sum_rows(parts):
    at = lax.broadcasted_iota(jnp.int32, parts[0].shape, 0)
    for distance in (1, 2, 4):
        low = at % (2 * distance) < distance
        parts = [
            jnp.where(low, a, b) + pltpu.roll(jnp.where(low, b, a), distance, 0)
            for a, b in zip(parts[0::2], parts[1::2])
        ]
    return parts[0]


def lane_rules():
    lanes = jnp.arange(LANES)
    used = lanes % (LANES // 2) < 3 * N
    mask = ((lanes[None, :] % N == jnp.arange(N)[:, None]) & used[None, :]).astype(f32)
    side = (lanes[:, None] // (LANES // 2) == jnp.arange(2 * LANES)[None, :] // LANES).astype(bf16)
    return mask, side


def matmul(left, right):
    return jnp.dot(left, right, preferred_element_type=f32)


def spread(rows_ref, m, base, mask, side):
    left = [rows_ref[m, pl.ds(base + j, 1), :] * mask for j in range(8)]
    return matmul(jnp.concatenate(left, 0).astype(bf16), side)


def lane_sums(product_ref, m, grads, lane, base, ones):
    sums = matmul(product_ref[m], ones)
    for j in range(8):
        grads = jnp.where(lane == base + j, sums[N * j : N * j + N], grads)
    return grads


def turned(ref, turn, x_at):
    width = ref.shape[-1] // 2
    return pl.ds(pl.multiple_of((turn ^ x_at) * width, width), width)


def three(tile, info):
    return jnp.concatenate([(tile * info[:, k + 1 : k + 2]).astype(bf16) for k in range(3)], -1)


def across(left, right, dims):
    return lax.dot_general(left, right, ((dims[0:1], dims[1:2]), ((), ())), preferred_element_type=f32)


def stacked(ref):
    kinds, rows, cols = ref.shape
    return ref[...].reshape(kinds * rows, cols)


def split_blocks(total, place_ref, sent_ref, keep_ref, scratch_ref, offset):
    scratch_ref[...] = total
    core = place_ref[1]
    for x in range(2):
        away = pl.ds(pl.multiple_of((2 * x + 1 - core) * LANES, LANES), LANES)
        here = pl.ds(pl.multiple_of((2 * x + core) * LANES, LANES), LANES)
        sent_ref[x, :, offset : offset + LANES] = scratch_ref[:, away].astype(bf16)
        keep_ref[x, :, offset : offset + LANES] = scratch_ref[:, here]


def tile_rows(ref):
    return ref[...].reshape(-1, ref.shape[-1])


def wide_product(tile_ref, info, w_refs, scratch_ref, x_at):
    total = None
    for turn, w_ref in enumerate(w_refs):
        left = three(tile_ref[:, turned(tile_ref, turn, x_at)], info)
        part = across(left, stacked(w_ref), (1, 0))
        total = part if total is None else total + part
    return total


def inner_kernel(place_ref, x_ref, info_ref, gain_ref, w0_ref, w1_ref,
                 normed_ref, sent_ref, keep_ref, tile_ref, scratch_ref):
    info = info_ref[...].T
    normed = tile_rows(x_ref).astype(f32) * info[:, :1] * gain_ref[...]
    normed = normed.astype(bf16)
    normed_ref[...] = normed
    tile_ref[...] = normed.astype(f32)
    total = wide_product(tile_ref, info, (w0_ref, w1_ref), scratch_ref, place_ref[0])
    split_blocks(total, place_ref, sent_ref, keep_ref, scratch_ref, 0)


def gate_kernel(place_ref, normed_ref, back_ref, info_ref, g0_ref, g1_ref, o0_ref, o1_ref,
                sent_ref, keep_ref, tile_ref, scratch_ref):
    info = info_ref[...].T
    tile_ref[...] = normed_ref[...].astype(f32)
    total = wide_product(tile_ref, info, (g0_ref, g1_ref), scratch_ref, place_ref[0])
    split_blocks(total, place_ref, sent_ref, keep_ref, scratch_ref, 0)
    tile_ref[...] = tile_rows(back_ref).astype(f32)
    total = wide_product(tile_ref, info, (o0_ref, o1_ref), scratch_ref, place_ref[0])
    split_blocks(total, place_ref, sent_ref, keep_ref, scratch_ref, LANES)


def gathered(scratch_ref, place_ref, refs):
    at = 2 * place_ref[0] + place_ref[1]
    for distance, ref in zip((0, 2, 1, 3), refs):
        lanes = pl.ds(pl.multiple_of((at ^ distance) * LANES, LANES), LANES)
        scratch_ref[:, lanes] = tile_of(ref).astype(f32)


def tile_of(ref):
    return ref[...].reshape(-1, ref.shape[-1])


def split_parts(total, place_ref, sent_ref, keep_ref):
    y = place_ref[2]
    half = total.shape[0] // 2
    low, high = total[:half], total[half:]
    mine = jnp.full(low.shape, y, jnp.int32) == 0
    sent_ref[...] = jnp.where(mine, high, low).astype(bf16).reshape(sent_ref.shape)
    keep_ref[...] = jnp.where(mine, low, high).reshape(keep_ref.shape)


def out_kernel(place_ref, a_ref, b_ref, c_ref, d_ref, info_ref, w0_ref, w1_ref,
               sent_ref, keep_ref, tile_ref, total_ref):
    gathered(tile_ref, place_ref, (a_ref, b_ref, c_ref, d_ref))
    left = three(tile_ref[...], info_ref[...].T)
    width = tile_ref.shape[1]
    for turn, w_ref in enumerate((w0_ref, w1_ref)):
        total = None
        for k in range(3):
            part = across(left[:, k * width : (k + 1) * width], w_ref[k], (1, 1))
            total = part if total is None else total + part
        total_ref[:, turned(total_ref, turn, place_ref[0])] = total
    split_parts(total_ref[...], place_ref, sent_ref, keep_ref)


def normed_kernel(place_ref, ga_ref, gb_ref, gc_ref, gd_ref, ia_ref, ib_ref, ic_ref, id_ref,
                  info_ref, x_ref, g0_ref, g1_ref, i0_ref, i1_ref,
                  sent_ref, keep_ref, gain_ref, tile_ref, total_ref):
    info = info_ref[...].T
    width = tile_ref.shape[1]
    gathered(tile_ref, place_ref, (ga_ref, gb_ref, gc_ref, gd_ref))
    gates = three(tile_ref[...], info)
    gathered(tile_ref, place_ref, (ia_ref, ib_ref, ic_ref, id_ref))
    inners = three(tile_ref[...], info)
    for turn, (g_ref, i_ref) in enumerate(((g0_ref, i0_ref), (g1_ref, i1_ref))):
        total = None
        for k in range(3):
            lanes = slice(k * width, (k + 1) * width)
            part = across(gates[:, lanes], g_ref[k], (1, 1)) + across(inners[:, lanes], i_ref[k], (1, 1))
            total = part if total is None else total + part
        total_ref[:, turned(total_ref, turn, place_ref[0])] = total
    total = total_ref[...]
    split_parts(total, place_ref, sent_ref, keep_ref)

    @pl.when((pl.program_id(0) == 0) & (pl.program_id(1) == 0))
    def _():
        gain_ref[...] = jnp.zeros_like(gain_ref)

    x_hat = tile_rows(x_ref).astype(f32) * info[:, :1]
    gain_ref[...] += jnp.sum((total * x_hat).reshape(-1, 8, total.shape[1]), axis=0)


def weight_grad_kernel(chunks, steps, place_ref, *refs):
    ins, (out0_ref, out1_ref, square_ref, tile_ref, sum_ref) = refs[: 6 * chunks], refs[6 * chunks :]
    at = pl.program_id(0)

    @pl.when(at == 0)
    def _():
        sum_ref[...] = jnp.zeros_like(sum_ref)

    for chunk in range(chunks):
        info_ref, left_ref, *blocks = ins[6 * chunk : 6 * chunk + 6]

        @pl.when((at >= chunk * steps) & (at < (chunk + 1) * steps))
        def _(info_ref=info_ref, left_ref=left_ref, blocks=blocks):
            gathered(tile_ref, place_ref, blocks)
            right = three(tile_ref[...], info_ref[...].T)
            left = left_ref[...].reshape(-1, left_ref.shape[-1])
            sum_ref[...] += across(left, right, (0, 0))

    @pl.when(at == chunks * steps - 1)
    def _():
        half = sum_ref.shape[0] // 2
        width = tile_ref.shape[1]
        for turn, out_ref in enumerate((out0_ref, out1_ref)):
            rows = pl.ds(pl.multiple_of((turn ^ place_ref[0]) * half, half), half)
            for k in range(3):
                out_ref[k] = sum_ref[rows, k * width : (k + 1) * width].astype(out_ref.dtype)
        total = sum_ref[...]
        square_ref[...] = jnp.sum((total * total).reshape(-1, 8, total.shape[1]), axis=0)


SCALARS = pl.BlockSpec(memory_space=pltpu.SMEM)


def whole(array):
    return pl.BlockSpec(array.shape, lambda *at: (0,) * array.ndim)


def shape_of(shape, dtype):
    return jax.ShapeDtypeStruct(shape, dtype)


def call(kernel, name, grid, in_specs, out_specs, out_shape, scratch, flops, moved, args):
    return pl.pallas_call(
        kernel,
        grid=grid,
        in_specs=in_specs,
        out_specs=out_specs,
        out_shape=out_shape,
        scratch_shapes=scratch,
        cost_estimate=pl.CostEstimate(flops=flops, bytes_accessed=moved, transcendentals=0),
        compiler_params=pltpu.CompilerParams(
            dimension_semantics=("arbitrary",) * len(grid), vmem_limit_bytes=48 * MEGA
        ),
        name=name,
    )(*args)


class Tiles:
    def __init__(self, micros, parts, rows):
        self.micros, self.pairs, self.rows = micros, parts // 2, rows
        self.grid = (micros, self.pairs)
        self.tile = 2 * rows

    def raw(self, width, first=0):
        return pl.BlockSpec((2, 1, self.rows, width), lambda m, z: (z, first + m, 0, 0))

    def flat(self, width):
        return pl.BlockSpec((self.tile, width), lambda m, z: (m * self.pairs + z, 0))

    def info(self):
        return pl.BlockSpec((8, self.tile), lambda m, z: (0, m * self.pairs + z))

    def kindred(self, which, width):
        return pl.BlockSpec((1, self.tile, width), lambda m, z: (which, m * self.pairs + z, 0))

    def blocks(self, width):
        return pl.BlockSpec((2, self.tile, width), lambda m, z: (0, m * self.pairs + z, 0))

    def parted(self, width):
        return pl.BlockSpec((1, 1, self.rows, width), lambda m, z: (m, z, 0, 0))


def inner_product(tiles, place, tokens, info, gain, w):
    width = tokens.shape[-1]
    chans = w[0].shape[-1]
    rows = tiles.micros * tiles.pairs * tiles.tile
    return call(
        inner_kernel, "inner_product", tiles.grid,
        [SCALARS, tiles.raw(width), tiles.info(), whole(gain), whole(w[0]), whole(w[1])],
        [tiles.flat(width), tiles.blocks(LANES), tiles.blocks(LANES)],
        [shape_of((rows, width), bf16), shape_of((2, rows, LANES), bf16), shape_of((2, rows, LANES), f32)],
        [pltpu.VMEM((tiles.tile, width), f32), pltpu.VMEM((tiles.tile, chans), f32)],
        6 * rows * width * chans, 8 * MEGA,
        (place, tokens, info, gain, *w),
    )


def gate_product(tiles, place, first, normed, back, info, w_gate, w_out):
    width = normed.shape[-1]
    chans = w_out[0].shape[-1]
    rows = normed.shape[0]
    return call(
        gate_kernel, "gate_product", tiles.grid,
        [SCALARS, tiles.flat(width), tiles.raw(width, first), tiles.info()]
        + [whole(w) for w in (*w_gate, *w_out)],
        [tiles.blocks(2 * LANES), tiles.blocks(2 * LANES)],
        [shape_of((2, rows, 2 * LANES), bf16), shape_of((2, rows, 2 * LANES), f32)],
        [pltpu.VMEM((tiles.tile, width), f32), pltpu.VMEM((tiles.tile, chans), f32)],
        12 * rows * width * chans, 16 * MEGA,
        (place, normed, back, info, *w_gate, *w_out),
    )


def out_product(tiles, place, pairs, info, w_out):
    width = 2 * w_out[0].shape[1]
    chans = w_out[0].shape[-1]
    rows = pairs[0].shape[1]
    parted = (tiles.micros, tiles.pairs, tiles.rows, width)
    return call(
        out_kernel, "out_product", tiles.grid,
        [SCALARS] + [tiles.kindred(0, LANES)] * 4 + [tiles.info(), whole(w_out[0]), whole(w_out[1])],
        [tiles.parted(width), tiles.parted(width)],
        [shape_of(parted, bf16), shape_of(parted, f32)],
        [pltpu.VMEM((tiles.tile, chans), f32), pltpu.VMEM((tiles.tile, width), f32)],
        6 * rows * width * chans, 8 * MEGA,
        (place, *pairs, info, *w_out),
    )


def normed_grad(tiles, place, pairs, inners, info, tokens, w_gate, w_inner):
    width = 2 * w_gate[0].shape[1]
    chans = w_gate[0].shape[-1]
    rows = inners[0].shape[0]
    parted = (tiles.micros, tiles.pairs, tiles.rows, width)
    return call(
        normed_kernel, "normed_grad", tiles.grid,
        [SCALARS] + [tiles.kindred(1, LANES)] * 4 + [tiles.flat(LANES)] * 4
        + [tiles.info(), tiles.raw(width)] + [whole(w) for w in (*w_gate, *w_inner)],
        [tiles.parted(width), tiles.parted(width), pl.BlockSpec((8, width), lambda m, z: (0, 0))],
        [shape_of(parted, bf16), shape_of(parted, f32), shape_of((8, width), f32)],
        [pltpu.VMEM((tiles.tile, chans), f32), pltpu.VMEM((tiles.tile, width), f32)],
        12 * rows * width * chans, 16 * MEGA,
        (place, *pairs, *inners, info, tokens, *w_gate, *w_inner),
    )


def weight_grad(place, infos, lefts, left_at, rights, right_at, span, dtype):
    chunks = len(lefts)
    width = lefts[0].shape[-1]
    chans = 4 * LANES
    steps = infos[0].shape[1] // span
    info_at = ((8, span), lambda m, chunk: (0, m))
    piece = (3, width // 2, chans)
    specs, args = [], []
    for chunk in range(chunks):
        def held(spec, chunk=chunk):
            shape, at = spec
            low = chunk * steps
            return pl.BlockSpec(shape, lambda i: at(jnp.clip(i - low, 0, steps - 1), chunk))

        specs += [held(info_at), held(left_at)] + [held(right_at)] * 4
        args += [infos[chunk], lefts[chunk], *rights[chunk]]
    return call(
        functools.partial(weight_grad_kernel, chunks, steps), "weight_grad", (chunks * steps,),
        [SCALARS] + specs,
        [pl.BlockSpec(piece, lambda i: (0, 0, 0))] * 2 + [pl.BlockSpec((8, 3 * chans), lambda i: (0, 0))],
        [shape_of(piece, dtype), shape_of(piece, dtype), shape_of((8, 3 * chans), f32)],
        [pltpu.VMEM((span, chans), f32), pltpu.VMEM((width, 3 * chans), f32)],
        6 * chunks * steps * span * width * chans, 24 * MEGA,
        (place, *args),
    )


def masked_sum(wide, info):
    width = wide.shape[1] // 3
    return sum(wide[:, k * width : (k + 1) * width] * info[:, k + 1 : k + 2] for k in range(3))


def halves(place_ref, micro, second, own_ref, x_ref, core_ref, both_ref):
    shape = own_ref.shape
    same_x = jnp.full(shape, place_ref[0] ^ micro, jnp.int32) == 0
    same_core = jnp.full(shape, place_ref[1] ^ second, jnp.int32) == 0
    own, across_x, across_core, both = (
        ref[...].astype(f32) for ref in (own_ref, x_ref, core_ref, both_ref)
    )
    return jnp.where(same_core, jnp.where(same_x, own, across_x), jnp.where(same_x, across_core, both))


def scan_scratch(micros):
    wide = pltpu.VMEM((micros, 8 * N, 2 * LANES), f32)
    product = pltpu.VMEM((micros, 8 * N, LANES), bf16)
    tile = pltpu.VMEM((micros, SCAN_ROWS, LANES), f32)
    return [pltpu.VMEM((micros, N, LANES), f32), wide, wide, product, product, tile, tile, tile]


def mix_forward_kernel(
    place_ref, keep_ref, own_ref, x_ref, core_ref, both_ref, act_ref, pair_ref, info_ref,
    dt_ref, mask_ref, side_ref, rate_ref, bias_ref, start_ref,
    kinds_ref, before_ref, step_ref, slope_ref, pull_ref, rows_ref, low_ref, grad_c_ref, final_ref,
    state_ref, wide_a, wide_b, product_a, product_b, drive_ref, y_ref, scaled_ref,
):
    micros, rows, _ = step_ref.shape
    block = pl.program_id(0)
    second = (2 * block) // pl.num_programs(0)
    rank = low_ref.shape[1]
    rate = rate_ref[...]
    mask = mask_ref[...]
    side = side_ref[...]
    ones = jnp.ones((LANES, LANES), bf16)
    lane = lax.broadcasted_iota(jnp.int32, (N, LANES), 1)
    dt_bias, skip = bias_ref[0:1], bias_ref[1:2]

    @pl.when(block == 0)
    def _():
        state_ref[...] = start_ref[...]

    for m in range(micros):
        shared = halves(place_ref, m, second, own_ref, x_ref, core_ref, both_ref)
        low = shared[:rank].astype(bf16)
        low_ref[m] = low
        dt_pre = masked_sum(across(low, dt_ref[...], (0, 0)), info_ref[m].T) + dt_bias
        small = jnp.exp(-jnp.abs(dt_pre))
        step = jnp.maximum(dt_pre, 0.0) + jnp.log1p(small)
        step_ref[m] = step
        slope_ref[m] = jnp.where(dt_pre >= 0, 1.0, small) / (1.0 + small)
        drive_ref[m] = step * act_ref[m].astype(f32)
        gate = pair_ref[m, :, :LANES]
        pull_ref[m] = pair_ref[m, :, LANES:] * (gate * jax.nn.sigmoid(gate))
        parts = []
        for left in (shared[rank : rank + N], shared[rank + N :]):
            for _ in range(3):
                part = left.astype(bf16).astype(f32)
                parts.append(part)
                left = left - part
            parts.append(jnp.zeros_like(left))
        rows_ref[m] = jnp.concatenate(parts, 0).T
        wide_a[m] = spread(rows_ref, m, 0, mask, side)

    def sixteen(turn, carried):
        states, grads = (list(part) for part in carried)
        for half in range(2):
            base = pl.multiple_of(turn * 16 + 8 * half, 8)
            wide, wide_next = (wide_a, wide_b) if half == 0 else (wide_b, wide_a)
            product, product_last = (product_a, product_b) if half == 0 else (product_b, product_a)
            following = jnp.minimum(base + 8, rows - 8)
            for m in range(micros):
                wide_next[m] = spread(rows_ref, m, following, mask, side)
                grads[m] = lane_sums(product_last, m, grads[m], lane, base - 8, ones)
            y_parts = [[] for _ in range(micros)]
            for j in range(8):
                for m in range(micros):
                    row = pl.ds(base + j, 1)
                    own = slice(N * j, N * j + N)
                    before = states[m]
                    before_ref[m, base + j] = before
                    before = before * keep_ref[m, block * rows + base + j]
                    state = (
                        jnp.exp(step_ref[m, row, :] * rate) * before
                        + drive_ref[m, row, :] * wide[m, own, :LANES]
                    )
                    states[m] = state
                    shown = state * wide[m, own, LANES:]
                    y_parts[m].append(shown[:8] + shown[8:])
                    product[m, own, :] = (state * pull_ref[m, row, :]).astype(bf16)
            for m in range(micros):
                y_ref[m, pl.ds(base, 8), :] = sum_rows(y_parts[m])
        return (tuple(states), tuple(grads))

    begin = (
        tuple(state_ref[m] for m in range(micros)),
        tuple(jnp.zeros((N, LANES), f32) for m in range(micros)),
    )
    states, grads = lax.fori_loop(0, rows // 16, sixteen, begin)
    for m in range(micros):
        state_ref[m] = states[m]
        grad_c_ref[m] = lane_sums(product_b, m, grads[m], lane, rows - 8, ones)
        final_ref[m] = states[m]
        gate, d_mixed = pair_ref[m, :, :LANES], pair_ref[m, :, LANES:]
        sigma = jax.nn.sigmoid(gate)
        y_scan = y_ref[m] + skip * act_ref[m].astype(f32)
        kinds_ref[0, m] = (y_scan * (gate * sigma)).astype(bf16)
        slope = sigma * (1.0 + gate * (1.0 - sigma))
        kinds_ref[1, m] = (d_mixed * y_scan * slope).astype(bf16)


def time_specs(micros, at):
    tall = pl.BlockSpec((micros, SCAN_ROWS, LANES), lambda i: (0, at(i), 0))
    return dict(
        tall=tall,
        pair=pl.BlockSpec((micros, SCAN_ROWS, 2 * LANES), lambda i: (0, at(i), 0)),
        turned=pl.BlockSpec((micros, LANES, SCAN_ROWS), lambda i: (0, 0, at(i))),
        wide=pl.BlockSpec((micros, N, SCAN_ROWS), lambda i: (0, 0, at(i))),
        states=pl.BlockSpec((micros, SCAN_ROWS, N, LANES), lambda i: (0, at(i), 0, 0)),
        info=pl.BlockSpec((micros, 8, SCAN_ROWS), lambda i: (0, 0, at(i))),
        fixed=pl.BlockSpec((micros, N, LANES), lambda i: (0, 0, 0)),
    )


def const(shape):
    return pl.BlockSpec(shape, lambda *at: (0,) * len(shape))


def mix_forward(place, keep, quarters, act, pair, info, dt, rules, rate, bias, start):
    micros, length, _ = act.shape
    blocks = length // SCAN_ROWS
    spec = time_specs(micros, lambda i: i)
    width = quarters[0].shape[0]
    quarter = pl.BlockSpec((width, SCAN_ROWS), lambda i: (0, i % (blocks // 2)))
    tall = jax.ShapeDtypeStruct((micros, length, LANES), f32)
    return pl.pallas_call(
        mix_forward_kernel,
        grid=(blocks,),
        in_specs=[
            SCALARS, SCALARS, *[quarter] * 4, spec["tall"], spec["pair"], spec["info"],
            const(dt.shape), const(rules[0].shape), const(rules[1].shape),
            const(rate.shape), const(bias.shape), spec["fixed"],
        ],
        out_specs=[
            pl.BlockSpec((2, micros, SCAN_ROWS, LANES), lambda i: (0, 0, i, 0)),
            spec["states"], *[spec["tall"]] * 4, spec["turned"], spec["wide"], spec["fixed"],
        ],
        out_shape=[
            jax.ShapeDtypeStruct((2, micros, length, LANES), bf16),
            jax.ShapeDtypeStruct((micros, length, N, LANES), f32),
            tall, tall, tall, tall,
            jax.ShapeDtypeStruct((micros, width - 2 * N, length), bf16),
            jax.ShapeDtypeStruct((micros, N, length), f32),
            jax.ShapeDtypeStruct((micros, N, LANES), f32),
        ],
        scratch_shapes=scan_scratch(micros),
        cost_estimate=pl.CostEstimate(
            flops=micros * length * N * LANES * 40,
            bytes_accessed=micros * length * N * LANES * 12,
            transcendentals=micros * length * N * LANES,
        ),
        compiler_params=pltpu.CompilerParams(
            dimension_semantics=("arbitrary",), vmem_limit_bytes=40 * MEGA
        ),
        name="mix_forward",
    )(place, keep, *quarters, act, pair, info, dt, *rules, rate, bias, start)


def mix_backward_kernel(
    place_ref, keep_ref, act_ref, info_ref, dt_ref, mask_ref, side_ref, rate_ref, bias_ref, start_ref,
    before_ref, step_ref, slope_ref, pull_ref, rows_ref, low_ref, grad_c_ref,
    shared_ref, d_act_ref, grad_dt_ref, sums_ref, grad_rate_ref, final_ref,
    state_ref, wide_a, wide_b, product_a, product_b, drive_ref, b_pull_ref, rate_pull_ref,
):
    micros, rows, _ = step_ref.shape
    block = pl.num_programs(0) - 1 - pl.program_id(0)
    rank = low_ref.shape[1]
    rate = rate_ref[...]
    mask = mask_ref[...]
    side = side_ref[...]
    skip = bias_ref[1:2]
    ones = jnp.ones((LANES, LANES), bf16)
    lane = lax.broadcasted_iota(jnp.int32, (N, LANES), 1)

    @pl.when(pl.program_id(0) == 0)
    def _():
        state_ref[...] = start_ref[...]
        grad_rate_ref[...] = jnp.zeros_like(grad_rate_ref)
        grad_dt_ref[...] = jnp.zeros_like(grad_dt_ref)
        sums_ref[...] = jnp.zeros_like(sums_ref)

    for m in range(micros):
        drive_ref[m] = step_ref[m] * act_ref[m].astype(f32)
        wide_a[m] = spread(rows_ref, m, rows - 8, mask, side)

    def sixteen(turn, carried):
        states, grads, rates = (list(part) for part in carried)
        for half in range(2):
            base = pl.multiple_of(rows - 8 - turn * 16 - 8 * half, 8)
            wide, wide_next = (wide_a, wide_b) if half == 0 else (wide_b, wide_a)
            product, product_last = (product_a, product_b) if half == 0 else (product_b, product_a)
            following = jnp.maximum(base - 8, 0)
            for m in range(micros):
                wide_next[m] = spread(rows_ref, m, following, mask, side)
                grads[m] = lane_sums(product_last, m, grads[m], lane, base + 8, ones)
            b_parts = [[None] * 8 for _ in range(micros)]
            rate_parts = [[None] * 8 for _ in range(micros)]
            for j in range(7, -1, -1):
                for m in range(micros):
                    row = pl.ds(base + j, 1)
                    own = slice(N * j, N * j + N)
                    step = step_ref[m, row, :]
                    adjoint = wide[m, own, LANES:] * pull_ref[m, row, :] + states[m]
                    passed = jnp.exp(step * rate) * (
                        adjoint * keep_ref[m, block * rows + base + j]
                    )
                    states[m] = passed
                    decay_pull = passed * before_ref[m, base + j]
                    shown = adjoint * wide[m, own, :LANES]
                    b_parts[m][j] = shown[:8] + shown[8:]
                    shown = decay_pull * rate
                    rate_parts[m][j] = shown[:8] + shown[8:]
                    rates[m] = rates[m] + decay_pull * step
                    product[m, own, :] = (adjoint * drive_ref[m, row, :]).astype(bf16)
            for m in range(micros):
                b_pull_ref[m, pl.ds(base, 8), :] = sum_rows(b_parts[m])
                rate_pull_ref[m, pl.ds(base, 8), :] = sum_rows(rate_parts[m])
        return (tuple(states), tuple(grads), tuple(rates))

    zeros = tuple(jnp.zeros((N, LANES), f32) for m in range(micros))
    begin = (tuple(state_ref[m] for m in range(micros)), zeros, zeros)
    states, grads, rates = lax.fori_loop(0, rows // 16, sixteen, begin)
    for m in range(micros):
        state_ref[m] = states[m]
        grad_rate_ref[...] += rates[m]
        final_ref[m] = states[m]
        act = act_ref[m].astype(f32)
        pull = pull_ref[m]
        b_pull = b_pull_ref[m]
        d_act_ref[m] = pull * skip + step_ref[m] * b_pull
        d_pre = ((rate_pull_ref[m] + act * b_pull) * slope_ref[m]).astype(bf16).astype(f32)
        sums_ref[0:8] += jnp.sum(d_pre.reshape(-1, 8, LANES), axis=0)
        sums_ref[8:16] += jnp.sum((pull * act).reshape(-1, 8, LANES), axis=0)
        d_pre3 = three(d_pre, info_ref[m].T)
        shared_ref[m, :rank] = across(dt_ref[...], d_pre3, (1, 1))
        shared_ref[m, rank : rank + N] = lane_sums(product_b, m, grads[m], lane, 0, ones)
        shared_ref[m, rank + N :] = grad_c_ref[m]
        grad_dt_ref[...] += across(low_ref[m], d_pre3, (1, 0))


def mix_backward(place, keep, act, info, dt, rules, rate, bias, start, saved):
    before, step, slope, pull, rows, low, grad_c = saved
    micros, length, _ = act.shape
    blocks = length // SCAN_ROWS
    spec = time_specs(micros, lambda i: blocks - 1 - i)
    rank = low.shape[1]
    width = rank + 2 * N
    return pl.pallas_call(
        mix_backward_kernel,
        grid=(blocks,),
        in_specs=[
            SCALARS, SCALARS, spec["tall"], spec["info"],
            const(dt.shape), const(rules[0].shape), const(rules[1].shape),
            const(rate.shape), const(bias.shape), spec["fixed"],
            spec["states"], *[spec["tall"]] * 4, spec["turned"], spec["wide"],
        ],
        out_specs=[
            pl.BlockSpec((micros, width, SCAN_ROWS), lambda i: (0, 0, blocks - 1 - i)),
            spec["tall"], const(dt.shape), const((16, LANES)), const((N, LANES)), spec["fixed"],
        ],
        out_shape=[
            jax.ShapeDtypeStruct((micros, width, length), f32),
            jax.ShapeDtypeStruct((micros, length, LANES), f32),
            jax.ShapeDtypeStruct(dt.shape, f32),
            jax.ShapeDtypeStruct((16, LANES), f32),
            jax.ShapeDtypeStruct((N, LANES), f32),
            jax.ShapeDtypeStruct((micros, N, LANES), f32),
        ],
        scratch_shapes=scan_scratch(micros),
        cost_estimate=pl.CostEstimate(
            flops=micros * length * N * LANES * 60,
            bytes_accessed=micros * length * N * LANES * 12,
            transcendentals=micros * length * N * LANES,
        ),
        compiler_params=pltpu.CompilerParams(
            dimension_semantics=("arbitrary",), vmem_limit_bytes=40 * MEGA
        ),
        name="mix_backward",
    )(place, keep, act, info, dt, *rules, rate, bias, start, *saved)


def shifted(scratch_ref, j, rows):
    return scratch_ref[8 - j : 8 - j + rows, :]


def conv_forward_kernel(inner_ref, edge_ref, info_ref, taps_ref, wx_ref,
                        act_ref, conv_ref, shared_ref, scratch_ref):
    rows = inner_ref.shape[1]
    scratch_ref[:8] = edge_ref[0]
    scratch_ref[8:] = inner_ref[0]
    info = info_ref[0].T
    total = taps_ref[K : K + 1] + taps_ref[0:1] * inner_ref[0]
    for j in range(1, K):
        total = total + taps_ref[j : j + 1] * (shifted(scratch_ref, j, rows) * info[:, 3 + j : 4 + j])
    conv_ref[0] = total
    act = (total * jax.nn.sigmoid(total)).astype(bf16)
    act_ref[0] = act
    shared_ref[0] = across(wx_ref[...], three(act.astype(f32), info), (1, 1))


def conv_forward(inner, edge, info, taps, wx):
    micros, rows, _ = inner.shape
    one = pl.BlockSpec((1, rows, LANES), lambda m: (m, 0, 0))
    width = wx.shape[0]
    return call(
        conv_forward_kernel, "conv_forward", (micros,),
        [
            one, pl.BlockSpec((1, 8, LANES), lambda m: (m, 0, 0)),
            pl.BlockSpec((1, 8, rows), lambda m: (m, 0, 0)), const(taps.shape), const(wx.shape),
        ],
        [one, one, pl.BlockSpec((1, width, rows), lambda m: (m, 0, 0))],
        [
            shape_of(inner.shape, bf16), shape_of(inner.shape, f32),
            shape_of((micros, width, rows), f32),
        ],
        [pltpu.VMEM((rows + 8, LANES), f32)],
        2 * micros * rows * wx.size, 4 * MEGA,
        (inner, edge, info, taps, wx),
    )


def conv_backward_kernel(place_ref, own_ref, x_ref, core_ref, both_ref, d_act_ref, conv_ref, inner_ref,
                         edge_ref, act_ref, info_ref, taps_ref, wx_ref,
                         d_inner_ref, grad_x_ref, sums_ref, head_ref, last_ref, scratch_ref, ahead_ref):
    rows = inner_ref.shape[1]
    micro = pl.program_id(0)
    info = info_ref[0].T

    @pl.when(micro == 0)
    def _():
        grad_x_ref[...] = jnp.zeros_like(grad_x_ref)
        sums_ref[...] = jnp.zeros_like(sums_ref)

    shared = jnp.concatenate(
        [
            halves(place_ref, micro, half, own_ref, x_ref, core_ref, both_ref)
            for half in range(2)
        ],
        1,
    ).astype(bf16)
    d_act = d_act_ref[0] + masked_sum(across(shared, wx_ref[...], (0, 0)), info)
    grad_x_ref[...] += across(shared, three(act_ref[0].astype(f32), info), (1, 0))
    conv = conv_ref[0]
    sigma = jax.nn.sigmoid(conv)
    d_conv = d_act * (sigma * (1.0 + conv * (1.0 - sigma)))
    head_ref[0] = d_conv[:8]
    scratch_ref[:8] = edge_ref[0]
    scratch_ref[8:] = inner_ref[0]
    ahead_ref[rows:] = jnp.zeros((8, LANES), f32)
    total = taps_ref[0:1] * d_conv
    sums_ref[0:8] += jnp.sum((d_conv * inner_ref[0]).reshape(-1, 8, LANES), axis=0)
    for j in range(1, K):
        masked = d_conv * info[:, 3 + j : 4 + j]
        pulled = (masked * shifted(scratch_ref, j, rows)).reshape(-1, 8, LANES)
        sums_ref[8 * j : 8 * j + 8] += jnp.sum(pulled, axis=0)
        ahead_ref[:rows] = masked
        total = total + taps_ref[j : j + 1] * ahead_ref[j : j + rows, :]
    sums_ref[8 * K : 8 * K + 8] += jnp.sum(d_conv.reshape(-1, 8, LANES), axis=0)
    d_inner_ref[0] = total.astype(bf16)
    last_ref[0] = total[rows - 8 :]


def conv_backward(place, quarters, d_act, conv, inner, edge, act, info, taps, wx):
    micros, rows, _ = inner.shape
    one = pl.BlockSpec((1, rows, LANES), lambda m: (m, 0, 0))
    eight = pl.BlockSpec((1, 8, LANES), lambda m: (m, 0, 0))
    sums = (8 * (K + 1), LANES)
    return call(
        conv_backward_kernel, "conv_backward", (micros,),
        [
            SCALARS, *[const(quarters[0].shape)] * 4, one, one, one, eight, one,
            pl.BlockSpec((1, 8, rows), lambda m: (m, 0, 0)), const(taps.shape), const(wx.shape),
        ],
        [one, const(wx.shape), const(sums), eight, eight],
        [
            shape_of(inner.shape, bf16), shape_of(wx.shape, f32), shape_of(sums, f32),
            shape_of((micros, 8, LANES), f32), shape_of((micros, 8, LANES), f32),
        ],
        [pltpu.VMEM((rows + 8, LANES), f32), pltpu.VMEM((rows + 8, LANES), f32)],
        4 * micros * rows * wx.size, 6 * MEGA,
        (place, *quarters, d_act, conv, inner, edge, act, info, taps, wx),
    )


def pack_kernel(plane, flag_ref, after_ref, w_ref, *out_refs):
    half = w_ref.shape[-1] // 2
    for turn, out_ref in enumerate(out_refs):
        lanes = pl.ds(pl.multiple_of((turn ^ flag_ref[0]) * half, half), half)
        at = (0, slice(None), lanes) if plane is None else (0, slice(None), plane, lanes)
        out_ref[0] = w_ref[at].astype(bf16)


def pack(flag, after, weight, plane=None):
    kinds, rows = weight.shape[:2]
    chans = weight.shape[-1]
    half = chans // 2
    return call(
        functools.partial(pack_kernel, plane), "pack", (kinds,),
        [SCALARS, SCALARS, pl.BlockSpec((1,) + weight.shape[1:], lambda k: (k,) + (0,) * (weight.ndim - 1))],
        [pl.BlockSpec((1, rows, half), lambda k: (k, 0, 0))] * 2,
        [shape_of((kinds, rows, half), bf16)] * 2,
        [], 0, weight.size * 6, (flag, after, weight),
    )


def adam_kernel(rate, flag_ref, clip_ref, w_ref, m_ref, v_ref, *refs):
    pieces, (grad_ref, new_ref, first_ref, second_ref) = refs[:4], refs[4:]
    half = w_ref.shape[-1] // 2
    clip = clip_ref[0]
    for plane in range(2):
        for turn in range(2):
            lanes = pl.ds(pl.multiple_of((turn ^ flag_ref[0]) * half, half), half)
            at = (0, slice(None), plane, lanes)
            grad = pieces[2 * plane + turn][0].astype(f32)
            new, first, second = adam_update(w_ref[at], grad, m_ref[at], v_ref[at], clip, rate)
            grad_ref[at] = grad
            new_ref[at] = new
            first_ref[at] = first
            second_ref[at] = second


def adam(flag, clip, weight, first, second, pieces, rate):
    kinds, rows, _, chans = weight.shape
    block = min(rows, 64)
    full = pl.BlockSpec((1, block, 2, chans), lambda k, r: (k, r, 0, 0))
    piece = pl.BlockSpec((1, block, chans // 2), lambda k, r: (k, r, 0))
    return call(
        functools.partial(adam_kernel, rate), "adam", (kinds, rows // block),
        [SCALARS, SCALARS, full, full, full] + [piece] * 4,
        [full] * 4,
        [shape_of(weight.shape, f32)] * 4,
        [], weight.size * 20, weight.size * 32,
        (flag, clip, weight, first, second, *pieces),
    )


def body(
    groups, parts, chans,
    tokens_in, modality, starts, cotangent,
    in_weight, in_first, in_second,
    dt_weight, dt_first, dt_second,
    out_weight, out_first, out_second,
    x_weight, x_first, x_second,
    channel_params, channel_first, channel_second,
    gain, gain_first, gain_second,
):
    micros, tok_rows, part_width = tokens_in.shape
    model = gain.shape[0]
    chan_width = in_weight.shape[3]
    half = chan_width // 2
    own = half // chans
    cores = chans // 2
    inner_all = chan_width * chans
    x_width = x_weight.shape[1]
    rank = x_width - 2 * N
    dt_rows = dt_weight.shape[1]
    span = parts * tok_rows
    edge = K - 1
    t_at = lax.axis_index("t")
    p_at = lax.axis_index("p")
    c_at = lax.axis_index("c")
    z_at, y_at = p_at // 2, p_at % 2
    x_at, core_at = c_at // cores, c_at % cores
    s_at = t_at * parts + p_at
    slice_at = s_at // (2 * groups)
    everywhere = ("t", "p", "c")
    place = jnp.stack([x_at, core_at, y_at, z_at]).astype(jnp.int32)

    def flat(t, p, c):
        return (t * parts + p) * chans + c

    def part_of(c, j):
        return 2 * (2 * (c % cores) + j) + c // cores

    devices = [(t, p, c) for t in range(groups) for p in range(parts) for c in range(chans)]

    def first_hop(turn):
        pairs = []
        for t, p, c in devices:
            s = t * parts + p
            to_slice, i = s // (2 * groups), (s % (2 * groups)) // groups
            j = turn ^ (to_slice // cores)
            to = flat(s % groups, 2 * (2 * (c % cores) + j) + i, c // cores * cores + to_slice % cores)
            pairs.append((flat(t, p, c), to))
        return pairs

    def second_hop(turn):
        return [
            (flat(t, p, c), flat(t, p - p % 2 + c // cores, (turn ^ (p % 2)) * cores + c % cores))
            for t, p, c in devices
        ]

    small_pairs = [(flat(t, p, c), flat(t, part_of(c, p % 2), p // 2)) for t, p, c in devices]

    def send(value, pairs, back=False):
        if back:
            pairs = [(b, a) for a, b in pairs]
        return lax.ppermute(value, everywhere, pairs)

    def swap(value, axis, distance):
        return lax.ppermute(value, axis, [(i, i ^ distance) for i in range(lax.axis_size(axis))])

    def crossed(pair, flag):
        first, second = pair
        return jnp.where(flag == 0, first, second), jnp.where(flag == 0, second, first)

    between = y_at ^ (z_at % 2)

    def token(*values):
        return sum(value[(0,) * value.ndim].astype(f32) for value in values)[None]

    def weights_there(pair):
        pair = [send(value, first_hop(turn)) for turn, value in enumerate(pair)]
        first = token(*pair)
        pair = crossed(pair, between)
        pair = [send(value, second_hop(turn)) for turn, value in enumerate(pair)]
        return pair, first, token(pair[0])

    def there_whole(pair):
        if groups > 1:
            pair = [lax.all_gather(value, "t", axis=1, tiled=True) for value in pair]
        return tuple(pair)

    group_squares = []

    def returned(pair):
        if groups > 1:
            pair = [
                lax.psum_scatter(value, "t", scatter_dimension=1, tiled=True) for value in pair
            ]
            group_squares.extend(jnp.sum(value * value) for value in pair)
            pair = [value.astype(bf16) for value in pair]
        halfway = [send(value, second_hop(turn), True) for turn, value in enumerate(pair)]
        pair = crossed(halfway, between)
        return [send(value, first_hop(turn), True) for turn, value in enumerate(pair)], halfway

    def along_groups(value, by):
        pairs = [(i, i + by) for i in range(groups) if 0 <= i + by < groups]
        return lax.ppermute(value, "t", pairs)

    def over_chans(value):
        distance = 1
        while distance < chans:
            value = value + swap(value, "c", distance)
            distance *= 2
        return value

    def pick(value, at, axis):
        return lax.dynamic_index_in_dim(value, at, axis, keepdims=False)

    def scattered_chans(sent, keep):
        total = keep + swap(sent, "c", 1).astype(f32)
        got = swap(pick(total, 1 - x_at, 0).astype(bf16), "c", cores)
        return pick(total, x_at, 0) + got.astype(f32)

    def gathered_chans(value):
        across_x = swap(value, "c", cores)
        across_core = swap(value, "c", 1)
        return (value, across_x, across_core, swap(across_x, "c", 1))

    parts_arrived = []

    def scattered_parts(sent, keep, late=None):
        total = keep + swap(sent, "p", 1).astype(f32)
        parts_arrived.append(total)
        total = total.reshape(total.shape[0], -1, 2, *total.shape[2:])
        got = swap(pick(total, 1 - z_at % 2, 2).astype(bf16), "p", 2)
        total = pick(total, z_at % 2, 2) + got.astype(f32)
        away = pick(total, 1 - z_at // 2, 1)
        if late is not None:
            away = away + 0.0 * late[0]
        got = swap(away.astype(bf16), "p", 4)
        return pick(total, z_at // 2, 1) + got.astype(f32)

    def after(value, *others):
        return value + (0.0 * token(*others)).astype(jnp.int32)

    def quarters_of(values, kind, fills):
        length = values[0].shape[2] // 2
        fills = list(fills)

        def half_of(value, at):
            return lax.dynamic_slice_in_dim(value, at * length, length, 2)

        def fill(arrived):
            return token(*fills.pop(0)(after(place, *arrived)))[0] if fills else None

        def tied(arrived, ran):
            return arrived if ran is None else [value + 0.0 * ran for value in arrived]

        totals = [
            half_of(value, core_at)
            + swap(half_of(value, 1 - core_at).astype(kind), "c", 1).astype(f32)
            for value in values
        ]
        ran = fill(totals)
        totals = [
            pick(total, x_at, 0)
            + swap(pick(total, 1 - x_at, 0).astype(kind), "c", cores).astype(f32)
            for total in totals
        ]
        distance = 1
        while distance < parts:
            last, ran = ran, fill(totals)
            totals = [total.astype(kind) for total in tied(totals, last)]
            totals = [
                total.astype(f32) + swap(total, "p", distance).astype(f32) for total in totals
            ]
            distance *= 2
        totals = tied(totals, ran)
        return [gathered_chans(total.astype(kind)) for total in totals]

    def over_all(value):
        value = over_chans(value)
        distance = 1
        while distance < parts:
            value = value + swap(value, "p", distance)
            distance *= 2
        return lax.psum(value, "t") if groups > 1 else value

    extra = jnp.pad(modality.astype(bf16)[:, None, :], ((0, 0), (0, 15), (0, part_width - tok_rows)))
    longer = jnp.concatenate([tokens_in, extra], 1)
    chunk = min(GROUP, micros)
    starts_of = range(0, micros, chunk)
    tokens_all = [lax.all_gather(longer[at : at + chunk], "p") for at in starts_of]
    flag = (slice_at // cores).astype(jnp.int32)[None]
    w_inner, _, arrived = weights_there(pack(flag, jnp.zeros((1,), f32), in_weight, 0))
    w_inner = there_whole(w_inner)
    small = jnp.concatenate([x_weight.reshape(3 * x_width, chan_width), channel_params], 0)
    own_lanes = y_at * half + z_at * own
    small = send(lax.dynamic_slice_in_dim(small, own_lanes, own, 1), small_pairs)
    w_gate, arrived, _ = weights_there(pack(flag, arrived, in_weight, 1))
    w_gate = there_whole(w_gate)
    dt16 = dt_weight.astype(bf16)
    dt_pair = crossed((dt16[..., :half], dt16[..., half:]), flag[0])
    out_pair = pack(flag, arrived, out_weight)
    out_rows = out_weight.shape[1]
    both = [jnp.concatenate(pair, 1) for pair in zip(out_pair, dt_pair)]
    both, _, _ = weights_there(both)
    w_out = there_whole([value[:, :out_rows] for value in both])
    dt_part = jnp.concatenate(
        crossed(there_whole([value[:, out_rows:] for value in both]), x_at), 1
    )
    dt_blocks = []
    for distance in range(chans):
        block = lax.dynamic_slice_in_dim(dt_part, (c_at ^ distance) * own, own, 2)
        dt_blocks.append(swap(block, "c", distance) if distance else block)
    dt_blocks = jnp.stack(dt_blocks)
    w_dt = jnp.concatenate([pick(dt_blocks, c_at ^ k, 0) for k in range(chans)], 1)
    w_dt = w_dt.transpose(1, 0, 2).reshape(rank, 3 * own)
    back_all = lax.all_gather(cotangent, "p")
    positions = t_at * span - edge + jnp.arange(span + 2 * edge, dtype=jnp.int32)
    segment = jnp.sum((starts[:, None, :] <= positions[None, :, None]).astype(jnp.int32), axis=2)
    keep_mask = 1.0 - jnp.any(
        starts[:, None, :] == positions[None, edge : edge + span, None], axis=2
    ).astype(f32)
    same_doc = [
        (segment[:, edge - j : 2 * edge - j + span] == segment[:, edge:]).astype(f32)
        for j in range(1, K)
    ]
    infos, infos3, inverses = [], [], []
    for at, tokens in zip(starts_of, tokens_all):
        squares = jnp.sum(jnp.square(tokens[:, :, :tok_rows].astype(f32)), axis=-1)
        squares = over_chans(squares).transpose(1, 0, 2).reshape(chunk, span)
        inverse = lax.rsqrt(squares / model + NORM_EPS)
        kinds = tokens[:, :, tok_rows, :tok_rows].transpose(1, 0, 2).reshape(chunk, span)
        kinds = kinds.astype(jnp.int32)
        rows = [inverse, *((kinds == k).astype(f32) for k in range(3))]
        rows += [same[at : at + chunk, :span] for same in same_doc] + [jnp.zeros_like(inverse)]
        inverses.append(inverse)
        infos3.append(jnp.stack(rows, 1))
        infos.append(jnp.stack([row.reshape(-1) for row in rows], 0))
    inv_own = lax.dynamic_slice_in_dim(
        jnp.concatenate(inverses, 0), p_at * tok_rows, tok_rows, 1
    )[..., None]
    gain_part = lax.dynamic_slice_in_dim(gain, c_at * part_width, part_width, 0)[None]

    w_x = small[: 3 * x_width].astype(bf16).reshape(3, x_width, own)
    w_x = w_x.transpose(1, 0, 2).reshape(x_width, 3 * own)
    channel = small[3 * x_width :]
    taps = channel[:8]
    biases = jnp.pad(channel[K + 1 : K + 3], ((0, 6), (0, 0)))
    neg_rate = -jnp.exp(channel[K + 3 :])
    rules = lane_rules()

    grad_dt_sum = grad_x_sum = grad_chan_sum = grad_gain_sum = 0.0
    rows_back, held = [], []
    all_normed, all_pairs, all_inners = [], [], []
    zero_state = jnp.zeros((chunk, N, own), f32)
    tiles = Tiles(chunk, parts, tok_rows)
    for tokens, info in zip(tokens_all, infos):
        normed, sent, keep = inner_product(tiles, place, tokens, info, gain_part, w_inner)
        all_normed.append(normed)
        held.append(scattered_chans(sent, keep).reshape(chunk, span, own))
    for at, inner in enumerate(held):
        edge_rows = jnp.zeros((chunk, 8, own), f32)
        if groups > 1:
            edge_rows = along_groups(inner[:, span - 8 :], 1)
        held[at] = (inner, edge_rows, *conv_forward(inner, edge_rows, infos3[at], taps, w_x))

    gates = [None] * len(held)

    def gate_fill(at):
        def run(order):
            gates[at] = gate_product(
                tiles, order, at * chunk, all_normed[at], back_all, infos[at], w_gate, w_out
            )
            return gates[at][:1]

        return run

    summed = quarters_of([stage[4] for stage in held], f32, [gate_fill(at) for at in range(len(held))])
    for at, quarters in enumerate(summed):
        pair = scattered_chans(*gates[at]).reshape(chunk, span, 2 * own)
        held[at] = (*held[at][:4], quarters, pair)
    for at, (inner, edge_rows, act, conv, quarters, pair) in enumerate(held):
        ms = slice(at * chunk, at * chunk + chunk)
        keeps = keep_mask[ms]
        args = (keeps, quarters, act, pair, infos3[at], w_dt, rules, neg_rate, biases)
        state_in = zero_state
        if groups > 1:
            first_pass = mix_forward(place, *args, zero_state)
            ends, step = first_pass[8], first_pass[2]
            passed_all = jnp.exp(jnp.sum(step, axis=1)[:, None, :] * neg_rate)
            passed_all = passed_all * jnp.prod(keeps, axis=1)[:, None, None]
            for _ in range(groups - 1):
                state_in = along_groups(passed_all * state_in + ends, 1)
        kinds_out, *saved, _ = mix_forward(place, *args, state_in)
        pairs = gathered_chans(kinds_out.reshape(2, chunk * span, own))
        all_pairs.append(pairs)
        held[at] = (keeps, act, saved, inner, edge_rows, conv)

    scanned = [*held[-1][2][1:2], *all_pairs[0][1:]]
    for at, (keeps, act, saved, inner, edge_rows, conv) in enumerate(held):
        order = after(place, *scanned)
        args = (keeps, act, infos3[at], w_dt, rules, neg_rate, biases)
        adj_in = zero_state
        if groups > 1:
            ends = mix_backward(order, *args, zero_state, saved)[5]
            passed_all = jnp.exp(jnp.sum(saved[1], axis=1)[:, None, :] * neg_rate)
            passed_all = passed_all * jnp.prod(keeps, axis=1)[:, None, None]
            for _ in range(groups - 1):
                adj_in = along_groups(passed_all * adj_in + ends, -1)
        shared, d_act, grad_dt, sums, grad_rate, _ = mix_backward(order, *args, adj_in, saved)
        grad_dt_sum += grad_dt
        sums = jnp.sum(sums.reshape(2, 8, own), axis=1)
        held[at] = (act, inner, edge_rows, conv, d_act, shared, sums, grad_rate * neg_rate)
        scanned = [d_act, *all_pairs[min(at + 1, len(held) - 1)][1:]]

    kept = f32 if groups > 1 else bf16

    def kindred(which):
        return ((1, span, own), lambda m, chunk_at: (which, m, 0))

    rows_at = ((span, part_width), lambda m, chunk_at: (m, 0))
    raw_at = ((parts, 1, tok_rows, part_width), lambda m, chunk_at: (0, chunk_at * chunk + m, 0, 0))
    backs = [back_all] * len(all_pairs)
    products = [None] * len(held)
    large = {}

    def out_fill(at):
        def run(order):
            products[at] = out_product(tiles, order, all_pairs[at], infos[at], w_out)
            return products[at][:1]

        return run

    def out_grad_fill(order):
        *pieces, square = weight_grad(order, infos, backs, raw_at, all_pairs, kindred(0), span, kept)
        large["out"] = (pieces, square)
        return (square,)

    def gate_grad_fill(order):
        *pieces, square = weight_grad(
            order, infos, all_normed, rows_at, all_pairs, kindred(1), span, kept
        )
        large["gate"] = (pieces, square)
        return (square,)

    fills = [*(out_fill(at) for at in range(len(held))), out_grad_fill, gate_grad_fill]
    summed = quarters_of([stage[5] for stage in held], bf16, fills)
    (g_out, out_sq), (g_gate, gate_sq) = large["out"], large["gate"]
    g_out, g_gate = returned(g_out), returned(g_gate)
    outs = [scattered_parts(*product) for product in products]
    for at, stage in enumerate(held):
        act, inner, edge_rows, conv, d_act, _, mix_sums, d_rate = stage
        first = at * chunk
        d_inner, grad_x, sums, head, last = conv_backward(
            place, summed[at], d_act, conv, inner, edge_rows, act, infos3[at], taps, w_x
        )
        if groups > 1:
            ahead = along_groups(head, -1)[:, :edge]
            for j in range(1, K):
                gone = taps[j] * ahead * same_doc[j - 1][first : first + chunk, span:, None]
                last = last.at[:, 8 - j :].add(gone[:, :j])
            d_inner = jnp.concatenate([d_inner[:, : span - 8], last.astype(bf16)], 1)
        grad_x_sum += grad_x
        sums = jnp.sum(sums.reshape(K + 1, 8, own), axis=1)
        grad_chan_sum += jnp.concatenate([sums, mix_sums, d_rate], 0)
        all_inners.append(gathered_chans(d_inner.reshape(chunk * span, own)))

    flat_at = ((span, own), lambda m, chunk_at: (m, 0))
    *g_inner, inner_sq = weight_grad(
        after(place, *g_out[1], *g_gate[1]), infos, all_normed, rows_at, all_inners, flat_at, span, kept
    )
    g_inner = returned(g_inner)
    order = after(place, inner_sq)
    for at in range(len(held)):
        sent, keep, gain_rows = normed_grad(
            tiles, order, all_pairs[at], all_inners[at], infos[at], tokens_all[at], w_gate, w_inner
        )
        grad_gain_sum += jnp.sum(gain_rows, axis=0)
        order = after(place, *g_inner[1], *g_out[0])
        rows_back.append(scattered_parts(sent, keep, token(*g_inner[0], *g_gate[0]) if at else None))

    grad_x_sum = grad_x_sum.reshape(x_width, 3, own).transpose(1, 0, 2)
    grad_dt_sum = grad_dt_sum.reshape(rank, 3, own).transpose(1, 0, 2)
    g_small = jnp.concatenate(
        [grad_x_sum.reshape(-1, own), grad_dt_sum.reshape(-1, own), grad_chan_sum], 0
    )
    if groups > 1:
        g_small = lax.psum(g_small, "t")
        large_sq = sum(group_squares)
    else:
        large_sq = jnp.sum(out_sq) + jnp.sum(gate_sq) + jnp.sum(inner_sq)
    local_sq = large_sq + jnp.sum(g_small * g_small) / groups
    here = (jnp.arange(chans) == c_at).astype(f32)
    tail = jnp.concatenate([(here[:, None] * grad_gain_sum).reshape(-1), local_sq[None]])
    tail = over_all(tail + 0.0 * token(g_inner[0][0], parts_arrived[-2])[0])
    grad_gain = tail[:model]
    grad_norm = jnp.sqrt(tail[model] + jnp.sum(grad_gain * grad_gain))
    clip_scale = CLIP_LIMIT / jnp.maximum(grad_norm, CLIP_LIMIT)

    grad_out = jnp.concatenate(crossed(g_out[0], flag[0]), -1).astype(f32)
    in_pieces = (*g_inner[0], *g_gate[0])
    small_back = lax.all_gather(send(g_small.astype(bf16), small_pairs, True), "p")
    small_back = small_back.reshape(chans, 2, -1, own).transpose(2, 1, 0, 3)
    small_back = small_back.reshape(-1, chan_width).astype(f32)
    grad_x = small_back[: 3 * x_width].reshape(3, x_width, chan_width)
    grad_dt = small_back[3 * x_width : 3 * x_width + 3 * rank].reshape(3, rank, chan_width)
    grad_dt = lax.dynamic_slice_in_dim(grad_dt, s_at * dt_rows, dt_rows, 1)
    grad_chan = small_back[3 * x_width + 3 * rank :]

    tok_float = tokens_in.astype(f32)
    mixed = (tok_float + jnp.concatenate(outs, 0)).astype(bf16)
    d_own = jnp.concatenate(rows_back, 0)
    x_hat_own = tok_float * inv_own
    d_hat = d_own * gain_part
    mean = over_chans(jnp.sum(d_hat * x_hat_own, axis=-1))[..., None] / model
    input_grad = cotangent.astype(f32) + inv_own * (d_hat - x_hat_own * mean)

    dt_new, dt_first_new, dt_second_new = adam_update(
        dt_weight, grad_dt, dt_first, dt_second, clip_scale, rank ** (-0.5)
    )
    out_new, out_first_new, out_second_new = adam_update(
        out_weight, grad_out, out_first, out_second, clip_scale, inner_all ** (-0.5)
    )
    x_new, x_first_new, x_second_new = adam_update(
        x_weight, grad_x, x_first, x_second, clip_scale, inner_all ** (-0.5)
    )
    chan_new, chan_first_new, chan_second_new = adam_update(
        channel_params, grad_chan, channel_first, channel_second, clip_scale, 0.5
    )
    gain_new, gain_first_new, gain_second_new = adam_update(
        gain, grad_gain, gain_first, gain_second, clip_scale, 0.5
    )
    grad_in, in_new, in_first_new, in_second_new = adam(
        after(flag, x_new, chan_new, dt_new), clip_scale[None], in_weight, in_first, in_second, in_pieces, model ** (-0.5)
    )
    return (
        mixed, input_grad, grad_norm,
        grad_in, in_new, in_first_new, in_second_new,
        grad_dt, dt_new, dt_first_new, dt_second_new,
        grad_out, out_new, out_first_new, out_second_new,
        grad_x, x_new, x_first_new, x_second_new,
        grad_chan, chan_new, chan_first_new, chan_second_new,
        grad_gain, gain_new, gain_first_new, gain_second_new,
        in_new.astype(bf16), dt_new.astype(bf16), out_new.astype(bf16), x_new.astype(bf16),
    )


def solution(mesh):
    chans = mesh.shape["ch"]
    parts = 2 * chans
    groups = mesh.shape["seq"] // parts
    inside = Mesh(mesh.devices.reshape(groups, parts, chans), ("t", "p", "c"))
    seq = ("t", "p")
    tok = P(None, seq, "c")
    wide = P(None, seq, None, "c")
    rows = P(None, seq, "c")
    flat = P(None, None, "c")
    chan = P(None, "c")
    return jax.shard_map(
        functools.partial(body, groups, parts, chans),
        mesh=inside,
        in_specs=(tok, P(None, seq), P(), tok)
        + (wide,) * 3 + (rows,) * 3 + (rows,) * 3 + (flat,) * 3 + (chan,) * 3 + (P(),) * 3,
        out_specs=(tok, tok, P())
        + (wide,) * 4 + (rows,) * 4 + (rows,) * 4 + (flat,) * 4 + (chan,) * 4 + (P(),) * 4
        + (wide, rows, rows, flat),
        check_vma=False,
    )
```

```python
import functools

import jax
import jax.numpy as jnp
from jax import lax
from jax.experimental import pallas as pl
from jax.experimental.pallas import tpu as pltpu
from jax.sharding import Mesh
from jax.sharding import PartitionSpec as P

N = 16
K = 4
STEP = 10

NORM_EPS = 1e-05
BETA_ONE = 0.9
BETA_TWO = 0.95
ADAM_EPS = 1e-08
DECAY = 0.1
CLIP_LIMIT = 1.0
LANES = 128
SCAN_ROWS = 128
MEGA = 1024 * 1024
GROUP = 2
f32 = jnp.float32
bf16 = jnp.bfloat16


def silu_grad(value):
    sigma = jax.nn.sigmoid(value)
    return sigma * (1.0 + value * (1.0 - sigma))


def adam_update(weight, gradient, first_moment, second, clip_scale, step_rate):
    clipped = gradient * clip_scale
    first_new = BETA_ONE * first_moment + (1.0 - BETA_ONE) * clipped
    second_new = BETA_TWO * second + (1.0 - BETA_TWO) * clipped * clipped
    first_hat = first_new * (1.0 / (1.0 - BETA_ONE**STEP))
    second_hat = second_new * (1.0 / (1.0 - BETA_TWO**STEP))
    weight_new = weight - step_rate * (
        first_hat / (jnp.sqrt(second_hat) + ADAM_EPS) + DECAY * weight
    )
    return (weight_new, first_new, second_new)


def sum_rows(parts):
    at = lax.broadcasted_iota(jnp.int32, parts[0].shape, 0)
    for distance in (1, 2, 4):
        low = at % (2 * distance) < distance
        parts = [
            jnp.where(low, a, b) + pltpu.roll(jnp.where(low, b, a), distance, 0)
            for a, b in zip(parts[0::2], parts[1::2])
        ]
    return parts[0]


def lane_rules():
    lanes = jnp.arange(LANES)
    used = lanes % (LANES // 2) < 3 * N
    mask = ((lanes[None, :] % N == jnp.arange(N)[:, None]) & used[None, :]).astype(f32)
    side = (lanes[:, None] // (LANES // 2) == jnp.arange(2 * LANES)[None, :] // LANES).astype(bf16)
    return mask, side


def matmul(left, right):
    return jnp.dot(left, right, preferred_element_type=f32)


def spread(rows_ref, m, base, mask, side):
    left = [rows_ref[m, pl.ds(base + j, 1), :] * mask for j in range(8)]
    return matmul(jnp.concatenate(left, 0).astype(bf16), side)


def lane_sums(product_ref, m, grads, lane, base, ones):
    sums = matmul(product_ref[m], ones)
    for j in range(8):
        grads = jnp.where(lane == base + j, sums[N * j : N * j + N], grads)
    return grads


def turned(ref, turn, x_at):
    width = ref.shape[-1] // 2
    return pl.ds(pl.multiple_of((turn ^ x_at) * width, width), width)


def three(tile, info):
    return jnp.concatenate([(tile * info[:, k + 1 : k + 2]).astype(bf16) for k in range(3)], -1)


def across(left, right, dims):
    return lax.dot_general(left, right, ((dims[0:1], dims[1:2]), ((), ())), preferred_element_type=f32)


def stacked(ref):
    kinds, rows, cols = ref.shape
    return ref[...].reshape(kinds * rows, cols)


def split_blocks(total, place_ref, sent_ref, keep_ref, scratch_ref, offset):
    scratch_ref[...] = total
    core = place_ref[1]
    for x in range(2):
        away = pl.ds(pl.multiple_of((2 * x + 1 - core) * LANES, LANES), LANES)
        here = pl.ds(pl.multiple_of((2 * x + core) * LANES, LANES), LANES)
        sent_ref[x, :, offset : offset + LANES] = scratch_ref[:, away].astype(bf16)
        keep_ref[x, :, offset : offset + LANES] = scratch_ref[:, here]


def tile_rows(ref):
    return ref[...].reshape(-1, ref.shape[-1])


def wide_product(tile_ref, info, w_refs, scratch_ref, x_at):
    total = None
    for turn, w_ref in enumerate(w_refs):
        left = three(tile_ref[:, turned(tile_ref, turn, x_at)], info)
        part = across(left, stacked(w_ref), (1, 0))
        total = part if total is None else total + part
    return total


def inner_kernel(place_ref, x_ref, info_ref, gain_ref, w0_ref, w1_ref,
                 normed_ref, sent_ref, keep_ref, tile_ref, scratch_ref):
    info = info_ref[...].T
    normed = tile_rows(x_ref).astype(f32) * info[:, :1] * gain_ref[...]
    normed = normed.astype(bf16)
    normed_ref[...] = normed
    tile_ref[...] = normed.astype(f32)
    total = wide_product(tile_ref, info, (w0_ref, w1_ref), scratch_ref, place_ref[0])
    split_blocks(total, place_ref, sent_ref, keep_ref, scratch_ref, 0)


def gate_kernel(place_ref, normed_ref, back_ref, info_ref, g0_ref, g1_ref, o0_ref, o1_ref,
                sent_ref, keep_ref, tile_ref, scratch_ref):
    info = info_ref[...].T
    tile_ref[...] = normed_ref[...].astype(f32)
    total = wide_product(tile_ref, info, (g0_ref, g1_ref), scratch_ref, place_ref[0])
    split_blocks(total, place_ref, sent_ref, keep_ref, scratch_ref, 0)
    tile_ref[...] = tile_rows(back_ref).astype(f32)
    total = wide_product(tile_ref, info, (o0_ref, o1_ref), scratch_ref, place_ref[0])
    split_blocks(total, place_ref, sent_ref, keep_ref, scratch_ref, LANES)


def gathered(scratch_ref, place_ref, refs):
    at = 2 * place_ref[0] + place_ref[1]
    for distance, ref in zip((0, 2, 1, 3), refs):
        lanes = pl.ds(pl.multiple_of((at ^ distance) * LANES, LANES), LANES)
        scratch_ref[:, lanes] = tile_of(ref).astype(f32)


def tile_of(ref):
    return ref[...].reshape(-1, ref.shape[-1])


def split_parts(total, place_ref, sent_ref, keep_ref):
    y = place_ref[2]
    half = total.shape[0] // 2
    low, high = total[:half], total[half:]
    mine = jnp.full(low.shape, y, jnp.int32) == 0
    sent_ref[...] = jnp.where(mine, high, low).astype(bf16).reshape(sent_ref.shape)
    keep_ref[...] = jnp.where(mine, low, high).reshape(keep_ref.shape)


def out_kernel(place_ref, a_ref, b_ref, c_ref, d_ref, info_ref, w0_ref, w1_ref,
               sent_ref, keep_ref, tile_ref, total_ref):
    gathered(tile_ref, place_ref, (a_ref, b_ref, c_ref, d_ref))
    left = three(tile_ref[...], info_ref[...].T)
    width = tile_ref.shape[1]
    for turn, w_ref in enumerate((w0_ref, w1_ref)):
        total = None
        for k in range(3):
            part = across(left[:, k * width : (k + 1) * width], w_ref[k], (1, 1))
            total = part if total is None else total + part
        total_ref[:, turned(total_ref, turn, place_ref[0])] = total
    split_parts(total_ref[...], place_ref, sent_ref, keep_ref)


def normed_kernel(place_ref, ga_ref, gb_ref, gc_ref, gd_ref, ia_ref, ib_ref, ic_ref, id_ref,
                  info_ref, x_ref, g0_ref, g1_ref, i0_ref, i1_ref,
                  sent_ref, keep_ref, gain_ref, tile_ref, total_ref):
    info = info_ref[...].T
    width = tile_ref.shape[1]
    gathered(tile_ref, place_ref, (ga_ref, gb_ref, gc_ref, gd_ref))
    gates = three(tile_ref[...], info)
    gathered(tile_ref, place_ref, (ia_ref, ib_ref, ic_ref, id_ref))
    inners = three(tile_ref[...], info)
    for turn, (g_ref, i_ref) in enumerate(((g0_ref, i0_ref), (g1_ref, i1_ref))):
        total = None
        for k in range(3):
            lanes = slice(k * width, (k + 1) * width)
            part = across(gates[:, lanes], g_ref[k], (1, 1)) + across(inners[:, lanes], i_ref[k], (1, 1))
            total = part if total is None else total + part
        total_ref[:, turned(total_ref, turn, place_ref[0])] = total
    total = total_ref[...]
    split_parts(total, place_ref, sent_ref, keep_ref)

    @pl.when((pl.program_id(0) == 0) & (pl.program_id(1) == 0))
    def _():
        gain_ref[...] = jnp.zeros_like(gain_ref)

    x_hat = tile_rows(x_ref).astype(f32) * info[:, :1]
    gain_ref[...] += jnp.sum((total * x_hat).reshape(-1, 8, total.shape[1]), axis=0)


def weight_grad_kernel(chunks, steps, place_ref, *refs):
    ins, (out0_ref, out1_ref, square_ref, tile_ref, sum_ref) = refs[: 6 * chunks], refs[6 * chunks :]
    at = pl.program_id(0)

    @pl.when(at == 0)
    def _():
        sum_ref[...] = jnp.zeros_like(sum_ref)

    for chunk in range(chunks):
        info_ref, left_ref, *blocks = ins[6 * chunk : 6 * chunk + 6]

        @pl.when((at >= chunk * steps) & (at < (chunk + 1) * steps))
        def _(info_ref=info_ref, left_ref=left_ref, blocks=blocks):
            gathered(tile_ref, place_ref, blocks)
            right = three(tile_ref[...], info_ref[...].T)
            left = left_ref[...].reshape(-1, left_ref.shape[-1])
            sum_ref[...] += across(left, right, (0, 0))

    @pl.when(at == chunks * steps - 1)
    def _():
        half = sum_ref.shape[0] // 2
        width = tile_ref.shape[1]
        for turn, out_ref in enumerate((out0_ref, out1_ref)):
            rows = pl.ds(pl.multiple_of((turn ^ place_ref[3]) * half, half), half)
            for k in range(3):
                out_ref[k] = sum_ref[rows, k * width : (k + 1) * width].astype(out_ref.dtype)
        total = sum_ref[...]
        square_ref[...] = jnp.sum((total * total).reshape(-1, 8, total.shape[1]), axis=0)


SCALARS = pl.BlockSpec(memory_space=pltpu.SMEM)


def whole(array):
    return pl.BlockSpec(array.shape, lambda *at: (0,) * array.ndim)


def plane(array, which):
    kinds, rows, lanes = array.shape
    return pl.BlockSpec((kinds, rows, lanes // 2), lambda *at: (0, 0, which))


def shape_of(shape, dtype):
    return jax.ShapeDtypeStruct(shape, dtype)


def call(kernel, name, grid, in_specs, out_specs, out_shape, scratch, flops, moved, args):
    return pl.pallas_call(
        kernel,
        grid=grid,
        in_specs=in_specs,
        out_specs=out_specs,
        out_shape=out_shape,
        scratch_shapes=scratch,
        cost_estimate=pl.CostEstimate(flops=flops, bytes_accessed=moved, transcendentals=0),
        compiler_params=pltpu.CompilerParams(
            dimension_semantics=("arbitrary",) * len(grid), vmem_limit_bytes=48 * MEGA
        ),
        name=name,
    )(*args)


class Tiles:
    def __init__(self, micros, parts, rows, first=0):
        self.micros, self.pairs, self.rows, self.first = micros, parts // 2, rows, first
        self.grid = (micros, self.pairs)
        self.tile = 2 * rows

    def raw(self, width):
        return pl.BlockSpec((2, 1, self.rows, width), lambda m, z: (z, self.first + m, 0, 0))

    def flat(self, width):
        return pl.BlockSpec((self.tile, width), lambda m, z: ((self.first + m) * self.pairs + z, 0))

    def info(self):
        return pl.BlockSpec((8, self.tile), lambda m, z: (0, (self.first + m) * self.pairs + z))

    def kindred(self, which, width):
        return pl.BlockSpec((1, self.tile, width), lambda m, z: (which, m * self.pairs + z, 0))

    def blocks(self, width):
        return pl.BlockSpec((2, self.tile, width), lambda m, z: (0, m * self.pairs + z, 0))

    def parted(self, width):
        return pl.BlockSpec((1, 1, self.rows, width), lambda m, z: (m, z, 0, 0))


def inner_product(tiles, place, tokens, info, gain, w_in):
    width = tokens.shape[-1]
    chans = w_in[0].shape[-1] // 2
    rows = tiles.micros * tiles.pairs * tiles.tile
    return call(
        inner_kernel, "inner_product", tiles.grid,
        [SCALARS, tiles.raw(width), tiles.info(), whole(gain), plane(w_in[0], 0), plane(w_in[1], 0)],
        [tiles.flat(width), tiles.blocks(LANES), tiles.blocks(LANES)],
        [shape_of((rows, width), bf16), shape_of((2, rows, LANES), bf16), shape_of((2, rows, LANES), f32)],
        [pltpu.VMEM((tiles.tile, width), f32), pltpu.VMEM((tiles.tile, chans), f32)],
        6 * rows * width * chans, 8 * MEGA,
        (place, tokens, info, gain, *w_in),
    )


def gate_product(tiles, place, normed, back, info, w_in, w_out):
    width = normed.shape[-1]
    chans = w_out[0].shape[-1]
    rows = normed.shape[0]
    return call(
        gate_kernel, "gate_product", tiles.grid,
        [SCALARS, tiles.flat(width), tiles.raw(width), tiles.info()]
        + [plane(w, 1) for w in w_in] + [whole(w) for w in w_out],
        [tiles.blocks(2 * LANES), tiles.blocks(2 * LANES)],
        [shape_of((2, rows, 2 * LANES), bf16), shape_of((2, rows, 2 * LANES), f32)],
        [pltpu.VMEM((tiles.tile, width), f32), pltpu.VMEM((tiles.tile, chans), f32)],
        12 * rows * width * chans, 16 * MEGA,
        (place, normed, back, info, *w_in, *w_out),
    )


def out_product(tiles, place, pairs, info, w_out):
    width = 2 * w_out[0].shape[1]
    chans = w_out[0].shape[-1]
    rows = pairs[0].shape[1]
    parted = (tiles.micros, tiles.pairs, tiles.rows, width)
    return call(
        out_kernel, "out_product", tiles.grid,
        [SCALARS] + [tiles.kindred(0, LANES)] * 4 + [tiles.info(), whole(w_out[0]), whole(w_out[1])],
        [tiles.parted(width), tiles.parted(width)],
        [shape_of(parted, bf16), shape_of(parted, f32)],
        [pltpu.VMEM((tiles.tile, chans), f32), pltpu.VMEM((tiles.tile, width), f32)],
        6 * rows * width * chans, 8 * MEGA,
        (place, *pairs, info, *w_out),
    )


def normed_grad(tiles, place, pairs, inners, info, tokens, w_in):
    width = 2 * w_in[0].shape[1]
    chans = w_in[0].shape[-1] // 2
    rows = pairs[0].shape[1]
    parted = (tiles.micros, tiles.pairs, tiles.rows, width)
    return call(
        normed_kernel, "normed_grad", tiles.grid,
        [SCALARS] + [tiles.kindred(1, LANES)] * 4 + [tiles.flat(LANES)] * 4
        + [tiles.info(), tiles.raw(width)] + [plane(w, which) for which in (1, 0) for w in w_in],
        [tiles.parted(width), tiles.parted(width), pl.BlockSpec((8, width), lambda m, z: (0, 0))],
        [shape_of(parted, bf16), shape_of(parted, f32), shape_of((8, width), f32)],
        [pltpu.VMEM((tiles.tile, chans), f32), pltpu.VMEM((tiles.tile, width), f32)],
        12 * rows * width * chans, 16 * MEGA,
        (place, *pairs, *inners, info, tokens, *w_in, *w_in),
    )


def weight_grad(place, info, lefts, left_at, rights, right_at, span, dtype):
    chunks = len(lefts)
    width = lefts[0].shape[-1]
    chans = 4 * LANES
    steps = info.shape[1] // span // chunks
    info_at = ((8, span), lambda m, chunk: (0, chunk * steps + m))
    piece = (3, width // 2, chans)
    specs, args = [], []
    for chunk in range(chunks):
        def held(spec, chunk=chunk):
            shape, at = spec
            low = chunk * steps
            return pl.BlockSpec(shape, lambda i: at(jnp.clip(i - low, 0, steps - 1), chunk))

        specs += [held(info_at), held(left_at)] + [held(right_at)] * 4
        args += [info, lefts[chunk], *rights[chunk]]
    return call(
        functools.partial(weight_grad_kernel, chunks, steps), "weight_grad", (chunks * steps,),
        [SCALARS] + specs,
        [pl.BlockSpec(piece, lambda i: (0, 0, 0))] * 2 + [pl.BlockSpec((8, 3 * chans), lambda i: (0, 0))],
        [shape_of(piece, dtype), shape_of(piece, dtype), shape_of((8, 3 * chans), f32)],
        [pltpu.VMEM((span, chans), f32), pltpu.VMEM((width, 3 * chans), f32)],
        6 * chunks * steps * span * width * chans, 24 * MEGA,
        (place, *args),
    )


def masked_sum(wide, info):
    width = wide.shape[1] // 3
    return sum(wide[:, k * width : (k + 1) * width] * info[:, k + 1 : k + 2] for k in range(3))


def one_of_four(place_ref, x, core, own_ref, x_ref, core_ref, both_ref):
    shape = own_ref.shape
    same_x = jnp.full(shape, place_ref[0] ^ x, jnp.int32) == 0
    same_core = jnp.full(shape, place_ref[1] ^ core, jnp.int32) == 0
    own, across_x, across_core, both = (
        ref[...].astype(f32) for ref in (own_ref, x_ref, core_ref, both_ref)
    )
    return jnp.where(same_core, jnp.where(same_x, own, across_x), jnp.where(same_x, across_core, both))


def wide_scratch(micros):
    return pltpu.VMEM((micros, 8 * N, 2 * LANES), f32)


def product_scratch(micros):
    return pltpu.VMEM((micros, 8 * N, LANES), bf16)


def state_scratch(micros):
    return pltpu.VMEM((micros, N, LANES), f32)


def tile_scratch(micros):
    return pltpu.VMEM((micros, SCAN_ROWS, LANES), f32)


def mix_forward_kernel(
    x, place_ref, keep_ref, own_ref, x_ref, core_ref, both_ref, act_ref, info_ref,
    dt_ref, mask_ref, side_ref, rate_ref, bias_ref, start_ref,
    y_ref, before_ref, step_ref, slope_ref, rows_ref, low_ref, final_ref,
    state_ref, wide_a, wide_b, drive_ref,
):
    micros, rows, _ = step_ref.shape
    block = pl.program_id(0)
    rank = low_ref.shape[1]
    rate = rate_ref[...]
    mask = mask_ref[...]
    side = side_ref[...]
    dt_bias = bias_ref[0:1]

    @pl.when(block == 0)
    def _():
        state_ref[...] = start_ref[...]

    for m in range(micros):
        shared = one_of_four(place_ref, x, m, own_ref, x_ref, core_ref, both_ref)
        low = shared[:rank].astype(bf16)
        low_ref[m] = low
        dt_pre = masked_sum(across(low, dt_ref[...], (0, 0)), info_ref[m].T) + dt_bias
        small = jnp.exp(-jnp.abs(dt_pre))
        step = jnp.maximum(dt_pre, 0.0) + jnp.log1p(small)
        step_ref[m] = step
        slope_ref[m] = jnp.where(dt_pre >= 0, 1.0, small) / (1.0 + small)
        drive_ref[m] = step * act_ref[m].astype(f32)
        parts = []
        for left in (shared[rank : rank + N], shared[rank + N :]):
            for _ in range(3):
                part = left.astype(bf16).astype(f32)
                parts.append(part)
                left = left - part
            parts.append(jnp.zeros_like(left))
        rows_ref[m] = jnp.concatenate(parts, 0).T
        wide_a[m] = spread(rows_ref, m, 0, mask, side)

    def sixteen(turn, states):
        states = list(states)
        for half in range(2):
            base = pl.multiple_of(turn * 16 + 8 * half, 8)
            wide, wide_next = (wide_a, wide_b) if half == 0 else (wide_b, wide_a)
            following = jnp.minimum(base + 8, rows - 8)
            for m in range(micros):
                wide_next[m] = spread(rows_ref, m, following, mask, side)
            y_parts = [[] for _ in range(micros)]
            for j in range(8):
                for m in range(micros):
                    row = pl.ds(base + j, 1)
                    own = slice(N * j, N * j + N)
                    before = states[m]
                    before_ref[m, base + j] = before
                    before = before * keep_ref[micros * x + m, block * rows + base + j]
                    state = (
                        jnp.exp(step_ref[m, row, :] * rate) * before
                        + drive_ref[m, row, :] * wide[m, own, :LANES]
                    )
                    states[m] = state
                    shown = state * wide[m, own, LANES:]
                    y_parts[m].append(shown[:8] + shown[8:])
            for m in range(micros):
                y_ref[m, pl.ds(base, 8), :] = sum_rows(y_parts[m])
        return tuple(states)

    states = lax.fori_loop(
        0, rows // 16, sixteen, tuple(state_ref[m] for m in range(micros))
    )
    for m in range(micros):
        state_ref[m] = states[m]
        final_ref[m] = states[m]


def blend_kernel(y_ref, act_ref, pair_ref, bias_ref, kinds_ref, pull_ref):
    skip = bias_ref[1:2]
    gate, d_mixed = pair_ref[0, :, :LANES], pair_ref[0, :, LANES:]
    sigma = jax.nn.sigmoid(gate)
    y_scan = y_ref[0] + skip * act_ref[0].astype(f32)
    opened = gate * sigma
    kinds_ref[0, 0] = (y_scan * opened).astype(bf16)
    kinds_ref[1, 0] = (d_mixed * y_scan * (sigma * (1.0 + gate * (1.0 - sigma)))).astype(bf16)
    pull_ref[0] = d_mixed * opened


def blend(x, y, act, pair, bias):
    micros, rows, _ = y.shape
    first = micros * x
    one = pl.BlockSpec((1, rows, LANES), lambda m: (m, 0, 0))
    return call(
        blend_kernel, "blend", (micros,),
        [
            one, pl.BlockSpec((1, rows, LANES), lambda m: (first + m, 0, 0)),
            pl.BlockSpec((1, rows, 2 * LANES), lambda m: (first + m, 0, 0)), const(bias.shape),
        ],
        [pl.BlockSpec((2, 1, rows, LANES), lambda m: (0, m, 0, 0)), one],
        [shape_of((2,) + y.shape, bf16), shape_of(y.shape, f32)],
        [], 20 * y.size, 20 * y.size, (y, act, pair, bias),
    )


def time_specs(micros, at, x):
    return dict(
        tall=pl.BlockSpec((micros, SCAN_ROWS, LANES), lambda i: (0, at(i), 0)),
        act=pl.BlockSpec((micros, SCAN_ROWS, LANES), lambda i: (x, at(i), 0)),
        turned=pl.BlockSpec((micros, LANES, SCAN_ROWS), lambda i: (0, 0, at(i))),
        states=pl.BlockSpec((micros, SCAN_ROWS, N, LANES), lambda i: (0, at(i), 0, 0)),
        info=pl.BlockSpec((micros, 8, SCAN_ROWS), lambda i: (x, 0, at(i))),
        fixed=pl.BlockSpec((micros, N, LANES), lambda i: (0, 0, 0)),
    )


def const(shape):
    return pl.BlockSpec(shape, lambda *at: (0,) * len(shape))


def mix_forward(place, x, keep, quarters, act, info, dt, rules, rate, bias, start):
    length = act.shape[1]
    micros = start.shape[0]
    blocks = length // SCAN_ROWS
    spec = time_specs(micros, lambda i: i, x)
    width = quarters[0].shape[0]
    quarter = pl.BlockSpec((width, SCAN_ROWS), lambda i: (0, i))
    tall = jax.ShapeDtypeStruct((micros, length, LANES), f32)
    return pl.pallas_call(
        functools.partial(mix_forward_kernel, x),
        grid=(blocks,),
        in_specs=[
            SCALARS, SCALARS, *[quarter] * 4, spec["act"], spec["info"],
            const(dt.shape), const(rules[0].shape), const(rules[1].shape),
            const(rate.shape), const(bias.shape), spec["fixed"],
        ],
        out_specs=[spec["tall"], spec["states"], *[spec["tall"]] * 3, spec["turned"], spec["fixed"]],
        out_shape=[
            tall, jax.ShapeDtypeStruct((micros, length, N, LANES), f32), tall, tall, tall,
            jax.ShapeDtypeStruct((micros, width - 2 * N, length), bf16),
            jax.ShapeDtypeStruct((micros, N, LANES), f32),
        ],
        scratch_shapes=[
            state_scratch(micros), wide_scratch(micros), wide_scratch(micros), tile_scratch(micros)
        ],
        cost_estimate=pl.CostEstimate(
            flops=micros * length * N * LANES * 40,
            bytes_accessed=micros * length * N * LANES * 12,
            transcendentals=micros * length * N * LANES,
        ),
        compiler_params=pltpu.CompilerParams(
            dimension_semantics=("arbitrary",), vmem_limit_bytes=40 * MEGA
        ),
        name="mix_forward",
    )(place, keep, *quarters, act, info, dt, *rules, rate, bias, start)


def mix_backward_kernel(
    x, place_ref, keep_ref, act_ref, info_ref, dt_ref, mask_ref, side_ref, rate_ref, bias_ref, start_ref,
    before_ref, step_ref, slope_ref, rows_ref, low_ref, last_ref, pull_ref,
    shared_ref, d_act_ref, grad_dt_ref, sums_ref, grad_rate_ref, final_ref,
    state_ref, after_ref, wide_a, wide_b, product_a, product_b, shown_a, shown_b,
    drive_ref, b_pull_ref, rate_pull_ref,
):
    micros, rows, _ = step_ref.shape
    block = pl.num_programs(0) - 1 - pl.program_id(0)
    rank = low_ref.shape[1]
    rate = rate_ref[...]
    mask = mask_ref[...]
    side = side_ref[...]
    skip = bias_ref[1:2]
    ones = jnp.ones((LANES, LANES), bf16)
    lane = lax.broadcasted_iota(jnp.int32, (N, LANES), 1)

    @pl.when(pl.program_id(0) == 0)
    def _():
        state_ref[...] = start_ref[...]
        after_ref[...] = last_ref[...]
        grad_rate_ref[...] = jnp.zeros_like(grad_rate_ref)
        grad_dt_ref[...] = jnp.zeros_like(grad_dt_ref)
        sums_ref[...] = jnp.zeros_like(sums_ref)

    for m in range(micros):
        drive_ref[m] = step_ref[m] * act_ref[m].astype(f32)
        wide_a[m] = spread(rows_ref, m, rows - 8, mask, side)

    def sixteen(turn, carried):
        states, afters, grads, grads_c, rates = (list(part) for part in carried)
        for half in range(2):
            base = pl.multiple_of(rows - 8 - turn * 16 - 8 * half, 8)
            wide, wide_next = (wide_a, wide_b) if half == 0 else (wide_b, wide_a)
            product, product_last = (product_a, product_b) if half == 0 else (product_b, product_a)
            seen, seen_last = (shown_a, shown_b) if half == 0 else (shown_b, shown_a)
            following = jnp.maximum(base - 8, 0)
            for m in range(micros):
                wide_next[m] = spread(rows_ref, m, following, mask, side)
                grads[m] = lane_sums(product_last, m, grads[m], lane, base + 8, ones)
                grads_c[m] = lane_sums(seen_last, m, grads_c[m], lane, base + 8, ones)
            b_parts = [[None] * 8 for _ in range(micros)]
            rate_parts = [[None] * 8 for _ in range(micros)]
            for j in range(7, -1, -1):
                for m in range(micros):
                    row = pl.ds(base + j, 1)
                    own = slice(N * j, N * j + N)
                    step = step_ref[m, row, :]
                    pull = pull_ref[m, row, :]
                    adjoint = wide[m, own, LANES:] * pull + states[m]
                    passed = jnp.exp(step * rate) * (
                        adjoint * keep_ref[micros * x + m, block * rows + base + j]
                    )
                    states[m] = passed
                    before = before_ref[m, base + j]
                    seen[m, own, :] = (afters[m] * pull).astype(bf16)
                    afters[m] = before
                    decay_pull = passed * before
                    shown = adjoint * wide[m, own, :LANES]
                    b_parts[m][j] = shown[:8] + shown[8:]
                    shown = decay_pull * rate
                    rate_parts[m][j] = shown[:8] + shown[8:]
                    rates[m] = rates[m] + decay_pull * step
                    product[m, own, :] = (adjoint * drive_ref[m, row, :]).astype(bf16)
            for m in range(micros):
                b_pull_ref[m, pl.ds(base, 8), :] = sum_rows(b_parts[m])
                rate_pull_ref[m, pl.ds(base, 8), :] = sum_rows(rate_parts[m])
        return tuple(tuple(part) for part in (states, afters, grads, grads_c, rates))

    zeros = tuple(jnp.zeros((N, LANES), f32) for m in range(micros))
    begin = (
        tuple(state_ref[m] for m in range(micros)),
        tuple(after_ref[m] for m in range(micros)),
        zeros, zeros, zeros,
    )
    states, afters, grads, grads_c, rates = lax.fori_loop(0, rows // 16, sixteen, begin)
    for m in range(micros):
        state_ref[m] = states[m]
        after_ref[m] = afters[m]
        grad_rate_ref[...] += rates[m]
        final_ref[m] = states[m]
        act = act_ref[m].astype(f32)
        pull = pull_ref[m]
        b_pull = b_pull_ref[m]
        d_act_ref[m] = pull * skip + step_ref[m] * b_pull
        d_pre = ((rate_pull_ref[m] + act * b_pull) * slope_ref[m]).astype(bf16).astype(f32)
        sums_ref[0:8] += jnp.sum(d_pre.reshape(-1, 8, LANES), axis=0)
        sums_ref[8:16] += jnp.sum((pull * act).reshape(-1, 8, LANES), axis=0)
        d_pre3 = three(d_pre, info_ref[m].T)
        shared_ref[m, :rank] = across(dt_ref[...], d_pre3, (1, 1))
        shared_ref[m, rank : rank + N] = lane_sums(product_b, m, grads[m], lane, 0, ones)
        shared_ref[m, rank + N :] = lane_sums(shown_b, m, grads_c[m], lane, 0, ones)
        grad_dt_ref[...] += across(low_ref[m], d_pre3, (1, 0))


def mix_backward(place, x, keep, act, info, dt, rules, rate, bias, start, saved):
    before, step, slope, rows, low, last, pull = saved
    length = act.shape[1]
    micros = start.shape[0]
    blocks = length // SCAN_ROWS
    spec = time_specs(micros, lambda i: blocks - 1 - i, x)
    rank = low.shape[1]
    width = rank + 2 * N
    product, tile = product_scratch(micros), tile_scratch(micros)
    return pl.pallas_call(
        functools.partial(mix_backward_kernel, x),
        grid=(blocks,),
        in_specs=[
            SCALARS, SCALARS, spec["act"], spec["info"],
            const(dt.shape), const(rules[0].shape), const(rules[1].shape),
            const(rate.shape), const(bias.shape), spec["fixed"],
            spec["states"], *[spec["tall"]] * 3, spec["turned"], spec["fixed"], spec["tall"],
        ],
        out_specs=[
            pl.BlockSpec((micros, width, SCAN_ROWS), lambda i: (0, 0, blocks - 1 - i)),
            spec["tall"], const(dt.shape), const((16, LANES)), const((N, LANES)), spec["fixed"],
        ],
        out_shape=[
            jax.ShapeDtypeStruct((micros, width, length), f32),
            jax.ShapeDtypeStruct((micros, length, LANES), f32),
            jax.ShapeDtypeStruct(dt.shape, f32),
            jax.ShapeDtypeStruct((16, LANES), f32),
            jax.ShapeDtypeStruct((N, LANES), f32),
            jax.ShapeDtypeStruct((micros, N, LANES), f32),
        ],
        scratch_shapes=[
            state_scratch(micros), state_scratch(micros), wide_scratch(micros), wide_scratch(micros),
            product, product, product, product, tile, tile, tile,
        ],
        cost_estimate=pl.CostEstimate(
            flops=micros * length * N * LANES * 60,
            bytes_accessed=micros * length * N * LANES * 12,
            transcendentals=micros * length * N * LANES,
        ),
        compiler_params=pltpu.CompilerParams(
            dimension_semantics=("arbitrary",), vmem_limit_bytes=40 * MEGA
        ),
        name="mix_backward",
    )(place, keep, act, info, dt, *rules, rate, bias, start, *saved)


def shifted(scratch_ref, j, rows):
    return scratch_ref[8 - j : 8 - j + rows, :]


def conv_forward_kernel(inner_ref, edge_ref, info_ref, taps_ref, wx_ref,
                        act_ref, conv_ref, shared_ref, scratch_ref):
    rows = inner_ref.shape[1]
    scratch_ref[:8] = edge_ref[0]
    scratch_ref[8:] = inner_ref[0]
    info = info_ref[0].T
    total = taps_ref[K : K + 1] + taps_ref[0:1] * inner_ref[0]
    for j in range(1, K):
        total = total + taps_ref[j : j + 1] * (shifted(scratch_ref, j, rows) * info[:, 3 + j : 4 + j])
    conv_ref[0] = total
    act = (total * jax.nn.sigmoid(total)).astype(bf16)
    act_ref[0] = act
    shared_ref[0] = across(wx_ref[...], three(act.astype(f32), info), (1, 1))


def conv_forward(inner, edge, info, taps, wx):
    micros, rows, _ = inner.shape
    one = pl.BlockSpec((1, rows, LANES), lambda m: (m, 0, 0))
    width = wx.shape[0]
    return call(
        conv_forward_kernel, "conv_forward", (micros,),
        [
            one, pl.BlockSpec((1, 8, LANES), lambda m: (m, 0, 0)),
            pl.BlockSpec((1, 8, rows), lambda m: (m, 0, 0)), const(taps.shape), const(wx.shape),
        ],
        [one, one, pl.BlockSpec((1, width, rows), lambda m: (m, 0, 0))],
        [
            shape_of(inner.shape, bf16), shape_of(inner.shape, f32),
            shape_of((micros, width, rows), f32),
        ],
        [pltpu.VMEM((rows + 8, LANES), f32)],
        2 * micros * rows * wx.size, 4 * MEGA,
        (inner, edge, info, taps, wx),
    )


def conv_backward_kernel(x, place_ref, own_ref, x_ref, core_ref, both_ref, d_act_ref, conv_ref, inner_ref,
                         edge_ref, act_ref, info_ref, taps_ref, wx_ref,
                         d_inner_ref, grad_x_ref, sums_ref, head_ref, last_ref, scratch_ref, ahead_ref):
    rows = inner_ref.shape[1]
    micro = pl.program_id(0)
    info = info_ref[0].T

    @pl.when(micro == 0)
    def _():
        grad_x_ref[...] = jnp.zeros_like(grad_x_ref)
        sums_ref[...] = jnp.zeros_like(sums_ref)

    shared = one_of_four(place_ref, x, micro, own_ref, x_ref, core_ref, both_ref).astype(bf16)
    d_act = d_act_ref[0] + masked_sum(across(shared, wx_ref[...], (0, 0)), info)
    grad_x_ref[...] += across(shared, three(act_ref[0].astype(f32), info), (1, 0))
    conv = conv_ref[0]
    sigma = jax.nn.sigmoid(conv)
    d_conv = d_act * (sigma * (1.0 + conv * (1.0 - sigma)))
    head_ref[0] = d_conv[:8]
    scratch_ref[:8] = edge_ref[0]
    scratch_ref[8:] = inner_ref[0]
    ahead_ref[rows:] = jnp.zeros((8, LANES), f32)
    total = taps_ref[0:1] * d_conv
    sums_ref[0:8] += jnp.sum((d_conv * inner_ref[0]).reshape(-1, 8, LANES), axis=0)
    for j in range(1, K):
        masked = d_conv * info[:, 3 + j : 4 + j]
        pulled = (masked * shifted(scratch_ref, j, rows)).reshape(-1, 8, LANES)
        sums_ref[8 * j : 8 * j + 8] += jnp.sum(pulled, axis=0)
        ahead_ref[:rows] = masked
        total = total + taps_ref[j : j + 1] * ahead_ref[j : j + rows, :]
    sums_ref[8 * K : 8 * K + 8] += jnp.sum(d_conv.reshape(-1, 8, LANES), axis=0)
    d_inner_ref[0] = total.astype(bf16)
    last_ref[0] = total[rows - 8 :]


def conv_backward(place, x, quarters, d_act, conv, inner, edge, act, info, taps, wx):
    micros, rows, _ = d_act.shape
    first = micros * x
    mine = pl.BlockSpec((1, rows, LANES), lambda m: (m, 0, 0))
    one = pl.BlockSpec((1, rows, LANES), lambda m: (first + m, 0, 0))
    eight = pl.BlockSpec((1, 8, LANES), lambda m: (m, 0, 0))
    sums = (8 * (K + 1), LANES)
    return call(
        functools.partial(conv_backward_kernel, x), "conv_backward", (micros,),
        [
            SCALARS, *[const(quarters[0].shape)] * 4, mine, one, one,
            pl.BlockSpec((1, 8, LANES), lambda m: (first + m, 0, 0)), one,
            pl.BlockSpec((1, 8, rows), lambda m: (first + m, 0, 0)), const(taps.shape), const(wx.shape),
        ],
        [mine, const(wx.shape), const(sums), eight, eight],
        [
            shape_of(d_act.shape, bf16), shape_of(wx.shape, f32), shape_of(sums, f32),
            shape_of((micros, 8, LANES), f32), shape_of((micros, 8, LANES), f32),
        ],
        [pltpu.VMEM((rows + 8, LANES), f32), pltpu.VMEM((rows + 8, LANES), f32)],
        4 * micros * rows * wx.size, 6 * MEGA,
        (place, *quarters, d_act, conv, inner, edge, act, info, taps, wx),
    )


def pack_kernel(flag_ref, after_ref, w_ref, *out_refs):
    half = w_ref.shape[-1] // 2
    for turn, out_ref in enumerate(out_refs):
        lanes = pl.ds(pl.multiple_of((turn ^ flag_ref[0]) * half, half), half)
        if len(w_ref.shape) == 3:
            out_ref[0] = w_ref[0, :, lanes].astype(bf16)
            continue
        for side in range(2):
            out_ref[0, :, side * half : side * half + half] = w_ref[0, :, side, lanes].astype(bf16)


def pack(flag, after, weight):
    kinds, rows = weight.shape[:2]
    width = weight.size // (kinds * rows * 2)
    return call(
        pack_kernel, "pack", (kinds,),
        [SCALARS, SCALARS, pl.BlockSpec((1,) + weight.shape[1:], lambda k: (k,) + (0,) * (weight.ndim - 1))],
        [pl.BlockSpec((1, rows, width), lambda k: (k, 0, 0))] * 2,
        [shape_of((kinds, rows, width), bf16)] * 2,
        [], 0, weight.size * 6, (flag, after, weight),
    )


def adam_kernel(rate, flag_ref, clip_ref, w_ref, m_ref, v_ref, *refs):
    pieces, (grad_ref, new_ref, first_ref, second_ref) = refs[:4], refs[4:]
    half = w_ref.shape[-1] // 2
    clip = clip_ref[0]
    for plane in range(2):
        for turn in range(2):
            lanes = pl.ds(pl.multiple_of((turn ^ flag_ref[0]) * half, half), half)
            at = (0, slice(None), plane, lanes)
            grad = pieces[2 * plane + turn][0].astype(f32)
            new, first, second = adam_update(w_ref[at], grad, m_ref[at], v_ref[at], clip, rate)
            grad_ref[at] = grad
            new_ref[at] = new
            first_ref[at] = first
            second_ref[at] = second


def adam(flag, clip, weight, first, second, pieces, rate):
    kinds, rows, _, chans = weight.shape
    block = min(rows, 64)
    full = pl.BlockSpec((1, block, 2, chans), lambda k, r: (k, r, 0, 0))
    piece = pl.BlockSpec((1, block, chans // 2), lambda k, r: (k, r, 0))
    return call(
        functools.partial(adam_kernel, rate), "adam", (kinds, rows // block),
        [SCALARS, SCALARS, full, full, full] + [piece] * 4,
        [full] * 4,
        [shape_of(weight.shape, f32)] * 4,
        [], weight.size * 20, weight.size * 32,
        (flag, clip, weight, first, second, *pieces),
    )


def body(
    groups, parts, chans,
    tokens_in, modality, starts, cotangent,
    in_weight, in_first, in_second,
    dt_weight, dt_first, dt_second,
    out_weight, out_first, out_second,
    x_weight, x_first, x_second,
    channel_params, channel_first, channel_second,
    gain, gain_first, gain_second,
):
    micros, tok_rows, part_width = tokens_in.shape
    model = gain.shape[0]
    chan_width = in_weight.shape[3]
    half = chan_width // 2
    own = half // chans
    cores = chans // 2
    inner_all = chan_width * chans
    x_width = x_weight.shape[1]
    rank = x_width - 2 * N
    dt_rows = dt_weight.shape[1]
    span = parts * tok_rows
    edge = K - 1
    t_at = lax.axis_index("t")
    p_at = lax.axis_index("p")
    c_at = lax.axis_index("c")
    z_at, y_at = p_at // 2, p_at % 2
    x_at, core_at = c_at // cores, c_at % cores
    s_at = t_at * parts + p_at
    slice_at = s_at // (2 * groups)
    everywhere = ("t", "p", "c")
    place = jnp.stack([x_at, core_at, y_at, z_at % 2]).astype(jnp.int32)
    half_at = (s_at % (2 * groups)) // groups

    def flat(t, p, c):
        return (t * parts + p) * chans + c

    def part_of(c, j):
        return 2 * (2 * (c % cores) + j) + c // cores

    devices = [(t, p, c) for t in range(groups) for p in range(parts) for c in range(chans)]

    def first_hop(turn):
        pairs = []
        for t, p, c in devices:
            s = t * parts + p
            to_slice, i = s // (2 * groups), (s % (2 * groups)) // groups
            j = turn ^ (to_slice // cores)
            to = flat(s % groups, 2 * (2 * (c % cores) + j) + i, c // cores * cores + to_slice % cores)
            pairs.append((flat(t, p, c), to))
        return pairs

    def second_hop(turn):
        return [
            (flat(t, p, c), flat(t, p - p % 2 + c // cores, (turn ^ (p % 2)) * cores + c % cores))
            for t, p, c in devices
        ]

    def home(turn):
        pairs = []
        for t, p, c in devices:
            s = t * parts + p
            i = (s % (2 * groups)) // groups
            keeper = flat(s % groups, part_of(c, turn ^ i), s // (2 * groups))
            pairs.append((keeper, flat(t, p, c)))
        return pairs

    small_pairs = [(flat(t, p, c), flat(t, part_of(c, p % 2), p // 2)) for t, p, c in devices]

    def send(value, pairs, back=False):
        if back:
            pairs = [(b, a) for a, b in pairs]
        return lax.ppermute(value, everywhere, pairs)

    def swap(value, axis, distance):
        return lax.ppermute(value, axis, [(i, i ^ distance) for i in range(lax.axis_size(axis))])

    def crossed(pair, flag):
        first, second = pair
        return jnp.where(flag == 0, first, second), jnp.where(flag == 0, second, first)

    between = y_at ^ (z_at % 2)

    def token(*values):
        return sum(value[(0,) * value.ndim].astype(f32) for value in values)[None]

    def weights_there(pair):
        pair = [send(value, first_hop(turn)) for turn, value in enumerate(pair)]
        first = token(*pair)
        pair = crossed(pair, between)
        pair = [send(value, second_hop(turn)) for turn, value in enumerate(pair)]
        return pair, first, token(pair[0])

    def there_whole(pair):
        if groups > 1:
            pair = [lax.all_gather(value, "t", axis=1, tiled=True) for value in pair]
        return tuple(pair)

    group_squares = []

    def returned(pair):
        if groups > 1:
            pair = [
                lax.psum_scatter(value, "t", scatter_dimension=1, tiled=True) for value in pair
            ]
            group_squares.extend(jnp.sum(value * value) for value in pair)
            pair = [value.astype(bf16) for value in pair]
        return [send(value, home(turn)) for turn, value in enumerate(pair)]

    def along_groups(value, by):
        pairs = [(i, i + by) for i in range(groups) if 0 <= i + by < groups]
        return lax.ppermute(value, "t", pairs)

    def over_chans(value):
        distance = 1
        while distance < chans:
            value = value + swap(value, "c", distance)
            distance *= 2
        return value

    def pick(value, at, axis):
        return lax.dynamic_index_in_dim(value, at, axis, keepdims=False)

    def scattered_chans(sent, keep, late=None):
        total = keep + swap(sent, "c", 1).astype(f32)
        away = pick(total, 1 - x_at, 0)
        if late is not None:
            away = away + 0.0 * late[0]
        got = swap(away.astype(bf16), "c", cores)
        return pick(total, x_at, 0) + got.astype(f32)

    def gathered_chans(value):
        across_x = swap(value, "c", cores)
        across_core = swap(value, "c", 1)
        return (value, across_x, across_core, swap(across_x, "c", 1))

    def scattered_parts(products, late=None):
        keeps = [keep for _, keep in products]
        count = len(keeps)

        def hop(pieces, distance):
            pieces = jnp.concatenate([piece.astype(bf16) for piece in pieces], 0)
            return jnp.split(swap(pieces, "p", distance), count, 0)

        got = hop([sent for sent, _ in products], 1)
        totals = [keep + piece.astype(f32) for keep, piece in zip(keeps, got)]
        arrived = totals[0]
        totals = [total.reshape(total.shape[0], -1, 2, *total.shape[2:]) for total in totals]
        got = hop([pick(total, 1 - z_at % 2, 2) for total in totals], 2)
        totals = [pick(total, z_at % 2, 2) + piece.astype(f32) for total, piece in zip(totals, got)]
        away = [pick(total, 1 - z_at // 2, 1) for total in totals]
        if late is not None:
            away = [value + 0.0 * late[0] for value in away]
        got = hop(away, 4)
        totals = [pick(total, z_at // 2, 1) + piece.astype(f32) for total, piece in zip(totals, got)]
        return jnp.concatenate(totals, 0), arrived

    def after(value, *others):
        return value + (0.0 * token(*others)).astype(jnp.int32)

    def summed(values, kind, fills, late):
        fills = list(fills)

        def fill(arrived):
            return token(*fills.pop(0)(after(place, arrived)))[0] if fills else None

        def tied(arrived, ran):
            return arrived if ran is None else arrived + 0.0 * ran

        away = jnp.stack([pick(value, 1 - core_at, 0) for value in values]).astype(kind)
        total = jnp.stack([pick(value, core_at, 0) for value in values])
        total = total + swap(away, "c", 1).astype(f32)
        ran = fill(total)
        away = pick(total, 1 - x_at, 0).astype(kind)
        total = pick(total, x_at, 0) + swap(away, "c", cores).astype(f32)
        distance = 1
        while distance < parts:
            last, ran = ran, fill(total)
            total = tied(total, last)
            if distance in late:
                total = total + 0.0 * late[distance][0]
            total = total.astype(kind)
            total = total.astype(f32) + swap(total, "p", distance).astype(f32)
            distance *= 2
        total = tied(total, ran)
        return gathered_chans(total.astype(kind)), total

    def over_all(value):
        value = over_chans(value)
        distance = 1
        while distance < parts:
            value = value + swap(value, "p", distance)
            distance *= 2
        return lax.psum(value, "t") if groups > 1 else value

    extra = jnp.pad(modality.astype(bf16)[:, None, :], ((0, 0), (0, 15), (0, part_width - tok_rows)))
    tokens_all = lax.all_gather(jnp.concatenate([tokens_in, extra], 1), "p")
    flag = (slice_at // cores).astype(jnp.int32)[None]
    owner_flag = half_at.astype(jnp.int32)[None]
    w_in, in_arrived, _ = weights_there(pack(flag, jnp.zeros((1,), f32), in_weight))
    w_in = there_whole(w_in)
    small = jnp.concatenate([x_weight.reshape(3 * x_width, chan_width), channel_params], 0)
    own_lanes = y_at * half + z_at * own
    small = send(lax.dynamic_slice_in_dim(small, own_lanes, own, 1), small_pairs)
    dt16 = dt_weight.astype(bf16)
    dt_pair = crossed((dt16[..., :half], dt16[..., half:]), flag[0])
    out_pair = pack(flag, in_arrived, out_weight)
    out_rows = out_weight.shape[1]
    both = [jnp.concatenate(pair, 1) for pair in zip(out_pair, dt_pair)]
    both, _, _ = weights_there(both)
    w_out = there_whole([value[:, :out_rows] for value in both])
    dt_part = jnp.concatenate(
        crossed(there_whole([value[:, out_rows:] for value in both]), x_at), 1
    )
    dt_blocks = []
    for distance in range(chans):
        block = lax.dynamic_slice_in_dim(dt_part, (c_at ^ distance) * own, own, 2)
        dt_blocks.append(swap(block, "c", distance) if distance else block)
    dt_blocks = jnp.stack(dt_blocks)
    w_dt = jnp.concatenate([pick(dt_blocks, c_at ^ k, 0) for k in range(chans)], 1)
    w_dt = w_dt.transpose(1, 0, 2).reshape(rank, 3 * own)
    back_all = lax.all_gather(cotangent, "p")
    positions = t_at * span - edge + jnp.arange(span + 2 * edge, dtype=jnp.int32)
    segment = jnp.sum((starts[:, None, :] <= positions[None, :, None]).astype(jnp.int32), axis=2)
    keep_mask = 1.0 - jnp.any(
        starts[:, None, :] == positions[None, edge : edge + span, None], axis=2
    ).astype(f32)
    same_doc = [
        (segment[:, edge - j : 2 * edge - j + span] == segment[:, edge:]).astype(f32)
        for j in range(1, K)
    ]
    squares = jnp.sum(jnp.square(tokens_all[:, :, :tok_rows].astype(f32)), axis=-1)
    squares = over_chans(squares).transpose(1, 0, 2).reshape(micros, span)
    inverse = lax.rsqrt(squares / model + NORM_EPS)
    kinds = tokens_all[:, :, tok_rows, :tok_rows].transpose(1, 0, 2).reshape(micros, span)
    kinds = kinds.astype(jnp.int32)
    rows = [inverse, *((kinds == k).astype(f32) for k in range(3))]
    rows += [same[:, :span] for same in same_doc] + [jnp.zeros_like(inverse)]
    info3 = jnp.stack(rows, 1)
    info = jnp.stack([row.reshape(-1) for row in rows], 0)
    inv_own = lax.dynamic_slice_in_dim(inverse, p_at * tok_rows, tok_rows, 1)[..., None]
    gain_part = lax.dynamic_slice_in_dim(gain, c_at * part_width, part_width, 0)[None]

    w_x = small[: 3 * x_width].astype(bf16).reshape(3, x_width, own)
    w_x = w_x.transpose(1, 0, 2).reshape(x_width, 3 * own)
    channel = small[3 * x_width :]
    taps = channel[:8]
    biases = jnp.pad(channel[K + 1 : K + 3], ((0, 6), (0, 0)))
    neg_rate = -jnp.exp(channel[K + 3 :])
    rules = lane_rules()

    grad_dt_sum = grad_x_sum = grad_chan_sum = grad_gain_sum = 0.0
    pairs_of = range(micros // 2)
    zero_state = jnp.zeros((2, N, own), f32)
    everything = Tiles(micros, parts, tok_rows)
    twos = [Tiles(2, parts, tok_rows, 2 * x) for x in pairs_of]
    normed, sent, keep = inner_product(everything, place, tokens_all, info, gain_part, w_in)
    inner = scattered_chans(sent, keep).reshape(micros, span, own)
    edge_rows = jnp.zeros((micros, 8, own), f32)
    if groups > 1:
        edge_rows = along_groups(inner[:, span - 8 :], 1)
    act, conv, shared = conv_forward(inner, edge_rows, info3, taps, w_x)
    quarters, quarter = summed(
        [shared[2 * x : 2 * x + 2] for x in pairs_of], f32, [], {}
    )
    sent, keep = gate_product(everything, after(place, quarter), normed, back_all, info, w_in, w_out)
    pair = scattered_chans(sent, keep).reshape(micros, span, 2 * own)
    held = []
    for x in pairs_of:
        args = (x, keep_mask, quarters, act, info3, w_dt, rules, neg_rate, biases)
        order = after(place, sent if x == 0 else held[-1][0])
        state_in = zero_state
        if groups > 1:
            first_pass = mix_forward(order, *args, zero_state)
            ends, step = first_pass[6], first_pass[2]
            passed_all = jnp.exp(jnp.sum(step, axis=1)[:, None, :] * neg_rate)
            passed_all = passed_all * jnp.prod(keep_mask[2 * x : 2 * x + 2], axis=1)[:, None, None]
            for _ in range(groups - 1):
                state_in = along_groups(passed_all * state_in + ends, 1)
        held.append(mix_forward(order, *args, state_in))

    all_pairs, pulls = [], []
    for x in pairs_of:
        kinds_out, pull = blend(x, held[x][0], act, pair, biases)
        pulls.append(pull)
        all_pairs.append(gathered_chans(kinds_out.reshape(2, 2 * span, own)))
    order = place
    shares, d_acts, mix_sums, d_rate = [], [], 0.0, 0.0
    for x in pairs_of:
        saved = (*held[x][1:], pulls[x])
        args = (x, keep_mask, act, info3, w_dt, rules, neg_rate, biases)
        adj_in = zero_state
        if groups > 1:
            ends = mix_backward(order, *args, zero_state, saved)[5]
            passed_all = jnp.exp(jnp.sum(saved[1], axis=1)[:, None, :] * neg_rate)
            passed_all = passed_all * jnp.prod(keep_mask[2 * x : 2 * x + 2], axis=1)[:, None, None]
            for _ in range(groups - 1):
                adj_in = along_groups(passed_all * adj_in + ends, -1)
        share, d_act, grad_dt, sums, grad_rate, _ = mix_backward(order, *args, adj_in, saved)
        order = after(place, d_act, *(blocks[k] for blocks in all_pairs for k in (1, 2)))
        shares.append(share)
        d_acts.append(d_act)
        grad_dt_sum += grad_dt
        mix_sums += jnp.sum(sums.reshape(2, 8, own), axis=1)
        d_rate += grad_rate * neg_rate

    kept = f32 if groups > 1 else bf16

    def kindred(which):
        return ((1, span, own), lambda m, x: (which, m, 0))

    def rows_at(width):
        return ((span, width), lambda m, x: (2 * x + m, 0))

    raw_at = ((parts, 1, tok_rows, part_width), lambda m, x: (0, 2 * x + m, 0, 0))
    count = len(all_pairs)
    products, large = [], {}

    def out_fill(order):
        for x in pairs_of:
            products.append(out_product(twos[x], order, all_pairs[x], info, w_out))
            order = after(place, products[-1][0])
        return [sent for sent, _ in products]

    def grad_fill(name, lefts, left_at, which):
        def run(order):
            *pieces, square = weight_grad(
                order, info, lefts, left_at, all_pairs, kindred(which), span, kept
            )
            large[name] = (pieces, square)
            return (square,)

        return run

    fills = [
        out_fill,
        grad_fill("out", [back_all] * count, raw_at, 0),
        grad_fill("gate", [normed] * count, rows_at(part_width), 1),
    ]
    quarters, _ = summed(shares, bf16, fills, {})
    (g_out, out_sq), (g_gate, gate_sq) = large["out"], large["gate"]
    g_out, g_gate = returned(g_out), returned(g_gate)
    outs, _ = scattered_parts(products)

    d_inners = []
    for x in pairs_of:
        d_inner, grad_x, sums, head, last = conv_backward(
            place, x, quarters, d_acts[x], conv, inner, edge_rows, act, info3, taps, w_x
        )
        if groups > 1:
            ahead = along_groups(head, -1)[:, :edge]
            for j in range(1, K):
                gone = taps[j] * ahead * same_doc[j - 1][2 * x : 2 * x + 2, span:, None]
                last = last.at[:, 8 - j :].add(gone[:, :j])
            d_inner = jnp.concatenate([d_inner[:, : span - 8], last.astype(bf16)], 1)
        d_inners.append(d_inner.reshape(2 * span, own))
        grad_x_sum += grad_x
        grad_chan_sum += jnp.sum(sums.reshape(K + 1, 8, own), axis=1)
    grad_chan_sum = jnp.concatenate([grad_chan_sum, mix_sums, d_rate], 0)
    inners = gathered_chans(jnp.concatenate(d_inners, 0))

    *g_inner, inner_sq = weight_grad(
        after(place, g_out[1]), info, [normed] * count, rows_at(part_width), [inners] * count,
        rows_at(own), span, kept,
    )
    g_inner = returned(g_inner)
    order = after(place, inner_sq)
    products = []
    for x in pairs_of:
        sent, keep, gain_rows = normed_grad(
            twos[x], order, all_pairs[x], inners, info, tokens_all, w_in
        )
        grad_gain_sum += jnp.sum(gain_rows, axis=0)
        products.append((sent, keep))
        order = after(place, sent, *g_gate)
    rows_back, rows_arrived = scattered_parts(products, token(*g_inner))

    grad_x_sum = grad_x_sum.reshape(x_width, 3, own).transpose(1, 0, 2)
    grad_dt_sum = grad_dt_sum.reshape(rank, 3, own).transpose(1, 0, 2)
    g_small = jnp.concatenate(
        [grad_x_sum.reshape(-1, own), grad_dt_sum.reshape(-1, own), grad_chan_sum], 0
    )
    if groups > 1:
        g_small = lax.psum(g_small, "t")
        large_sq = sum(group_squares)
    else:
        large_sq = jnp.sum(out_sq) + jnp.sum(gate_sq) + jnp.sum(inner_sq)
    local_sq = large_sq + jnp.sum(g_small * g_small) / groups
    here = (jnp.arange(chans) == c_at).astype(f32)
    tail = jnp.concatenate([(here[:, None] * grad_gain_sum).reshape(-1), local_sq[None]])
    tail = over_all(tail + 0.0 * token(g_inner[0])[0])
    grad_gain = tail[:model]
    grad_norm = jnp.sqrt(tail[model] + jnp.sum(grad_gain * grad_gain))
    clip_scale = CLIP_LIMIT / jnp.maximum(grad_norm, CLIP_LIMIT)

    grad_out = jnp.concatenate(crossed(g_out, half_at), -1).astype(f32)
    in_pieces = (*g_inner, *g_gate)
    small_back = lax.all_gather(send(g_small.astype(bf16), small_pairs, True), "p")
    small_back = small_back.reshape(chans, 2, -1, own).transpose(2, 1, 0, 3)
    small_back = small_back.reshape(-1, chan_width).astype(f32)
    grad_x = small_back[: 3 * x_width].reshape(3, x_width, chan_width)
    grad_dt = small_back[3 * x_width : 3 * x_width + 3 * rank].reshape(3, rank, chan_width)
    grad_dt = lax.dynamic_slice_in_dim(grad_dt, s_at * dt_rows, dt_rows, 1)
    grad_chan = small_back[3 * x_width + 3 * rank :]

    tok_float = tokens_in.astype(f32)
    mixed = (tok_float + outs).astype(bf16)
    d_own = rows_back
    x_hat_own = tok_float * inv_own
    d_hat = d_own * gain_part
    mean = over_chans(jnp.sum(d_hat * x_hat_own, axis=-1))[..., None] / model
    input_grad = cotangent.astype(f32) + inv_own * (d_hat - x_hat_own * mean)

    dt_new, dt_first_new, dt_second_new = adam_update(
        dt_weight, grad_dt, dt_first, dt_second, clip_scale, rank ** (-0.5)
    )
    out_new, out_first_new, out_second_new = adam_update(
        out_weight, grad_out, out_first, out_second, clip_scale, inner_all ** (-0.5)
    )
    x_new, x_first_new, x_second_new = adam_update(
        x_weight, grad_x, x_first, x_second, clip_scale, inner_all ** (-0.5)
    )
    chan_new, chan_first_new, chan_second_new = adam_update(
        channel_params, grad_chan, channel_first, channel_second, clip_scale, 0.5
    )
    gain_new, gain_first_new, gain_second_new = adam_update(
        gain, grad_gain, gain_first, gain_second, clip_scale, 0.5
    )
    grad_in, in_new, in_first_new, in_second_new = adam(
        after(owner_flag, x_new, chan_new, dt_new), clip_scale[None], in_weight, in_first, in_second, in_pieces, model ** (-0.5)
    )
    return (
        mixed, input_grad, grad_norm,
        grad_in, in_new, in_first_new, in_second_new,
        grad_dt, dt_new, dt_first_new, dt_second_new,
        grad_out, out_new, out_first_new, out_second_new,
        grad_x, x_new, x_first_new, x_second_new,
        grad_chan, chan_new, chan_first_new, chan_second_new,
        grad_gain, gain_new, gain_first_new, gain_second_new,
        in_new.astype(bf16), dt_new.astype(bf16), out_new.astype(bf16), x_new.astype(bf16),
    )


def solution(mesh):
    chans = mesh.shape["ch"]
    parts = 2 * chans
    groups = mesh.shape["seq"] // parts
    inside = Mesh(mesh.devices.reshape(groups, parts, chans), ("t", "p", "c"))
    seq = ("t", "p")
    tok = P(None, seq, "c")
    wide = P(None, seq, None, "c")
    rows = P(None, seq, "c")
    flat = P(None, None, "c")
    chan = P(None, "c")
    return jax.shard_map(
        functools.partial(body, groups, parts, chans),
        mesh=inside,
        in_specs=(tok, P(None, seq), P(), tok)
        + (wide,) * 3 + (rows,) * 3 + (rows,) * 3 + (flat,) * 3 + (chan,) * 3 + (P(),) * 3,
        out_specs=(tok, tok, P())
        + (wide,) * 4 + (rows,) * 4 + (rows,) * 4 + (flat,) * 4 + (chan,) * 4 + (P(),) * 4
        + (wide, rows, rows, flat),
        check_vma=False,
    )
```

```python
import functools

import jax
import jax.numpy as jnp
from jax import lax
from jax.experimental import pallas as pl
from jax.experimental.pallas import tpu as pltpu
from jax.sharding import Mesh
from jax.sharding import PartitionSpec as P

N = 16
K = 4
STEP = 10

NORM_EPS = 1e-05
BETA_ONE = 0.9
BETA_TWO = 0.95
ADAM_EPS = 1e-08
DECAY = 0.1
CLIP_LIMIT = 1.0
LANES = 128
SCAN_ROWS = 128
MEGA = 1024 * 1024
GROUP = 2
f32 = jnp.float32
bf16 = jnp.bfloat16


def silu_grad(value):
    sigma = jax.nn.sigmoid(value)
    return sigma * (1.0 + value * (1.0 - sigma))


def adam_update(weight, gradient, first_moment, second, clip_scale, step_rate):
    clipped = gradient * clip_scale
    first_new = BETA_ONE * first_moment + (1.0 - BETA_ONE) * clipped
    second_new = BETA_TWO * second + (1.0 - BETA_TWO) * clipped * clipped
    first_hat = first_new * (1.0 / (1.0 - BETA_ONE**STEP))
    second_hat = second_new * (1.0 / (1.0 - BETA_TWO**STEP))
    weight_new = weight - step_rate * (
        first_hat / (jnp.sqrt(second_hat) + ADAM_EPS) + DECAY * weight
    )
    return (weight_new, first_new, second_new)


def sum_rows(parts):
    at = lax.broadcasted_iota(jnp.int32, parts[0].shape, 0)
    for distance in (1, 2, 4):
        low = at % (2 * distance) < distance
        parts = [
            jnp.where(low, a, b) + pltpu.roll(jnp.where(low, b, a), distance, 0)
            for a, b in zip(parts[0::2], parts[1::2])
        ]
    return parts[0]


def lane_rules():
    lanes = jnp.arange(LANES)
    used = lanes % (LANES // 2) < 3 * N
    mask = ((lanes[None, :] % N == jnp.arange(N)[:, None]) & used[None, :]).astype(f32)
    side = (lanes[:, None] // (LANES // 2) == jnp.arange(2 * LANES)[None, :] // LANES).astype(bf16)
    return mask, side


def matmul(left, right):
    return jnp.dot(left, right, preferred_element_type=f32)


def spread(rows_ref, m, base, mask, side):
    left = [rows_ref[m, pl.ds(base + j, 1), :] * mask for j in range(8)]
    return matmul(jnp.concatenate(left, 0).astype(bf16), side)


def lane_sums(product_ref, m, grads, lane, base, ones):
    sums = matmul(product_ref[m], ones)
    for j in range(8):
        grads = jnp.where(lane == base + j, sums[N * j : N * j + N], grads)
    return grads


def turned(ref, turn, x_at):
    width = ref.shape[-1] // 2
    return pl.ds(pl.multiple_of((turn ^ x_at) * width, width), width)


def three(tile, info):
    return jnp.concatenate([(tile * info[:, k + 1 : k + 2]).astype(bf16) for k in range(3)], -1)


def across(left, right, dims):
    return lax.dot_general(left, right, ((dims[0:1], dims[1:2]), ((), ())), preferred_element_type=f32)


def stacked(ref):
    kinds, rows, cols = ref.shape
    return ref[...].reshape(kinds * rows, cols)


def split_blocks(total, place_ref, sent_ref, keep_ref, scratch_ref, offset):
    scratch_ref[...] = total
    core = place_ref[1]
    for x in range(2):
        away = pl.ds(pl.multiple_of((2 * x + 1 - core) * LANES, LANES), LANES)
        here = pl.ds(pl.multiple_of((2 * x + core) * LANES, LANES), LANES)
        sent_ref[x, :, offset : offset + LANES] = scratch_ref[:, away].astype(bf16)
        keep_ref[x, :, offset : offset + LANES] = scratch_ref[:, here]


def tile_rows(ref):
    return ref[...].reshape(-1, ref.shape[-1])


def wide_product(tile_ref, info, w_refs, scratch_ref, x_at):
    total = None
    for turn, w_ref in enumerate(w_refs):
        left = three(tile_ref[:, turned(tile_ref, turn, x_at)], info)
        part = across(left, stacked(w_ref), (1, 0))
        total = part if total is None else total + part
    return total


def inner_kernel(place_ref, x_ref, info_ref, gain_ref, w0_ref, w1_ref,
                 normed_ref, sent_ref, keep_ref, tile_ref, scratch_ref):
    info = info_ref[...].T
    normed = tile_rows(x_ref).astype(f32) * info[:, :1] * gain_ref[...]
    normed = normed.astype(bf16)
    normed_ref[...] = normed
    tile_ref[...] = normed.astype(f32)
    total = wide_product(tile_ref, info, (w0_ref, w1_ref), scratch_ref, place_ref[0])
    split_blocks(total, place_ref, sent_ref, keep_ref, scratch_ref, 0)


def gate_kernel(place_ref, normed_ref, back_ref, info_ref, g0_ref, g1_ref, o0_ref, o1_ref,
                sent_ref, keep_ref, tile_ref, scratch_ref):
    info = info_ref[...].T
    tile_ref[...] = normed_ref[...].astype(f32)
    total = wide_product(tile_ref, info, (g0_ref, g1_ref), scratch_ref, place_ref[0])
    split_blocks(total, place_ref, sent_ref, keep_ref, scratch_ref, 0)
    tile_ref[...] = tile_rows(back_ref).astype(f32)
    total = wide_product(tile_ref, info, (o0_ref, o1_ref), scratch_ref, place_ref[0])
    split_blocks(total, place_ref, sent_ref, keep_ref, scratch_ref, LANES)


def gathered(scratch_ref, place_ref, refs):
    at = 2 * place_ref[0] + place_ref[1]
    for distance, ref in zip((0, 2, 1, 3), refs):
        lanes = pl.ds(pl.multiple_of((at ^ distance) * LANES, LANES), LANES)
        scratch_ref[:, lanes] = tile_of(ref).astype(f32)


def tile_of(ref):
    return ref[...].reshape(-1, ref.shape[-1])


def split_parts(total, place_ref, sent_ref, keep_ref):
    y = place_ref[2]
    half = total.shape[0] // 2
    low, high = total[:half], total[half:]
    mine = jnp.full(low.shape, y, jnp.int32) == 0
    sent_ref[...] = jnp.where(mine, high, low).astype(bf16).reshape(sent_ref.shape)
    keep_ref[...] = jnp.where(mine, low, high).reshape(keep_ref.shape)


def out_kernel(place_ref, a_ref, b_ref, c_ref, d_ref, info_ref, w0_ref, w1_ref,
               sent_ref, keep_ref, tile_ref, total_ref):
    gathered(tile_ref, place_ref, (a_ref, b_ref, c_ref, d_ref))
    left = three(tile_ref[...], info_ref[...].T)
    width = tile_ref.shape[1]
    for turn, w_ref in enumerate((w0_ref, w1_ref)):
        total = None
        for k in range(3):
            part = across(left[:, k * width : (k + 1) * width], w_ref[k], (1, 1))
            total = part if total is None else total + part
        total_ref[:, turned(total_ref, turn, place_ref[0])] = total
    split_parts(total_ref[...], place_ref, sent_ref, keep_ref)


def normed_kernel(place_ref, ga_ref, gb_ref, gc_ref, gd_ref, ia_ref, ib_ref, ic_ref, id_ref,
                  info_ref, x_ref, g0_ref, g1_ref, i0_ref, i1_ref,
                  sent_ref, keep_ref, gain_ref, tile_ref, total_ref):
    info = info_ref[...].T
    width = tile_ref.shape[1]
    gathered(tile_ref, place_ref, (ga_ref, gb_ref, gc_ref, gd_ref))
    gates = three(tile_ref[...], info)
    gathered(tile_ref, place_ref, (ia_ref, ib_ref, ic_ref, id_ref))
    inners = three(tile_ref[...], info)
    for turn, (g_ref, i_ref) in enumerate(((g0_ref, i0_ref), (g1_ref, i1_ref))):
        total = None
        for k in range(3):
            lanes = slice(k * width, (k + 1) * width)
            part = across(gates[:, lanes], g_ref[k], (1, 1)) + across(inners[:, lanes], i_ref[k], (1, 1))
            total = part if total is None else total + part
        total_ref[:, turned(total_ref, turn, place_ref[0])] = total
    total = total_ref[...]
    split_parts(total, place_ref, sent_ref, keep_ref)

    @pl.when((pl.program_id(0) == 0) & (pl.program_id(1) == 0))
    def _():
        gain_ref[...] = jnp.zeros_like(gain_ref)

    x_hat = tile_rows(x_ref).astype(f32) * info[:, :1]
    gain_ref[...] += jnp.sum((total * x_hat).reshape(-1, 8, total.shape[1]), axis=0)


def weight_grad_kernel(chunks, steps, place_ref, *refs):
    ins, (out0_ref, out1_ref, square_ref, tile_ref, sum_ref) = refs[: 6 * chunks], refs[6 * chunks :]
    at = pl.program_id(0)

    @pl.when(at == 0)
    def _():
        sum_ref[...] = jnp.zeros_like(sum_ref)

    for chunk in range(chunks):
        info_ref, left_ref, *blocks = ins[6 * chunk : 6 * chunk + 6]

        @pl.when((at >= chunk * steps) & (at < (chunk + 1) * steps))
        def _(info_ref=info_ref, left_ref=left_ref, blocks=blocks):
            gathered(tile_ref, place_ref, blocks)
            right = three(tile_ref[...], info_ref[...].T)
            left = left_ref[...].reshape(-1, left_ref.shape[-1])
            sum_ref[...] += across(left, right, (0, 0))

    @pl.when(at == chunks * steps - 1)
    def _():
        half = sum_ref.shape[0] // 2
        width = tile_ref.shape[1]
        for turn, out_ref in enumerate((out0_ref, out1_ref)):
            rows = pl.ds(pl.multiple_of((turn ^ place_ref[3]) * half, half), half)
            for k in range(3):
                out_ref[k] = sum_ref[rows, k * width : (k + 1) * width].astype(out_ref.dtype)
        total = sum_ref[...]
        square_ref[...] = jnp.sum((total * total).reshape(-1, 8, total.shape[1]), axis=0)


SCALARS = pl.BlockSpec(memory_space=pltpu.SMEM)


def whole(array):
    return pl.BlockSpec(array.shape, lambda *at: (0,) * array.ndim)


def plane(array, which):
    kinds, rows, lanes = array.shape
    return pl.BlockSpec((kinds, rows, lanes // 2), lambda *at: (0, 0, which))


def shape_of(shape, dtype):
    return jax.ShapeDtypeStruct(shape, dtype)


def call(kernel, name, grid, in_specs, out_specs, out_shape, scratch, flops, moved, args):
    return pl.pallas_call(
        kernel,
        grid=grid,
        in_specs=in_specs,
        out_specs=out_specs,
        out_shape=out_shape,
        scratch_shapes=scratch,
        cost_estimate=pl.CostEstimate(flops=flops, bytes_accessed=moved, transcendentals=0),
        compiler_params=pltpu.CompilerParams(
            dimension_semantics=("arbitrary",) * len(grid), vmem_limit_bytes=48 * MEGA
        ),
        name=name,
    )(*args)


class Tiles:
    def __init__(self, micros, parts, rows, first=0):
        self.micros, self.pairs, self.rows, self.first = micros, parts // 2, rows, first
        self.grid = (micros, self.pairs)
        self.tile = 2 * rows

    def raw(self, width):
        return pl.BlockSpec((2, 1, self.rows, width), lambda m, z: (z, self.first + m, 0, 0))

    def flat(self, width):
        return pl.BlockSpec((self.tile, width), lambda m, z: ((self.first + m) * self.pairs + z, 0))

    def info(self):
        return pl.BlockSpec((8, self.tile), lambda m, z: (0, (self.first + m) * self.pairs + z))

    def kindred(self, which, width):
        return pl.BlockSpec((1, self.tile, width), lambda m, z: (which, m * self.pairs + z, 0))

    def blocks(self, width):
        return pl.BlockSpec((2, self.tile, width), lambda m, z: (0, m * self.pairs + z, 0))

    def parted(self, width):
        return pl.BlockSpec((1, 1, self.rows, width), lambda m, z: (m, z, 0, 0))


def inner_product(tiles, place, tokens, info, gain, w_in):
    width = tokens.shape[-1]
    chans = w_in[0].shape[-1] // 2
    rows = tiles.micros * tiles.pairs * tiles.tile
    return call(
        inner_kernel, "inner_product", tiles.grid,
        [SCALARS, tiles.raw(width), tiles.info(), whole(gain), plane(w_in[0], 0), plane(w_in[1], 0)],
        [tiles.flat(width), tiles.blocks(LANES), tiles.blocks(LANES)],
        [shape_of((rows, width), bf16), shape_of((2, rows, LANES), bf16), shape_of((2, rows, LANES), f32)],
        [pltpu.VMEM((tiles.tile, width), f32), pltpu.VMEM((tiles.tile, chans), f32)],
        6 * rows * width * chans, 8 * MEGA,
        (place, tokens, info, gain, *w_in),
    )


def gate_product(tiles, place, normed, back, info, w_in, w_out):
    width = normed.shape[-1]
    chans = w_out[0].shape[-1]
    rows = normed.shape[0]
    return call(
        gate_kernel, "gate_product", tiles.grid,
        [SCALARS, tiles.flat(width), tiles.raw(width), tiles.info()]
        + [plane(w, 1) for w in w_in] + [whole(w) for w in w_out],
        [tiles.blocks(2 * LANES), tiles.blocks(2 * LANES)],
        [shape_of((2, rows, 2 * LANES), bf16), shape_of((2, rows, 2 * LANES), f32)],
        [pltpu.VMEM((tiles.tile, width), f32), pltpu.VMEM((tiles.tile, chans), f32)],
        12 * rows * width * chans, 16 * MEGA,
        (place, normed, back, info, *w_in, *w_out),
    )


def out_product(tiles, place, pairs, info, w_out):
    width = 2 * w_out[0].shape[1]
    chans = w_out[0].shape[-1]
    rows = pairs[0].shape[1]
    parted = (tiles.micros, tiles.pairs, tiles.rows, width)
    return call(
        out_kernel, "out_product", tiles.grid,
        [SCALARS] + [tiles.kindred(0, LANES)] * 4 + [tiles.info(), whole(w_out[0]), whole(w_out[1])],
        [tiles.parted(width), tiles.parted(width)],
        [shape_of(parted, bf16), shape_of(parted, f32)],
        [pltpu.VMEM((tiles.tile, chans), f32), pltpu.VMEM((tiles.tile, width), f32)],
        6 * rows * width * chans, 8 * MEGA,
        (place, *pairs, info, *w_out),
    )


def normed_grad(tiles, place, pairs, inners, info, tokens, w_in):
    width = 2 * w_in[0].shape[1]
    chans = w_in[0].shape[-1] // 2
    rows = pairs[0].shape[1]
    parted = (tiles.micros, tiles.pairs, tiles.rows, width)
    return call(
        normed_kernel, "normed_grad", tiles.grid,
        [SCALARS] + [tiles.kindred(1, LANES)] * 4 + [tiles.flat(LANES)] * 4
        + [tiles.info(), tiles.raw(width)] + [plane(w, which) for which in (1, 0) for w in w_in],
        [tiles.parted(width), tiles.parted(width), pl.BlockSpec((8, width), lambda m, z: (0, 0))],
        [shape_of(parted, bf16), shape_of(parted, f32), shape_of((8, width), f32)],
        [pltpu.VMEM((tiles.tile, chans), f32), pltpu.VMEM((tiles.tile, width), f32)],
        12 * rows * width * chans, 16 * MEGA,
        (place, *pairs, *inners, info, tokens, *w_in, *w_in),
    )


def weight_grad(place, info, lefts, left_at, rights, right_at, span, dtype):
    chunks = len(lefts)
    width = lefts[0].shape[-1]
    chans = 4 * LANES
    steps = info.shape[1] // span // chunks
    info_at = ((8, span), lambda m, chunk: (0, chunk * steps + m))
    piece = (3, width // 2, chans)
    specs, args = [], []
    for chunk in range(chunks):
        def held(spec, chunk=chunk):
            shape, at = spec
            low = chunk * steps
            return pl.BlockSpec(shape, lambda i: at(jnp.clip(i - low, 0, steps - 1), chunk))

        specs += [held(info_at), held(left_at)] + [held(right_at)] * 4
        args += [info, lefts[chunk], *rights[chunk]]
    return call(
        functools.partial(weight_grad_kernel, chunks, steps), "weight_grad", (chunks * steps,),
        [SCALARS] + specs,
        [pl.BlockSpec(piece, lambda i: (0, 0, 0))] * 2 + [pl.BlockSpec((8, 3 * chans), lambda i: (0, 0))],
        [shape_of(piece, dtype), shape_of(piece, dtype), shape_of((8, 3 * chans), f32)],
        [pltpu.VMEM((span, chans), f32), pltpu.VMEM((width, 3 * chans), f32)],
        6 * chunks * steps * span * width * chans, 24 * MEGA,
        (place, *args),
    )


def masked_sum(wide, info):
    width = wide.shape[1] // 3
    return sum(wide[:, k * width : (k + 1) * width] * info[:, k + 1 : k + 2] for k in range(3))


def one_of_four(place_ref, x, core, own_ref, x_ref, core_ref, both_ref):
    shape = own_ref.shape
    same_x = jnp.full(shape, place_ref[0] ^ x, jnp.int32) == 0
    same_core = jnp.full(shape, place_ref[1] ^ core, jnp.int32) == 0
    own, across_x, across_core, both = (
        ref[...].astype(f32) for ref in (own_ref, x_ref, core_ref, both_ref)
    )
    return jnp.where(same_core, jnp.where(same_x, own, across_x), jnp.where(same_x, across_core, both))


def wide_scratch(micros):
    return pltpu.VMEM((micros, 8 * N, 2 * LANES), f32)


def product_scratch(micros):
    return pltpu.VMEM((micros, 8 * N, LANES), bf16)


def state_scratch(micros):
    return pltpu.VMEM((micros, N, LANES), f32)


def tile_scratch(micros):
    return pltpu.VMEM((micros, SCAN_ROWS, LANES), f32)


def mix_forward_kernel(
    x, place_ref, keep_ref, own_ref, x_ref, core_ref, both_ref, act_ref, info_ref,
    dt_ref, mask_ref, side_ref, rate_ref, bias_ref, start_ref,
    y_ref, before_ref, step_ref, slope_ref, rows_ref, low_ref, final_ref,
    state_ref, wide_a, wide_b, drive_ref,
):
    micros, rows, _ = step_ref.shape
    block = pl.program_id(0)
    rank = low_ref.shape[1]
    rate = rate_ref[...]
    mask = mask_ref[...]
    side = side_ref[...]
    dt_bias = bias_ref[0:1]

    @pl.when(block == 0)
    def _():
        state_ref[...] = start_ref[...]

    for m in range(micros):
        shared = one_of_four(place_ref, x, m, own_ref, x_ref, core_ref, both_ref)
        low = shared[:rank].astype(bf16)
        low_ref[m] = low
        dt_pre = masked_sum(across(low, dt_ref[...], (0, 0)), info_ref[m].T) + dt_bias
        small = jnp.exp(-jnp.abs(dt_pre))
        step = jnp.maximum(dt_pre, 0.0) + jnp.log1p(small)
        step_ref[m] = step
        slope_ref[m] = jnp.where(dt_pre >= 0, 1.0, small) / (1.0 + small)
        drive_ref[m] = step * act_ref[m].astype(f32)
        parts = []
        for left in (shared[rank : rank + N], shared[rank + N :]):
            for _ in range(3):
                part = left.astype(bf16).astype(f32)
                parts.append(part)
                left = left - part
            parts.append(jnp.zeros_like(left))
        rows_ref[m] = jnp.concatenate(parts, 0).T
        wide_a[m] = spread(rows_ref, m, 0, mask, side)

    def sixteen(turn, states):
        states = list(states)
        for half in range(2):
            base = pl.multiple_of(turn * 16 + 8 * half, 8)
            wide, wide_next = (wide_a, wide_b) if half == 0 else (wide_b, wide_a)
            following = jnp.minimum(base + 8, rows - 8)
            for m in range(micros):
                wide_next[m] = spread(rows_ref, m, following, mask, side)
            y_parts = [[] for _ in range(micros)]
            for j in range(8):
                for m in range(micros):
                    row = pl.ds(base + j, 1)
                    own = slice(N * j, N * j + N)
                    before = states[m]
                    before_ref[m, base + j] = before
                    before = before * keep_ref[micros * x + m, block * rows + base + j]
                    state = (
                        jnp.exp(step_ref[m, row, :] * rate) * before
                        + drive_ref[m, row, :] * wide[m, own, :LANES]
                    )
                    states[m] = state
                    shown = state * wide[m, own, LANES:]
                    y_parts[m].append(shown[:8] + shown[8:])
            for m in range(micros):
                y_ref[m, pl.ds(base, 8), :] = sum_rows(y_parts[m])
        return tuple(states)

    states = lax.fori_loop(
        0, rows // 16, sixteen, tuple(state_ref[m] for m in range(micros))
    )
    for m in range(micros):
        state_ref[m] = states[m]
        final_ref[m] = states[m]


def blend_kernel(y_ref, act_ref, pair_ref, bias_ref, kinds_ref, pull_ref):
    skip = bias_ref[1:2]
    gate, d_mixed = pair_ref[0, :, :LANES], pair_ref[0, :, LANES:]
    sigma = jax.nn.sigmoid(gate)
    y_scan = y_ref[0] + skip * act_ref[0].astype(f32)
    opened = gate * sigma
    kinds_ref[0, 0] = (y_scan * opened).astype(bf16)
    kinds_ref[1, 0] = (d_mixed * y_scan * (sigma * (1.0 + gate * (1.0 - sigma)))).astype(bf16)
    pull_ref[0] = d_mixed * opened


def blend(x, y, act, pair, bias):
    micros, rows, _ = y.shape
    first = micros * x
    one = pl.BlockSpec((1, rows, LANES), lambda m: (m, 0, 0))
    return call(
        blend_kernel, "blend", (micros,),
        [
            one, pl.BlockSpec((1, rows, LANES), lambda m: (first + m, 0, 0)),
            pl.BlockSpec((1, rows, 2 * LANES), lambda m: (first + m, 0, 0)), const(bias.shape),
        ],
        [pl.BlockSpec((2, 1, rows, LANES), lambda m: (0, m, 0, 0)), one],
        [shape_of((2,) + y.shape, bf16), shape_of(y.shape, f32)],
        [], 20 * y.size, 20 * y.size, (y, act, pair, bias),
    )


def time_specs(micros, at, x):
    return dict(
        tall=pl.BlockSpec((micros, SCAN_ROWS, LANES), lambda i: (0, at(i), 0)),
        act=pl.BlockSpec((micros, SCAN_ROWS, LANES), lambda i: (x, at(i), 0)),
        turned=pl.BlockSpec((micros, LANES, SCAN_ROWS), lambda i: (0, 0, at(i))),
        states=pl.BlockSpec((micros, SCAN_ROWS, N, LANES), lambda i: (0, at(i), 0, 0)),
        info=pl.BlockSpec((micros, 8, SCAN_ROWS), lambda i: (x, 0, at(i))),
        fixed=pl.BlockSpec((micros, N, LANES), lambda i: (0, 0, 0)),
    )


def const(shape):
    return pl.BlockSpec(shape, lambda *at: (0,) * len(shape))


def mix_forward(place, x, keep, quarters, act, info, dt, rules, rate, bias, start):
    length = act.shape[1]
    micros = start.shape[0]
    blocks = length // SCAN_ROWS
    spec = time_specs(micros, lambda i: i, x)
    width = quarters[0].shape[0]
    quarter = pl.BlockSpec((width, SCAN_ROWS), lambda i: (0, i))
    tall = jax.ShapeDtypeStruct((micros, length, LANES), f32)
    return pl.pallas_call(
        functools.partial(mix_forward_kernel, x),
        grid=(blocks,),
        in_specs=[
            SCALARS, SCALARS, *[quarter] * 4, spec["act"], spec["info"],
            const(dt.shape), const(rules[0].shape), const(rules[1].shape),
            const(rate.shape), const(bias.shape), spec["fixed"],
        ],
        out_specs=[spec["tall"], spec["states"], *[spec["tall"]] * 3, spec["turned"], spec["fixed"]],
        out_shape=[
            tall, jax.ShapeDtypeStruct((micros, length, N, LANES), f32), tall, tall, tall,
            jax.ShapeDtypeStruct((micros, width - 2 * N, length), bf16),
            jax.ShapeDtypeStruct((micros, N, LANES), f32),
        ],
        scratch_shapes=[
            state_scratch(micros), wide_scratch(micros), wide_scratch(micros), tile_scratch(micros)
        ],
        cost_estimate=pl.CostEstimate(
            flops=micros * length * N * LANES * 40,
            bytes_accessed=micros * length * N * LANES * 12,
            transcendentals=micros * length * N * LANES,
        ),
        compiler_params=pltpu.CompilerParams(
            dimension_semantics=("arbitrary",), vmem_limit_bytes=40 * MEGA
        ),
        name="mix_forward",
    )(place, keep, *quarters, act, info, dt, *rules, rate, bias, start)


def mix_backward_kernel(
    x, place_ref, keep_ref, act_ref, info_ref, dt_ref, mask_ref, side_ref, rate_ref, bias_ref, start_ref,
    before_ref, step_ref, slope_ref, rows_ref, low_ref, last_ref, pull_ref,
    shared_ref, d_act_ref, grad_dt_ref, sums_ref, grad_rate_ref, final_ref,
    state_ref, after_ref, wide_a, wide_b, product_a, product_b, shown_a, shown_b,
    drive_ref, b_pull_ref, rate_pull_ref,
):
    micros, rows, _ = step_ref.shape
    block = pl.num_programs(0) - 1 - pl.program_id(0)
    rank = low_ref.shape[1]
    rate = rate_ref[...]
    mask = mask_ref[...]
    side = side_ref[...]
    skip = bias_ref[1:2]
    ones = jnp.ones((LANES, LANES), bf16)
    lane = lax.broadcasted_iota(jnp.int32, (N, LANES), 1)

    @pl.when(pl.program_id(0) == 0)
    def _():
        state_ref[...] = start_ref[...]
        after_ref[...] = last_ref[...]
        grad_rate_ref[...] = jnp.zeros_like(grad_rate_ref)
        grad_dt_ref[...] = jnp.zeros_like(grad_dt_ref)
        sums_ref[...] = jnp.zeros_like(sums_ref)

    for m in range(micros):
        drive_ref[m] = step_ref[m] * act_ref[m].astype(f32)
        wide_a[m] = spread(rows_ref, m, rows - 8, mask, side)

    def sixteen(turn, carried):
        states, afters, grads, grads_c, rates = (list(part) for part in carried)
        for half in range(2):
            base = pl.multiple_of(rows - 8 - turn * 16 - 8 * half, 8)
            wide, wide_next = (wide_a, wide_b) if half == 0 else (wide_b, wide_a)
            product, product_last = (product_a, product_b) if half == 0 else (product_b, product_a)
            seen, seen_last = (shown_a, shown_b) if half == 0 else (shown_b, shown_a)
            following = jnp.maximum(base - 8, 0)
            for m in range(micros):
                wide_next[m] = spread(rows_ref, m, following, mask, side)
                grads[m] = lane_sums(product_last, m, grads[m], lane, base + 8, ones)
                grads_c[m] = lane_sums(seen_last, m, grads_c[m], lane, base + 8, ones)
            b_parts = [[None] * 8 for _ in range(micros)]
            rate_parts = [[None] * 8 for _ in range(micros)]
            for j in range(7, -1, -1):
                for m in range(micros):
                    row = pl.ds(base + j, 1)
                    own = slice(N * j, N * j + N)
                    step = step_ref[m, row, :]
                    pull = pull_ref[m, row, :]
                    adjoint = wide[m, own, LANES:] * pull + states[m]
                    passed = jnp.exp(step * rate) * (
                        adjoint * keep_ref[micros * x + m, block * rows + base + j]
                    )
                    states[m] = passed
                    before = before_ref[m, base + j]
                    seen[m, own, :] = (afters[m] * pull).astype(bf16)
                    afters[m] = before
                    decay_pull = passed * before
                    shown = adjoint * wide[m, own, :LANES]
                    b_parts[m][j] = shown[:8] + shown[8:]
                    shown = decay_pull * rate
                    rate_parts[m][j] = shown[:8] + shown[8:]
                    rates[m] = rates[m] + decay_pull * step
                    product[m, own, :] = (adjoint * drive_ref[m, row, :]).astype(bf16)
            for m in range(micros):
                b_pull_ref[m, pl.ds(base, 8), :] = sum_rows(b_parts[m])
                rate_pull_ref[m, pl.ds(base, 8), :] = sum_rows(rate_parts[m])
        return tuple(tuple(part) for part in (states, afters, grads, grads_c, rates))

    zeros = tuple(jnp.zeros((N, LANES), f32) for m in range(micros))
    begin = (
        tuple(state_ref[m] for m in range(micros)),
        tuple(after_ref[m] for m in range(micros)),
        zeros, zeros, zeros,
    )
    states, afters, grads, grads_c, rates = lax.fori_loop(0, rows // 16, sixteen, begin)
    for m in range(micros):
        state_ref[m] = states[m]
        after_ref[m] = afters[m]
        grad_rate_ref[...] += rates[m]
        final_ref[m] = states[m]
        act = act_ref[m].astype(f32)
        pull = pull_ref[m]
        b_pull = b_pull_ref[m]
        d_act_ref[m] = pull * skip + step_ref[m] * b_pull
        d_pre = ((rate_pull_ref[m] + act * b_pull) * slope_ref[m]).astype(bf16).astype(f32)
        sums_ref[0:8] += jnp.sum(d_pre.reshape(-1, 8, LANES), axis=0)
        sums_ref[8:16] += jnp.sum((pull * act).reshape(-1, 8, LANES), axis=0)
        d_pre3 = three(d_pre, info_ref[m].T)
        shared_ref[m, :rank] = across(dt_ref[...], d_pre3, (1, 1))
        shared_ref[m, rank : rank + N] = lane_sums(product_b, m, grads[m], lane, 0, ones)
        shared_ref[m, rank + N :] = lane_sums(shown_b, m, grads_c[m], lane, 0, ones)
        grad_dt_ref[...] += across(low_ref[m], d_pre3, (1, 0))


def mix_backward(place, x, keep, act, info, dt, rules, rate, bias, start, saved):
    before, step, slope, rows, low, last, pull = saved
    length = act.shape[1]
    micros = start.shape[0]
    blocks = length // SCAN_ROWS
    spec = time_specs(micros, lambda i: blocks - 1 - i, x)
    rank = low.shape[1]
    width = rank + 2 * N
    product, tile = product_scratch(micros), tile_scratch(micros)
    return pl.pallas_call(
        functools.partial(mix_backward_kernel, x),
        grid=(blocks,),
        in_specs=[
            SCALARS, SCALARS, spec["act"], spec["info"],
            const(dt.shape), const(rules[0].shape), const(rules[1].shape),
            const(rate.shape), const(bias.shape), spec["fixed"],
            spec["states"], *[spec["tall"]] * 3, spec["turned"], spec["fixed"], spec["tall"],
        ],
        out_specs=[
            pl.BlockSpec((micros, width, SCAN_ROWS), lambda i: (0, 0, blocks - 1 - i)),
            spec["tall"], const(dt.shape), const((16, LANES)), const((N, LANES)), spec["fixed"],
        ],
        out_shape=[
            jax.ShapeDtypeStruct((micros, width, length), f32),
            jax.ShapeDtypeStruct((micros, length, LANES), f32),
            jax.ShapeDtypeStruct(dt.shape, f32),
            jax.ShapeDtypeStruct((16, LANES), f32),
            jax.ShapeDtypeStruct((N, LANES), f32),
            jax.ShapeDtypeStruct((micros, N, LANES), f32),
        ],
        scratch_shapes=[
            state_scratch(micros), state_scratch(micros), wide_scratch(micros), wide_scratch(micros),
            product, product, product, product, tile, tile, tile,
        ],
        cost_estimate=pl.CostEstimate(
            flops=micros * length * N * LANES * 60,
            bytes_accessed=micros * length * N * LANES * 12,
            transcendentals=micros * length * N * LANES,
        ),
        compiler_params=pltpu.CompilerParams(
            dimension_semantics=("arbitrary",), vmem_limit_bytes=40 * MEGA
        ),
        name="mix_backward",
    )(place, keep, act, info, dt, *rules, rate, bias, start, *saved)


def shifted(scratch_ref, j, rows):
    return scratch_ref[8 - j : 8 - j + rows, :]


def conv_forward_kernel(inner_ref, edge_ref, info_ref, taps_ref, wx_ref,
                        act_ref, conv_ref, shared_ref, scratch_ref):
    rows = inner_ref.shape[1]
    scratch_ref[:8] = edge_ref[0]
    scratch_ref[8:] = inner_ref[0]
    info = info_ref[0].T
    total = taps_ref[K : K + 1] + taps_ref[0:1] * inner_ref[0]
    for j in range(1, K):
        total = total + taps_ref[j : j + 1] * (shifted(scratch_ref, j, rows) * info[:, 3 + j : 4 + j])
    conv_ref[0] = total
    act = (total * jax.nn.sigmoid(total)).astype(bf16)
    act_ref[0] = act
    shared_ref[0] = across(wx_ref[...], three(act.astype(f32), info), (1, 1))


def conv_forward(inner, edge, info, taps, wx):
    micros, rows, _ = inner.shape
    one = pl.BlockSpec((1, rows, LANES), lambda m: (m, 0, 0))
    width = wx.shape[0]
    return call(
        conv_forward_kernel, "conv_forward", (micros,),
        [
            one, pl.BlockSpec((1, 8, LANES), lambda m: (m, 0, 0)),
            pl.BlockSpec((1, 8, rows), lambda m: (m, 0, 0)), const(taps.shape), const(wx.shape),
        ],
        [one, one, pl.BlockSpec((1, width, rows), lambda m: (m, 0, 0))],
        [
            shape_of(inner.shape, bf16), shape_of(inner.shape, f32),
            shape_of((micros, width, rows), f32),
        ],
        [pltpu.VMEM((rows + 8, LANES), f32)],
        2 * micros * rows * wx.size, 4 * MEGA,
        (inner, edge, info, taps, wx),
    )


def conv_backward_kernel(x, place_ref, own_ref, x_ref, core_ref, both_ref, d_act_ref, conv_ref, inner_ref,
                         edge_ref, act_ref, info_ref, taps_ref, wx_ref,
                         d_inner_ref, grad_x_ref, sums_ref, head_ref, last_ref, scratch_ref, ahead_ref):
    rows = inner_ref.shape[1]
    micro = pl.program_id(0)
    info = info_ref[0].T

    @pl.when(micro == 0)
    def _():
        grad_x_ref[...] = jnp.zeros_like(grad_x_ref)
        sums_ref[...] = jnp.zeros_like(sums_ref)

    shared = one_of_four(place_ref, x, micro, own_ref, x_ref, core_ref, both_ref).astype(bf16)
    d_act = d_act_ref[0] + masked_sum(across(shared, wx_ref[...], (0, 0)), info)
    grad_x_ref[...] += across(shared, three(act_ref[0].astype(f32), info), (1, 0))
    conv = conv_ref[0]
    sigma = jax.nn.sigmoid(conv)
    d_conv = d_act * (sigma * (1.0 + conv * (1.0 - sigma)))
    head_ref[0] = d_conv[:8]
    scratch_ref[:8] = edge_ref[0]
    scratch_ref[8:] = inner_ref[0]
    ahead_ref[rows:] = jnp.zeros((8, LANES), f32)
    total = taps_ref[0:1] * d_conv
    sums_ref[0:8] += jnp.sum((d_conv * inner_ref[0]).reshape(-1, 8, LANES), axis=0)
    for j in range(1, K):
        masked = d_conv * info[:, 3 + j : 4 + j]
        pulled = (masked * shifted(scratch_ref, j, rows)).reshape(-1, 8, LANES)
        sums_ref[8 * j : 8 * j + 8] += jnp.sum(pulled, axis=0)
        ahead_ref[:rows] = masked
        total = total + taps_ref[j : j + 1] * ahead_ref[j : j + rows, :]
    sums_ref[8 * K : 8 * K + 8] += jnp.sum(d_conv.reshape(-1, 8, LANES), axis=0)
    d_inner_ref[0] = total.astype(bf16)
    last_ref[0] = total[rows - 8 :]


def conv_backward(place, x, quarters, d_act, conv, inner, edge, act, info, taps, wx):
    micros, rows, _ = d_act.shape
    first = micros * x
    mine = pl.BlockSpec((1, rows, LANES), lambda m: (m, 0, 0))
    one = pl.BlockSpec((1, rows, LANES), lambda m: (first + m, 0, 0))
    eight = pl.BlockSpec((1, 8, LANES), lambda m: (m, 0, 0))
    sums = (8 * (K + 1), LANES)
    return call(
        functools.partial(conv_backward_kernel, x), "conv_backward", (micros,),
        [
            SCALARS, *[const(quarters[0].shape)] * 4, mine, one, one,
            pl.BlockSpec((1, 8, LANES), lambda m: (first + m, 0, 0)), one,
            pl.BlockSpec((1, 8, rows), lambda m: (first + m, 0, 0)), const(taps.shape), const(wx.shape),
        ],
        [mine, const(wx.shape), const(sums), eight, eight],
        [
            shape_of(d_act.shape, bf16), shape_of(wx.shape, f32), shape_of(sums, f32),
            shape_of((micros, 8, LANES), f32), shape_of((micros, 8, LANES), f32),
        ],
        [pltpu.VMEM((rows + 8, LANES), f32), pltpu.VMEM((rows + 8, LANES), f32)],
        4 * micros * rows * wx.size, 6 * MEGA,
        (place, *quarters, d_act, conv, inner, edge, act, info, taps, wx),
    )


def pack_kernel(flag_ref, after_ref, w_ref, *out_refs):
    half = w_ref.shape[-1] // 2
    for turn, out_ref in enumerate(out_refs):
        lanes = pl.ds(pl.multiple_of((turn ^ flag_ref[0]) * half, half), half)
        if len(w_ref.shape) == 3:
            out_ref[0] = w_ref[0, :, lanes].astype(bf16)
            continue
        for side in range(2):
            out_ref[0, :, side * half : side * half + half] = w_ref[0, :, side, lanes].astype(bf16)


def pack(flag, after, weight):
    kinds, rows = weight.shape[:2]
    width = weight.size // (kinds * rows * 2)
    return call(
        pack_kernel, "pack", (kinds,),
        [SCALARS, SCALARS, pl.BlockSpec((1,) + weight.shape[1:], lambda k: (k,) + (0,) * (weight.ndim - 1))],
        [pl.BlockSpec((1, rows, width), lambda k: (k, 0, 0))] * 2,
        [shape_of((kinds, rows, width), bf16)] * 2,
        [], 0, weight.size * 6, (flag, after, weight),
    )


def adam_kernel(rate, flag_ref, clip_ref, w_ref, m_ref, v_ref, *refs):
    pieces, (grad_ref, new_ref, first_ref, second_ref) = refs[:4], refs[4:]
    half = w_ref.shape[-1] // 2
    clip = clip_ref[0]
    for plane in range(2):
        for turn in range(2):
            lanes = pl.ds(pl.multiple_of((turn ^ flag_ref[0]) * half, half), half)
            at = (0, slice(None), plane, lanes)
            grad = pieces[2 * plane + turn][0].astype(f32)
            new, first, second = adam_update(w_ref[at], grad, m_ref[at], v_ref[at], clip, rate)
            grad_ref[at] = grad
            new_ref[at] = new
            first_ref[at] = first
            second_ref[at] = second


def adam(flag, clip, weight, first, second, pieces, rate):
    kinds, rows, _, chans = weight.shape
    block = min(rows, 64)
    full = pl.BlockSpec((1, block, 2, chans), lambda k, r: (k, r, 0, 0))
    piece = pl.BlockSpec((1, block, chans // 2), lambda k, r: (k, r, 0))
    return call(
        functools.partial(adam_kernel, rate), "adam", (kinds, rows // block),
        [SCALARS, SCALARS, full, full, full] + [piece] * 4,
        [full] * 4,
        [shape_of(weight.shape, f32)] * 4,
        [], weight.size * 20, weight.size * 32,
        (flag, clip, weight, first, second, *pieces),
    )


def body(
    groups, parts, chans,
    tokens_in, modality, starts, cotangent,
    in_weight, in_first, in_second,
    dt_weight, dt_first, dt_second,
    out_weight, out_first, out_second,
    x_weight, x_first, x_second,
    channel_params, channel_first, channel_second,
    gain, gain_first, gain_second,
):
    micros, tok_rows, part_width = tokens_in.shape
    model = gain.shape[0]
    chan_width = in_weight.shape[3]
    half = chan_width // 2
    own = half // chans
    cores = chans // 2
    inner_all = chan_width * chans
    x_width = x_weight.shape[1]
    rank = x_width - 2 * N
    dt_rows = dt_weight.shape[1]
    span = parts * tok_rows
    edge = K - 1
    t_at = lax.axis_index("t")
    p_at = lax.axis_index("p")
    c_at = lax.axis_index("c")
    z_at, y_at = p_at // 2, p_at % 2
    x_at, core_at = c_at // cores, c_at % cores
    s_at = t_at * parts + p_at
    slice_at = s_at // (2 * groups)
    everywhere = ("t", "p", "c")
    place = jnp.stack([x_at, core_at, y_at, z_at % 2]).astype(jnp.int32)
    half_at = (s_at % (2 * groups)) // groups

    def flat(t, p, c):
        return (t * parts + p) * chans + c

    def part_of(c, j):
        return 2 * (2 * (c % cores) + j) + c // cores

    devices = [(t, p, c) for t in range(groups) for p in range(parts) for c in range(chans)]

    def first_hop(turn):
        pairs = []
        for t, p, c in devices:
            s = t * parts + p
            to_slice, i = s // (2 * groups), (s % (2 * groups)) // groups
            j = turn ^ (to_slice // cores)
            to = flat(s % groups, 2 * (2 * (c % cores) + j) + i, c // cores * cores + to_slice % cores)
            pairs.append((flat(t, p, c), to))
        return pairs

    def second_hop(turn):
        return [
            (flat(t, p, c), flat(t, p - p % 2 + c // cores, (turn ^ (p % 2)) * cores + c % cores))
            for t, p, c in devices
        ]

    def home(turn):
        pairs = []
        for t, p, c in devices:
            s = t * parts + p
            i = (s % (2 * groups)) // groups
            keeper = flat(s % groups, part_of(c, turn ^ i), s // (2 * groups))
            pairs.append((keeper, flat(t, p, c)))
        return pairs

    small_pairs = [(flat(t, p, c), flat(t, part_of(c, p % 2), p // 2)) for t, p, c in devices]

    def send(value, pairs, back=False):
        if back:
            pairs = [(b, a) for a, b in pairs]
        return lax.ppermute(value, everywhere, pairs)

    def swap(value, axis, distance):
        return lax.ppermute(value, axis, [(i, i ^ distance) for i in range(lax.axis_size(axis))])

    def crossed(pair, flag):
        first, second = pair
        return jnp.where(flag == 0, first, second), jnp.where(flag == 0, second, first)

    between = y_at ^ (z_at % 2)

    def token(*values):
        return sum(value[(0,) * value.ndim].astype(f32) for value in values)[None]

    def weights_there(pair):
        pair = [send(value, first_hop(turn)) for turn, value in enumerate(pair)]
        first = token(*pair)
        pair = crossed(pair, between)
        pair = [send(value, second_hop(turn)) for turn, value in enumerate(pair)]
        return pair, first, token(pair[0])

    def there_whole(pair):
        if groups > 1:
            pair = [lax.all_gather(value, "t", axis=1, tiled=True) for value in pair]
        return tuple(pair)

    group_squares = []

    def returned(pair):
        if groups > 1:
            pair = [
                lax.psum_scatter(value, "t", scatter_dimension=1, tiled=True) for value in pair
            ]
            group_squares.extend(jnp.sum(value * value) for value in pair)
            pair = [value.astype(bf16) for value in pair]
        return [send(value, home(turn)) for turn, value in enumerate(pair)]

    def along_groups(value, by):
        pairs = [(i, i + by) for i in range(groups) if 0 <= i + by < groups]
        return lax.ppermute(value, "t", pairs)

    def over(value, axis):
        count = lax.axis_size(axis)
        terms = [swap(value, axis, k) if k else value for k in range(count)]
        while len(terms) > 1:
            terms = [a + b for a, b in zip(terms[0::2], terms[1::2])]
        return terms[0]

    def over_chans(value):
        return over(value, "c")

    def pick(value, at, axis):
        return lax.dynamic_index_in_dim(value, at, axis, keepdims=False)

    def scattered_chans(sent, keep, late=None):
        total = keep + swap(sent, "c", 1).astype(f32)
        away = pick(total, 1 - x_at, 0)
        if late is not None:
            away = away + 0.0 * late[0]
        got = swap(away.astype(bf16), "c", cores)
        return pick(total, x_at, 0) + got.astype(f32)

    def gathered_chans(value):
        across_x = swap(value, "c", cores)
        across_core = swap(value, "c", 1)
        return (value, across_x, across_core, swap(across_x, "c", 1))

    def scattered_parts(products, late=None):
        keeps = [keep for _, keep in products]
        count = len(keeps)

        def hop(pieces, distance):
            pieces = jnp.concatenate([piece.astype(bf16) for piece in pieces], 0)
            return jnp.split(swap(pieces, "p", distance), count, 0)

        got = hop([sent for sent, _ in products], 1)
        totals = [keep + piece.astype(f32) for keep, piece in zip(keeps, got)]
        arrived = totals[0]
        totals = [total.reshape(total.shape[0], -1, 2, *total.shape[2:]) for total in totals]
        got = hop([pick(total, 1 - z_at % 2, 2) for total in totals], 2)
        totals = [pick(total, z_at % 2, 2) + piece.astype(f32) for total, piece in zip(totals, got)]
        away = [pick(total, 1 - z_at // 2, 1) for total in totals]
        if late is not None:
            away = [value + 0.0 * late[0] for value in away]
        got = hop(away, 4)
        totals = [pick(total, z_at // 2, 1) + piece.astype(f32) for total, piece in zip(totals, got)]
        return jnp.concatenate(totals, 0), arrived

    def after(value, *others):
        return value + (0.0 * token(*others)).astype(jnp.int32)

    def summed(values, kind, fills, late):
        fills = list(fills)

        def fill(arrived):
            return token(*fills.pop(0)(after(place, arrived)))[0] if fills else None

        def tied(arrived, ran):
            return arrived if ran is None else arrived + 0.0 * ran

        away = jnp.stack([pick(value, 1 - core_at, 0) for value in values]).astype(kind)
        total = jnp.stack([pick(value, core_at, 0) for value in values])
        total = total + swap(away, "c", 1).astype(f32)
        ran = fill(total)
        away = pick(total, 1 - x_at, 0).astype(kind)
        total = pick(total, x_at, 0) + swap(away, "c", cores).astype(f32)
        distance = 1
        while distance < parts:
            last, ran = ran, fill(total)
            total = tied(total, last)
            if distance in late:
                total = total + 0.0 * late[distance][0]
            total = total.astype(kind)
            total = total.astype(f32) + swap(total, "p", distance).astype(f32)
            distance *= 2
        total = tied(total, ran)
        return gathered_chans(total.astype(kind))

    def over_all(value):
        value = over(over(value, "c"), "p")
        return lax.psum(value, "t") if groups > 1 else value

    extra = jnp.pad(modality.astype(bf16)[:, None, :], ((0, 0), (0, 15), (0, part_width - tok_rows)))
    tokens_all = lax.all_gather(jnp.concatenate([tokens_in, extra], 1), "p")
    flag = (slice_at // cores).astype(jnp.int32)[None]
    owner_flag = half_at.astype(jnp.int32)[None]
    w_in, in_arrived, _ = weights_there(pack(flag, jnp.zeros((1,), f32), in_weight))
    w_in = there_whole(w_in)
    small = jnp.concatenate([x_weight.reshape(3 * x_width, chan_width), channel_params], 0)
    own_lanes = y_at * half + z_at * own
    small = send(lax.dynamic_slice_in_dim(small, own_lanes, own, 1), small_pairs)
    dt16 = dt_weight.astype(bf16)
    dt_pair = crossed((dt16[..., :half], dt16[..., half:]), flag[0])
    out_pair = pack(flag, in_arrived, out_weight)
    out_rows = out_weight.shape[1]
    both = [jnp.concatenate(pair, 1) for pair in zip(out_pair, dt_pair)]
    both, _, _ = weights_there(both)
    w_out = there_whole([value[:, :out_rows] for value in both])
    dt_part = jnp.concatenate(
        crossed(there_whole([value[:, out_rows:] for value in both]), x_at), 1
    )
    dt_blocks = []
    for distance in range(chans):
        block = lax.dynamic_slice_in_dim(dt_part, (c_at ^ distance) * own, own, 2)
        dt_blocks.append(swap(block, "c", distance) if distance else block)
    dt_blocks = jnp.stack(dt_blocks)
    w_dt = jnp.concatenate([pick(dt_blocks, c_at ^ k, 0) for k in range(chans)], 1)
    w_dt = w_dt.transpose(1, 0, 2).reshape(rank, 3 * own)
    back_all = lax.all_gather(cotangent, "p")
    positions = t_at * span - edge + jnp.arange(span + 2 * edge, dtype=jnp.int32)
    segment = jnp.sum((starts[:, None, :] <= positions[None, :, None]).astype(jnp.int32), axis=2)
    keep_mask = 1.0 - jnp.any(
        starts[:, None, :] == positions[None, edge : edge + span, None], axis=2
    ).astype(f32)
    same_doc = [
        (segment[:, edge - j : 2 * edge - j + span] == segment[:, edge:]).astype(f32)
        for j in range(1, K)
    ]
    squares = jnp.sum(jnp.square(tokens_all[:, :, :tok_rows].astype(f32)), axis=-1)
    squares = over_chans(squares).transpose(1, 0, 2).reshape(micros, span)
    inverse = lax.rsqrt(squares / model + NORM_EPS)
    kinds = tokens_all[:, :, tok_rows, :tok_rows].transpose(1, 0, 2).reshape(micros, span)
    kinds = kinds.astype(jnp.int32)
    rows = [inverse, *((kinds == k).astype(f32) for k in range(3))]
    rows += [same[:, :span] for same in same_doc] + [jnp.zeros_like(inverse)]
    info3 = jnp.stack(rows, 1)
    info = jnp.stack([row.reshape(-1) for row in rows], 0)
    inv_own = lax.dynamic_slice_in_dim(inverse, p_at * tok_rows, tok_rows, 1)[..., None]
    gain_part = lax.dynamic_slice_in_dim(gain, c_at * part_width, part_width, 0)[None]

    w_x = small[: 3 * x_width].astype(bf16).reshape(3, x_width, own)
    w_x = w_x.transpose(1, 0, 2).reshape(x_width, 3 * own)
    channel = small[3 * x_width :]
    taps = channel[:8]
    biases = jnp.pad(channel[K + 1 : K + 3], ((0, 6), (0, 0)))
    neg_rate = -jnp.exp(channel[K + 3 :])
    rules = lane_rules()

    grad_dt_sum = grad_x_sum = grad_chan_sum = grad_gain_sum = 0.0
    pairs_of = range(micros // 2)
    zero_state = jnp.zeros((2, N, own), f32)
    everything = Tiles(micros, parts, tok_rows)
    twos = [Tiles(2, parts, tok_rows, 2 * x) for x in pairs_of]
    normed, sent, keep = inner_product(everything, place, tokens_all, info, gain_part, w_in)
    inner = scattered_chans(sent, keep).reshape(micros, span, own)
    edge_rows = jnp.zeros((micros, 8, own), f32)
    if groups > 1:
        edge_rows = along_groups(inner[:, span - 8 :], 1)
    act, conv, shared = conv_forward(inner, edge_rows, info3, taps, w_x)
    quarters = summed(
        [shared[2 * x : 2 * x + 2] for x in pairs_of], f32, [], {}
    )
    sent, keep = gate_product(everything, after(place, *quarters), normed, back_all, info, w_in, w_out)
    pair = scattered_chans(sent, keep).reshape(micros, span, 2 * own)
    held = []
    for x in pairs_of:
        args = (x, keep_mask, quarters, act, info3, w_dt, rules, neg_rate, biases)
        order = after(place, sent if x == 0 else held[-1][0])
        state_in = zero_state
        if groups > 1:
            first_pass = mix_forward(order, *args, zero_state)
            ends, step = first_pass[6], first_pass[2]
            passed_all = jnp.exp(jnp.sum(step, axis=1)[:, None, :] * neg_rate)
            passed_all = passed_all * jnp.prod(keep_mask[2 * x : 2 * x + 2], axis=1)[:, None, None]
            for _ in range(groups - 1):
                state_in = along_groups(passed_all * state_in + ends, 1)
        held.append(mix_forward(order, *args, state_in))

    all_pairs, pulls = [], []
    for x in pairs_of:
        kinds_out, pull = blend(x, held[x][0], act, pair, biases)
        pulls.append(pull)
        all_pairs.append(gathered_chans(kinds_out.reshape(2, 2 * span, own)))
    order = place
    shares, d_acts, mix_sums, d_rate = [], [], 0.0, 0.0
    for x in pairs_of:
        saved = (*held[x][1:], pulls[x])
        args = (x, keep_mask, act, info3, w_dt, rules, neg_rate, biases)
        adj_in = zero_state
        if groups > 1:
            ends = mix_backward(order, *args, zero_state, saved)[5]
            passed_all = jnp.exp(jnp.sum(saved[1], axis=1)[:, None, :] * neg_rate)
            passed_all = passed_all * jnp.prod(keep_mask[2 * x : 2 * x + 2], axis=1)[:, None, None]
            for _ in range(groups - 1):
                adj_in = along_groups(passed_all * adj_in + ends, -1)
        share, d_act, grad_dt, sums, grad_rate, _ = mix_backward(order, *args, adj_in, saved)
        order = after(place, d_act, *(blocks[k] for blocks in all_pairs for k in (1, 2)))
        shares.append(share)
        d_acts.append(d_act)
        grad_dt_sum += grad_dt
        mix_sums += jnp.sum(sums.reshape(2, 8, own), axis=1)
        d_rate += grad_rate * neg_rate

    kept = f32 if groups > 1 else bf16

    def kindred(which):
        return ((1, span, own), lambda m, x: (which, m, 0))

    def rows_at(width):
        return ((span, width), lambda m, x: (2 * x + m, 0))

    raw_at = ((parts, 1, tok_rows, part_width), lambda m, x: (0, 2 * x + m, 0, 0))
    count = len(all_pairs)
    products, large = [], {}

    def out_fill(order):
        for x in pairs_of:
            products.append(out_product(twos[x], order, all_pairs[x], info, w_out))
            order = after(place, products[-1][0])
        return [sent for sent, _ in products]

    def grad_fill(name, lefts, left_at, which):
        def run(order):
            *pieces, square = weight_grad(
                order, info, lefts, left_at, all_pairs, kindred(which), span, kept
            )
            large[name] = (pieces, square)
            return (square,)

        return run

    fills = [
        out_fill,
        grad_fill("out", [back_all] * count, raw_at, 0),
    ]
    quarters = summed(shares, bf16, fills, {})
    g_out, out_sq = large["out"]
    g_out = returned(g_out)
    outs, _ = scattered_parts(products)

    d_inners = []
    for x in pairs_of:
        d_inner, grad_x, sums, head, last = conv_backward(
            place, x, quarters, d_acts[x], conv, inner, edge_rows, act, info3, taps, w_x
        )
        if groups > 1:
            ahead = along_groups(head, -1)[:, :edge]
            for j in range(1, K):
                gone = taps[j] * ahead * same_doc[j - 1][2 * x : 2 * x + 2, span:, None]
                last = last.at[:, 8 - j :].add(gone[:, :j])
            d_inner = jnp.concatenate([d_inner[:, : span - 8], last.astype(bf16)], 1)
        d_inners.append(d_inner.reshape(2 * span, own))
        grad_x_sum += grad_x
        grad_chan_sum += jnp.sum(sums.reshape(K + 1, 8, own), axis=1)
    grad_chan_sum = jnp.concatenate([grad_chan_sum, mix_sums, d_rate], 0)
    inners = gathered_chans(jnp.concatenate(d_inners, 0))
    grad_fill("gate", [normed] * count, rows_at(part_width), 1)(after(place, *d_inners))
    g_gate, gate_sq = large["gate"]
    g_gate = returned(g_gate)

    *g_inner, inner_sq = weight_grad(
        after(place, gate_sq), info, [normed] * count, rows_at(part_width), [inners] * count,
        rows_at(own), span, kept,
    )
    g_inner = returned(g_inner)
    order = after(place, inner_sq)
    products = []
    for x in pairs_of:
        sent, keep, gain_rows = normed_grad(
            twos[x], order, all_pairs[x], inners, info, tokens_all, w_in
        )
        grad_gain_sum += jnp.sum(gain_rows, axis=0)
        products.append((sent, keep))
        order = after(place, sent, *g_gate)
    rows_back, _ = scattered_parts(products)

    grad_x_sum = grad_x_sum.reshape(x_width, 3, own).transpose(1, 0, 2)
    grad_dt_sum = grad_dt_sum.reshape(rank, 3, own).transpose(1, 0, 2)
    g_small = jnp.concatenate(
        [grad_x_sum.reshape(-1, own), grad_dt_sum.reshape(-1, own), grad_chan_sum], 0
    )
    if groups > 1:
        g_small = lax.psum(g_small, "t")
        large_sq = sum(group_squares)
    else:
        large_sq = jnp.sum(out_sq) + jnp.sum(gate_sq) + jnp.sum(inner_sq)
    local_sq = large_sq + jnp.sum(g_small * g_small) / groups
    here = (jnp.arange(chans) == c_at).astype(f32)
    tail = jnp.concatenate([(here[:, None] * grad_gain_sum).reshape(-1), local_sq[None]])
    tail = over_all(tail + 0.0 * token(*g_inner)[0])
    grad_gain = tail[:model]
    grad_norm = jnp.sqrt(tail[model] + jnp.sum(grad_gain * grad_gain))
    clip_scale = CLIP_LIMIT / jnp.maximum(grad_norm, CLIP_LIMIT)

    grad_out = jnp.concatenate(crossed(g_out, half_at), -1).astype(f32)
    in_pieces = (*g_inner, *g_gate)
    small_back = lax.all_gather(send(g_small.astype(bf16), small_pairs, True), "p")
    small_back = small_back.reshape(chans, 2, -1, own).transpose(2, 1, 0, 3)
    small_back = small_back.reshape(-1, chan_width).astype(f32)
    grad_x = small_back[: 3 * x_width].reshape(3, x_width, chan_width)
    grad_dt = small_back[3 * x_width : 3 * x_width + 3 * rank].reshape(3, rank, chan_width)
    grad_dt = lax.dynamic_slice_in_dim(grad_dt, s_at * dt_rows, dt_rows, 1)
    grad_chan = small_back[3 * x_width + 3 * rank :]

    tok_float = tokens_in.astype(f32)
    mixed = (tok_float + outs).astype(bf16)
    dt_new, dt_first_new, dt_second_new = adam_update(
        dt_weight, grad_dt, dt_first, dt_second, clip_scale, rank ** (-0.5)
    )
    out_new, out_first_new, out_second_new = adam_update(
        out_weight, grad_out, out_first, out_second, clip_scale, inner_all ** (-0.5)
    )
    x_new, x_first_new, x_second_new = adam_update(
        x_weight, grad_x, x_first, x_second, clip_scale, inner_all ** (-0.5)
    )
    chan_new, chan_first_new, chan_second_new = adam_update(
        channel_params, grad_chan, channel_first, channel_second, clip_scale, 0.5
    )
    gain_new, gain_first_new, gain_second_new = adam_update(
        gain, grad_gain, gain_first, gain_second, clip_scale, 0.5
    )
    grad_in, in_new, in_first_new, in_second_new = adam(
        after(owner_flag, x_new, chan_new, dt_new), clip_scale[None], in_weight, in_first, in_second, in_pieces, model ** (-0.5)
    )
    d_own = rows_back
    x_hat_own = tok_float * inv_own
    d_hat = d_own * gain_part
    mean = jnp.sum(d_hat * x_hat_own, axis=-1) + 0.0 * token(in_new)
    mean = over_chans(mean)[..., None] / model
    input_grad = cotangent.astype(f32) + inv_own * (d_hat - x_hat_own * mean)
    return (
        mixed, input_grad, grad_norm,
        grad_in, in_new, in_first_new, in_second_new,
        grad_dt, dt_new, dt_first_new, dt_second_new,
        grad_out, out_new, out_first_new, out_second_new,
        grad_x, x_new, x_first_new, x_second_new,
        grad_chan, chan_new, chan_first_new, chan_second_new,
        grad_gain, gain_new, gain_first_new, gain_second_new,
        in_new.astype(bf16), dt_new.astype(bf16), out_new.astype(bf16), x_new.astype(bf16),
    )


def solution(mesh):
    chans = mesh.shape["ch"]
    parts = 2 * chans
    groups = mesh.shape["seq"] // parts
    inside = Mesh(mesh.devices.reshape(groups, parts, chans), ("t", "p", "c"))
    seq = ("t", "p")
    tok = P(None, seq, "c")
    wide = P(None, seq, None, "c")
    rows = P(None, seq, "c")
    flat = P(None, None, "c")
    chan = P(None, "c")
    return jax.shard_map(
        functools.partial(body, groups, parts, chans),
        mesh=inside,
        in_specs=(tok, P(None, seq), P(), tok)
        + (wide,) * 3 + (rows,) * 3 + (rows,) * 3 + (flat,) * 3 + (chan,) * 3 + (P(),) * 3,
        out_specs=(tok, tok, P())
        + (wide,) * 4 + (rows,) * 4 + (rows,) * 4 + (flat,) * 4 + (chan,) * 4 + (P(),) * 4
        + (wide, rows, rows, flat),
        check_vma=False,
    )
```

```python
import functools

import jax
import jax.numpy as jnp
from jax import lax
from jax.experimental import pallas as pl
from jax.experimental.pallas import tpu as pltpu
from jax.sharding import Mesh
from jax.sharding import PartitionSpec as P

N = 16
K = 4
STEP = 10

NORM_EPS = 1e-05
BETA_ONE = 0.9
BETA_TWO = 0.95
ADAM_EPS = 1e-08
DECAY = 0.1
CLIP_LIMIT = 1.0
LANES = 128
SCAN_ROWS = 128
MEGA = 1024 * 1024
GROUP = 2
f32 = jnp.float32
bf16 = jnp.bfloat16


def silu_grad(value):
    sigma = jax.nn.sigmoid(value)
    return sigma * (1.0 + value * (1.0 - sigma))


def adam_update(weight, gradient, first_moment, second, clip_scale, step_rate):
    clipped = gradient * clip_scale
    first_new = BETA_ONE * first_moment + (1.0 - BETA_ONE) * clipped
    second_new = BETA_TWO * second + (1.0 - BETA_TWO) * clipped * clipped
    first_hat = first_new * (1.0 / (1.0 - BETA_ONE**STEP))
    second_hat = second_new * (1.0 / (1.0 - BETA_TWO**STEP))
    weight_new = weight - step_rate * (
        first_hat / (jnp.sqrt(second_hat) + ADAM_EPS) + DECAY * weight
    )
    return (weight_new, first_new, second_new)


def sum_rows(parts):
    at = lax.broadcasted_iota(jnp.int32, parts[0].shape, 0)
    for distance in (1, 2, 4):
        low = at % (2 * distance) < distance
        parts = [
            jnp.where(low, a, b) + pltpu.roll(jnp.where(low, b, a), distance, 0)
            for a, b in zip(parts[0::2], parts[1::2])
        ]
    return parts[0]


def lane_rules():
    lanes = jnp.arange(LANES)
    used = lanes % (LANES // 2) < 3 * N
    mask = ((lanes[None, :] % N == jnp.arange(N)[:, None]) & used[None, :]).astype(f32)
    side = (lanes[:, None] // (LANES // 2) == jnp.arange(2 * LANES)[None, :] // LANES).astype(bf16)
    return mask, side


def matmul(left, right):
    return jnp.dot(left, right, preferred_element_type=f32)


def spread(rows_ref, m, base, mask, side):
    left = [rows_ref[m, pl.ds(base + j, 1), :] * mask for j in range(8)]
    return matmul(jnp.concatenate(left, 0).astype(bf16), side)


def lane_sums(product_ref, m, grads, lane, base, ones):
    sums = matmul(product_ref[m], ones)
    for j in range(8):
        grads = jnp.where(lane == base + j, sums[N * j : N * j + N], grads)
    return grads


def turned(ref, turn, x_at):
    width = ref.shape[-1] // 2
    return pl.ds(pl.multiple_of((turn ^ x_at) * width, width), width)


def three(tile, info):
    return jnp.concatenate([(tile * info[:, k + 1 : k + 2]).astype(bf16) for k in range(3)], -1)


def across(left, right, dims):
    return lax.dot_general(left, right, ((dims[0:1], dims[1:2]), ((), ())), preferred_element_type=f32)


def stacked(ref):
    kinds, rows, cols = ref.shape
    return ref[...].reshape(kinds * rows, cols)


def split_blocks(total, place_ref, sent_ref, keep_ref, scratch_ref, offset):
    scratch_ref[...] = total
    core = place_ref[1]
    for x in range(2):
        away = pl.ds(pl.multiple_of((2 * x + 1 - core) * LANES, LANES), LANES)
        here = pl.ds(pl.multiple_of((2 * x + core) * LANES, LANES), LANES)
        sent_ref[x, :, offset : offset + LANES] = scratch_ref[:, away].astype(bf16)
        keep_ref[x, :, offset : offset + LANES] = scratch_ref[:, here]


def tile_rows(ref):
    return ref[...].reshape(-1, ref.shape[-1])


def wide_product(tile_ref, info, w_refs, scratch_ref, x_at):
    total = None
    for turn, w_ref in enumerate(w_refs):
        left = three(tile_ref[:, turned(tile_ref, turn, x_at)], info)
        part = across(left, stacked(w_ref), (1, 0))
        total = part if total is None else total + part
    return total


def inner_kernel(place_ref, x_ref, info_ref, gain_ref, w0_ref, w1_ref,
                 normed_ref, sent_ref, keep_ref, tile_ref, scratch_ref):
    info = info_ref[...].T
    normed = tile_rows(x_ref).astype(f32) * info[:, :1] * gain_ref[...]
    normed = normed.astype(bf16)
    normed_ref[...] = normed
    tile_ref[...] = normed.astype(f32)
    total = wide_product(tile_ref, info, (w0_ref, w1_ref), scratch_ref, place_ref[0])
    split_blocks(total, place_ref, sent_ref, keep_ref, scratch_ref, 0)


def gate_kernel(place_ref, normed_ref, back_ref, info_ref, g0_ref, g1_ref, o0_ref, o1_ref,
                sent_ref, keep_ref, tile_ref, scratch_ref):
    info = info_ref[...].T
    tile_ref[...] = normed_ref[...].astype(f32)
    total = wide_product(tile_ref, info, (g0_ref, g1_ref), scratch_ref, place_ref[0])
    split_blocks(total, place_ref, sent_ref, keep_ref, scratch_ref, 0)
    tile_ref[...] = tile_rows(back_ref).astype(f32)
    total = wide_product(tile_ref, info, (o0_ref, o1_ref), scratch_ref, place_ref[0])
    split_blocks(total, place_ref, sent_ref, keep_ref, scratch_ref, LANES)


def gathered(scratch_ref, place_ref, refs):
    at = 2 * place_ref[0] + place_ref[1]
    for distance, ref in zip((0, 2, 1, 3), refs):
        lanes = pl.ds(pl.multiple_of((at ^ distance) * LANES, LANES), LANES)
        scratch_ref[:, lanes] = tile_of(ref).astype(f32)


def tile_of(ref):
    return ref[...].reshape(-1, ref.shape[-1])


def split_parts(total, place_ref, sent_ref, keep_ref):
    y = place_ref[2]
    half = total.shape[0] // 2
    low, high = total[:half], total[half:]
    mine = jnp.full(low.shape, y, jnp.int32) == 0
    sent_ref[...] = jnp.where(mine, high, low).astype(bf16).reshape(sent_ref.shape)
    keep_ref[...] = jnp.where(mine, low, high).reshape(keep_ref.shape)


def out_kernel(place_ref, a_ref, b_ref, c_ref, d_ref, info_ref, w0_ref, w1_ref,
               sent_ref, keep_ref, tile_ref, total_ref):
    gathered(tile_ref, place_ref, (a_ref, b_ref, c_ref, d_ref))
    left = three(tile_ref[...], info_ref[...].T)
    width = tile_ref.shape[1]
    for turn, w_ref in enumerate((w0_ref, w1_ref)):
        total = None
        for k in range(3):
            part = across(left[:, k * width : (k + 1) * width], w_ref[k], (1, 1))
            total = part if total is None else total + part
        total_ref[:, turned(total_ref, turn, place_ref[0])] = total
    split_parts(total_ref[...], place_ref, sent_ref, keep_ref)


def normed_kernel(place_ref, ga_ref, gb_ref, gc_ref, gd_ref, ia_ref, ib_ref, ic_ref, id_ref,
                  info_ref, x_ref, g0_ref, g1_ref, i0_ref, i1_ref,
                  sent_ref, keep_ref, gain_ref, tile_ref, total_ref):
    info = info_ref[...].T
    width = tile_ref.shape[1]
    gathered(tile_ref, place_ref, (ga_ref, gb_ref, gc_ref, gd_ref))
    gates = three(tile_ref[...], info)
    gathered(tile_ref, place_ref, (ia_ref, ib_ref, ic_ref, id_ref))
    inners = three(tile_ref[...], info)
    for turn, (g_ref, i_ref) in enumerate(((g0_ref, i0_ref), (g1_ref, i1_ref))):
        total = None
        for k in range(3):
            lanes = slice(k * width, (k + 1) * width)
            part = across(gates[:, lanes], g_ref[k], (1, 1)) + across(inners[:, lanes], i_ref[k], (1, 1))
            total = part if total is None else total + part
        total_ref[:, turned(total_ref, turn, place_ref[0])] = total
    total = total_ref[...]
    split_parts(total, place_ref, sent_ref, keep_ref)

    @pl.when((pl.program_id(0) == 0) & (pl.program_id(1) == 0))
    def _():
        gain_ref[...] = jnp.zeros_like(gain_ref)

    x_hat = tile_rows(x_ref).astype(f32) * info[:, :1]
    gain_ref[...] += jnp.sum((total * x_hat).reshape(-1, 8, total.shape[1]), axis=0)


def weight_grad_kernel(chunks, steps, place_ref, *refs):
    ins, (out0_ref, out1_ref, square_ref, tile_ref, sum_ref) = refs[: 6 * chunks], refs[6 * chunks :]
    at = pl.program_id(0)

    @pl.when(at == 0)
    def _():
        sum_ref[...] = jnp.zeros_like(sum_ref)

    for chunk in range(chunks):
        info_ref, left_ref, *blocks = ins[6 * chunk : 6 * chunk + 6]

        @pl.when((at >= chunk * steps) & (at < (chunk + 1) * steps))
        def _(info_ref=info_ref, left_ref=left_ref, blocks=blocks):
            gathered(tile_ref, place_ref, blocks)
            right = three(tile_ref[...], info_ref[...].T)
            left = left_ref[...].reshape(-1, left_ref.shape[-1])
            sum_ref[...] += across(left, right, (0, 0))

    @pl.when(at == chunks * steps - 1)
    def _():
        half = sum_ref.shape[0] // 2
        width = tile_ref.shape[1]
        for turn, out_ref in enumerate((out0_ref, out1_ref)):
            rows = pl.ds(pl.multiple_of((turn ^ place_ref[3]) * half, half), half)
            for k in range(3):
                out_ref[k] = sum_ref[rows, k * width : (k + 1) * width].astype(out_ref.dtype)
        total = sum_ref[...]
        square_ref[...] = jnp.sum((total * total).reshape(-1, 8, total.shape[1]), axis=0)


SCALARS = pl.BlockSpec(memory_space=pltpu.SMEM)


def whole(array):
    return pl.BlockSpec(array.shape, lambda *at: (0,) * array.ndim)


def plane(array, which):
    kinds, rows, lanes = array.shape
    return pl.BlockSpec((kinds, rows, lanes // 2), lambda *at: (0, 0, which))


def shape_of(shape, dtype):
    return jax.ShapeDtypeStruct(shape, dtype)


def call(kernel, name, grid, in_specs, out_specs, out_shape, scratch, flops, moved, args):
    return pl.pallas_call(
        kernel,
        grid=grid,
        in_specs=in_specs,
        out_specs=out_specs,
        out_shape=out_shape,
        scratch_shapes=scratch,
        cost_estimate=pl.CostEstimate(flops=flops, bytes_accessed=moved, transcendentals=0),
        compiler_params=pltpu.CompilerParams(
            dimension_semantics=("arbitrary",) * len(grid), vmem_limit_bytes=48 * MEGA
        ),
        name=name,
    )(*args)


class Tiles:
    def __init__(self, micros, parts, rows, first=0):
        self.micros, self.pairs, self.rows, self.first = micros, parts // 2, rows, first
        self.grid = (micros, self.pairs)
        self.tile = 2 * rows

    def raw(self, width):
        return pl.BlockSpec((2, 1, self.rows, width), lambda m, z: (z, self.first + m, 0, 0))

    def flat(self, width):
        return pl.BlockSpec((self.tile, width), lambda m, z: ((self.first + m) * self.pairs + z, 0))

    def info(self):
        return pl.BlockSpec((8, self.tile), lambda m, z: (0, (self.first + m) * self.pairs + z))

    def kindred(self, which, width):
        return pl.BlockSpec((1, self.tile, width), lambda m, z: (which, m * self.pairs + z, 0))

    def blocks(self, width):
        return pl.BlockSpec((2, self.tile, width), lambda m, z: (0, m * self.pairs + z, 0))

    def parted(self, width):
        return pl.BlockSpec((1, 1, self.rows, width), lambda m, z: (m, z, 0, 0))


def inner_product(tiles, place, tokens, info, gain, w_in):
    width = tokens.shape[-1]
    chans = w_in[0].shape[-1] // 2
    rows = tiles.micros * tiles.pairs * tiles.tile
    return call(
        inner_kernel, "inner_product", tiles.grid,
        [SCALARS, tiles.raw(width), tiles.info(), whole(gain), plane(w_in[0], 0), plane(w_in[1], 0)],
        [tiles.flat(width), tiles.blocks(LANES), tiles.blocks(LANES)],
        [shape_of((rows, width), bf16), shape_of((2, rows, LANES), bf16), shape_of((2, rows, LANES), f32)],
        [pltpu.VMEM((tiles.tile, width), f32), pltpu.VMEM((tiles.tile, chans), f32)],
        6 * rows * width * chans, 8 * MEGA,
        (place, tokens, info, gain, *w_in),
    )


def gate_product(tiles, place, normed, back, info, w_in, w_out):
    width = normed.shape[-1]
    chans = w_out[0].shape[-1]
    rows = normed.shape[0]
    return call(
        gate_kernel, "gate_product", tiles.grid,
        [SCALARS, tiles.flat(width), tiles.raw(width), tiles.info()]
        + [plane(w, 1) for w in w_in] + [whole(w) for w in w_out],
        [tiles.blocks(2 * LANES), tiles.blocks(2 * LANES)],
        [shape_of((2, rows, 2 * LANES), bf16), shape_of((2, rows, 2 * LANES), f32)],
        [pltpu.VMEM((tiles.tile, width), f32), pltpu.VMEM((tiles.tile, chans), f32)],
        12 * rows * width * chans, 16 * MEGA,
        (place, normed, back, info, *w_in, *w_out),
    )


def out_product(tiles, place, pairs, info, w_out):
    width = 2 * w_out[0].shape[1]
    chans = w_out[0].shape[-1]
    rows = pairs[0].shape[1]
    parted = (tiles.micros, tiles.pairs, tiles.rows, width)
    return call(
        out_kernel, "out_product", tiles.grid,
        [SCALARS] + [tiles.kindred(0, LANES)] * 4 + [tiles.info(), whole(w_out[0]), whole(w_out[1])],
        [tiles.parted(width), tiles.parted(width)],
        [shape_of(parted, bf16), shape_of(parted, f32)],
        [pltpu.VMEM((tiles.tile, chans), f32), pltpu.VMEM((tiles.tile, width), f32)],
        6 * rows * width * chans, 8 * MEGA,
        (place, *pairs, info, *w_out),
    )


def normed_grad(tiles, place, pairs, inners, info, tokens, w_in):
    width = 2 * w_in[0].shape[1]
    chans = w_in[0].shape[-1] // 2
    rows = pairs[0].shape[1]
    parted = (tiles.micros, tiles.pairs, tiles.rows, width)
    return call(
        normed_kernel, "normed_grad", tiles.grid,
        [SCALARS] + [tiles.kindred(1, LANES)] * 4 + [tiles.flat(LANES)] * 4
        + [tiles.info(), tiles.raw(width)] + [plane(w, which) for which in (1, 0) for w in w_in],
        [tiles.parted(width), tiles.parted(width), pl.BlockSpec((8, width), lambda m, z: (0, 0))],
        [shape_of(parted, bf16), shape_of(parted, f32), shape_of((8, width), f32)],
        [pltpu.VMEM((tiles.tile, chans), f32), pltpu.VMEM((tiles.tile, width), f32)],
        12 * rows * width * chans, 16 * MEGA,
        (place, *pairs, *inners, info, tokens, *w_in, *w_in),
    )


def weight_grad(place, info, lefts, left_at, rights, right_at, span, dtype):
    chunks = len(lefts)
    width = lefts[0].shape[-1]
    chans = 4 * LANES
    steps = info.shape[1] // span // chunks
    info_at = ((8, span), lambda m, chunk: (0, chunk * steps + m))
    piece = (3, width // 2, chans)
    specs, args = [], []
    for chunk in range(chunks):
        def held(spec, chunk=chunk):
            shape, at = spec
            low = chunk * steps
            return pl.BlockSpec(shape, lambda i: at(jnp.clip(i - low, 0, steps - 1), chunk))

        specs += [held(info_at), held(left_at)] + [held(right_at)] * 4
        args += [info, lefts[chunk], *rights[chunk]]
    return call(
        functools.partial(weight_grad_kernel, chunks, steps), "weight_grad", (chunks * steps,),
        [SCALARS] + specs,
        [pl.BlockSpec(piece, lambda i: (0, 0, 0))] * 2 + [pl.BlockSpec((8, 3 * chans), lambda i: (0, 0))],
        [shape_of(piece, dtype), shape_of(piece, dtype), shape_of((8, 3 * chans), f32)],
        [pltpu.VMEM((span, chans), f32), pltpu.VMEM((width, 3 * chans), f32)],
        6 * chunks * steps * span * width * chans, 24 * MEGA,
        (place, *args),
    )


def masked_sum(wide, info):
    width = wide.shape[1] // 3
    return sum(wide[:, k * width : (k + 1) * width] * info[:, k + 1 : k + 2] for k in range(3))


def one_of_four(place_ref, x, core, own_ref, x_ref, core_ref, both_ref):
    shape = own_ref.shape
    same_x = jnp.full(shape, place_ref[0] ^ x, jnp.int32) == 0
    same_core = jnp.full(shape, place_ref[1] ^ core, jnp.int32) == 0
    own, across_x, across_core, both = (
        ref[...].astype(f32) for ref in (own_ref, x_ref, core_ref, both_ref)
    )
    return jnp.where(same_core, jnp.where(same_x, own, across_x), jnp.where(same_x, across_core, both))


def wide_scratch(micros):
    return pltpu.VMEM((micros, 8 * N, 2 * LANES), f32)


def product_scratch(micros):
    return pltpu.VMEM((micros, 8 * N, LANES), bf16)


def state_scratch(micros):
    return pltpu.VMEM((micros, N, LANES), f32)


def tile_scratch(micros):
    return pltpu.VMEM((micros, SCAN_ROWS, LANES), f32)


def mix_forward_kernel(
    x, place_ref, keep_ref, own_ref, x_ref, core_ref, both_ref, act_ref, info_ref,
    dt_ref, mask_ref, side_ref, rate_ref, bias_ref, start_ref,
    y_ref, before_ref, step_ref, slope_ref, rows_ref, low_ref, final_ref,
    state_ref, wide_a, wide_b, drive_ref,
):
    micros, rows, _ = step_ref.shape
    block = pl.program_id(0)
    rank = low_ref.shape[1]
    rate = rate_ref[...]
    mask = mask_ref[...]
    side = side_ref[...]
    dt_bias = bias_ref[0:1]

    @pl.when(block == 0)
    def _():
        state_ref[...] = start_ref[...]

    for m in range(micros):
        shared = one_of_four(place_ref, x, m, own_ref, x_ref, core_ref, both_ref)
        low = shared[:rank].astype(bf16)
        low_ref[m] = low
        dt_pre = masked_sum(across(low, dt_ref[...], (0, 0)), info_ref[m].T) + dt_bias
        small = jnp.exp(-jnp.abs(dt_pre))
        step = jnp.maximum(dt_pre, 0.0) + jnp.log1p(small)
        step_ref[m] = step
        slope_ref[m] = jnp.where(dt_pre >= 0, 1.0, small) / (1.0 + small)
        drive_ref[m] = step * act_ref[m].astype(f32)
        parts = []
        for left in (shared[rank : rank + N], shared[rank + N :]):
            for _ in range(3):
                part = left.astype(bf16).astype(f32)
                parts.append(part)
                left = left - part
            parts.append(jnp.zeros_like(left))
        rows_ref[m] = jnp.concatenate(parts, 0).T
        wide_a[m] = spread(rows_ref, m, 0, mask, side)

    def sixteen(turn, states):
        states = list(states)
        for half in range(2):
            base = pl.multiple_of(turn * 16 + 8 * half, 8)
            wide, wide_next = (wide_a, wide_b) if half == 0 else (wide_b, wide_a)
            following = jnp.minimum(base + 8, rows - 8)
            for m in range(micros):
                wide_next[m] = spread(rows_ref, m, following, mask, side)
            y_parts = [[] for _ in range(micros)]
            for j in range(8):
                for m in range(micros):
                    row = pl.ds(base + j, 1)
                    own = slice(N * j, N * j + N)
                    before = states[m]
                    before_ref[m, base + j] = before
                    before = before * keep_ref[micros * x + m, block * rows + base + j]
                    state = (
                        jnp.exp(step_ref[m, row, :] * rate) * before
                        + drive_ref[m, row, :] * wide[m, own, :LANES]
                    )
                    states[m] = state
                    shown = state * wide[m, own, LANES:]
                    y_parts[m].append(shown[:8] + shown[8:])
            for m in range(micros):
                y_ref[m, pl.ds(base, 8), :] = sum_rows(y_parts[m])
        return tuple(states)

    states = lax.fori_loop(
        0, rows // 16, sixteen, tuple(state_ref[m] for m in range(micros))
    )
    for m in range(micros):
        state_ref[m] = states[m]
        final_ref[m] = states[m]


def blend_kernel(y_ref, act_ref, pair_ref, bias_ref, kinds_ref, pull_ref):
    skip = bias_ref[1:2]
    gate, d_mixed = pair_ref[0, :, :LANES], pair_ref[0, :, LANES:]
    sigma = jax.nn.sigmoid(gate)
    y_scan = y_ref[0] + skip * act_ref[0].astype(f32)
    opened = gate * sigma
    kinds_ref[0, 0] = (y_scan * opened).astype(bf16)
    kinds_ref[1, 0] = (d_mixed * y_scan * (sigma * (1.0 + gate * (1.0 - sigma)))).astype(bf16)
    pull_ref[0] = d_mixed * opened


def blend(x, y, act, pair, bias):
    micros, rows, _ = y.shape
    first = micros * x
    one = pl.BlockSpec((1, rows, LANES), lambda m: (m, 0, 0))
    return call(
        blend_kernel, "blend", (micros,),
        [
            one, pl.BlockSpec((1, rows, LANES), lambda m: (first + m, 0, 0)),
            pl.BlockSpec((1, rows, 2 * LANES), lambda m: (first + m, 0, 0)), const(bias.shape),
        ],
        [pl.BlockSpec((2, 1, rows, LANES), lambda m: (0, m, 0, 0)), one],
        [shape_of((2,) + y.shape, bf16), shape_of(y.shape, f32)],
        [], 20 * y.size, 20 * y.size, (y, act, pair, bias),
    )


def time_specs(micros, at, x):
    return dict(
        tall=pl.BlockSpec((micros, SCAN_ROWS, LANES), lambda i: (0, at(i), 0)),
        act=pl.BlockSpec((micros, SCAN_ROWS, LANES), lambda i: (x, at(i), 0)),
        turned=pl.BlockSpec((micros, LANES, SCAN_ROWS), lambda i: (0, 0, at(i))),
        states=pl.BlockSpec((micros, SCAN_ROWS, N, LANES), lambda i: (0, at(i), 0, 0)),
        info=pl.BlockSpec((micros, 8, SCAN_ROWS), lambda i: (x, 0, at(i))),
        fixed=pl.BlockSpec((micros, N, LANES), lambda i: (0, 0, 0)),
    )


def const(shape):
    return pl.BlockSpec(shape, lambda *at: (0,) * len(shape))


def mix_forward(place, x, keep, quarters, act, info, dt, rules, rate, bias, start):
    length = act.shape[1]
    micros = start.shape[0]
    blocks = length // SCAN_ROWS
    spec = time_specs(micros, lambda i: i, x)
    width = quarters[0].shape[0]
    quarter = pl.BlockSpec((width, SCAN_ROWS), lambda i: (0, i))
    tall = jax.ShapeDtypeStruct((micros, length, LANES), f32)
    return pl.pallas_call(
        functools.partial(mix_forward_kernel, x),
        grid=(blocks,),
        in_specs=[
            SCALARS, SCALARS, *[quarter] * 4, spec["act"], spec["info"],
            const(dt.shape), const(rules[0].shape), const(rules[1].shape),
            const(rate.shape), const(bias.shape), spec["fixed"],
        ],
        out_specs=[spec["tall"], spec["states"], *[spec["tall"]] * 3, spec["turned"], spec["fixed"]],
        out_shape=[
            tall, jax.ShapeDtypeStruct((micros, length, N, LANES), f32), tall, tall, tall,
            jax.ShapeDtypeStruct((micros, width - 2 * N, length), bf16),
            jax.ShapeDtypeStruct((micros, N, LANES), f32),
        ],
        scratch_shapes=[
            state_scratch(micros), wide_scratch(micros), wide_scratch(micros), tile_scratch(micros)
        ],
        cost_estimate=pl.CostEstimate(
            flops=micros * length * N * LANES * 40,
            bytes_accessed=micros * length * N * LANES * 12,
            transcendentals=micros * length * N * LANES,
        ),
        compiler_params=pltpu.CompilerParams(
            dimension_semantics=("arbitrary",), vmem_limit_bytes=40 * MEGA
        ),
        name="mix_forward",
    )(place, keep, *quarters, act, info, dt, *rules, rate, bias, start)


def mix_backward_kernel(
    x, place_ref, keep_ref, act_ref, info_ref, dt_ref, mask_ref, side_ref, rate_ref, bias_ref, start_ref,
    before_ref, step_ref, slope_ref, rows_ref, low_ref, last_ref, pull_ref,
    shared_ref, d_act_ref, grad_dt_ref, sums_ref, grad_rate_ref, final_ref,
    state_ref, after_ref, wide_a, wide_b, product_a, product_b, shown_a, shown_b,
    drive_ref, b_pull_ref, rate_pull_ref,
):
    micros, rows, _ = step_ref.shape
    block = pl.num_programs(0) - 1 - pl.program_id(0)
    rank = low_ref.shape[1]
    rate = rate_ref[...]
    mask = mask_ref[...]
    side = side_ref[...]
    skip = bias_ref[1:2]
    ones = jnp.ones((LANES, LANES), bf16)
    lane = lax.broadcasted_iota(jnp.int32, (N, LANES), 1)

    @pl.when(pl.program_id(0) == 0)
    def _():
        state_ref[...] = start_ref[...]
        after_ref[...] = last_ref[...]
        grad_rate_ref[...] = jnp.zeros_like(grad_rate_ref)
        grad_dt_ref[...] = jnp.zeros_like(grad_dt_ref)
        sums_ref[...] = jnp.zeros_like(sums_ref)

    for m in range(micros):
        drive_ref[m] = step_ref[m] * act_ref[m].astype(f32)
        wide_a[m] = spread(rows_ref, m, rows - 8, mask, side)

    def sixteen(turn, carried):
        states, afters, grads, grads_c, rates = (list(part) for part in carried)
        for half in range(2):
            base = pl.multiple_of(rows - 8 - turn * 16 - 8 * half, 8)
            wide, wide_next = (wide_a, wide_b) if half == 0 else (wide_b, wide_a)
            product, product_last = (product_a, product_b) if half == 0 else (product_b, product_a)
            seen, seen_last = (shown_a, shown_b) if half == 0 else (shown_b, shown_a)
            following = jnp.maximum(base - 8, 0)
            for m in range(micros):
                wide_next[m] = spread(rows_ref, m, following, mask, side)
                grads[m] = lane_sums(product_last, m, grads[m], lane, base + 8, ones)
                grads_c[m] = lane_sums(seen_last, m, grads_c[m], lane, base + 8, ones)
            b_parts = [[None] * 8 for _ in range(micros)]
            rate_parts = [[None] * 8 for _ in range(micros)]
            for j in range(7, -1, -1):
                for m in range(micros):
                    row = pl.ds(base + j, 1)
                    own = slice(N * j, N * j + N)
                    step = step_ref[m, row, :]
                    pull = pull_ref[m, row, :]
                    adjoint = wide[m, own, LANES:] * pull + states[m]
                    passed = jnp.exp(step * rate) * (
                        adjoint * keep_ref[micros * x + m, block * rows + base + j]
                    )
                    states[m] = passed
                    before = before_ref[m, base + j]
                    seen[m, own, :] = (afters[m] * pull).astype(bf16)
                    afters[m] = before
                    decay_pull = passed * before
                    shown = adjoint * wide[m, own, :LANES]
                    b_parts[m][j] = shown[:8] + shown[8:]
                    shown = decay_pull * rate
                    rate_parts[m][j] = shown[:8] + shown[8:]
                    rates[m] = rates[m] + decay_pull * step
                    product[m, own, :] = (adjoint * drive_ref[m, row, :]).astype(bf16)
            for m in range(micros):
                b_pull_ref[m, pl.ds(base, 8), :] = sum_rows(b_parts[m])
                rate_pull_ref[m, pl.ds(base, 8), :] = sum_rows(rate_parts[m])
        return tuple(tuple(part) for part in (states, afters, grads, grads_c, rates))

    zeros = tuple(jnp.zeros((N, LANES), f32) for m in range(micros))
    begin = (
        tuple(state_ref[m] for m in range(micros)),
        tuple(after_ref[m] for m in range(micros)),
        zeros, zeros, zeros,
    )
    states, afters, grads, grads_c, rates = lax.fori_loop(0, rows // 16, sixteen, begin)
    for m in range(micros):
        state_ref[m] = states[m]
        after_ref[m] = afters[m]
        grad_rate_ref[...] += rates[m]
        final_ref[m] = states[m]
        act = act_ref[m].astype(f32)
        pull = pull_ref[m]
        b_pull = b_pull_ref[m]
        d_act_ref[m] = pull * skip + step_ref[m] * b_pull
        d_pre = ((rate_pull_ref[m] + act * b_pull) * slope_ref[m]).astype(bf16).astype(f32)
        sums_ref[0:8] += jnp.sum(d_pre.reshape(-1, 8, LANES), axis=0)
        sums_ref[8:16] += jnp.sum((pull * act).reshape(-1, 8, LANES), axis=0)
        d_pre3 = three(d_pre, info_ref[m].T)
        shared_ref[m, :rank] = across(dt_ref[...], d_pre3, (1, 1))
        shared_ref[m, rank : rank + N] = lane_sums(product_b, m, grads[m], lane, 0, ones)
        shared_ref[m, rank + N :] = lane_sums(shown_b, m, grads_c[m], lane, 0, ones)
        grad_dt_ref[...] += across(low_ref[m], d_pre3, (1, 0))


def mix_backward(place, x, keep, act, info, dt, rules, rate, bias, start, saved):
    before, step, slope, rows, low, last, pull = saved
    length = act.shape[1]
    micros = start.shape[0]
    blocks = length // SCAN_ROWS
    spec = time_specs(micros, lambda i: blocks - 1 - i, x)
    rank = low.shape[1]
    width = rank + 2 * N
    product, tile = product_scratch(micros), tile_scratch(micros)
    return pl.pallas_call(
        functools.partial(mix_backward_kernel, x),
        grid=(blocks,),
        in_specs=[
            SCALARS, SCALARS, spec["act"], spec["info"],
            const(dt.shape), const(rules[0].shape), const(rules[1].shape),
            const(rate.shape), const(bias.shape), spec["fixed"],
            spec["states"], *[spec["tall"]] * 3, spec["turned"], spec["fixed"], spec["tall"],
        ],
        out_specs=[
            pl.BlockSpec((micros, width, SCAN_ROWS), lambda i: (0, 0, blocks - 1 - i)),
            spec["tall"], const(dt.shape), const((16, LANES)), const((N, LANES)), spec["fixed"],
        ],
        out_shape=[
            jax.ShapeDtypeStruct((micros, width, length), f32),
            jax.ShapeDtypeStruct((micros, length, LANES), f32),
            jax.ShapeDtypeStruct(dt.shape, f32),
            jax.ShapeDtypeStruct((16, LANES), f32),
            jax.ShapeDtypeStruct((N, LANES), f32),
            jax.ShapeDtypeStruct((micros, N, LANES), f32),
        ],
        scratch_shapes=[
            state_scratch(micros), state_scratch(micros), wide_scratch(micros), wide_scratch(micros),
            product, product, product, product, tile, tile, tile,
        ],
        cost_estimate=pl.CostEstimate(
            flops=micros * length * N * LANES * 60,
            bytes_accessed=micros * length * N * LANES * 12,
            transcendentals=micros * length * N * LANES,
        ),
        compiler_params=pltpu.CompilerParams(
            dimension_semantics=("arbitrary",), vmem_limit_bytes=40 * MEGA
        ),
        name="mix_backward",
    )(place, keep, act, info, dt, *rules, rate, bias, start, *saved)


def shifted(scratch_ref, j, rows):
    return scratch_ref[8 - j : 8 - j + rows, :]


def conv_forward_kernel(inner_ref, edge_ref, info_ref, taps_ref, wx_ref,
                        act_ref, conv_ref, shared_ref, scratch_ref):
    rows = inner_ref.shape[1]
    scratch_ref[:8] = edge_ref[0]
    scratch_ref[8:] = inner_ref[0]
    info = info_ref[0].T
    total = taps_ref[K : K + 1] + taps_ref[0:1] * inner_ref[0]
    for j in range(1, K):
        total = total + taps_ref[j : j + 1] * (shifted(scratch_ref, j, rows) * info[:, 3 + j : 4 + j])
    conv_ref[0] = total
    act = (total * jax.nn.sigmoid(total)).astype(bf16)
    act_ref[0] = act
    shared_ref[0] = across(wx_ref[...], three(act.astype(f32), info), (1, 1))


def conv_forward(inner, edge, info, taps, wx):
    micros, rows, _ = inner.shape
    one = pl.BlockSpec((1, rows, LANES), lambda m: (m, 0, 0))
    width = wx.shape[0]
    return call(
        conv_forward_kernel, "conv_forward", (micros,),
        [
            one, pl.BlockSpec((1, 8, LANES), lambda m: (m, 0, 0)),
            pl.BlockSpec((1, 8, rows), lambda m: (m, 0, 0)), const(taps.shape), const(wx.shape),
        ],
        [one, one, pl.BlockSpec((1, width, rows), lambda m: (m, 0, 0))],
        [
            shape_of(inner.shape, bf16), shape_of(inner.shape, f32),
            shape_of((micros, width, rows), f32),
        ],
        [pltpu.VMEM((rows + 8, LANES), f32)],
        2 * micros * rows * wx.size, 4 * MEGA,
        (inner, edge, info, taps, wx),
    )


def conv_backward_kernel(x, place_ref, own_ref, x_ref, core_ref, both_ref, d_act_ref, conv_ref, inner_ref,
                         edge_ref, act_ref, info_ref, taps_ref, wx_ref,
                         d_inner_ref, grad_x_ref, sums_ref, head_ref, last_ref, scratch_ref, ahead_ref):
    rows = inner_ref.shape[1]
    micro = pl.program_id(0)
    info = info_ref[0].T

    @pl.when(micro == 0)
    def _():
        grad_x_ref[...] = jnp.zeros_like(grad_x_ref)
        sums_ref[...] = jnp.zeros_like(sums_ref)

    shared = one_of_four(place_ref, x, micro, own_ref, x_ref, core_ref, both_ref).astype(bf16)
    d_act = d_act_ref[0] + masked_sum(across(shared, wx_ref[...], (0, 0)), info)
    grad_x_ref[...] += across(shared, three(act_ref[0].astype(f32), info), (1, 0))
    conv = conv_ref[0]
    sigma = jax.nn.sigmoid(conv)
    d_conv = d_act * (sigma * (1.0 + conv * (1.0 - sigma)))
    head_ref[0] = d_conv[:8]
    scratch_ref[:8] = edge_ref[0]
    scratch_ref[8:] = inner_ref[0]
    ahead_ref[rows:] = jnp.zeros((8, LANES), f32)
    total = taps_ref[0:1] * d_conv
    sums_ref[0:8] += jnp.sum((d_conv * inner_ref[0]).reshape(-1, 8, LANES), axis=0)
    for j in range(1, K):
        masked = d_conv * info[:, 3 + j : 4 + j]
        pulled = (masked * shifted(scratch_ref, j, rows)).reshape(-1, 8, LANES)
        sums_ref[8 * j : 8 * j + 8] += jnp.sum(pulled, axis=0)
        ahead_ref[:rows] = masked
        total = total + taps_ref[j : j + 1] * ahead_ref[j : j + rows, :]
    sums_ref[8 * K : 8 * K + 8] += jnp.sum(d_conv.reshape(-1, 8, LANES), axis=0)
    d_inner_ref[0] = total.astype(bf16)
    last_ref[0] = total[rows - 8 :]


def conv_backward(place, x, quarters, d_act, conv, inner, edge, act, info, taps, wx):
    micros, rows, _ = d_act.shape
    first = micros * x
    mine = pl.BlockSpec((1, rows, LANES), lambda m: (m, 0, 0))
    one = pl.BlockSpec((1, rows, LANES), lambda m: (first + m, 0, 0))
    eight = pl.BlockSpec((1, 8, LANES), lambda m: (m, 0, 0))
    sums = (8 * (K + 1), LANES)
    return call(
        functools.partial(conv_backward_kernel, x), "conv_backward", (micros,),
        [
            SCALARS, *[const(quarters[0].shape)] * 4, mine, one, one,
            pl.BlockSpec((1, 8, LANES), lambda m: (first + m, 0, 0)), one,
            pl.BlockSpec((1, 8, rows), lambda m: (first + m, 0, 0)), const(taps.shape), const(wx.shape),
        ],
        [mine, const(wx.shape), const(sums), eight, eight],
        [
            shape_of(d_act.shape, bf16), shape_of(wx.shape, f32), shape_of(sums, f32),
            shape_of((micros, 8, LANES), f32), shape_of((micros, 8, LANES), f32),
        ],
        [pltpu.VMEM((rows + 8, LANES), f32), pltpu.VMEM((rows + 8, LANES), f32)],
        4 * micros * rows * wx.size, 6 * MEGA,
        (place, *quarters, d_act, conv, inner, edge, act, info, taps, wx),
    )


def pack_kernel(flag_ref, after_ref, w_ref, *out_refs):
    half = w_ref.shape[-1] // 2
    for turn, out_ref in enumerate(out_refs):
        lanes = pl.ds(pl.multiple_of((turn ^ flag_ref[0]) * half, half), half)
        if len(w_ref.shape) == 3:
            out_ref[0] = w_ref[0, :, lanes].astype(bf16)
            continue
        for side in range(2):
            out_ref[0, :, side * half : side * half + half] = w_ref[0, :, side, lanes].astype(bf16)


def pack(flag, after, weight):
    kinds, rows = weight.shape[:2]
    width = weight.size // (kinds * rows * 2)
    return call(
        pack_kernel, "pack", (kinds,),
        [SCALARS, SCALARS, pl.BlockSpec((1,) + weight.shape[1:], lambda k: (k,) + (0,) * (weight.ndim - 1))],
        [pl.BlockSpec((1, rows, width), lambda k: (k, 0, 0))] * 2,
        [shape_of((kinds, rows, width), bf16)] * 2,
        [], 0, weight.size * 6, (flag, after, weight),
    )


def adam_kernel(rate, flag_ref, clip_ref, w_ref, m_ref, v_ref, *refs):
    pieces, (grad_ref, new_ref, first_ref, second_ref) = refs[:4], refs[4:]
    half = w_ref.shape[-1] // 2
    clip = clip_ref[0]
    for plane in range(2):
        for turn in range(2):
            lanes = pl.ds(pl.multiple_of((turn ^ flag_ref[0]) * half, half), half)
            at = (0, slice(None), plane, lanes)
            grad = pieces[2 * plane + turn][0].astype(f32)
            new, first, second = adam_update(w_ref[at], grad, m_ref[at], v_ref[at], clip, rate)
            grad_ref[at] = grad
            new_ref[at] = new
            first_ref[at] = first
            second_ref[at] = second


def adam(flag, clip, weight, first, second, pieces, rate):
    kinds, rows, _, chans = weight.shape
    block = min(rows, 64)
    full = pl.BlockSpec((1, block, 2, chans), lambda k, r: (k, r, 0, 0))
    piece = pl.BlockSpec((1, block, chans // 2), lambda k, r: (k, r, 0))
    return call(
        functools.partial(adam_kernel, rate), "adam", (kinds, rows // block),
        [SCALARS, SCALARS, full, full, full] + [piece] * 4,
        [full] * 4,
        [shape_of(weight.shape, f32)] * 4,
        [], weight.size * 20, weight.size * 32,
        (flag, clip, weight, first, second, *pieces),
    )


def body(
    groups, parts, chans,
    tokens_in, modality, starts, cotangent,
    in_weight, in_first, in_second,
    dt_weight, dt_first, dt_second,
    out_weight, out_first, out_second,
    x_weight, x_first, x_second,
    channel_params, channel_first, channel_second,
    gain, gain_first, gain_second,
):
    micros, tok_rows, part_width = tokens_in.shape
    model = gain.shape[0]
    chan_width = in_weight.shape[3]
    half = chan_width // 2
    own = half // chans
    cores = chans // 2
    inner_all = chan_width * chans
    x_width = x_weight.shape[1]
    rank = x_width - 2 * N
    dt_rows = dt_weight.shape[1]
    span = parts * tok_rows
    edge = K - 1
    t_at = lax.axis_index("t")
    p_at = lax.axis_index("p")
    c_at = lax.axis_index("c")
    z_at, y_at = p_at // 2, p_at % 2
    x_at, core_at = c_at // cores, c_at % cores
    s_at = t_at * parts + p_at
    slice_at = s_at // (2 * groups)
    everywhere = ("t", "p", "c")
    place = jnp.stack([x_at, core_at, y_at, z_at % 2]).astype(jnp.int32)
    half_at = (s_at % (2 * groups)) // groups

    def flat(t, p, c):
        return (t * parts + p) * chans + c

    def part_of(c, j):
        return 2 * (2 * (c % cores) + j) + c // cores

    devices = [(t, p, c) for t in range(groups) for p in range(parts) for c in range(chans)]

    def first_hop(turn):
        pairs = []
        for t, p, c in devices:
            s = t * parts + p
            to_slice, i = s // (2 * groups), (s % (2 * groups)) // groups
            j = turn ^ (to_slice // cores)
            to = flat(s % groups, 2 * (2 * (c % cores) + j) + i, c // cores * cores + to_slice % cores)
            pairs.append((flat(t, p, c), to))
        return pairs

    def second_hop(turn):
        return [
            (flat(t, p, c), flat(t, p - p % 2 + c // cores, (turn ^ (p % 2)) * cores + c % cores))
            for t, p, c in devices
        ]

    def home(turn):
        pairs = []
        for t, p, c in devices:
            s = t * parts + p
            i = (s % (2 * groups)) // groups
            keeper = flat(s % groups, part_of(c, turn ^ i), s // (2 * groups))
            pairs.append((keeper, flat(t, p, c)))
        return pairs

    small_pairs = [(flat(t, p, c), flat(t, part_of(c, p % 2), p // 2)) for t, p, c in devices]

    def send(value, pairs, back=False):
        if back:
            pairs = [(b, a) for a, b in pairs]
        return lax.ppermute(value, everywhere, pairs)

    def swap(value, axis, distance):
        return lax.ppermute(value, axis, [(i, i ^ distance) for i in range(lax.axis_size(axis))])

    def crossed(pair, flag):
        first, second = pair
        return jnp.where(flag == 0, first, second), jnp.where(flag == 0, second, first)

    between = y_at ^ (z_at % 2)

    def token(*values):
        return sum(value[(0,) * value.ndim].astype(f32) for value in values)[None]

    def weights_there(pair):
        pair = [send(value, first_hop(turn)) for turn, value in enumerate(pair)]
        first = token(*pair)
        pair = crossed(pair, between)
        pair = [send(value, second_hop(turn)) for turn, value in enumerate(pair)]
        return pair, first, token(pair[0])

    def there_whole(pair):
        if groups > 1:
            pair = [lax.all_gather(value, "t", axis=1, tiled=True) for value in pair]
        return tuple(pair)

    group_squares = []

    def returned(pair):
        if groups > 1:
            pair = [
                lax.psum_scatter(value, "t", scatter_dimension=1, tiled=True) for value in pair
            ]
            group_squares.extend(jnp.sum(value * value) for value in pair)
            pair = [value.astype(bf16) for value in pair]
        return [send(value, home(turn)) for turn, value in enumerate(pair)]

    def along_groups(value, by):
        pairs = [(i, i + by) for i in range(groups) if 0 <= i + by < groups]
        return lax.ppermute(value, "t", pairs)

    def over_chans(value):
        distance = 1
        while distance < chans:
            value = value + swap(value, "c", distance)
            distance *= 2
        return value

    def pick(value, at, axis):
        return lax.dynamic_index_in_dim(value, at, axis, keepdims=False)

    def scattered_chans(sent, keep, late=None):
        total = keep + swap(sent, "c", 1).astype(f32)
        away = pick(total, 1 - x_at, 0)
        if late is not None:
            away = away + 0.0 * late[0]
        got = swap(away.astype(bf16), "c", cores)
        return pick(total, x_at, 0) + got.astype(f32)

    def gathered_chans(value):
        across_x = swap(value, "c", cores)
        across_core = swap(value, "c", 1)
        return (value, across_x, across_core, swap(across_x, "c", 1))

    def scattered_parts(products, late=None):
        keeps = [keep for _, keep in products]
        count = len(keeps)

        def hop(pieces, distance):
            pieces = jnp.concatenate([piece.astype(bf16) for piece in pieces], 0)
            return jnp.split(swap(pieces, "p", distance), count, 0)

        got = hop([sent for sent, _ in products], 1)
        totals = [keep + piece.astype(f32) for keep, piece in zip(keeps, got)]
        arrived = totals[0]
        totals = [total.reshape(total.shape[0], -1, 2, *total.shape[2:]) for total in totals]
        away = [pick(total, 1 - z_at % 2, 2) for total in totals]
        if late is not None:
            away = [value + late for value in away]
        got = hop(away, 2)
        totals = [pick(total, z_at % 2, 2) + piece.astype(f32) for total, piece in zip(totals, got)]
        away = [pick(total, 1 - z_at // 2, 1) for total in totals]
        got = hop(away, 4)
        totals = [pick(total, z_at // 2, 1) + piece.astype(f32) for total, piece in zip(totals, got)]
        return jnp.concatenate(totals, 0), arrived

    def after(value, *others):
        return value + (0.0 * token(*others)).astype(jnp.int32)

    def summed(values, kind, fills, late):
        fills = list(fills)

        def fill(arrived):
            return token(*fills.pop(0)(after(place, arrived)))[0] if fills else None

        def tied(arrived, ran):
            return arrived if ran is None else arrived + 0.0 * ran

        away = jnp.stack([pick(value, 1 - core_at, 0) for value in values]).astype(kind)
        total = jnp.stack([pick(value, core_at, 0) for value in values])
        total = total + swap(away, "c", 1).astype(f32)
        ran = fill(total)
        away = pick(total, 1 - x_at, 0).astype(kind)
        total = pick(total, x_at, 0) + swap(away, "c", cores).astype(f32)
        distance = 1
        while distance < parts:
            last, ran = ran, fill(total)
            total = tied(total, last)
            if distance in late:
                total = total + 0.0 * late[distance][0]
            total = total.astype(kind)
            total = total.astype(f32) + swap(total, "p", distance).astype(f32)
            distance *= 2
        total = tied(total, ran)
        return gathered_chans(total.astype(kind)), total

    def over_all(value):
        value = over_chans(value)
        distance = 1
        while distance < parts:
            value = value + swap(value, "p", distance)
            distance *= 2
        return lax.psum(value, "t") if groups > 1 else value

    extra = jnp.pad(modality.astype(bf16)[:, None, :], ((0, 0), (0, 15), (0, part_width - tok_rows)))
    tokens_all = lax.all_gather(jnp.concatenate([tokens_in, extra], 1), "p")
    flag = (slice_at // cores).astype(jnp.int32)[None]
    owner_flag = half_at.astype(jnp.int32)[None]
    w_in, in_arrived, _ = weights_there(pack(flag, jnp.zeros((1,), f32), in_weight))
    w_in = there_whole(w_in)
    small = jnp.concatenate([x_weight.reshape(3 * x_width, chan_width), channel_params], 0)
    own_lanes = y_at * half + z_at * own
    small = send(lax.dynamic_slice_in_dim(small, own_lanes, own, 1), small_pairs)
    dt16 = dt_weight.astype(bf16)
    dt_pair = crossed((dt16[..., :half], dt16[..., half:]), flag[0])
    out_pair = pack(flag, in_arrived, out_weight)
    out_rows = out_weight.shape[1]
    both = [jnp.concatenate(pair, 1) for pair in zip(out_pair, dt_pair)]
    both, _, _ = weights_there(both)
    w_out = there_whole([value[:, :out_rows] for value in both])
    dt_part = jnp.concatenate(
        crossed(there_whole([value[:, out_rows:] for value in both]), x_at), 1
    )
    dt_blocks = []
    for distance in range(chans):
        block = lax.dynamic_slice_in_dim(dt_part, (c_at ^ distance) * own, own, 2)
        dt_blocks.append(swap(block, "c", distance) if distance else block)
    dt_blocks = jnp.stack(dt_blocks)
    w_dt = jnp.concatenate([pick(dt_blocks, c_at ^ k, 0) for k in range(chans)], 1)
    w_dt = w_dt.transpose(1, 0, 2).reshape(rank, 3 * own)
    back_all = lax.all_gather(cotangent, "p")
    positions = t_at * span - edge + jnp.arange(span + 2 * edge, dtype=jnp.int32)
    segment = jnp.sum((starts[:, None, :] <= positions[None, :, None]).astype(jnp.int32), axis=2)
    keep_mask = 1.0 - jnp.any(
        starts[:, None, :] == positions[None, edge : edge + span, None], axis=2
    ).astype(f32)
    same_doc = [
        (segment[:, edge - j : 2 * edge - j + span] == segment[:, edge:]).astype(f32)
        for j in range(1, K)
    ]
    squares = jnp.sum(jnp.square(tokens_all[:, :, :tok_rows].astype(f32)), axis=-1)
    squares = over_chans(squares).transpose(1, 0, 2).reshape(micros, span)
    inverse = lax.rsqrt(squares / model + NORM_EPS)
    kinds = tokens_all[:, :, tok_rows, :tok_rows].transpose(1, 0, 2).reshape(micros, span)
    kinds = kinds.astype(jnp.int32)
    rows = [inverse, *((kinds == k).astype(f32) for k in range(3))]
    rows += [same[:, :span] for same in same_doc] + [jnp.zeros_like(inverse)]
    info3 = jnp.stack(rows, 1)
    info = jnp.stack([row.reshape(-1) for row in rows], 0)
    inv_own = lax.dynamic_slice_in_dim(inverse, p_at * tok_rows, tok_rows, 1)[..., None]
    gain_part = lax.dynamic_slice_in_dim(gain, c_at * part_width, part_width, 0)[None]

    w_x = small[: 3 * x_width].astype(bf16).reshape(3, x_width, own)
    w_x = w_x.transpose(1, 0, 2).reshape(x_width, 3 * own)
    channel = small[3 * x_width :]
    taps = channel[:8]
    biases = jnp.pad(channel[K + 1 : K + 3], ((0, 6), (0, 0)))
    neg_rate = -jnp.exp(channel[K + 3 :])
    rules = lane_rules()

    grad_dt_sum = grad_x_sum = grad_chan_sum = grad_gain_sum = 0.0
    pairs_of = range(micros // 2)
    zero_state = jnp.zeros((2, N, own), f32)
    everything = Tiles(micros, parts, tok_rows)
    twos = [Tiles(2, parts, tok_rows, 2 * x) for x in pairs_of]
    normed, sent, keep = inner_product(everything, place, tokens_all, info, gain_part, w_in)
    inner = scattered_chans(sent, keep).reshape(micros, span, own)
    edge_rows = jnp.zeros((micros, 8, own), f32)
    if groups > 1:
        edge_rows = along_groups(inner[:, span - 8 :], 1)
    act, conv, shared = conv_forward(inner, edge_rows, info3, taps, w_x)
    quarters, quarter = summed(
        [shared[2 * x : 2 * x + 2] for x in pairs_of], f32, [], {}
    )
    sent, keep = gate_product(everything, after(place, quarter), normed, back_all, info, w_in, w_out)
    pair = scattered_chans(sent, keep, token(*quarters[1:], w_dt)).reshape(micros, span, 2 * own)
    held = []
    for x in pairs_of:
        args = (x, keep_mask, quarters, act, info3, w_dt, rules, neg_rate, biases)
        order = after(place, sent if x == 0 else held[-1][0])
        state_in = zero_state
        if groups > 1:
            first_pass = mix_forward(order, *args, zero_state)
            ends, step = first_pass[6], first_pass[2]
            passed_all = jnp.exp(jnp.sum(step, axis=1)[:, None, :] * neg_rate)
            passed_all = passed_all * jnp.prod(keep_mask[2 * x : 2 * x + 2], axis=1)[:, None, None]
            for _ in range(groups - 1):
                state_in = along_groups(passed_all * state_in + ends, 1)
        held.append(mix_forward(order, *args, state_in))

    all_pairs, pulls = [], []
    for x in pairs_of:
        kinds_out, pull = blend(x, held[x][0], act, pair, biases)
        pulls.append(pull)
        all_pairs.append(gathered_chans(kinds_out.reshape(2, 2 * span, own)))
    order = place
    shares, d_acts, mix_sums, d_rate = [], [], 0.0, 0.0
    for x in pairs_of:
        saved = (*held[x][1:], pulls[x])
        args = (x, keep_mask, act, info3, w_dt, rules, neg_rate, biases)
        adj_in = zero_state
        if groups > 1:
            ends = mix_backward(order, *args, zero_state, saved)[5]
            passed_all = jnp.exp(jnp.sum(saved[1], axis=1)[:, None, :] * neg_rate)
            passed_all = passed_all * jnp.prod(keep_mask[2 * x : 2 * x + 2], axis=1)[:, None, None]
            for _ in range(groups - 1):
                adj_in = along_groups(passed_all * adj_in + ends, -1)
        share, d_act, grad_dt, sums, grad_rate, _ = mix_backward(order, *args, adj_in, saved)
        order = after(place, d_act, *(blocks[k] for blocks in all_pairs for k in (1, 2)))
        shares.append(share)
        d_acts.append(d_act)
        grad_dt_sum += grad_dt
        mix_sums += jnp.sum(sums.reshape(2, 8, own), axis=1)
        d_rate += grad_rate * neg_rate

    kept = f32 if groups > 1 else bf16

    def kindred(which):
        return ((1, span, own), lambda m, x: (which, m, 0))

    def rows_at(width):
        return ((span, width), lambda m, x: (2 * x + m, 0))

    raw_at = ((parts, 1, tok_rows, part_width), lambda m, x: (0, 2 * x + m, 0, 0))
    count = len(all_pairs)
    products, large = [], {}

    def out_fill(order):
        for x in pairs_of:
            products.append(out_product(twos[x], order, all_pairs[x], info, w_out))
            order = after(place, products[-1][0])
        return [sent for sent, _ in products]

    def grad_fill(name, lefts, left_at, which):
        def run(order):
            *pieces, square = weight_grad(
                order, info, lefts, left_at, all_pairs, kindred(which), span, kept
            )
            large[name] = (pieces, square)
            return (square,)

        return run

    fills = [
        out_fill,
        grad_fill("out", [back_all] * count, raw_at, 0),
        grad_fill("gate", [normed] * count, rows_at(part_width), 1),
    ]
    quarters, _ = summed(shares, bf16, fills, {})
    (g_out, out_sq), (g_gate, gate_sq) = large["out"], large["gate"]
    early_products = products

    d_inners = []
    for x in pairs_of:
        d_inner, grad_x, sums, head, last = conv_backward(
            place, x, quarters, d_acts[x], conv, inner, edge_rows, act, info3, taps, w_x
        )
        if groups > 1:
            ahead = along_groups(head, -1)[:, :edge]
            for j in range(1, K):
                gone = taps[j] * ahead * same_doc[j - 1][2 * x : 2 * x + 2, span:, None]
                last = last.at[:, 8 - j :].add(gone[:, :j])
            d_inner = jnp.concatenate([d_inner[:, : span - 8], last.astype(bf16)], 1)
        d_inners.append(d_inner.reshape(2 * span, own))
        grad_x_sum += grad_x
        grad_chan_sum += jnp.sum(sums.reshape(K + 1, 8, own), axis=1)
    grad_chan_sum = jnp.concatenate([grad_chan_sum, mix_sums, d_rate], 0)
    inners = gathered_chans(jnp.concatenate(d_inners, 0))

    *g_inner, inner_sq = weight_grad(
        place, info, [normed] * count, rows_at(part_width), [inners] * count,
        rows_at(own), span, kept,
    )
    g_inner = returned(g_inner)
    behind = 0.0 * token(inner_sq)[0]
    g_gate = returned([value + behind.astype(value.dtype) for value in g_gate])
    g_out = returned([value + behind.astype(value.dtype) for value in g_out])
    outs, _ = scattered_parts(early_products, late=behind)
    order = after(place, inner_sq)
    products = []
    for x in pairs_of:
        sent, keep, gain_rows = normed_grad(
            twos[x], order, all_pairs[x], inners, info, tokens_all, w_in
        )
        grad_gain_sum += jnp.sum(gain_rows, axis=0)
        products.append((sent, keep))
        order = after(place, sent)
    rows_back, _ = scattered_parts(products)

    grad_x_sum = grad_x_sum.reshape(x_width, 3, own).transpose(1, 0, 2)
    grad_dt_sum = grad_dt_sum.reshape(rank, 3, own).transpose(1, 0, 2)
    g_small = jnp.concatenate(
        [grad_x_sum.reshape(-1, own), grad_dt_sum.reshape(-1, own), grad_chan_sum], 0
    )
    if groups > 1:
        g_small = lax.psum(g_small, "t")
        large_sq = sum(group_squares)
    else:
        large_sq = jnp.sum(out_sq) + jnp.sum(gate_sq) + jnp.sum(inner_sq)
    local_sq = large_sq + jnp.sum(g_small * g_small) / groups
    here = (jnp.arange(chans) == c_at).astype(f32)
    tail = jnp.concatenate([(here[:, None] * grad_gain_sum).reshape(-1), local_sq[None]])
    tail = over_all(tail + 0.0 * token(*g_inner, *g_gate)[0])
    grad_gain = tail[:model]
    grad_norm = jnp.sqrt(tail[model] + jnp.sum(grad_gain * grad_gain))
    clip_scale = CLIP_LIMIT / jnp.maximum(grad_norm, CLIP_LIMIT)

    grad_out = jnp.concatenate(crossed(g_out, half_at), -1).astype(f32)
    in_pieces = (*g_inner, *g_gate)
    small_back = lax.all_gather(send(g_small.astype(bf16), small_pairs, True), "p")
    small_back = small_back.reshape(chans, 2, -1, own).transpose(2, 1, 0, 3)
    small_back = small_back.reshape(-1, chan_width).astype(f32) + 0.0 * tail[model]
    grad_x = small_back[: 3 * x_width].reshape(3, x_width, chan_width)
    grad_dt = small_back[3 * x_width : 3 * x_width + 3 * rank].reshape(3, rank, chan_width)
    grad_dt = lax.dynamic_slice_in_dim(grad_dt, s_at * dt_rows, dt_rows, 1)
    grad_chan = small_back[3 * x_width + 3 * rank :]

    tok_float = tokens_in.astype(f32)
    mixed = (tok_float + outs).astype(bf16)
    d_own = rows_back
    x_hat_own = tok_float * inv_own
    d_hat = d_own * gain_part
    mean = over_chans(jnp.sum(d_hat * x_hat_own, axis=-1))[..., None] / model
    input_grad = cotangent.astype(f32) + inv_own * (d_hat - x_hat_own * mean)

    dt_new, dt_first_new, dt_second_new = adam_update(
        dt_weight, grad_dt, dt_first, dt_second, clip_scale, rank ** (-0.5)
    )
    out_new, out_first_new, out_second_new = adam_update(
        out_weight, grad_out, out_first, out_second, clip_scale, inner_all ** (-0.5)
    )
    x_new, x_first_new, x_second_new = adam_update(
        x_weight, grad_x, x_first, x_second, clip_scale, inner_all ** (-0.5)
    )
    chan_new, chan_first_new, chan_second_new = adam_update(
        channel_params, grad_chan, channel_first, channel_second, clip_scale, 0.5
    )
    gain_new, gain_first_new, gain_second_new = adam_update(
        gain, grad_gain, gain_first, gain_second, clip_scale, 0.5
    )
    grad_in, in_new, in_first_new, in_second_new = adam(
        after(owner_flag, x_new, chan_new, dt_new), clip_scale[None], in_weight, in_first, in_second, in_pieces, model ** (-0.5)
    )
    return (
        mixed, input_grad, grad_norm,
        grad_in, in_new, in_first_new, in_second_new,
        grad_dt, dt_new, dt_first_new, dt_second_new,
        grad_out, out_new, out_first_new, out_second_new,
        grad_x, x_new, x_first_new, x_second_new,
        grad_chan, chan_new, chan_first_new, chan_second_new,
        grad_gain, gain_new, gain_first_new, gain_second_new,
        in_new.astype(bf16), dt_new.astype(bf16), out_new.astype(bf16), x_new.astype(bf16),
    )


def solution(mesh):
    chans = mesh.shape["ch"]
    parts = 2 * chans
    groups = mesh.shape["seq"] // parts
    inside = Mesh(mesh.devices.reshape(groups, parts, chans), ("t", "p", "c"))
    seq = ("t", "p")
    tok = P(None, seq, "c")
    wide = P(None, seq, None, "c")
    rows = P(None, seq, "c")
    flat = P(None, None, "c")
    chan = P(None, "c")
    return jax.shard_map(
        functools.partial(body, groups, parts, chans),
        mesh=inside,
        in_specs=(tok, P(None, seq), P(), tok)
        + (wide,) * 3 + (rows,) * 3 + (rows,) * 3 + (flat,) * 3 + (chan,) * 3 + (P(),) * 3,
        out_specs=(tok, tok, P())
        + (wide,) * 4 + (rows,) * 4 + (rows,) * 4 + (flat,) * 4 + (chan,) * 4 + (P(),) * 4
        + (wide, rows, rows, flat),
        check_vma=False,
    )
```
